32 devices in a mesh: tm: 4 (over y, core), seq: 8 (over z, x).
Axes of the slice: x: 2, y: 2, z: 4, core: 2. Of those that a mesh axis runs over, the one named last changes fastest.
Arguments:
- queries: bfloat16 [4, 192, 4096], P('tm', 'seq'), may hold values from -144 to 144
- keys_proj: bfloat16 [4, 192, 4096], P('tm', 'seq'), may hold values from -12 to 12
- values: bfloat16 [4, 192, 4096], P('tm', 'seq'), may hold values from -4 to 4
- hidden: bfloat16 [4, 192, 4096], P('tm', 'seq'), may hold values from -4 to 4
- fresh_latent: bfloat16 [192, 4096], P('seq'), may hold values from -4 to 4
- gate_table: float32 [50, 4096], replicated, may hold values from 0.5 to 2.5
- noise_step: int32 [4], P('tm'), may hold values from 0 to 49, as said below
- pattern: int32 [4, 4], replicated, may hold values from 0 to 1, as said below
Outputs:
- advanced: bfloat16 [4, 192, 4096], P('tm', 'seq')
- next_cache: bfloat16 [4, 2, 192, 4096], P('tm', None, None, 'seq')
The draws below stay inside these ranges and needn't reach their ends.
Inputs may be any that keep to these rules, and one draw needn't show every extreme that they name: pattern[i][0] is 1 for every i, and pattern[i][j] is 0 where j > i. noise_step[0] is 0, noise_step[3] is 49, and all 4 values are distinct.
All inputs are finite; a program needn't handle non-finite values.
Results may differ from the reference program's by a relative error of at most 0.0036.
Values may be sent and summed in bfloat16 or wider, within the bound.
No kernel may reach another device: no remote copies, remote signals or barrier semaphores. Data moves between devices by JAX's collectives and lax.ppermute only.
A program may use at most 64 MiB of HBM per device.

```python
import math
import jax
import jax.numpy as jnp
from jax import lax

HD = 128
HEADS = 32
STEPS = 50
WID = 4096
GROUPS = 4
GROUP_TOK = 192


def paired_draw(key):
    base_keys = jnp.clip(jax.random.normal(jax.random.fold_in(key, 101), (GROUPS, GROUP_TOK, WID), jnp.float32), -4.0, 4.0)
    base_queries = 2.0 * jnp.clip(jax.random.normal(jax.random.fold_in(key, 202), (GROUPS, GROUP_TOK, WID), jnp.float32), -4.0, 4.0)
    keys_out = base_keys
    queries_out = base_queries
    return (queries_out, keys_out)


def draw_queries(key, part):
    return paired_draw(key)[0].astype(jnp.bfloat16)


def draw_keys_proj(key, part):
    return paired_draw(key)[1].astype(jnp.bfloat16)


def draw_pattern(key, part):
    coins = jax.random.randint(jax.random.fold_in(key, 404), (GROUPS, GROUPS), 0, 2, jnp.int32)
    row_index = jnp.arange(GROUPS, dtype=jnp.int32)[:, None]
    col_index = jnp.arange(GROUPS, dtype=jnp.int32)[None, :]
    return jnp.where(col_index == 0, 1, jnp.where(col_index <= row_index, coins, 0)).astype(jnp.int32)


def draw_noise_step(key, part):
    middle = 1 + jax.random.permutation(jax.random.fold_in(key, 505), STEPS - 2)[:GROUPS - 2].astype(jnp.int32)
    first = jnp.zeros((1,), jnp.int32)
    final = jnp.full((1,), STEPS - 1, jnp.int32)
    return jnp.concatenate([first, middle, final], axis=0).astype(jnp.int32)


def steps_of(rng, shape, shards, least, largest):
    def one(position, shards_of):
        steps = jax.random.uniform(jax.random.fold_in(jax.random.fold_in(rng, 6), position), (shards_of,), jnp.float32, least / len(shards), largest / len(shards))
        return jnp.repeat(jnp.exp(steps), shape[position] // shards_of).reshape((-1,) + (1,) * (len(shape) - position - 1))

    loudness = one(*shards[0])
    for cut in shards[1:]:
        loudness = loudness * one(*cut)
    return loudness


def noise(key, dims, deviation, most, shards=(), kind=jnp.bfloat16):
    array = deviation * jax.random.normal(key, dims, jnp.float32)
    if shards:
        array = array * steps_of(key, dims, shards, -0.22, 0.18)
    return jnp.clip(array, -most, most).astype(kind)


def setup_inputs(seed: int = 0) -> dict:
    splits = jax.random.split(jax.random.key(seed), 9)
    return {
        "queries": draw_queries(jax.random.fold_in(splits[8], 71), 0),
        "keys_proj": draw_keys_proj(jax.random.fold_in(splits[8], 71), 0),
        "values": noise(splits[2], (GROUPS, GROUP_TOK, WID), 1.0, 4.0, ((0, 4), (1, 8))),
        "hidden": noise(splits[3], (GROUPS, GROUP_TOK, WID), 1.0, 4.0, ((0, 4), (1, 8))),
        "fresh_latent": noise(splits[4], (GROUP_TOK, WID), 1.0, 4.0, ((0, 8),)),
        "gate_table": jnp.clip(jax.random.uniform(splits[5], (STEPS, WID), jnp.float32, 0.5, 2.5), 0.5, 2.5),
        "noise_step": draw_noise_step(jax.random.fold_in(splits[8], 71), 0),
        "pattern": draw_pattern(jax.random.fold_in(splits[8], 71), 0),
    }


def group_attention(query_group, reach_row, key_heads, value_heads):
    query_heads = jnp.transpose(query_group.reshape(GROUP_TOK, HEADS, HD), (1, 0, 2))
    live = jnp.repeat(reach_row, GROUP_TOK) > 0
    scale_factor = 1.0 / math.sqrt(HD)

    def one_head(inputs):
        query_one, key_one, value_one = inputs
        scores = jnp.dot(query_one, key_one.T, preferred_element_type=jnp.float32) * scale_factor
        scores = jnp.where(live[None, :], scores, jnp.float32(-1e+30))
        highest = lax.optimization_barrier(jnp.max(scores, axis=-1, keepdims=True))
        raised = jnp.exp(scores - highest)
        total = lax.optimization_barrier(jnp.sum(raised, axis=-1))
        probs = raised.astype(jnp.bfloat16)
        numer = jnp.dot(probs, value_one, preferred_element_type=jnp.float32)
        return numer / total[:, None]
    result = lax.map(one_head, (query_heads, key_heads, value_heads))
    return jnp.transpose(result, (1, 0, 2)).reshape(GROUP_TOK, WID).astype(jnp.bfloat16)

def reference(queries, keys_proj, values, hidden, fresh_latent, gate_table, noise_step, pattern):
    key_heads = jnp.transpose(keys_proj.reshape(GROUPS * GROUP_TOK, HEADS, HD), (1, 0, 2))
    value_heads = jnp.transpose(values.reshape(GROUPS * GROUP_TOK, HEADS, HD), (1, 0, 2))

    def per_group(inputs):
        query_group, reach_row = inputs
        return group_attention(query_group, reach_row, key_heads, value_heads)
    attended = lax.map(per_group, (queries, pattern))
    gates = gate_table[noise_step]
    updated = (hidden.astype(jnp.float32) + gates[:, None, :] * attended.astype(jnp.float32)).astype(jnp.bfloat16)
    advanced = jnp.concatenate([updated[1:], fresh_latent[None]], axis=0)
    blank = jnp.zeros((1, GROUP_TOK, WID), keys_proj.dtype)
    next_keys = jnp.concatenate([keys_proj[1:], blank], axis=0)
    next_values = jnp.concatenate([values[1:], blank], axis=0)
    next_cache = jnp.stack([next_keys, next_values], axis=1)
    return (advanced, next_cache)
```

```python
import functools
import math

import jax
import jax.numpy as jnp
from jax import lax
from jax.experimental import pallas as pl
from jax.experimental.pallas import tpu as pltpu
from jax.sharding import PartitionSpec as P

HD = 128
BOTH = ("tm", "seq")
VMEM = pltpu.VMEM
SMEM = pltpu.SMEM


def shifted(block, axis, distance):
    devices = range(lax.axis_size(axis))
    route = [(i - distance, i) for i in devices if i - distance in devices]
    return lax.ppermute(block, axis, route)


def pack_kernel(seq_count, noise_ref, q_ref, k_ref, v_ref, h_ref, gate_ref, out_ref, moved_ref):
    tok = q_ref.shape[1]
    wide = out_ref.shape[1] // 3
    count = out_ref.shape[0] // tok
    tm_count = count // seq_count
    for pair in range(count // 2):
        for place, ref in enumerate((q_ref, k_ref, v_ref)):
            rows = []
            for dest in (2 * pair, 2 * pair + 1):
                start = ((dest % seq_count) * tm_count + dest // seq_count) * wide
                rows.append(ref[0, :, start : start + wide].astype(jnp.float32))
            both = jnp.concatenate(rows, axis=0).astype(jnp.bfloat16)
            out_ref[2 * pair * tok : 2 * (pair + 1) * tok, place * wide : (place + 1) * wide] = both
    gate = gate_ref[pl.ds(noise_ref[0], 1), :]
    high = gate.astype(jnp.bfloat16).astype(jnp.float32)
    middle = (gate - high).astype(jnp.bfloat16).astype(jnp.float32)
    low = gate - high - middle
    parts = jnp.concatenate([high, middle, low, jnp.zeros((5, gate.shape[1]), jnp.float32)], axis=0)
    moved_ref[...] = jnp.concatenate([h_ref[0].astype(jnp.float32), parts], axis=0).astype(jnp.bfloat16)


def attend_kernel(tok, pattern_ref, x_ref, out_ref, cache_ref):
    groups = cache_ref.shape[0]
    wide = out_ref.shape[1]
    rows = x_ref.shape[0] // groups
    factor = math.log2(math.e) / math.sqrt(HD)
    for group in range(1, groups):
        span = (group + 1) * rows
        column = lax.broadcasted_iota(jnp.int32, (1, span), 1)
        kept = jnp.zeros((1, span), jnp.int32)
        for source in range(group + 1):
            inside = (column >= source * rows) & (column < (source + 1) * rows)
            kept = jnp.where(inside, pattern_ref[group, source], kept)
        for head in range(0, wide, HD):
            query = x_ref[group * rows : span, head : head + HD]
            key = x_ref[:span, wide + head : wide + head + HD]
            value = x_ref[:span, 2 * wide + head : 2 * wide + head + HD]
            scores = lax.dot_general(
                query, key, (((1,), (1,)), ((), ())), preferred_element_type=jnp.float32
            )
            scores = jnp.where(kept > 0, scores, -1e30)
            highest = jnp.max(scores, axis=-1, keepdims=True)
            raised = jnp.exp2((scores - highest) * factor)
            total = jnp.sum(raised, axis=-1, keepdims=True)
            numer = jnp.dot(raised.astype(jnp.bfloat16), value, preferred_element_type=jnp.float32)
            out_ref[(group - 1) * rows : group * rows, head : head + HD] = (numer / total).astype(
                jnp.bfloat16
            )
        cache_ref[group - 1] = x_ref[group * rows : span, wide:]
    out_ref[(groups - 1) * rows :, :] = jnp.zeros((rows, wide), jnp.bfloat16)
    cache_ref[groups - 1] = jnp.zeros((rows, 2 * wide), jnp.bfloat16)


def cache_kernel(in_ref, out_ref):
    wide = in_ref.shape[2] // 2
    for part in range(in_ref.shape[0]):
        for kind in range(2):
            out_ref[0, kind, :, part * wide : (part + 1) * wide] = in_ref[
                part, :, kind * wide : (kind + 1) * wide
            ]


def update_kernel(seq_count, tm_count, att_ref, moved_ref, fresh_ref, out_ref):
    tok = out_ref.shape[1]
    wide = att_ref.shape[1]
    count = att_ref.shape[0] // tok
    last = lax.axis_index("tm") == tm_count - 1

    @pl.when(last)
    def take_fresh():
        out_ref[0] = fresh_ref[...]

    @pl.when(jnp.logical_not(last))
    def take_update():
        for pair in range(count // 2):
            rows = att_ref[2 * pair * tok : 2 * (pair + 1) * tok, :].astype(jnp.float32)
            for half in range(2):
                source = 2 * pair + half
                start = ((source % seq_count) * tm_count + source // seq_count) * wide
                moved = moved_ref[:, start : start + wide].astype(jnp.float32)
                gate = (moved[tok : tok + 1] + moved[tok + 1 : tok + 2]) + moved[tok + 2 : tok + 3]
                result = moved[:tok] + gate * rows[half * tok : (half + 1) * tok]
                out_ref[0, :, start : start + wide] = result.astype(jnp.bfloat16)


def whole(space=VMEM):
    return pl.BlockSpec(memory_space=space)


def spread_body(queries, keys_proj, values, hidden, fresh_latent, gate_table, noise_step, pattern):
    tm_count, seq_count = lax.axis_size("tm"), lax.axis_size("seq")
    count = tm_count * seq_count
    _, tok, width = queries.shape
    wide = width // count
    group_tok = tok * seq_count
    kind = queries.dtype

    packed, residual = pl.pallas_call(
        functools.partial(pack_kernel, seq_count),
        out_shape=(
            jax.ShapeDtypeStruct((count * tok, 3 * wide), kind),
            jax.ShapeDtypeStruct((tok + 8, width), kind),
        ),
        in_specs=[whole(SMEM)] + [whole()] * 5,
        out_specs=(whole(), whole()),
        name="pack",
    )(noise_step, queries, keys_proj, values, hidden, gate_table)

    exchanged = lax.all_to_all(packed, BOTH, split_axis=0, concat_axis=0, tiled=True)
    moved = shifted(residual, "tm", -1)

    attended, handed = pl.pallas_call(
        functools.partial(attend_kernel, tok),
        out_shape=(
            jax.ShapeDtypeStruct((count * tok, wide), kind),
            jax.ShapeDtypeStruct((tm_count, group_tok, 2 * wide), kind),
        ),
        in_specs=[whole(SMEM), whole()],
        out_specs=(whole(), whole()),
        name="attend",
    )(pattern, exchanged)

    returned = lax.all_to_all(attended, BOTH, split_axis=0, concat_axis=0, tiled=True)
    handed = lax.all_to_all(handed, "tm", split_axis=0, concat_axis=0, tiled=True)

    next_cache = pl.pallas_call(
        cache_kernel,
        out_shape=jax.ShapeDtypeStruct((1, 2, group_tok, tm_count * wide), kind),
        in_specs=[whole()],
        out_specs=whole(),
        name="cache",
    )(handed)
    advanced = pl.pallas_call(
        functools.partial(update_kernel, seq_count, tm_count),
        out_shape=jax.ShapeDtypeStruct((1, tok, width), kind),
        in_specs=[whole()] * 3,
        out_specs=whole(),
        name="update",
    )(returned, moved, fresh_latent)
    return (advanced, next_cache)


def absorb(state, query_heads, key_piece, value_piece, scale_factor):
    accum, totals, highest = state
    row_count, head_count, head_dim = query_heads.shape
    key_heads = key_piece.reshape(key_piece.shape[0], head_count, head_dim)
    value_heads = value_piece.reshape(value_piece.shape[0], head_count, head_dim)
    scores = (
        jnp.einsum("qhd,khd->qhk", query_heads, key_heads, preferred_element_type=jnp.float32)
        * scale_factor
    )
    raised = jnp.maximum(highest, jnp.max(scores, axis=-1))
    fade = jnp.exp(highest - raised)
    weights = jnp.exp(scores - raised[..., None])
    totals = totals * fade + jnp.sum(weights, axis=-1)
    accum = accum * fade[..., None] + jnp.einsum(
        "qhk,khd->qhd",
        weights.astype(jnp.bfloat16),
        value_heads,
        preferred_element_type=jnp.float32,
    )
    return (accum, totals, raised)


def gather_body(queries, keys_proj, values, hidden, fresh_latent, gate_table, noise_step, pattern):
    group_index = lax.axis_index("tm")
    final_index = lax.axis_size("tm") - 1
    query_tok, key_tok, value_tok = (
        lax.all_to_all(queries[0], "seq", split_axis=1, concat_axis=0, tiled=True),
        lax.all_to_all(keys_proj[0], "seq", split_axis=1, concat_axis=0, tiled=True),
        lax.all_to_all(values[0], "seq", split_axis=1, concat_axis=0, tiled=True),
    )
    row_count, local_width = query_tok.shape
    head_count = local_width // HD
    query_heads = query_tok.reshape(row_count, head_count, HD)
    scale_factor = 1.0 / math.sqrt(HD)
    reach = lax.dynamic_index_in_dim(pattern, group_index, 0, keepdims=False)
    start_state = (
        jnp.zeros((row_count, head_count, HD), jnp.float32),
        jnp.zeros((row_count, head_count), jnp.float32),
        jnp.full((row_count, head_count), -1e30, jnp.float32),
    )

    def one_block(current, inputs):
        key_block, value_block, flag = inputs
        return (
            lax.cond(
                flag > 0,
                lambda state: absorb(state, query_heads, key_block, value_block, scale_factor),
                lambda state: state,
                current,
            ),
            None,
        )

    key_piece = lax.all_gather(key_tok, "tm", axis=0, tiled=False)
    value_piece = lax.all_gather(value_tok, "tm", axis=0, tiled=False)
    state, unused = lax.scan(one_block, start_state, (key_piece, value_piece, reach))
    cache_keys, cache_values = shifted((key_tok, value_tok), "tm", -1)
    accum, totals, highest = state
    attended_head = (accum / totals[..., None]).reshape(row_count, local_width).astype(jnp.bfloat16)
    attended = lax.all_to_all(attended_head, "seq", split_axis=0, concat_axis=1, tiled=True)
    gate_row = lax.dynamic_index_in_dim(gate_table, noise_step[0], 0, keepdims=False)
    updated = (
        hidden[0].astype(jnp.float32) + gate_row[None, :] * attended.astype(jnp.float32)
    ).astype(jnp.bfloat16)
    moved = shifted(updated, "tm", -1)
    advanced = jnp.where(group_index == final_index, fresh_latent, moved)[None]
    next_cache = jnp.stack([cache_keys, cache_values], axis=0)[None]
    return (advanced, next_cache)


def body(queries, *others):
    tm_count, seq_count = lax.axis_size("tm"), lax.axis_size("seq")
    _, tok, width = queries.shape
    count = tm_count * seq_count
    even = width % (count * HD) == 0 and tok % 8 == 0 and seq_count % 2 == 0
    return (spread_body if even else gather_body)(queries, *others)


def solution(mesh):
    placed = (
        P("tm", "seq", None),
        P("tm", "seq", None),
        P("tm", "seq", None),
        P("tm", "seq", None),
        P("seq", None),
        P(),
        P("tm"),
        P(),
    )
    return jax.shard_map(
        body,
        mesh=mesh,
        in_specs=placed,
        out_specs=(P("tm", "seq", None), P("tm", None, None, "seq")),
        check_vma=False,
    )
```

```python
import functools
import math

import jax
import jax.numpy as jnp
from jax import lax
from jax.experimental import pallas as pl
from jax.experimental.pallas import tpu as pltpu
from jax.sharding import PartitionSpec as P

HD = 128
BOTH = ("tm", "seq")
VMEM = pltpu.VMEM
SMEM = pltpu.SMEM


def shifted(block, axis, distance):
    devices = range(lax.axis_size(axis))
    route = [(i - distance, i) for i in devices if i - distance in devices]
    return lax.ppermute(block, axis, route)


def pack_kernel(seq_count, q_ref, k_ref, v_ref, out_ref):
    tok = q_ref.shape[1]
    wide = out_ref.shape[1] // 3
    count = out_ref.shape[0] // tok
    tm_count = count // seq_count
    for place, ref in enumerate((q_ref, k_ref, v_ref)):
        for pair in range(count // 2):
            rows = []
            for dest in (2 * pair, 2 * pair + 1):
                start = ((dest % seq_count) * tm_count + dest // seq_count) * wide
                rows.append(ref[0, :, start : start + wide].astype(jnp.float32))
            both = jnp.concatenate(rows, axis=0).astype(jnp.bfloat16)
            out_ref[2 * pair * tok : 2 * (pair + 1) * tok, place * wide : (place + 1) * wide] = both


def residual_kernel(noise_ref, h_ref, gate_ref, out_ref):
    gate = gate_ref[pl.ds(noise_ref[0], 1), :]
    high = gate.astype(jnp.bfloat16).astype(jnp.float32)
    middle = (gate - high).astype(jnp.bfloat16).astype(jnp.float32)
    low = gate - high - middle
    parts = jnp.concatenate([high, middle, low, jnp.zeros((5, gate.shape[1]), jnp.float32)], axis=0)
    out_ref[...] = jnp.concatenate([h_ref[0].astype(jnp.float32), parts], axis=0).astype(jnp.bfloat16)


def attend_kernel(groups, pattern_ref, x_ref, out_ref, *hand_refs):
    wide = out_ref.shape[1]
    rows = x_ref.shape[0] // groups
    factor = math.log2(math.e) / math.sqrt(HD)
    here = lax.axis_index("tm")
    for distance, hand_ref in enumerate(hand_refs, 1):
        group = lax.rem(here + groups - distance + 1, groups)
        hand_ref[...] = x_ref[pl.ds(pl.multiple_of(group * rows, rows), rows), wide:]
    for group in range(1, groups):
        span = (group + 1) * rows
        column = lax.broadcasted_iota(jnp.int32, (1, span), 1)
        kept = jnp.zeros((1, span), jnp.int32)
        for source in range(group + 1):
            inside = (column >= source * rows) & (column < (source + 1) * rows)
            kept = jnp.where(inside, pattern_ref[group, source], kept)
        for head in range(0, wide, HD):
            query = x_ref[group * rows : span, head : head + HD]
            key = x_ref[:span, wide + head : wide + head + HD]
            value = x_ref[:span, 2 * wide + head : 2 * wide + head + HD]
            scores = lax.dot_general(
                query, key, (((1,), (1,)), ((), ())), preferred_element_type=jnp.float32
            )
            scores = jnp.where(kept > 0, scores, -1e30)
            highest = jnp.max(scores, axis=-1, keepdims=True)
            raised = jnp.exp2((scores - highest) * factor)
            total = jnp.sum(raised, axis=-1, keepdims=True)
            numer = jnp.dot(raised.astype(jnp.bfloat16), value, preferred_element_type=jnp.float32)
            out_ref[(group - 1) * rows : group * rows, head : head + HD] = (numer / total).astype(
                jnp.bfloat16
            )
    out_ref[(groups - 1) * rows :, :] = jnp.zeros((rows, wide), jnp.bfloat16)


def cache_kernel(x_ref, *refs):
    hand_refs, out_ref = refs[:-1], refs[-1]
    groups = len(refs)
    wide = x_ref.shape[1] // 3
    rows = out_ref.shape[2]
    here = lax.axis_index("tm")

    @pl.when(here == groups - 1)
    def clear():
        out_ref[...] = jnp.zeros_like(out_ref)

    @pl.when(here < groups - 1)
    def place():
        own = x_ref[pl.ds(pl.multiple_of((here + 1) * rows, rows), rows), wide:]
        for distance, block in enumerate((own,) + hand_refs):
            source = lax.rem(here + distance, groups)
            lanes = pl.ds(pl.multiple_of(source * wide, wide), wide)
            for kind in range(2):
                out_ref[0, kind, :, lanes] = block[:, kind * wide : (kind + 1) * wide]


def update_kernel(seq_count, tm_count, att_ref, moved_ref, fresh_ref, out_ref):
    tok = out_ref.shape[1]
    wide = att_ref.shape[1]
    count = att_ref.shape[0] // tok
    last = lax.axis_index("tm") == tm_count - 1

    @pl.when(last)
    def take_fresh():
        out_ref[0] = fresh_ref[...]

    @pl.when(jnp.logical_not(last))
    def take_update():
        for pair in range(count // 2):
            rows = att_ref[2 * pair * tok : 2 * (pair + 1) * tok, :].astype(jnp.float32)
            for half in range(2):
                source = 2 * pair + half
                start = ((source % seq_count) * tm_count + source // seq_count) * wide
                moved = moved_ref[:, start : start + wide].astype(jnp.float32)
                gate = (moved[tok : tok + 1] + moved[tok + 1 : tok + 2]) + moved[tok + 2 : tok + 3]
                result = moved[:tok] + gate * rows[half * tok : (half + 1) * tok]
                out_ref[0, :, start : start + wide] = result.astype(jnp.bfloat16)


def whole(space=VMEM):
    return pl.BlockSpec(memory_space=space)


def run(kernel, name, out_shape, specs, operands, flops=0):
    def size(a):
        return math.prod(a.shape) * a.dtype.itemsize

    outs = jax.tree.leaves(out_shape)
    moved = sum(map(size, operands)) + sum(map(size, outs))
    return pl.pallas_call(
        kernel,
        out_shape=out_shape,
        in_specs=specs,
        out_specs=jax.tree.map(lambda a: whole(), out_shape),
        compiler_params=pltpu.CompilerParams(vmem_limit_bytes=4 * moved + (4 << 20)),
        cost_estimate=pl.CostEstimate(flops=flops, bytes_accessed=moved, transcendentals=0),
        name=name,
    )(*operands)


def spread_body(queries, keys_proj, values, hidden, fresh_latent, gate_table, noise_step, pattern):
    tm_count, seq_count = lax.axis_size("tm"), lax.axis_size("seq")
    count = tm_count * seq_count
    _, tok, width = queries.shape
    wide = width // count
    group_tok = tok * seq_count
    shape = functools.partial(jax.ShapeDtypeStruct, dtype=queries.dtype)

    packed = run(
        functools.partial(pack_kernel, seq_count),
        "pack",
        shape((count * tok, 3 * wide)),
        [whole()] * 3,
        (queries, keys_proj, values),
    )
    exchanged = lax.all_to_all(packed, BOTH, split_axis=0, concat_axis=0, tiled=True)

    residual = run(
        residual_kernel,
        "residual",
        shape((tok + 8, width)),
        [whole(SMEM)] + [whole()] * 2,
        (noise_step, hidden, gate_table),
    )
    moved = shifted(residual, "tm", -1)

    attended, *hands = run(
        functools.partial(attend_kernel, tm_count),
        "attend",
        [shape((count * tok, wide))] + [shape((group_tok, 2 * wide))] * (tm_count - 1),
        [whole(SMEM), whole()],
        (pattern, exchanged),
        flops=2 * count * tok * count * tok * wide,
    )
    returned = lax.all_to_all(attended, BOTH, split_axis=0, concat_axis=0, tiled=True)
    handed = []
    for distance, hand in enumerate(hands, 1):
        route = [(i, (i - distance) % tm_count) for i in range(tm_count)]
        handed.append(lax.ppermute(hand, "tm", [(i, j) for i, j in route if j < tm_count - 1]))

    next_cache = run(
        cache_kernel,
        "cache",
        shape((1, 2, group_tok, tm_count * wide)),
        [whole()] * tm_count,
        (exchanged, *handed),
    )
    advanced = run(
        functools.partial(update_kernel, seq_count, tm_count),
        "update",
        shape((1, tok, width)),
        [whole()] * 3,
        (returned, moved, fresh_latent),
    )
    return (advanced, next_cache)


def absorb(state, query_heads, key_piece, value_piece, scale_factor):
    accum, totals, highest = state
    row_count, head_count, head_dim = query_heads.shape
    key_heads = key_piece.reshape(key_piece.shape[0], head_count, head_dim)
    value_heads = value_piece.reshape(value_piece.shape[0], head_count, head_dim)
    scores = (
        jnp.einsum("qhd,khd->qhk", query_heads, key_heads, preferred_element_type=jnp.float32)
        * scale_factor
    )
    raised = jnp.maximum(highest, jnp.max(scores, axis=-1))
    fade = jnp.exp(highest - raised)
    weights = jnp.exp(scores - raised[..., None])
    totals = totals * fade + jnp.sum(weights, axis=-1)
    accum = accum * fade[..., None] + jnp.einsum(
        "qhk,khd->qhd",
        weights.astype(jnp.bfloat16),
        value_heads,
        preferred_element_type=jnp.float32,
    )
    return (accum, totals, raised)


def gather_body(queries, keys_proj, values, hidden, fresh_latent, gate_table, noise_step, pattern):
    group_index = lax.axis_index("tm")
    final_index = lax.axis_size("tm") - 1
    query_tok, key_tok, value_tok = (
        lax.all_to_all(queries[0], "seq", split_axis=1, concat_axis=0, tiled=True),
        lax.all_to_all(keys_proj[0], "seq", split_axis=1, concat_axis=0, tiled=True),
        lax.all_to_all(values[0], "seq", split_axis=1, concat_axis=0, tiled=True),
    )
    row_count, local_width = query_tok.shape
    head_count = local_width // HD
    query_heads = query_tok.reshape(row_count, head_count, HD)
    scale_factor = 1.0 / math.sqrt(HD)
    reach = lax.dynamic_index_in_dim(pattern, group_index, 0, keepdims=False)
    start_state = (
        jnp.zeros((row_count, head_count, HD), jnp.float32),
        jnp.zeros((row_count, head_count), jnp.float32),
        jnp.full((row_count, head_count), -1e30, jnp.float32),
    )

    def one_block(current, inputs):
        key_block, value_block, flag = inputs
        return (
            lax.cond(
                flag > 0,
                lambda state: absorb(state, query_heads, key_block, value_block, scale_factor),
                lambda state: state,
                current,
            ),
            None,
        )

    key_piece = lax.all_gather(key_tok, "tm", axis=0, tiled=False)
    value_piece = lax.all_gather(value_tok, "tm", axis=0, tiled=False)
    state, unused = lax.scan(one_block, start_state, (key_piece, value_piece, reach))
    cache_keys, cache_values = shifted((key_tok, value_tok), "tm", -1)
    accum, totals, highest = state
    attended_head = (accum / totals[..., None]).reshape(row_count, local_width).astype(jnp.bfloat16)
    attended = lax.all_to_all(attended_head, "seq", split_axis=0, concat_axis=1, tiled=True)
    gate_row = lax.dynamic_index_in_dim(gate_table, noise_step[0], 0, keepdims=False)
    updated = (
        hidden[0].astype(jnp.float32) + gate_row[None, :] * attended.astype(jnp.float32)
    ).astype(jnp.bfloat16)
    moved = shifted(updated, "tm", -1)
    advanced = jnp.where(group_index == final_index, fresh_latent, moved)[None]
    next_cache = jnp.stack([cache_keys, cache_values], axis=0)[None]
    return (advanced, next_cache)


def body(queries, *others):
    tm_count, seq_count = lax.axis_size("tm"), lax.axis_size("seq")
    _, tok, width = queries.shape
    count = tm_count * seq_count
    even = width % (count * HD) == 0 and tok % 8 == 0 and seq_count % 2 == 0
    return (spread_body if even else gather_body)(queries, *others)


def solution(mesh):
    placed = (
        P("tm", "seq", None),
        P("tm", "seq", None),
        P("tm", "seq", None),
        P("tm", "seq", None),
        P("seq", None),
        P(),
        P("tm"),
        P(),
    )
    return jax.shard_map(
        body,
        mesh=mesh,
        in_specs=placed,
        out_specs=(P("tm", "seq", None), P("tm", None, None, "seq")),
        check_vma=False,
    )
```

```python
import functools
import math

import jax
import jax.numpy as jnp
from jax import lax
from jax.experimental import pallas as pl
from jax.experimental.pallas import tpu as pltpu
from jax.sharding import PartitionSpec as P

HD = 128
BOTH = ("tm", "seq")
VMEM = pltpu.VMEM
SMEM = pltpu.SMEM


def shifted(block, axis, distance):
    devices = range(lax.axis_size(axis))
    route = [(i - distance, i) for i in devices if i - distance in devices]
    return lax.ppermute(block, axis, route)


def pack_kernel(seq_count, q_hbm, k_hbm, v_hbm, out_ref, *scratch):
    held, sems = scratch
    tok = held.shape[1]
    wide = out_ref.shape[1] // 3
    count = out_ref.shape[0] // tok
    tm_count = count // seq_count
    copies = [
        pltpu.make_async_copy(ref.at[0], held.at[place], sems.at[place])
        for place, ref in enumerate((q_hbm, k_hbm, v_hbm))
    ]
    for copy in copies:
        copy.start()
    for place, copy in enumerate(copies):
        copy.wait()
        for pair in range(count // 2):
            rows = []
            for dest in (2 * pair, 2 * pair + 1):
                start = ((dest % seq_count) * tm_count + dest // seq_count) * wide
                rows.append(held[place, :, start : start + wide].astype(jnp.float32))
            both = jnp.concatenate(rows, axis=0).astype(jnp.bfloat16)
            out_ref[2 * pair * tok : 2 * (pair + 1) * tok, place * wide : (place + 1) * wide] = both


def residual_kernel(noise_ref, h_ref, gate_ref, after_ref, out_ref):
    gate = gate_ref[pl.ds(noise_ref[0], 1), :]
    high = gate.astype(jnp.bfloat16).astype(jnp.float32)
    middle = (gate - high).astype(jnp.bfloat16).astype(jnp.float32)
    low = gate - high - middle
    parts = jnp.concatenate([high, middle, low, jnp.zeros((5, gate.shape[1]), jnp.float32)], axis=0)
    out_ref[...] = jnp.concatenate([h_ref[0].astype(jnp.float32), parts], axis=0).astype(jnp.bfloat16)


def partner(here, distance, groups):
    return here ^ distance if groups & (groups - 1) == 0 else (here + groups - distance) % groups


def attend_kernel(groups, pattern_ref, x_ref, after_ref, out_ref, *hand_refs):
    wide = out_ref.shape[1]
    rows = x_ref.shape[0] // groups
    factor = math.log2(math.e) / math.sqrt(HD)
    here = lax.axis_index("tm")
    for distance, hand_ref in enumerate(hand_refs, 1):
        group = lax.rem(partner(here, distance, groups) + 1, groups)
        hand_ref[...] = x_ref[pl.ds(pl.multiple_of(group * rows, rows), rows), wide:]
    for group in range(1, groups):
        span = (group + 1) * rows
        column = lax.broadcasted_iota(jnp.int32, (1, span), 1)
        kept = jnp.zeros((1, span), jnp.int32)
        for source in range(group + 1):
            inside = (column >= source * rows) & (column < (source + 1) * rows)
            kept = jnp.where(inside, pattern_ref[group, source], kept)
        for head in range(0, wide, HD):
            query = x_ref[group * rows : span, head : head + HD]
            key = x_ref[:span, wide + head : wide + head + HD]
            value = x_ref[:span, 2 * wide + head : 2 * wide + head + HD]
            scores = lax.dot_general(
                query, key, (((1,), (1,)), ((), ())), preferred_element_type=jnp.float32
            )
            scores = jnp.where(kept > 0, scores, -1e30)
            highest = jnp.max(scores, axis=-1, keepdims=True)
            raised = jnp.exp2((scores - highest) * factor)
            total = jnp.sum(raised, axis=-1, keepdims=True)
            numer = jnp.dot(raised.astype(jnp.bfloat16), value, preferred_element_type=jnp.float32)
            out_ref[(group - 1) * rows : group * rows, head : head + HD] = (numer / total).astype(
                jnp.bfloat16
            )
    out_ref[(groups - 1) * rows :, :] = jnp.zeros((rows, wide), jnp.bfloat16)


def cache_kernel(x_ref, *refs):
    hand_refs, out_ref = refs[:-1], refs[-1]
    groups = len(refs)
    wide = x_ref.shape[1] // 3
    rows = out_ref.shape[2]
    here = lax.axis_index("tm")

    @pl.when(here == groups - 1)
    def clear():
        out_ref[...] = jnp.zeros_like(out_ref)

    @pl.when(here < groups - 1)
    def place():
        own = x_ref[pl.ds(pl.multiple_of((here + 1) * rows, rows), rows), wide:]
        for distance, block in enumerate((own,) + hand_refs):
            source = partner(here, groups - distance if groups & (groups - 1) else distance, groups)
            lanes = pl.ds(pl.multiple_of(source * wide, wide), wide)
            for kind in range(2):
                out_ref[0, kind, :, lanes] = block[:, kind * wide : (kind + 1) * wide]


def update_kernel(seq_count, tm_count, att_ref, moved_ref, fresh_ref, out_ref):
    tok = out_ref.shape[1]
    wide = att_ref.shape[1]
    count = att_ref.shape[0] // tok
    last = lax.axis_index("tm") == tm_count - 1

    @pl.when(last)
    def take_fresh():
        out_ref[0] = fresh_ref[...]

    @pl.when(jnp.logical_not(last))
    def take_update():
        for pair in range(count // 2):
            rows = att_ref[2 * pair * tok : 2 * (pair + 1) * tok, :].astype(jnp.float32)
            for half in range(2):
                source = 2 * pair + half
                start = ((source % seq_count) * tm_count + source // seq_count) * wide
                moved = moved_ref[:, start : start + wide].astype(jnp.float32)
                gate = (moved[tok : tok + 1] + moved[tok + 1 : tok + 2]) + moved[tok + 2 : tok + 3]
                result = moved[:tok] + gate * rows[half * tok : (half + 1) * tok]
                out_ref[0, :, start : start + wide] = result.astype(jnp.bfloat16)


def whole(space=VMEM):
    return pl.BlockSpec(memory_space=space)


def run(kernel, name, out_shape, specs, operands, flops=0, scratch=()):
    def size(a):
        return math.prod(a.shape) * a.dtype.itemsize

    outs = jax.tree.leaves(out_shape)
    moved = sum(map(size, operands)) + sum(map(size, outs))
    return pl.pallas_call(
        kernel,
        out_shape=out_shape,
        in_specs=specs,
        out_specs=jax.tree.map(lambda a: whole(), out_shape),
        scratch_shapes=scratch,
        compiler_params=pltpu.CompilerParams(vmem_limit_bytes=4 * moved + (4 << 20)),
        cost_estimate=pl.CostEstimate(flops=flops, bytes_accessed=moved, transcendentals=0),
        name=name,
    )(*operands)


def spread_body(queries, keys_proj, values, hidden, fresh_latent, gate_table, noise_step, pattern):
    tm_count, seq_count = lax.axis_size("tm"), lax.axis_size("seq")
    count = tm_count * seq_count
    _, tok, width = queries.shape
    wide = width // count
    group_tok = tok * seq_count
    shape = functools.partial(jax.ShapeDtypeStruct, dtype=queries.dtype)

    packed = run(
        functools.partial(pack_kernel, seq_count),
        "pack",
        shape((count * tok, 3 * wide)),
        [whole(pltpu.HBM)] * 3,
        [pltpu.with_memory_space_constraint(a, pltpu.HBM) for a in (queries, keys_proj, values)],
        scratch=[VMEM((3, tok, width), queries.dtype), pltpu.SemaphoreType.DMA((3,))],
    )
    exchanged = lax.all_to_all(packed, BOTH, split_axis=0, concat_axis=0, tiled=True)

    residual = run(
        residual_kernel,
        "residual",
        shape((tok + 8, width)),
        [whole(SMEM), whole(), whole(), whole(pl.ANY)],
        (noise_step, hidden, gate_table, packed),
    )
    moved = shifted(residual, "tm", -1)

    attended, *hands = run(
        functools.partial(attend_kernel, tm_count),
        "attend",
        [shape((count * tok, wide))] + [shape((group_tok, 2 * wide))] * (tm_count - 1),
        [whole(SMEM), whole(), whole(pl.ANY)],
        (pattern, exchanged, moved),
        flops=2 * count * tok * count * tok * wide,
    )
    returned = lax.all_to_all(attended, BOTH, split_axis=0, concat_axis=0, tiled=True)
    handed = []
    for distance, hand in enumerate(hands, 1):
        route = [(i, partner(i, distance, tm_count)) for i in range(tm_count)]
        handed.append(lax.ppermute(hand, "tm", [(i, j) for i, j in route if j < tm_count - 1]))

    next_cache = run(
        cache_kernel,
        "cache",
        shape((1, 2, group_tok, tm_count * wide)),
        [whole()] * tm_count,
        (exchanged, *handed),
    )
    advanced = run(
        functools.partial(update_kernel, seq_count, tm_count),
        "update",
        shape((1, tok, width)),
        [whole()] * 3,
        (returned, moved, fresh_latent),
    )
    return (advanced, next_cache)


def absorb(state, query_heads, key_piece, value_piece, scale_factor):
    accum, totals, highest = state
    row_count, head_count, head_dim = query_heads.shape
    key_heads = key_piece.reshape(key_piece.shape[0], head_count, head_dim)
    value_heads = value_piece.reshape(value_piece.shape[0], head_count, head_dim)
    scores = (
        jnp.einsum("qhd,khd->qhk", query_heads, key_heads, preferred_element_type=jnp.float32)
        * scale_factor
    )
    raised = jnp.maximum(highest, jnp.max(scores, axis=-1))
    fade = jnp.exp(highest - raised)
    weights = jnp.exp(scores - raised[..., None])
    totals = totals * fade + jnp.sum(weights, axis=-1)
    accum = accum * fade[..., None] + jnp.einsum(
        "qhk,khd->qhd",
        weights.astype(jnp.bfloat16),
        value_heads,
        preferred_element_type=jnp.float32,
    )
    return (accum, totals, raised)


def gather_body(queries, keys_proj, values, hidden, fresh_latent, gate_table, noise_step, pattern):
    group_index = lax.axis_index("tm")
    final_index = lax.axis_size("tm") - 1
    query_tok, key_tok, value_tok = (
        lax.all_to_all(queries[0], "seq", split_axis=1, concat_axis=0, tiled=True),
        lax.all_to_all(keys_proj[0], "seq", split_axis=1, concat_axis=0, tiled=True),
        lax.all_to_all(values[0], "seq", split_axis=1, concat_axis=0, tiled=True),
    )
    row_count, local_width = query_tok.shape
    head_count = local_width // HD
    query_heads = query_tok.reshape(row_count, head_count, HD)
    scale_factor = 1.0 / math.sqrt(HD)
    reach = lax.dynamic_index_in_dim(pattern, group_index, 0, keepdims=False)
    start_state = (
        jnp.zeros((row_count, head_count, HD), jnp.float32),
        jnp.zeros((row_count, head_count), jnp.float32),
        jnp.full((row_count, head_count), -1e30, jnp.float32),
    )

    def one_block(current, inputs):
        key_block, value_block, flag = inputs
        return (
            lax.cond(
                flag > 0,
                lambda state: absorb(state, query_heads, key_block, value_block, scale_factor),
                lambda state: state,
                current,
            ),
            None,
        )

    key_piece = lax.all_gather(key_tok, "tm", axis=0, tiled=False)
    value_piece = lax.all_gather(value_tok, "tm", axis=0, tiled=False)
    state, unused = lax.scan(one_block, start_state, (key_piece, value_piece, reach))
    cache_keys, cache_values = shifted((key_tok, value_tok), "tm", -1)
    accum, totals, highest = state
    attended_head = (accum / totals[..., None]).reshape(row_count, local_width).astype(jnp.bfloat16)
    attended = lax.all_to_all(attended_head, "seq", split_axis=0, concat_axis=1, tiled=True)
    gate_row = lax.dynamic_index_in_dim(gate_table, noise_step[0], 0, keepdims=False)
    updated = (
        hidden[0].astype(jnp.float32) + gate_row[None, :] * attended.astype(jnp.float32)
    ).astype(jnp.bfloat16)
    moved = shifted(updated, "tm", -1)
    advanced = jnp.where(group_index == final_index, fresh_latent, moved)[None]
    next_cache = jnp.stack([cache_keys, cache_values], axis=0)[None]
    return (advanced, next_cache)


def body(queries, *others):
    tm_count, seq_count = lax.axis_size("tm"), lax.axis_size("seq")
    _, tok, width = queries.shape
    count = tm_count * seq_count
    even = width % (count * HD) == 0 and tok % 8 == 0 and seq_count % 2 == 0
    return (spread_body if even else gather_body)(queries, *others)


def solution(mesh):
    placed = (
        P("tm", "seq", None),
        P("tm", "seq", None),
        P("tm", "seq", None),
        P("tm", "seq", None),
        P("seq", None),
        P(),
        P("tm"),
        P(),
    )
    return jax.shard_map(
        body,
        mesh=mesh,
        in_specs=placed,
        out_specs=(P("tm", "seq", None), P("tm", None, None, "seq")),
        check_vma=False,
    )
```

```python
import functools
import math

import jax
import jax.numpy as jnp
from jax import lax
from jax.experimental import pallas as pl
from jax.experimental.pallas import tpu as pltpu
from jax.sharding import PartitionSpec as P

HD = 128
BOTH = ("tm", "seq")
VMEM = pltpu.VMEM
SMEM = pltpu.SMEM


def shifted(block, axis, distance):
    devices = range(lax.axis_size(axis))
    route = [(i - distance, i) for i in devices if i - distance in devices]
    return lax.ppermute(block, axis, route)


def pack_kernel(seq_count, q_hbm, k_hbm, v_hbm, out_ref, *scratch):
    held, sems = scratch
    tok = held.shape[1]
    wide = out_ref.shape[1] // 3
    count = out_ref.shape[0] // tok
    tm_count = count // seq_count
    copies = [
        pltpu.make_async_copy(ref.at[0], held.at[place], sems.at[place])
        for place, ref in enumerate((q_hbm, k_hbm, v_hbm))
    ]
    for copy in copies:
        copy.start()
    for place, copy in enumerate(copies):
        copy.wait()
        for pair in range(count // 2):
            rows = []
            for dest in (2 * pair, 2 * pair + 1):
                start = ((dest % seq_count) * tm_count + dest // seq_count) * wide
                rows.append(held[place, :, start : start + wide].astype(jnp.float32))
            both = jnp.concatenate(rows, axis=0).astype(jnp.bfloat16)
            out_ref[2 * pair * tok : 2 * (pair + 1) * tok, place * wide : (place + 1) * wide] = both


def residual_kernel(noise_ref, h_ref, gate_ref, after_ref, out_ref):
    gate = gate_ref[pl.ds(noise_ref[0], 1), :]
    high = gate.astype(jnp.bfloat16).astype(jnp.float32)
    middle = (gate - high).astype(jnp.bfloat16).astype(jnp.float32)
    low = gate - high - middle
    parts = jnp.concatenate([high, middle, low, jnp.zeros((5, gate.shape[1]), jnp.float32)], axis=0)
    out_ref[...] = jnp.concatenate([h_ref[0].astype(jnp.float32), parts], axis=0).astype(jnp.bfloat16)


def partner(here, distance, groups):
    return here ^ distance if groups & (groups - 1) == 0 else (here + groups - distance) % groups


def attend_kernel(groups, pattern_ref, x_ref, after_ref, out_ref, *hand_refs):
    wide = out_ref.shape[1]
    rows = x_ref.shape[0] // groups
    factor = math.log2(math.e) / math.sqrt(HD)
    here = lax.axis_index("tm")
    for distance, hand_ref in enumerate(hand_refs, 1):
        group = lax.rem(partner(here, distance, groups) + 1, groups)
        hand_ref[...] = x_ref[pl.ds(pl.multiple_of(group * rows, rows), rows), wide:]
    for group in range(1, groups):
        span = (group + 1) * rows
        column = lax.broadcasted_iota(jnp.int32, (1, span), 1)
        kept = jnp.zeros((1, span), jnp.int32)
        for source in range(group + 1):
            inside = (column >= source * rows) & (column < (source + 1) * rows)
            kept = jnp.where(inside, pattern_ref[group, source], kept)
        for head in range(0, wide, HD):
            query = x_ref[group * rows : span, head : head + HD]
            key = x_ref[:span, wide + head : wide + head + HD]
            value = x_ref[:span, 2 * wide + head : 2 * wide + head + HD]
            scores = lax.dot_general(
                query, key, (((1,), (1,)), ((), ())), preferred_element_type=jnp.float32
            )
            scores = jnp.where(kept > 0, scores, -1e30)
            highest = jnp.max(scores, axis=-1, keepdims=True)
            raised = jnp.exp2((scores - highest) * factor)
            total = jnp.sum(raised, axis=-1, keepdims=True)
            numer = jnp.dot(raised.astype(jnp.bfloat16), value, preferred_element_type=jnp.float32)
            out_ref[(group - 1) * rows : group * rows, head : head + HD] = (numer / total).astype(
                jnp.bfloat16
            )
    out_ref[(groups - 1) * rows :, :] = jnp.zeros((rows, wide), jnp.bfloat16)


def cache_kernel(x_ref, *refs):
    hand_refs, out_ref = refs[:-2], refs[-1]
    groups = len(hand_refs) + 1
    wide = x_ref.shape[1] // 3
    rows = out_ref.shape[2]
    here = lax.axis_index("tm")

    @pl.when(here == groups - 1)
    def clear():
        out_ref[...] = jnp.zeros_like(out_ref)

    @pl.when(here < groups - 1)
    def place():
        own = x_ref[pl.ds(pl.multiple_of((here + 1) * rows, rows), rows), wide:]
        for distance, block in enumerate((own,) + hand_refs):
            source = partner(here, groups - distance if groups & (groups - 1) else distance, groups)
            lanes = pl.ds(pl.multiple_of(source * wide, wide), wide)
            for kind in range(2):
                out_ref[0, kind, :, lanes] = block[:, kind * wide : (kind + 1) * wide]


def update_kernel(seq_count, tm_count, att_ref, moved_ref, fresh_ref, out_ref):
    tok = out_ref.shape[1]
    wide = att_ref.shape[1]
    count = att_ref.shape[0] // tok
    last = lax.axis_index("tm") == tm_count - 1

    @pl.when(last)
    def take_fresh():
        out_ref[0] = fresh_ref[...]

    @pl.when(jnp.logical_not(last))
    def take_update():
        for pair in range(count // 2):
            rows = att_ref[2 * pair * tok : 2 * (pair + 1) * tok, :].astype(jnp.float32)
            for half in range(2):
                source = 2 * pair + half
                start = ((source % seq_count) * tm_count + source // seq_count) * wide
                moved = moved_ref[:, start : start + wide].astype(jnp.float32)
                gate = (moved[tok : tok + 1] + moved[tok + 1 : tok + 2]) + moved[tok + 2 : tok + 3]
                result = moved[:tok] + gate * rows[half * tok : (half + 1) * tok]
                out_ref[0, :, start : start + wide] = result.astype(jnp.bfloat16)


def whole(space=VMEM):
    return pl.BlockSpec(memory_space=space)


def run(kernel, name, out_shape, specs, operands, flops=0, scratch=(), space=VMEM):
    def size(a):
        return math.prod(a.shape) * a.dtype.itemsize

    outs = jax.tree.leaves(out_shape)
    moved = sum(map(size, operands)) + sum(map(size, outs))
    return pl.pallas_call(
        kernel,
        out_shape=jax.tree.map(lambda a: space(a.shape, a.dtype), out_shape),
        in_specs=specs,
        out_specs=jax.tree.map(lambda a: whole(), out_shape),
        scratch_shapes=scratch,
        compiler_params=pltpu.CompilerParams(vmem_limit_bytes=4 * moved + (4 << 20)),
        cost_estimate=pl.CostEstimate(flops=flops, bytes_accessed=moved, transcendentals=0),
        name=name,
    )(*operands)


def spread_body(queries, keys_proj, values, hidden, fresh_latent, gate_table, noise_step, pattern):
    tm_count, seq_count = lax.axis_size("tm"), lax.axis_size("seq")
    count = tm_count * seq_count
    _, tok, width = queries.shape
    wide = width // count
    group_tok = tok * seq_count
    shape = functools.partial(jax.ShapeDtypeStruct, dtype=queries.dtype)

    packed = run(
        functools.partial(pack_kernel, seq_count),
        "pack",
        shape((count * tok, 3 * wide)),
        [whole(pltpu.HBM)] * 3,
        [pltpu.with_memory_space_constraint(a, pltpu.HBM) for a in (queries, keys_proj, values)],
        scratch=[VMEM((3, tok, width), queries.dtype), pltpu.SemaphoreType.DMA((3,))],
    )
    exchanged = lax.all_to_all(packed, BOTH, split_axis=0, concat_axis=0, tiled=True)

    residual = run(
        residual_kernel,
        "residual",
        shape((tok + 8, width)),
        [whole(SMEM), whole(), whole(), whole(pl.ANY)],
        (noise_step, hidden, gate_table, packed),
    )
    moved = shifted(residual, "tm", -1)

    attended, *hands = run(
        functools.partial(attend_kernel, tm_count),
        "attend",
        [shape((count * tok, wide))] + [shape((group_tok, 2 * wide))] * (tm_count - 1),
        [whole(SMEM), whole(), whole(pl.ANY)],
        (pattern, exchanged, moved),
        flops=2 * count * tok * count * tok * wide,
    )
    returned = lax.all_to_all(attended, BOTH, split_axis=0, concat_axis=0, tiled=True)
    handed = [None] * len(hands)
    for distance in range(tm_count - 1, 0, -1):
        route = [(i, partner(i, distance, tm_count)) for i in range(tm_count)]
        handed[distance - 1] = lax.ppermute(
            hands[distance - 1], "tm", [(i, j) for i, j in route if j < tm_count - 1]
        )

    advanced = run(
        functools.partial(update_kernel, seq_count, tm_count),
        "update",
        shape((1, tok, width)),
        [whole()] * 3,
        (returned, moved, fresh_latent),
        space=pltpu.HBM,
    )
    next_cache = run(
        cache_kernel,
        "cache",
        shape((1, 2, group_tok, tm_count * wide)),
        [whole()] * tm_count + [whole(pltpu.HBM)],
        (exchanged, *handed, pltpu.with_memory_space_constraint(advanced, pltpu.HBM)),
        space=pltpu.HBM,
    )
    return (advanced, next_cache)


def absorb(state, query_heads, key_piece, value_piece, scale_factor):
    accum, totals, highest = state
    row_count, head_count, head_dim = query_heads.shape
    key_heads = key_piece.reshape(key_piece.shape[0], head_count, head_dim)
    value_heads = value_piece.reshape(value_piece.shape[0], head_count, head_dim)
    scores = (
        jnp.einsum("qhd,khd->qhk", query_heads, key_heads, preferred_element_type=jnp.float32)
        * scale_factor
    )
    raised = jnp.maximum(highest, jnp.max(scores, axis=-1))
    fade = jnp.exp(highest - raised)
    weights = jnp.exp(scores - raised[..., None])
    totals = totals * fade + jnp.sum(weights, axis=-1)
    accum = accum * fade[..., None] + jnp.einsum(
        "qhk,khd->qhd",
        weights.astype(jnp.bfloat16),
        value_heads,
        preferred_element_type=jnp.float32,
    )
    return (accum, totals, raised)


def gather_body(queries, keys_proj, values, hidden, fresh_latent, gate_table, noise_step, pattern):
    group_index = lax.axis_index("tm")
    final_index = lax.axis_size("tm") - 1
    query_tok, key_tok, value_tok = (
        lax.all_to_all(queries[0], "seq", split_axis=1, concat_axis=0, tiled=True),
        lax.all_to_all(keys_proj[0], "seq", split_axis=1, concat_axis=0, tiled=True),
        lax.all_to_all(values[0], "seq", split_axis=1, concat_axis=0, tiled=True),
    )
    row_count, local_width = query_tok.shape
    head_count = local_width // HD
    query_heads = query_tok.reshape(row_count, head_count, HD)
    scale_factor = 1.0 / math.sqrt(HD)
    reach = lax.dynamic_index_in_dim(pattern, group_index, 0, keepdims=False)
    start_state = (
        jnp.zeros((row_count, head_count, HD), jnp.float32),
        jnp.zeros((row_count, head_count), jnp.float32),
        jnp.full((row_count, head_count), -1e30, jnp.float32),
    )

    def one_block(current, inputs):
        key_block, value_block, flag = inputs
        return (
            lax.cond(
                flag > 0,
                lambda state: absorb(state, query_heads, key_block, value_block, scale_factor),
                lambda state: state,
                current,
            ),
            None,
        )

    key_piece = lax.all_gather(key_tok, "tm", axis=0, tiled=False)
    value_piece = lax.all_gather(value_tok, "tm", axis=0, tiled=False)
    state, unused = lax.scan(one_block, start_state, (key_piece, value_piece, reach))
    cache_keys, cache_values = shifted((key_tok, value_tok), "tm", -1)
    accum, totals, highest = state
    attended_head = (accum / totals[..., None]).reshape(row_count, local_width).astype(jnp.bfloat16)
    attended = lax.all_to_all(attended_head, "seq", split_axis=0, concat_axis=1, tiled=True)
    gate_row = lax.dynamic_index_in_dim(gate_table, noise_step[0], 0, keepdims=False)
    updated = (
        hidden[0].astype(jnp.float32) + gate_row[None, :] * attended.astype(jnp.float32)
    ).astype(jnp.bfloat16)
    moved = shifted(updated, "tm", -1)
    advanced = jnp.where(group_index == final_index, fresh_latent, moved)[None]
    next_cache = jnp.stack([cache_keys, cache_values], axis=0)[None]
    return (advanced, next_cache)


def body(queries, *others):
    tm_count, seq_count = lax.axis_size("tm"), lax.axis_size("seq")
    _, tok, width = queries.shape
    count = tm_count * seq_count
    even = width % (count * HD) == 0 and tok % 8 == 0 and seq_count % 2 == 0
    return (spread_body if even else gather_body)(queries, *others)


def solution(mesh):
    placed = (
        P("tm", "seq", None),
        P("tm", "seq", None),
        P("tm", "seq", None),
        P("tm", "seq", None),
        P("seq", None),
        P(),
        P("tm"),
        P(),
    )
    return jax.shard_map(
        body,
        mesh=mesh,
        in_specs=placed,
        out_specs=(P("tm", "seq", None), P("tm", None, None, "seq")),
        check_vma=False,
    )
```

```python
import functools
import math

import jax
import jax.numpy as jnp
from jax import lax
from jax.experimental import pallas as pl
from jax.experimental.pallas import tpu as pltpu
from jax.sharding import PartitionSpec as P

HD = 128
BOTH = ("tm", "seq")
VMEM = pltpu.VMEM
SMEM = pltpu.SMEM


def shifted(block, axis, distance):
    devices = range(lax.axis_size(axis))
    route = [(i - distance, i) for i in devices if i - distance in devices]
    return lax.ppermute(block, axis, route)


def pack_kernel(seq_count, q_hbm, k_hbm, v_hbm, out_ref, *scratch):
    held, sems = scratch
    tok = held.shape[1]
    wide = out_ref.shape[1] // 3
    count = out_ref.shape[0] // tok
    tm_count = count // seq_count
    copies = [
        pltpu.make_async_copy(ref.at[0], held.at[place], sems.at[place])
        for place, ref in enumerate((q_hbm, k_hbm, v_hbm))
    ]
    for copy in copies:
        copy.start()
    for place, copy in enumerate(copies):
        copy.wait()
        for pair in range(count // 2):
            rows = []
            for dest in (2 * pair, 2 * pair + 1):
                start = ((dest % seq_count) * tm_count + dest // seq_count) * wide
                rows.append(held[place, :, start : start + wide].astype(jnp.float32))
            both = jnp.concatenate(rows, axis=0).astype(jnp.bfloat16)
            out_ref[2 * pair * tok : 2 * (pair + 1) * tok, place * wide : (place + 1) * wide] = both


def residual_kernel(noise_ref, h_ref, gate_ref, after_ref, out_ref):
    gate = gate_ref[pl.ds(noise_ref[0], 1), :]
    high = gate.astype(jnp.bfloat16).astype(jnp.float32)
    middle = (gate - high).astype(jnp.bfloat16).astype(jnp.float32)
    low = gate - high - middle
    parts = jnp.concatenate([high, middle, low, jnp.zeros((5, gate.shape[1]), jnp.float32)], axis=0)
    out_ref[...] = jnp.concatenate([h_ref[0].astype(jnp.float32), parts], axis=0).astype(jnp.bfloat16)


def partner(here, distance, groups):
    return here ^ distance if groups & (groups - 1) == 0 else (here + groups - distance) % groups


def distances(groups):
    return range(groups - 1, 0, -1)


def attend_kernel(groups, pattern_ref, x_ref, after_ref, out_ref, *hand_refs):
    wide = out_ref.shape[1]
    rows = x_ref.shape[0] // groups
    factor = math.log2(math.e) / math.sqrt(HD)
    here = lax.axis_index("tm")
    for distance, hand_ref in zip(distances(groups), hand_refs):
        group = lax.rem(partner(here, distance, groups) + 1, groups)
        hand_ref[...] = x_ref[pl.ds(pl.multiple_of(group * rows, rows), rows), wide:]
    for group in range(1, groups):
        span = (group + 1) * rows
        column = lax.broadcasted_iota(jnp.int32, (1, span), 1)
        kept = jnp.zeros((1, span), jnp.int32)
        for source in range(group + 1):
            inside = (column >= source * rows) & (column < (source + 1) * rows)
            kept = jnp.where(inside, pattern_ref[group, source], kept)
        for head in range(0, wide, HD):
            query = x_ref[group * rows : span, head : head + HD]
            key = x_ref[:span, wide + head : wide + head + HD]
            value = x_ref[:span, 2 * wide + head : 2 * wide + head + HD]
            scores = lax.dot_general(
                query, key, (((1,), (1,)), ((), ())), preferred_element_type=jnp.float32
            )
            scores = jnp.where(kept > 0, scores, -1e30)
            highest = jnp.max(scores, axis=-1, keepdims=True)
            raised = jnp.exp2((scores - highest) * factor)
            total = jnp.sum(raised, axis=-1, keepdims=True)
            numer = jnp.dot(raised.astype(jnp.bfloat16), value, preferred_element_type=jnp.float32)
            out_ref[(group - 1) * rows : group * rows, head : head + HD] = (numer / total).astype(
                jnp.bfloat16
            )
    out_ref[(groups - 1) * rows :, :] = jnp.zeros((rows, wide), jnp.bfloat16)


def cache_kernel(x_ref, *refs):
    hand_refs, out_ref = refs[:-2], refs[-1]
    groups = len(hand_refs) + 1
    wide = x_ref.shape[1] // 3
    rows = out_ref.shape[2]
    here = lax.axis_index("tm")

    @pl.when(here == groups - 1)
    def clear():
        out_ref[...] = jnp.zeros_like(out_ref)

    @pl.when(here < groups - 1)
    def place():
        own = x_ref[pl.ds(pl.multiple_of((here + 1) * rows, rows), rows), wide:]
        for distance, block in zip((0, *distances(groups)), (own,) + hand_refs):
            source = partner(here, groups - distance if groups & (groups - 1) else distance, groups)
            lanes = pl.ds(pl.multiple_of(source * wide, wide), wide)
            for kind in range(2):
                out_ref[0, kind, :, lanes] = block[:, kind * wide : (kind + 1) * wide]


def update_kernel(seq_count, tm_count, att_ref, moved_ref, fresh_ref, out_ref):
    tok = out_ref.shape[1]
    wide = att_ref.shape[1]
    count = att_ref.shape[0] // tok
    last = lax.axis_index("tm") == tm_count - 1

    @pl.when(last)
    def take_fresh():
        out_ref[0] = fresh_ref[...]

    @pl.when(jnp.logical_not(last))
    def take_update():
        for pair in range(count // 2):
            rows = att_ref[2 * pair * tok : 2 * (pair + 1) * tok, :].astype(jnp.float32)
            for half in range(2):
                source = 2 * pair + half
                start = ((source % seq_count) * tm_count + source // seq_count) * wide
                moved = moved_ref[:, start : start + wide].astype(jnp.float32)
                gate = (moved[tok : tok + 1] + moved[tok + 1 : tok + 2]) + moved[tok + 2 : tok + 3]
                result = moved[:tok] + gate * rows[half * tok : (half + 1) * tok]
                out_ref[0, :, start : start + wide] = result.astype(jnp.bfloat16)


def whole(space=VMEM):
    return pl.BlockSpec(memory_space=space)


def run(kernel, name, out_shape, specs, operands, flops=0, scratch=(), space=VMEM):
    def size(a):
        return math.prod(a.shape) * a.dtype.itemsize

    outs = jax.tree.leaves(out_shape)
    moved = sum(map(size, operands)) + sum(map(size, outs))
    return pl.pallas_call(
        kernel,
        out_shape=jax.tree.map(lambda a: space(a.shape, a.dtype), out_shape),
        in_specs=specs,
        out_specs=jax.tree.map(lambda a: whole(), out_shape),
        scratch_shapes=scratch,
        compiler_params=pltpu.CompilerParams(vmem_limit_bytes=4 * moved + (4 << 20)),
        cost_estimate=pl.CostEstimate(flops=flops, bytes_accessed=moved, transcendentals=0),
        name=name,
    )(*operands)


def spread_body(queries, keys_proj, values, hidden, fresh_latent, gate_table, noise_step, pattern):
    tm_count, seq_count = lax.axis_size("tm"), lax.axis_size("seq")
    count = tm_count * seq_count
    _, tok, width = queries.shape
    wide = width // count
    group_tok = tok * seq_count
    shape = functools.partial(jax.ShapeDtypeStruct, dtype=queries.dtype)

    packed = run(
        functools.partial(pack_kernel, seq_count),
        "pack",
        shape((count * tok, 3 * wide)),
        [whole(pltpu.HBM)] * 3,
        [pltpu.with_memory_space_constraint(a, pltpu.HBM) for a in (queries, keys_proj, values)],
        scratch=[VMEM((3, tok, width), queries.dtype), pltpu.SemaphoreType.DMA((3,))],
    )
    exchanged = lax.all_to_all(packed, BOTH, split_axis=0, concat_axis=0, tiled=True)

    residual = run(
        residual_kernel,
        "residual",
        shape((tok + 8, width)),
        [whole(SMEM), whole(), whole(), whole(pl.ANY)],
        (noise_step, hidden, gate_table, packed),
    )
    moved = shifted(residual, "tm", -1)

    attended, *hands = run(
        functools.partial(attend_kernel, tm_count),
        "attend",
        [shape((count * tok, wide))] + [shape((group_tok, 2 * wide))] * (tm_count - 1),
        [whole(SMEM), whole(), whole(pl.ANY)],
        (pattern, exchanged, moved),
        flops=2 * count * tok * count * tok * wide,
    )
    returned = lax.all_to_all(attended, BOTH, split_axis=0, concat_axis=0, tiled=True)
    handed = []
    for distance, hand in zip(distances(tm_count), hands):
        route = [(i, partner(i, distance, tm_count)) for i in range(tm_count)]
        handed.append(lax.ppermute(hand, "tm", [(i, j) for i, j in route if j < tm_count - 1]))

    advanced = run(
        functools.partial(update_kernel, seq_count, tm_count),
        "update",
        shape((1, tok, width)),
        [whole()] * 3,
        (returned, moved, fresh_latent),
        space=pltpu.HBM,
    )
    next_cache = run(
        cache_kernel,
        "cache",
        shape((1, 2, group_tok, tm_count * wide)),
        [whole()] * tm_count + [whole(pltpu.HBM)],
        (exchanged, *handed, pltpu.with_memory_space_constraint(advanced, pltpu.HBM)),
        space=pltpu.HBM,
    )
    return (advanced, next_cache)


def absorb(state, query_heads, key_piece, value_piece, scale_factor):
    accum, totals, highest = state
    row_count, head_count, head_dim = query_heads.shape
    key_heads = key_piece.reshape(key_piece.shape[0], head_count, head_dim)
    value_heads = value_piece.reshape(value_piece.shape[0], head_count, head_dim)
    scores = (
        jnp.einsum("qhd,khd->qhk", query_heads, key_heads, preferred_element_type=jnp.float32)
        * scale_factor
    )
    raised = jnp.maximum(highest, jnp.max(scores, axis=-1))
    fade = jnp.exp(highest - raised)
    weights = jnp.exp(scores - raised[..., None])
    totals = totals * fade + jnp.sum(weights, axis=-1)
    accum = accum * fade[..., None] + jnp.einsum(
        "qhk,khd->qhd",
        weights.astype(jnp.bfloat16),
        value_heads,
        preferred_element_type=jnp.float32,
    )
    return (accum, totals, raised)


def gather_body(queries, keys_proj, values, hidden, fresh_latent, gate_table, noise_step, pattern):
    group_index = lax.axis_index("tm")
    final_index = lax.axis_size("tm") - 1
    query_tok, key_tok, value_tok = (
        lax.all_to_all(queries[0], "seq", split_axis=1, concat_axis=0, tiled=True),
        lax.all_to_all(keys_proj[0], "seq", split_axis=1, concat_axis=0, tiled=True),
        lax.all_to_all(values[0], "seq", split_axis=1, concat_axis=0, tiled=True),
    )
    row_count, local_width = query_tok.shape
    head_count = local_width // HD
    query_heads = query_tok.reshape(row_count, head_count, HD)
    scale_factor = 1.0 / math.sqrt(HD)
    reach = lax.dynamic_index_in_dim(pattern, group_index, 0, keepdims=False)
    start_state = (
        jnp.zeros((row_count, head_count, HD), jnp.float32),
        jnp.zeros((row_count, head_count), jnp.float32),
        jnp.full((row_count, head_count), -1e30, jnp.float32),
    )

    def one_block(current, inputs):
        key_block, value_block, flag = inputs
        return (
            lax.cond(
                flag > 0,
                lambda state: absorb(state, query_heads, key_block, value_block, scale_factor),
                lambda state: state,
                current,
            ),
            None,
        )

    key_piece = lax.all_gather(key_tok, "tm", axis=0, tiled=False)
    value_piece = lax.all_gather(value_tok, "tm", axis=0, tiled=False)
    state, unused = lax.scan(one_block, start_state, (key_piece, value_piece, reach))
    cache_keys, cache_values = shifted((key_tok, value_tok), "tm", -1)
    accum, totals, highest = state
    attended_head = (accum / totals[..., None]).reshape(row_count, local_width).astype(jnp.bfloat16)
    attended = lax.all_to_all(attended_head, "seq", split_axis=0, concat_axis=1, tiled=True)
    gate_row = lax.dynamic_index_in_dim(gate_table, noise_step[0], 0, keepdims=False)
    updated = (
        hidden[0].astype(jnp.float32) + gate_row[None, :] * attended.astype(jnp.float32)
    ).astype(jnp.bfloat16)
    moved = shifted(updated, "tm", -1)
    advanced = jnp.where(group_index == final_index, fresh_latent, moved)[None]
    next_cache = jnp.stack([cache_keys, cache_values], axis=0)[None]
    return (advanced, next_cache)


def body(queries, *others):
    tm_count, seq_count = lax.axis_size("tm"), lax.axis_size("seq")
    _, tok, width = queries.shape
    count = tm_count * seq_count
    even = width % (count * HD) == 0 and tok % 8 == 0 and seq_count % 2 == 0
    return (spread_body if even else gather_body)(queries, *others)


def solution(mesh):
    placed = (
        P("tm", "seq", None),
        P("tm", "seq", None),
        P("tm", "seq", None),
        P("tm", "seq", None),
        P("seq", None),
        P(),
        P("tm"),
        P(),
    )
    return jax.shard_map(
        body,
        mesh=mesh,
        in_specs=placed,
        out_specs=(P("tm", "seq", None), P("tm", None, None, "seq")),
        check_vma=False,
    )
```

```python
import functools
import math

import jax
import jax.numpy as jnp
from jax import lax
from jax.experimental import pallas as pl
from jax.experimental.pallas import tpu as pltpu
from jax.sharding import PartitionSpec as P

HD = 128
BOTH = ("tm", "seq")
VMEM = pltpu.VMEM
SMEM = pltpu.SMEM
HBM = pltpu.HBM


def shifted(block, axis, distance):
    devices = range(lax.axis_size(axis))
    route = [(i - distance, i) for i in devices if i - distance in devices]
    return lax.ppermute(block, axis, route)


def pack_kernel(seq_count, q_hbm, k_hbm, v_hbm, out_hbm, sem):
    count, _, wide = out_hbm.shape
    wide //= 3
    tm_count = count // seq_count
    for place, ref in enumerate((q_hbm, k_hbm, v_hbm)):
        for dest in range(count):
            start = ((dest % seq_count) * tm_count + dest // seq_count) * wide
            pltpu.make_async_copy(
                ref.at[0, :, start : start + wide],
                out_hbm.at[dest, :, place * wide : (place + 1) * wide],
                sem,
            ).start()
    pltpu.make_async_copy(out_hbm, out_hbm, sem).wait()


def residual_kernel(noise_ref, h_ref, gate_ref, after_ref, out_ref):
    gate = gate_ref[pl.ds(noise_ref[0], 1), :]
    high = gate.astype(jnp.bfloat16).astype(jnp.float32)
    middle = (gate - high).astype(jnp.bfloat16).astype(jnp.float32)
    low = gate - high - middle
    parts = jnp.concatenate([high, middle, low, jnp.zeros((5, gate.shape[1]), jnp.float32)], axis=0)
    out_ref[...] = jnp.concatenate([h_ref[0].astype(jnp.float32), parts], axis=0).astype(jnp.bfloat16)


def partner(here, distance, groups):
    return here ^ distance if groups & (groups - 1) == 0 else (here + groups - distance) % groups


def distances(groups):
    return range(groups - 1, 0, -1)


def attend_kernel(groups, pattern_ref, x_ref, after_ref, out_hbm, *refs):
    *hand_refs, held, sems = refs
    wide = held.shape[2]
    rows = held.shape[1]
    factor = math.log2(math.e) / math.sqrt(HD)
    here = lax.axis_index("tm")
    copies = []
    for group in range(groups - 1, 0, -1):
        span = (group + 1) * rows
        column = lax.broadcasted_iota(jnp.int32, (1, span), 1)
        kept = jnp.zeros((1, span), jnp.int32)
        for source in range(group + 1):
            inside = (column >= source * rows) & (column < (source + 1) * rows)
            kept = jnp.where(inside, pattern_ref[group, source], kept)
        for head in range(0, wide, HD):
            query = x_ref[group * rows : span, head : head + HD]
            key = x_ref[:span, wide + head : wide + head + HD]
            value = x_ref[:span, 2 * wide + head : 2 * wide + head + HD]
            scores = lax.dot_general(
                query, key, (((1,), (1,)), ((), ())), preferred_element_type=jnp.float32
            )
            scores = jnp.where(kept > 0, scores, -1e30)
            highest = jnp.max(scores, axis=-1, keepdims=True)
            raised = jnp.exp2((scores - highest) * factor)
            total = jnp.sum(raised, axis=-1, keepdims=True)
            numer = jnp.dot(raised.astype(jnp.bfloat16), value, preferred_element_type=jnp.float32)
            held[group - 1, :, head : head + HD] = (numer / total).astype(jnp.bfloat16)
        for place in (group - 1, groups - 1) if group == groups - 1 else (group - 1,):
            copies.append(
                pltpu.make_async_copy(
                    held.at[group - 1], out_hbm.at[place * rows : (place + 1) * rows], sems.at[place]
                )
            )
            copies[-1].start()
    for distance, hand_ref in zip(distances(groups), hand_refs):
        group = lax.rem(partner(here, distance, groups) + 1, groups)
        hand_ref[...] = x_ref[pl.ds(pl.multiple_of(group * rows, rows), rows), wide:]
    for copy in copies:
        copy.wait()


def cache_kernel(x_ref, *refs):
    hand_refs, out_ref = refs[:-2], refs[-1]
    groups = len(hand_refs) + 1
    wide = x_ref.shape[1] // 3
    rows = out_ref.shape[2]
    here = lax.axis_index("tm")

    @pl.when(here == groups - 1)
    def clear():
        out_ref[...] = jnp.zeros_like(out_ref)

    @pl.when(here < groups - 1)
    def place():
        own = x_ref[pl.ds(pl.multiple_of((here + 1) * rows, rows), rows), wide:]
        for distance, block in zip((0, *distances(groups)), (own,) + hand_refs):
            source = partner(here, groups - distance if groups & (groups - 1) else distance, groups)
            lanes = pl.ds(pl.multiple_of(source * wide, wide), wide)
            for kind in range(2):
                out_ref[0, kind, :, lanes] = block[:, kind * wide : (kind + 1) * wide]


def update_kernel(seq_count, tm_count, att_ref, moved_ref, fresh_ref, out_ref):
    tok = out_ref.shape[1]
    wide = att_ref.shape[1]
    count = att_ref.shape[0] // tok
    last = lax.axis_index("tm") == tm_count - 1

    @pl.when(last)
    def take_fresh():
        out_ref[0] = fresh_ref[...]

    @pl.when(jnp.logical_not(last))
    def take_update():
        for pair in range(count // 2):
            rows = att_ref[2 * pair * tok : 2 * (pair + 1) * tok, :].astype(jnp.float32)
            for half in range(2):
                source = 2 * pair + half
                start = ((source % seq_count) * tm_count + source // seq_count) * wide
                moved = moved_ref[:, start : start + wide].astype(jnp.float32)
                gate = (moved[tok : tok + 1] + moved[tok + 1 : tok + 2]) + moved[tok + 2 : tok + 3]
                result = moved[:tok] + gate * rows[half * tok : (half + 1) * tok]
                out_ref[0, :, start : start + wide] = result.astype(jnp.bfloat16)


def whole(space=VMEM):
    return pl.BlockSpec(memory_space=space)


def run(kernel, name, outs, specs, operands, flops=0, scratch=()):
    def size(a):
        return math.prod(a.shape) * jnp.dtype(a.dtype).itemsize

    moved = sum(map(size, operands)) + sum(map(size, outs))
    results = pl.pallas_call(
        kernel,
        out_shape=outs,
        in_specs=specs,
        out_specs=[whole(getattr(a, "memory_space", VMEM)) for a in outs],
        scratch_shapes=scratch,
        compiler_params=pltpu.CompilerParams(vmem_limit_bytes=4 * moved + (4 << 20)),
        cost_estimate=pl.CostEstimate(flops=flops, bytes_accessed=moved, transcendentals=0),
        name=name,
    )(*operands)
    return results if len(outs) > 1 else results[0]


def spread_body(queries, keys_proj, values, hidden, fresh_latent, gate_table, noise_step, pattern):
    tm_count, seq_count = lax.axis_size("tm"), lax.axis_size("seq")
    count = tm_count * seq_count
    _, tok, width = queries.shape
    wide = width // count
    group_tok = tok * seq_count
    kind = queries.dtype
    DMA = pltpu.SemaphoreType.DMA

    packed = run(
        functools.partial(pack_kernel, seq_count),
        "pack",
        [HBM((count, tok, 3 * wide), kind)],
        [whole(HBM)] * 3,
        [pltpu.with_memory_space_constraint(a, HBM) for a in (queries, keys_proj, values)],
        scratch=[DMA],
    )
    exchanged = lax.all_to_all(packed, BOTH, split_axis=0, concat_axis=0, tiled=True)
    exchanged = exchanged.reshape(count * tok, 3 * wide)

    residual = run(
        residual_kernel,
        "residual",
        [VMEM((tok + 8, width), kind)],
        [whole(SMEM), whole(), whole(), whole(HBM)],
        (noise_step, hidden, gate_table, pltpu.with_memory_space_constraint(packed, HBM)),
    )
    moved = shifted(residual, "tm", -1)

    attended, *hands = run(
        functools.partial(attend_kernel, tm_count),
        "attend",
        [HBM((count * tok, wide), kind)] + [VMEM((group_tok, 2 * wide), kind)] * (tm_count - 1),
        [whole(SMEM), whole(), whole(pl.ANY)],
        (pattern, exchanged, moved),
        flops=2 * count * tok * count * tok * wide,
        scratch=[VMEM((tm_count - 1, group_tok, wide), kind), DMA((tm_count,))],
    )
    returned = lax.all_to_all(attended, BOTH, split_axis=0, concat_axis=0, tiled=True)
    handed = []
    for distance, hand in zip(distances(tm_count), hands):
        route = [(i, partner(i, distance, tm_count)) for i in range(tm_count)]
        handed.append(lax.ppermute(hand, "tm", [(i, j) for i, j in route if j < tm_count - 1]))

    advanced = run(
        functools.partial(update_kernel, seq_count, tm_count),
        "update",
        [jax.ShapeDtypeStruct((1, tok, width), kind)],
        [whole()] * 3,
        (returned, moved, fresh_latent),
    )
    next_cache = run(
        cache_kernel,
        "cache",
        [jax.ShapeDtypeStruct((1, 2, group_tok, tm_count * wide), kind)],
        [whole()] * tm_count + [whole(HBM)],
        (exchanged, *handed, pltpu.with_memory_space_constraint(advanced, HBM)),
    )
    return (advanced, next_cache)


def absorb(state, query_heads, key_piece, value_piece, scale_factor):
    accum, totals, highest = state
    row_count, head_count, head_dim = query_heads.shape
    key_heads = key_piece.reshape(key_piece.shape[0], head_count, head_dim)
    value_heads = value_piece.reshape(value_piece.shape[0], head_count, head_dim)
    scores = (
        jnp.einsum("qhd,khd->qhk", query_heads, key_heads, preferred_element_type=jnp.float32)
        * scale_factor
    )
    raised = jnp.maximum(highest, jnp.max(scores, axis=-1))
    fade = jnp.exp(highest - raised)
    weights = jnp.exp(scores - raised[..., None])
    totals = totals * fade + jnp.sum(weights, axis=-1)
    accum = accum * fade[..., None] + jnp.einsum(
        "qhk,khd->qhd",
        weights.astype(jnp.bfloat16),
        value_heads,
        preferred_element_type=jnp.float32,
    )
    return (accum, totals, raised)


def gather_body(queries, keys_proj, values, hidden, fresh_latent, gate_table, noise_step, pattern):
    group_index = lax.axis_index("tm")
    final_index = lax.axis_size("tm") - 1
    query_tok, key_tok, value_tok = (
        lax.all_to_all(queries[0], "seq", split_axis=1, concat_axis=0, tiled=True),
        lax.all_to_all(keys_proj[0], "seq", split_axis=1, concat_axis=0, tiled=True),
        lax.all_to_all(values[0], "seq", split_axis=1, concat_axis=0, tiled=True),
    )
    row_count, local_width = query_tok.shape
    head_count = local_width // HD
    query_heads = query_tok.reshape(row_count, head_count, HD)
    scale_factor = 1.0 / math.sqrt(HD)
    reach = lax.dynamic_index_in_dim(pattern, group_index, 0, keepdims=False)
    start_state = (
        jnp.zeros((row_count, head_count, HD), jnp.float32),
        jnp.zeros((row_count, head_count), jnp.float32),
        jnp.full((row_count, head_count), -1e30, jnp.float32),
    )

    def one_block(current, inputs):
        key_block, value_block, flag = inputs
        return (
            lax.cond(
                flag > 0,
                lambda state: absorb(state, query_heads, key_block, value_block, scale_factor),
                lambda state: state,
                current,
            ),
            None,
        )

    key_piece = lax.all_gather(key_tok, "tm", axis=0, tiled=False)
    value_piece = lax.all_gather(value_tok, "tm", axis=0, tiled=False)
    state, unused = lax.scan(one_block, start_state, (key_piece, value_piece, reach))
    cache_keys, cache_values = shifted((key_tok, value_tok), "tm", -1)
    accum, totals, highest = state
    attended_head = (accum / totals[..., None]).reshape(row_count, local_width).astype(jnp.bfloat16)
    attended = lax.all_to_all(attended_head, "seq", split_axis=0, concat_axis=1, tiled=True)
    gate_row = lax.dynamic_index_in_dim(gate_table, noise_step[0], 0, keepdims=False)
    updated = (
        hidden[0].astype(jnp.float32) + gate_row[None, :] * attended.astype(jnp.float32)
    ).astype(jnp.bfloat16)
    moved = shifted(updated, "tm", -1)
    advanced = jnp.where(group_index == final_index, fresh_latent, moved)[None]
    next_cache = jnp.stack([cache_keys, cache_values], axis=0)[None]
    return (advanced, next_cache)


def body(queries, *others):
    tm_count, seq_count = lax.axis_size("tm"), lax.axis_size("seq")
    _, tok, width = queries.shape
    count = tm_count * seq_count
    even = width % (count * HD) == 0 and tok % 8 == 0 and seq_count % 2 == 0
    return (spread_body if even else gather_body)(queries, *others)


def solution(mesh):
    placed = (
        P("tm", "seq", None),
        P("tm", "seq", None),
        P("tm", "seq", None),
        P("tm", "seq", None),
        P("seq", None),
        P(),
        P("tm"),
        P(),
    )
    return jax.shard_map(
        body,
        mesh=mesh,
        in_specs=placed,
        out_specs=(P("tm", "seq", None), P("tm", None, None, "seq")),
        check_vma=False,
    )
```

```python
import functools
import math

import jax
import jax.numpy as jnp
from jax import lax
from jax.experimental import pallas as pl
from jax.experimental.pallas import tpu as pltpu
from jax.sharding import PartitionSpec as P

HD = 128
BOTH = ("tm", "seq")
VMEM = pltpu.VMEM
SMEM = pltpu.SMEM
HBM = pltpu.HBM


def shifted(block, axis, distance):
    devices = range(lax.axis_size(axis))
    route = [(i - distance, i) for i in devices if i - distance in devices]
    return lax.ppermute(block, axis, route)


def pack_kernel(seq_count, halves, q_hbm, k_hbm, v_hbm, out_hbm, held, block, in_sems, out_sems):
    tok, width = held.shape[1:]
    wide = out_hbm.shape[1] // 3
    count = out_hbm.shape[0] // tok
    tm_count = count // seq_count
    span, part = width // halves, seq_count // halves
    copies = []
    for half in range(halves):
        columns = slice(half * span, (half + 1) * span)
        for place, ref in enumerate((q_hbm, k_hbm, v_hbm)):
            copies.append(
                pltpu.make_async_copy(
                    ref.at[0, :, columns], held.at[place, :, columns], in_sems.at[half, place]
                )
            )
            copies[-1].start()
    outs = []
    for half in range(halves):
        for place in range(3):
            copies[3 * half + place].wait()
            for tm in range(tm_count):
                for seq in range(half * part, (half + 1) * part, 2):
                    rows = []
                    for member in (seq, seq + 1):
                        start = (member * tm_count + tm) * wide
                        rows.append(held[place, :, start : start + wide].astype(jnp.float32))
                    first = (tm * seq_count + seq) * tok
                    block[first : first + 2 * tok, place * wide : (place + 1) * wide] = jnp.concatenate(
                        rows, axis=0
                    ).astype(jnp.bfloat16)
        for tm in range(tm_count):
            first = (tm * seq_count + half * part) * tok
            rows = slice(first, first + part * tok)
            outs.append(
                pltpu.make_async_copy(block.at[rows], out_hbm.at[rows], out_sems.at[half, tm])
            )
            outs[-1].start()
    for out in outs:
        out.wait()


def residual_kernel(noise_ref, h_ref, gate_ref, after_ref, out_ref):
    gate = gate_ref[pl.ds(noise_ref[0], 1), :]
    high = gate.astype(jnp.bfloat16).astype(jnp.float32)
    middle = (gate - high).astype(jnp.bfloat16).astype(jnp.float32)
    low = gate - high - middle
    parts = jnp.concatenate([high, middle, low, jnp.zeros((5, gate.shape[1]), jnp.float32)], axis=0)
    out_ref[...] = jnp.concatenate([h_ref[0].astype(jnp.float32), parts], axis=0).astype(jnp.bfloat16)


def partner(here, distance, groups):
    return here ^ distance if groups & (groups - 1) == 0 else (here + groups - distance) % groups


def distances(groups):
    return range(groups - 1, 0, -1)


def attend_kernel(groups, pattern_ref, x_ref, after_ref, out_hbm, *refs):
    *hand_refs, held, sems = refs
    wide = held.shape[2]
    rows = held.shape[1]
    factor = math.log2(math.e) / math.sqrt(HD)
    here = lax.axis_index("tm")
    copies = []
    turned = [jnp.transpose(x_ref[:, 2 * wide + head : 2 * wide + head + HD]) for head in range(0, wide, HD)]
    for group in range(groups - 1, 0, -1):
        for head in range(0, wide, HD):
            query = x_ref[group * rows : (group + 1) * rows, head : head + HD]
            scores, peaks = [], []
            for source in range(group + 1):
                key = x_ref[source * rows : (source + 1) * rows, wide + head : wide + head + HD]
                block = lax.dot_general(
                    key, query, (((1,), (1,)), ((), ())), preferred_element_type=jnp.float32
                )
                peak = jnp.max(block, axis=0, keepdims=True)
                scores.append(block)
                peaks.append(jnp.where(pattern_ref[group, source] > 0, peak, -1e30))
            highest = functools.reduce(jnp.maximum, peaks) * factor
            total, probs = 0.0, []
            for source in range(group + 1):
                offset = jnp.where(pattern_ref[group, source] > 0, -highest, -1e30)
                raised = jnp.exp2(scores[source] * factor + offset)
                total += jnp.sum(raised, axis=0, keepdims=True)
                probs.append(raised.astype(jnp.bfloat16))
            numer = jnp.dot(
                turned[head // HD][:, : (group + 1) * rows],
                jnp.concatenate(probs, axis=0),
                preferred_element_type=jnp.float32,
            )
            held[group - 1, :, head : head + HD] = jnp.transpose(numer / total).astype(jnp.bfloat16)
        for place in (group - 1, groups - 1) if group == groups - 1 else (group - 1,):
            copies.append(
                pltpu.make_async_copy(
                    held.at[group - 1], out_hbm.at[place * rows : (place + 1) * rows], sems.at[place]
                )
            )
            copies[-1].start()
    for distance, hand_ref in zip(distances(groups), hand_refs):
        group = lax.rem(partner(here, distance, groups) + 1, groups)
        hand_ref[...] = x_ref[pl.ds(pl.multiple_of(group * rows, rows), rows), wide:]
    for copy in copies:
        copy.wait()


def cache_kernel(x_ref, *refs):
    hand_refs, out_ref = refs[:-2], refs[-1]
    groups = len(hand_refs) + 1
    wide = x_ref.shape[1] // 3
    rows = out_ref.shape[2]
    here = lax.axis_index("tm")

    @pl.when(here == groups - 1)
    def clear():
        out_ref[...] = jnp.zeros_like(out_ref)

    @pl.when(here < groups - 1)
    def place():
        own = x_ref[pl.ds(pl.multiple_of((here + 1) * rows, rows), rows), wide:]
        for distance, block in zip((0, *distances(groups)), (own,) + hand_refs):
            source = partner(here, groups - distance if groups & (groups - 1) else distance, groups)
            lanes = pl.ds(pl.multiple_of(source * wide, wide), wide)
            for kind in range(2):
                out_ref[0, kind, :, lanes] = block[:, kind * wide : (kind + 1) * wide]


def update_kernel(seq_count, tm_count, att_ref, moved_ref, fresh_ref, out_ref):
    tok = out_ref.shape[1]
    wide = att_ref.shape[1]
    count = att_ref.shape[0] // tok
    last = lax.axis_index("tm") == tm_count - 1

    @pl.when(last)
    def take_fresh():
        out_ref[0] = fresh_ref[...]

    @pl.when(jnp.logical_not(last))
    def take_update():
        for pair in range(count // 2):
            rows = att_ref[2 * pair * tok : 2 * (pair + 1) * tok, :].astype(jnp.float32)
            for half in range(2):
                source = 2 * pair + half
                start = ((source % seq_count) * tm_count + source // seq_count) * wide
                moved = moved_ref[:, start : start + wide].astype(jnp.float32)
                gate = (moved[tok : tok + 1] + moved[tok + 1 : tok + 2]) + moved[tok + 2 : tok + 3]
                result = moved[:tok] + gate * rows[half * tok : (half + 1) * tok]
                out_ref[0, :, start : start + wide] = result.astype(jnp.bfloat16)


def whole(space=VMEM):
    return pl.BlockSpec(memory_space=space)


def run(kernel, name, outs, specs, operands, flops=0, scratch=()):
    def size(a):
        return math.prod(a.shape) * jnp.dtype(a.dtype).itemsize

    moved = sum(map(size, operands)) + sum(map(size, outs))
    results = pl.pallas_call(
        kernel,
        out_shape=outs,
        in_specs=specs,
        out_specs=[whole(getattr(a, "memory_space", VMEM)) for a in outs],
        scratch_shapes=scratch,
        compiler_params=pltpu.CompilerParams(vmem_limit_bytes=4 * moved + (4 << 20)),
        cost_estimate=pl.CostEstimate(flops=flops, bytes_accessed=moved, transcendentals=0),
        name=name,
    )(*operands)
    return results if len(outs) > 1 else results[0]


def spread_body(queries, keys_proj, values, hidden, fresh_latent, gate_table, noise_step, pattern):
    tm_count, seq_count = lax.axis_size("tm"), lax.axis_size("seq")
    count = tm_count * seq_count
    _, tok, width = queries.shape
    wide = width // count
    group_tok = tok * seq_count
    kind = queries.dtype
    DMA = pltpu.SemaphoreType.DMA
    halves = 2 if seq_count % 4 == 0 else 1

    packed = run(
        functools.partial(pack_kernel, seq_count, halves),
        "pack",
        [HBM((count * tok, 3 * wide), kind)],
        [whole(HBM)] * 3,
        [pltpu.with_memory_space_constraint(a, HBM) for a in (queries, keys_proj, values)],
        scratch=[
            VMEM((3, tok, width), kind),
            VMEM((count * tok, 3 * wide), kind),
            DMA((halves, 3)),
            DMA((halves, tm_count)),
        ],
    )
    exchanged = lax.all_to_all(packed, BOTH, split_axis=0, concat_axis=0, tiled=True)

    residual = run(
        residual_kernel,
        "residual",
        [VMEM((tok + 8, width), kind)],
        [whole(SMEM), whole(), whole(), whole(HBM)],
        (noise_step, hidden, gate_table, pltpu.with_memory_space_constraint(packed, HBM)),
    )
    moved = shifted(residual, "tm", -1)

    attended, *hands = run(
        functools.partial(attend_kernel, tm_count),
        "attend",
        [HBM((count * tok, wide), kind)] + [VMEM((group_tok, 2 * wide), kind)] * (tm_count - 1),
        [whole(SMEM), whole(), whole(pl.ANY)],
        (pattern, exchanged, moved),
        flops=2 * count * tok * count * tok * wide,
        scratch=[VMEM((tm_count - 1, group_tok, wide), kind), DMA((tm_count,))],
    )
    returned = lax.all_to_all(attended, BOTH, split_axis=0, concat_axis=0, tiled=True)
    handed = []
    for distance, hand in zip(distances(tm_count), hands):
        route = [(i, partner(i, distance, tm_count)) for i in range(tm_count)]
        handed.append(lax.ppermute(hand, "tm", [(i, j) for i, j in route if j < tm_count - 1]))

    advanced = run(
        functools.partial(update_kernel, seq_count, tm_count),
        "update",
        [jax.ShapeDtypeStruct((1, tok, width), kind)],
        [whole()] * 3,
        (returned, moved, fresh_latent),
    )
    next_cache = run(
        cache_kernel,
        "cache",
        [jax.ShapeDtypeStruct((1, 2, group_tok, tm_count * wide), kind)],
        [whole()] * tm_count + [whole(HBM)],
        (exchanged, *handed, pltpu.with_memory_space_constraint(advanced, HBM)),
    )
    return (advanced, next_cache)


def absorb(state, query_heads, key_piece, value_piece, scale_factor):
    accum, totals, highest = state
    row_count, head_count, head_dim = query_heads.shape
    key_heads = key_piece.reshape(key_piece.shape[0], head_count, head_dim)
    value_heads = value_piece.reshape(value_piece.shape[0], head_count, head_dim)
    scores = (
        jnp.einsum("qhd,khd->qhk", query_heads, key_heads, preferred_element_type=jnp.float32)
        * scale_factor
    )
    raised = jnp.maximum(highest, jnp.max(scores, axis=-1))
    fade = jnp.exp(highest - raised)
    weights = jnp.exp(scores - raised[..., None])
    totals = totals * fade + jnp.sum(weights, axis=-1)
    accum = accum * fade[..., None] + jnp.einsum(
        "qhk,khd->qhd",
        weights.astype(jnp.bfloat16),
        value_heads,
        preferred_element_type=jnp.float32,
    )
    return (accum, totals, raised)


def gather_body(queries, keys_proj, values, hidden, fresh_latent, gate_table, noise_step, pattern):
    group_index = lax.axis_index("tm")
    final_index = lax.axis_size("tm") - 1
    query_tok, key_tok, value_tok = (
        lax.all_to_all(queries[0], "seq", split_axis=1, concat_axis=0, tiled=True),
        lax.all_to_all(keys_proj[0], "seq", split_axis=1, concat_axis=0, tiled=True),
        lax.all_to_all(values[0], "seq", split_axis=1, concat_axis=0, tiled=True),
    )
    row_count, local_width = query_tok.shape
    head_count = local_width // HD
    query_heads = query_tok.reshape(row_count, head_count, HD)
    scale_factor = 1.0 / math.sqrt(HD)
    reach = lax.dynamic_index_in_dim(pattern, group_index, 0, keepdims=False)
    start_state = (
        jnp.zeros((row_count, head_count, HD), jnp.float32),
        jnp.zeros((row_count, head_count), jnp.float32),
        jnp.full((row_count, head_count), -1e30, jnp.float32),
    )

    def one_block(current, inputs):
        key_block, value_block, flag = inputs
        return (
            lax.cond(
                flag > 0,
                lambda state: absorb(state, query_heads, key_block, value_block, scale_factor),
                lambda state: state,
                current,
            ),
            None,
        )

    key_piece = lax.all_gather(key_tok, "tm", axis=0, tiled=False)
    value_piece = lax.all_gather(value_tok, "tm", axis=0, tiled=False)
    state, unused = lax.scan(one_block, start_state, (key_piece, value_piece, reach))
    cache_keys, cache_values = shifted((key_tok, value_tok), "tm", -1)
    accum, totals, highest = state
    attended_head = (accum / totals[..., None]).reshape(row_count, local_width).astype(jnp.bfloat16)
    attended = lax.all_to_all(attended_head, "seq", split_axis=0, concat_axis=1, tiled=True)
    gate_row = lax.dynamic_index_in_dim(gate_table, noise_step[0], 0, keepdims=False)
    updated = (
        hidden[0].astype(jnp.float32) + gate_row[None, :] * attended.astype(jnp.float32)
    ).astype(jnp.bfloat16)
    moved = shifted(updated, "tm", -1)
    advanced = jnp.where(group_index == final_index, fresh_latent, moved)[None]
    next_cache = jnp.stack([cache_keys, cache_values], axis=0)[None]
    return (advanced, next_cache)


def body(queries, *others):
    tm_count, seq_count = lax.axis_size("tm"), lax.axis_size("seq")
    _, tok, width = queries.shape
    count = tm_count * seq_count
    even = width % (count * HD) == 0 and tok % 8 == 0 and seq_count % 2 == 0
    return (spread_body if even else gather_body)(queries, *others)


def solution(mesh):
    placed = (
        P("tm", "seq", None),
        P("tm", "seq", None),
        P("tm", "seq", None),
        P("tm", "seq", None),
        P("seq", None),
        P(),
        P("tm"),
        P(),
    )
    return jax.shard_map(
        body,
        mesh=mesh,
        in_specs=placed,
        out_specs=(P("tm", "seq", None), P("tm", None, None, "seq")),
        check_vma=False,
    )
```

```python
import functools
import math

import jax
import jax.numpy as jnp
from jax import lax
from jax.experimental import pallas as pl
from jax.experimental.pallas import tpu as pltpu
from jax.sharding import PartitionSpec as P

HD = 128
BOTH = ("tm", "seq")
VMEM = pltpu.VMEM
SMEM = pltpu.SMEM
HBM = pltpu.HBM


def shifted(block, axis, distance):
    devices = range(lax.axis_size(axis))
    route = [(i - distance, i) for i in devices if i - distance in devices]
    return lax.ppermute(block, axis, route)


def mixed(index, count):
    if count & (count - 1):
        return index
    return sum(((index >> bit) & 1) * (count >> (bit + 1)) for bit in range(count.bit_length() - 1))


def pack_kernel(seq_count, halves, q_hbm, k_hbm, v_hbm, out_hbm, held, block, in_sems, out_sems):
    tok, width = held.shape[1:]
    wide = out_hbm.shape[1] // 3
    count = out_hbm.shape[0] // tok
    tm_count = count // seq_count
    span = width // halves
    copies = []
    for half in range(halves):
        columns = slice(half * span, (half + 1) * span)
        for place, ref in enumerate((q_hbm, k_hbm, v_hbm)):
            copies.append(
                pltpu.make_async_copy(
                    ref.at[0, :, columns], held.at[place, :, columns], in_sems.at[half, place]
                )
            )
            copies[-1].start()
    for copy in copies:
        copy.wait()
    for place in range(3):
        for pair in range(count // 2):
            rows = []
            for dest in (2 * pair, 2 * pair + 1):
                start = (mixed(dest % seq_count, seq_count) * tm_count + dest // seq_count) * wide
                rows.append(held[place, :, start : start + wide].astype(jnp.float32))
            block[2 * pair * tok : 2 * (pair + 1) * tok, place * wide : (place + 1) * wide] = jnp.concatenate(
                rows, axis=0
            ).astype(jnp.bfloat16)
    outs = []
    for tm in range(tm_count):
        rows = slice(tm * seq_count * tok, (tm + 1) * seq_count * tok)
        outs.append(pltpu.make_async_copy(block.at[rows], out_hbm.at[rows], out_sems.at[tm]))
        outs[-1].start()
    for out in outs:
        out.wait()


def residual_kernel(noise_ref, h_ref, gate_ref, after_ref, out_ref):
    gate = gate_ref[pl.ds(noise_ref[0], 1), :]
    high = gate.astype(jnp.bfloat16).astype(jnp.float32)
    middle = (gate - high).astype(jnp.bfloat16).astype(jnp.float32)
    low = gate - high - middle
    parts = jnp.concatenate([high, middle, low, jnp.zeros((5, gate.shape[1]), jnp.float32)], axis=0)
    out_ref[...] = jnp.concatenate([h_ref[0].astype(jnp.float32), parts], axis=0).astype(jnp.bfloat16)


def partner(here, distance, groups):
    return here ^ distance if groups & (groups - 1) == 0 else (here + groups - distance) % groups


def distances(groups):
    return range(groups - 1, 0, -1)


def attend_kernel(groups, pattern_ref, x_ref, after_ref, out_hbm, *refs):
    *hand_refs, held, sems = refs
    wide = held.shape[2]
    rows = held.shape[1]
    factor = math.log2(math.e) / math.sqrt(HD)
    here = lax.axis_index("tm")
    copies = []
    turned = [jnp.transpose(x_ref[:, 2 * wide + head : 2 * wide + head + HD]) for head in range(0, wide, HD)]
    for group in range(groups - 1, 0, -1):
        for head in range(0, wide, HD):
            query = x_ref[group * rows : (group + 1) * rows, head : head + HD]
            scores, peaks = [], []
            for source in range(group + 1):
                key = x_ref[source * rows : (source + 1) * rows, wide + head : wide + head + HD]
                block = lax.dot_general(
                    key, query, (((1,), (1,)), ((), ())), preferred_element_type=jnp.float32
                )
                peak = jnp.max(block, axis=0, keepdims=True)
                scores.append(block)
                peaks.append(jnp.where(pattern_ref[group, source] > 0, peak, -1e30))
            highest = functools.reduce(jnp.maximum, peaks) * factor
            total, probs = 0.0, []
            for source in range(group + 1):
                offset = jnp.where(pattern_ref[group, source] > 0, -highest, -1e30)
                raised = jnp.exp2(scores[source] * factor + offset)
                total += jnp.sum(raised, axis=0, keepdims=True)
                probs.append(raised.astype(jnp.bfloat16))
            numer = jnp.dot(
                turned[head // HD][:, : (group + 1) * rows],
                jnp.concatenate(probs, axis=0),
                preferred_element_type=jnp.float32,
            )
            held[group - 1, :, head : head + HD] = jnp.transpose(numer / total).astype(jnp.bfloat16)
        for place in (group - 1, groups - 1) if group == groups - 1 else (group - 1,):
            copies.append(
                pltpu.make_async_copy(
                    held.at[group - 1], out_hbm.at[place * rows : (place + 1) * rows], sems.at[place]
                )
            )
            copies[-1].start()
    for distance, hand_ref in zip(distances(groups), hand_refs):
        group = lax.rem(partner(here, distance, groups) + 1, groups)
        hand_ref[...] = x_ref[pl.ds(pl.multiple_of(group * rows, rows), rows), wide:]
    for copy in copies:
        copy.wait()


def cache_kernel(seq_count, x_ref, *refs):
    hand_refs, out_ref = refs[:-2], refs[-1]
    groups = len(hand_refs) + 1
    wide = x_ref.shape[1] // 3
    rows = out_ref.shape[2]
    here = lax.axis_index("tm")

    @pl.when(here == groups - 1)
    def clear():
        out_ref[...] = jnp.zeros_like(out_ref)

    @pl.when(here < groups - 1)
    def place():
        own = x_ref[pl.ds(pl.multiple_of((here + 1) * rows, rows), rows), wide:]
        tok = rows // seq_count
        for distance, block in zip((0, *distances(groups)), (own,) + hand_refs):
            source = partner(here, groups - distance if groups & (groups - 1) else distance, groups)
            lanes = pl.ds(pl.multiple_of(source * wide, wide), wide)
            block = block[...].astype(jnp.float32)
            for seq in range(0, seq_count, 2):
                starts = [mixed(member, seq_count) * tok for member in (seq, seq + 1)]
                pair = jnp.concatenate([block[start : start + tok] for start in starts], axis=0)
                pair = pair.astype(jnp.bfloat16)
                for kind in range(2):
                    out_ref[0, kind, seq * tok : (seq + 2) * tok, lanes] = pair[
                        :, kind * wide : (kind + 1) * wide
                    ]


def update_kernel(seq_count, tm_count, att_ref, moved_ref, fresh_ref, out_ref):
    tok = out_ref.shape[1]
    wide = att_ref.shape[1]
    count = att_ref.shape[0] // tok
    last = lax.axis_index("tm") == tm_count - 1

    @pl.when(last)
    def take_fresh():
        out_ref[0] = fresh_ref[...]

    @pl.when(jnp.logical_not(last))
    def take_update():
        for pair in range(count // 2):
            rows = att_ref[2 * pair * tok : 2 * (pair + 1) * tok, :].astype(jnp.float32)
            for half in range(2):
                source = 2 * pair + half
                start = (mixed(source % seq_count, seq_count) * tm_count + source // seq_count) * wide
                moved = moved_ref[:, start : start + wide].astype(jnp.float32)
                gate = (moved[tok : tok + 1] + moved[tok + 1 : tok + 2]) + moved[tok + 2 : tok + 3]
                result = moved[:tok] + gate * rows[half * tok : (half + 1) * tok]
                out_ref[0, :, start : start + wide] = result.astype(jnp.bfloat16)


def whole(space=VMEM):
    return pl.BlockSpec(memory_space=space)


def run(kernel, name, outs, specs, operands, flops=0, scratch=()):
    def size(a):
        return math.prod(a.shape) * jnp.dtype(a.dtype).itemsize

    moved = sum(map(size, operands)) + sum(map(size, outs))
    results = pl.pallas_call(
        kernel,
        out_shape=outs,
        in_specs=specs,
        out_specs=[whole(getattr(a, "memory_space", VMEM)) for a in outs],
        scratch_shapes=scratch,
        compiler_params=pltpu.CompilerParams(vmem_limit_bytes=4 * moved + (4 << 20)),
        cost_estimate=pl.CostEstimate(flops=flops, bytes_accessed=moved, transcendentals=0),
        name=name,
    )(*operands)
    return results if len(outs) > 1 else results[0]


def spread_body(queries, keys_proj, values, hidden, fresh_latent, gate_table, noise_step, pattern):
    tm_count, seq_count = lax.axis_size("tm"), lax.axis_size("seq")
    count = tm_count * seq_count
    _, tok, width = queries.shape
    wide = width // count
    group_tok = tok * seq_count
    kind = queries.dtype
    DMA = pltpu.SemaphoreType.DMA
    halves = 2 if seq_count % 4 == 0 else 1

    packed = run(
        functools.partial(pack_kernel, seq_count, halves),
        "pack",
        [HBM((count * tok, 3 * wide), kind)],
        [whole(HBM)] * 3,
        [pltpu.with_memory_space_constraint(a, HBM) for a in (queries, keys_proj, values)],
        scratch=[
            VMEM((3, tok, width), kind),
            VMEM((count * tok, 3 * wide), kind),
            DMA((halves, 3)),
            DMA((tm_count,)),
        ],
    )
    order = [tm * seq_count + mixed(s, seq_count) for tm in range(tm_count) for s in range(seq_count)]
    exchange = functools.partial(
        lax.all_to_all, axis_name=BOTH, split_axis=0, concat_axis=0, tiled=True, axis_index_groups=[order]
    )
    exchanged = exchange(packed)

    residual = run(
        residual_kernel,
        "residual",
        [VMEM((tok + 8, width), kind)],
        [whole(SMEM), whole(), whole(), whole(HBM)],
        (noise_step, hidden, gate_table, pltpu.with_memory_space_constraint(packed, HBM)),
    )
    moved = shifted(residual, "tm", -1)

    attended, *hands = run(
        functools.partial(attend_kernel, tm_count),
        "attend",
        [HBM((count * tok, wide), kind)] + [VMEM((group_tok, 2 * wide), kind)] * (tm_count - 1),
        [whole(SMEM), whole(), whole(pl.ANY)],
        (pattern, exchanged, moved),
        flops=2 * count * tok * count * tok * wide,
        scratch=[VMEM((tm_count - 1, group_tok, wide), kind), DMA((tm_count,))],
    )
    returned = exchange(attended)
    handed = []
    for distance, hand in zip(distances(tm_count), hands):
        route = [(i, partner(i, distance, tm_count)) for i in range(tm_count)]
        handed.append(lax.ppermute(hand, "tm", [(i, j) for i, j in route if j < tm_count - 1]))

    advanced = run(
        functools.partial(update_kernel, seq_count, tm_count),
        "update",
        [jax.ShapeDtypeStruct((1, tok, width), kind)],
        [whole()] * 3,
        (returned, moved, fresh_latent),
    )
    next_cache = run(
        functools.partial(cache_kernel, seq_count),
        "cache",
        [jax.ShapeDtypeStruct((1, 2, group_tok, tm_count * wide), kind)],
        [whole()] * tm_count + [whole(HBM)],
        (exchanged, *handed, pltpu.with_memory_space_constraint(advanced, HBM)),
    )
    return (advanced, next_cache)


def absorb(state, query_heads, key_piece, value_piece, scale_factor):
    accum, totals, highest = state
    row_count, head_count, head_dim = query_heads.shape
    key_heads = key_piece.reshape(key_piece.shape[0], head_count, head_dim)
    value_heads = value_piece.reshape(value_piece.shape[0], head_count, head_dim)
    scores = (
        jnp.einsum("qhd,khd->qhk", query_heads, key_heads, preferred_element_type=jnp.float32)
        * scale_factor
    )
    raised = jnp.maximum(highest, jnp.max(scores, axis=-1))
    fade = jnp.exp(highest - raised)
    weights = jnp.exp(scores - raised[..., None])
    totals = totals * fade + jnp.sum(weights, axis=-1)
    accum = accum * fade[..., None] + jnp.einsum(
        "qhk,khd->qhd",
        weights.astype(jnp.bfloat16),
        value_heads,
        preferred_element_type=jnp.float32,
    )
    return (accum, totals, raised)


def gather_body(queries, keys_proj, values, hidden, fresh_latent, gate_table, noise_step, pattern):
    group_index = lax.axis_index("tm")
    final_index = lax.axis_size("tm") - 1
    query_tok, key_tok, value_tok = (
        lax.all_to_all(queries[0], "seq", split_axis=1, concat_axis=0, tiled=True),
        lax.all_to_all(keys_proj[0], "seq", split_axis=1, concat_axis=0, tiled=True),
        lax.all_to_all(values[0], "seq", split_axis=1, concat_axis=0, tiled=True),
    )
    row_count, local_width = query_tok.shape
    head_count = local_width // HD
    query_heads = query_tok.reshape(row_count, head_count, HD)
    scale_factor = 1.0 / math.sqrt(HD)
    reach = lax.dynamic_index_in_dim(pattern, group_index, 0, keepdims=False)
    start_state = (
        jnp.zeros((row_count, head_count, HD), jnp.float32),
        jnp.zeros((row_count, head_count), jnp.float32),
        jnp.full((row_count, head_count), -1e30, jnp.float32),
    )

    def one_block(current, inputs):
        key_block, value_block, flag = inputs
        return (
            lax.cond(
                flag > 0,
                lambda state: absorb(state, query_heads, key_block, value_block, scale_factor),
                lambda state: state,
                current,
            ),
            None,
        )

    key_piece = lax.all_gather(key_tok, "tm", axis=0, tiled=False)
    value_piece = lax.all_gather(value_tok, "tm", axis=0, tiled=False)
    state, unused = lax.scan(one_block, start_state, (key_piece, value_piece, reach))
    cache_keys, cache_values = shifted((key_tok, value_tok), "tm", -1)
    accum, totals, highest = state
    attended_head = (accum / totals[..., None]).reshape(row_count, local_width).astype(jnp.bfloat16)
    attended = lax.all_to_all(attended_head, "seq", split_axis=0, concat_axis=1, tiled=True)
    gate_row = lax.dynamic_index_in_dim(gate_table, noise_step[0], 0, keepdims=False)
    updated = (
        hidden[0].astype(jnp.float32) + gate_row[None, :] * attended.astype(jnp.float32)
    ).astype(jnp.bfloat16)
    moved = shifted(updated, "tm", -1)
    advanced = jnp.where(group_index == final_index, fresh_latent, moved)[None]
    next_cache = jnp.stack([cache_keys, cache_values], axis=0)[None]
    return (advanced, next_cache)


def body(queries, *others):
    tm_count, seq_count = lax.axis_size("tm"), lax.axis_size("seq")
    _, tok, width = queries.shape
    count = tm_count * seq_count
    even = width % (count * HD) == 0 and tok % 8 == 0 and seq_count % 2 == 0
    return (spread_body if even else gather_body)(queries, *others)


def solution(mesh):
    placed = (
        P("tm", "seq", None),
        P("tm", "seq", None),
        P("tm", "seq", None),
        P("tm", "seq", None),
        P("seq", None),
        P(),
        P("tm"),
        P(),
    )
    return jax.shard_map(
        body,
        mesh=mesh,
        in_specs=placed,
        out_specs=(P("tm", "seq", None), P("tm", None, None, "seq")),
        check_vma=False,
    )
```

```python
import functools
import math

import jax
import jax.numpy as jnp
from jax import lax
from jax.experimental import pallas as pl
from jax.experimental.pallas import tpu as pltpu
from jax.sharding import PartitionSpec as P

HD = 128
BOTH = ("tm", "seq")
VMEM = pltpu.VMEM
SMEM = pltpu.SMEM
HBM = pltpu.HBM


def shifted(block, axis, distance):
    devices = range(lax.axis_size(axis))
    route = [(i - distance, i) for i in devices if i - distance in devices]
    return lax.ppermute(block, axis, route)


def mixed(index, count):
    return (index + count // 2) % count


def pack_kernel(seq_count, halves, q_hbm, k_hbm, v_hbm, out_hbm, held, block, in_sems, out_sems):
    tok, width = held.shape[1:]
    wide = out_hbm.shape[1] // 3
    count = out_hbm.shape[0] // tok
    tm_count = count // seq_count
    span, part = width // halves, seq_count // halves
    copies = []
    for half in range(halves):
        columns = slice(half * span, (half + 1) * span)
        for place, ref in enumerate((q_hbm, k_hbm, v_hbm)):
            copies.append(
                pltpu.make_async_copy(
                    ref.at[0, :, columns], held.at[place, :, columns], in_sems.at[half, place]
                )
            )
            copies[-1].start()
    outs = []
    for half in range(halves):
        for place in range(3):
            copies[3 * half + place].wait()
            for tm in range(tm_count):
                for seq in range(half * part, (half + 1) * part, 2):
                    rows = []
                    for member in (seq, seq + 1):
                        start = (member * tm_count + tm) * wide
                        rows.append(held[place, :, start : start + wide].astype(jnp.float32))
                    first = (tm * seq_count + mixed(seq, seq_count)) * tok
                    block[first : first + 2 * tok, place * wide : (place + 1) * wide] = jnp.concatenate(
                        rows, axis=0
                    ).astype(jnp.bfloat16)
        for tm in range(tm_count):
            first = (tm * seq_count + mixed(half * part, seq_count)) * tok
            rows = slice(first, first + part * tok)
            outs.append(
                pltpu.make_async_copy(block.at[rows], out_hbm.at[rows], out_sems.at[half, tm])
            )
            outs[-1].start()
    for out in outs:
        out.wait()


def residual_kernel(noise_ref, h_ref, gate_ref, after_ref, out_ref):
    gate = gate_ref[pl.ds(noise_ref[0], 1), :]
    high = gate.astype(jnp.bfloat16).astype(jnp.float32)
    middle = (gate - high).astype(jnp.bfloat16).astype(jnp.float32)
    low = gate - high - middle
    parts = jnp.concatenate([high, middle, low, jnp.zeros((5, gate.shape[1]), jnp.float32)], axis=0)
    out_ref[...] = jnp.concatenate([h_ref[0].astype(jnp.float32), parts], axis=0).astype(jnp.bfloat16)


def partner(here, distance, groups):
    return here ^ distance if groups & (groups - 1) == 0 else (here + groups - distance) % groups


def distances(groups):
    return range(groups - 1, 0, -1)


def attend_kernel(groups, pattern_ref, x_ref, after_ref, out_hbm, *refs):
    *hand_refs, held, sems = refs
    wide = held.shape[2]
    rows = held.shape[1]
    factor = math.log2(math.e) / math.sqrt(HD)
    here = lax.axis_index("tm")
    copies = []
    turned = [jnp.transpose(x_ref[:, 2 * wide + head : 2 * wide + head + HD]) for head in range(0, wide, HD)]
    for group in range(groups - 1, 0, -1):
        for head in range(0, wide, HD):
            query = x_ref[group * rows : (group + 1) * rows, head : head + HD]
            scores, peaks = [], []
            for source in range(group + 1):
                key = x_ref[source * rows : (source + 1) * rows, wide + head : wide + head + HD]
                block = lax.dot_general(
                    key, query, (((1,), (1,)), ((), ())), preferred_element_type=jnp.float32
                )
                peak = jnp.max(block, axis=0, keepdims=True)
                scores.append(block)
                peaks.append(jnp.where(pattern_ref[group, source] > 0, peak, -1e30))
            highest = functools.reduce(jnp.maximum, peaks) * factor
            total, probs = 0.0, []
            for source in range(group + 1):
                offset = jnp.where(pattern_ref[group, source] > 0, -highest, -1e30)
                raised = jnp.exp2(scores[source] * factor + offset)
                total += jnp.sum(raised, axis=0, keepdims=True)
                probs.append(raised.astype(jnp.bfloat16))
            numer = jnp.dot(
                turned[head // HD][:, : (group + 1) * rows],
                jnp.concatenate(probs, axis=0),
                preferred_element_type=jnp.float32,
            )
            held[group - 1, :, head : head + HD] = jnp.transpose(numer / total).astype(jnp.bfloat16)
        for place in (group - 1, groups - 1) if group == groups - 1 else (group - 1,):
            copies.append(
                pltpu.make_async_copy(
                    held.at[group - 1], out_hbm.at[place * rows : (place + 1) * rows], sems.at[place]
                )
            )
            copies[-1].start()
    for distance, hand_ref in zip(distances(groups), hand_refs):
        group = lax.rem(partner(here, distance, groups) + 1, groups)
        hand_ref[...] = x_ref[pl.ds(pl.multiple_of(group * rows, rows), rows), wide:]
    for copy in copies:
        copy.wait()


def cache_kernel(seq_count, x_ref, *refs):
    hand_refs, out_ref = refs[:-2], refs[-1]
    groups = len(hand_refs) + 1
    wide = x_ref.shape[1] // 3
    rows = out_ref.shape[2]
    here = lax.axis_index("tm")

    @pl.when(here == groups - 1)
    def clear():
        out_ref[...] = jnp.zeros_like(out_ref)

    @pl.when(here < groups - 1)
    def place():
        own = x_ref[pl.ds(pl.multiple_of((here + 1) * rows, rows), rows), wide:]
        tok = rows // seq_count
        for distance, block in zip((0, *distances(groups)), (own,) + hand_refs):
            source = partner(here, groups - distance if groups & (groups - 1) else distance, groups)
            lanes = pl.ds(pl.multiple_of(source * wide, wide), wide)
            for half in range(2):
                start = half * (rows // 2)
                place = mixed(half * (seq_count // 2), seq_count) * tok
                for kind in range(2):
                    out_ref[0, kind, start : start + rows // 2, lanes] = block[
                        place : place + rows // 2, kind * wide : (kind + 1) * wide
                    ]


def update_kernel(seq_count, tm_count, att_ref, moved_ref, fresh_ref, out_ref):
    tok = out_ref.shape[1]
    wide = att_ref.shape[1]
    count = att_ref.shape[0] // tok
    last = lax.axis_index("tm") == tm_count - 1

    @pl.when(last)
    def take_fresh():
        out_ref[0] = fresh_ref[...]

    @pl.when(jnp.logical_not(last))
    def take_update():
        for pair in range(count // 2):
            rows = att_ref[2 * pair * tok : 2 * (pair + 1) * tok, :].astype(jnp.float32)
            for half in range(2):
                source = 2 * pair + half
                start = (mixed(source % seq_count, seq_count) * tm_count + source // seq_count) * wide
                moved = moved_ref[:, start : start + wide].astype(jnp.float32)
                gate = (moved[tok : tok + 1] + moved[tok + 1 : tok + 2]) + moved[tok + 2 : tok + 3]
                result = moved[:tok] + gate * rows[half * tok : (half + 1) * tok]
                out_ref[0, :, start : start + wide] = result.astype(jnp.bfloat16)


def whole(space=VMEM):
    return pl.BlockSpec(memory_space=space)


def run(kernel, name, outs, specs, operands, flops=0, scratch=()):
    def size(a):
        return math.prod(a.shape) * jnp.dtype(a.dtype).itemsize

    moved = sum(map(size, operands)) + sum(map(size, outs))
    results = pl.pallas_call(
        kernel,
        out_shape=outs,
        in_specs=specs,
        out_specs=[whole(getattr(a, "memory_space", VMEM)) for a in outs],
        scratch_shapes=scratch,
        compiler_params=pltpu.CompilerParams(vmem_limit_bytes=4 * moved + (4 << 20)),
        cost_estimate=pl.CostEstimate(flops=flops, bytes_accessed=moved, transcendentals=0),
        name=name,
    )(*operands)
    return results if len(outs) > 1 else results[0]


def spread_body(queries, keys_proj, values, hidden, fresh_latent, gate_table, noise_step, pattern):
    tm_count, seq_count = lax.axis_size("tm"), lax.axis_size("seq")
    count = tm_count * seq_count
    _, tok, width = queries.shape
    wide = width // count
    group_tok = tok * seq_count
    kind = queries.dtype
    DMA = pltpu.SemaphoreType.DMA
    halves = 2

    packed = run(
        functools.partial(pack_kernel, seq_count, halves),
        "pack",
        [HBM((count * tok, 3 * wide), kind)],
        [whole(HBM)] * 3,
        [pltpu.with_memory_space_constraint(a, HBM) for a in (queries, keys_proj, values)],
        scratch=[
            VMEM((3, tok, width), kind),
            VMEM((count * tok, 3 * wide), kind),
            DMA((halves, 3)),
            DMA((halves, tm_count)),
        ],
    )
    order = [tm * seq_count + mixed(s, seq_count) for tm in range(tm_count) for s in range(seq_count)]
    exchange = functools.partial(
        lax.all_to_all, axis_name=BOTH, split_axis=0, concat_axis=0, tiled=True, axis_index_groups=[order]
    )
    exchanged = exchange(packed)

    residual = run(
        residual_kernel,
        "residual",
        [VMEM((tok + 8, width), kind)],
        [whole(SMEM), whole(), whole(), whole(HBM)],
        (noise_step, hidden, gate_table, pltpu.with_memory_space_constraint(packed, HBM)),
    )
    moved = shifted(residual, "tm", -1)

    attended, *hands = run(
        functools.partial(attend_kernel, tm_count),
        "attend",
        [HBM((count * tok, wide), kind)] + [VMEM((group_tok, 2 * wide), kind)] * (tm_count - 1),
        [whole(SMEM), whole(), whole(pl.ANY)],
        (pattern, exchanged, moved),
        flops=2 * count * tok * count * tok * wide,
        scratch=[VMEM((tm_count - 1, group_tok, wide), kind), DMA((tm_count,))],
    )
    returned = exchange(attended)
    handed = []
    for distance, hand in zip(distances(tm_count), hands):
        route = [(i, partner(i, distance, tm_count)) for i in range(tm_count)]
        handed.append(lax.ppermute(hand, "tm", [(i, j) for i, j in route if j < tm_count - 1]))

    advanced = run(
        functools.partial(update_kernel, seq_count, tm_count),
        "update",
        [jax.ShapeDtypeStruct((1, tok, width), kind)],
        [whole()] * 3,
        (returned, moved, fresh_latent),
    )
    next_cache = run(
        functools.partial(cache_kernel, seq_count),
        "cache",
        [jax.ShapeDtypeStruct((1, 2, group_tok, tm_count * wide), kind)],
        [whole()] * tm_count + [whole(HBM)],
        (exchanged, *handed, pltpu.with_memory_space_constraint(advanced, HBM)),
    )
    return (advanced, next_cache)


def absorb(state, query_heads, key_piece, value_piece, scale_factor):
    accum, totals, highest = state
    row_count, head_count, head_dim = query_heads.shape
    key_heads = key_piece.reshape(key_piece.shape[0], head_count, head_dim)
    value_heads = value_piece.reshape(value_piece.shape[0], head_count, head_dim)
    scores = (
        jnp.einsum("qhd,khd->qhk", query_heads, key_heads, preferred_element_type=jnp.float32)
        * scale_factor
    )
    raised = jnp.maximum(highest, jnp.max(scores, axis=-1))
    fade = jnp.exp(highest - raised)
    weights = jnp.exp(scores - raised[..., None])
    totals = totals * fade + jnp.sum(weights, axis=-1)
    accum = accum * fade[..., None] + jnp.einsum(
        "qhk,khd->qhd",
        weights.astype(jnp.bfloat16),
        value_heads,
        preferred_element_type=jnp.float32,
    )
    return (accum, totals, raised)


def gather_body(queries, keys_proj, values, hidden, fresh_latent, gate_table, noise_step, pattern):
    group_index = lax.axis_index("tm")
    final_index = lax.axis_size("tm") - 1
    query_tok, key_tok, value_tok = (
        lax.all_to_all(queries[0], "seq", split_axis=1, concat_axis=0, tiled=True),
        lax.all_to_all(keys_proj[0], "seq", split_axis=1, concat_axis=0, tiled=True),
        lax.all_to_all(values[0], "seq", split_axis=1, concat_axis=0, tiled=True),
    )
    row_count, local_width = query_tok.shape
    head_count = local_width // HD
    query_heads = query_tok.reshape(row_count, head_count, HD)
    scale_factor = 1.0 / math.sqrt(HD)
    reach = lax.dynamic_index_in_dim(pattern, group_index, 0, keepdims=False)
    start_state = (
        jnp.zeros((row_count, head_count, HD), jnp.float32),
        jnp.zeros((row_count, head_count), jnp.float32),
        jnp.full((row_count, head_count), -1e30, jnp.float32),
    )

    def one_block(current, inputs):
        key_block, value_block, flag = inputs
        return (
            lax.cond(
                flag > 0,
                lambda state: absorb(state, query_heads, key_block, value_block, scale_factor),
                lambda state: state,
                current,
            ),
            None,
        )

    key_piece = lax.all_gather(key_tok, "tm", axis=0, tiled=False)
    value_piece = lax.all_gather(value_tok, "tm", axis=0, tiled=False)
    state, unused = lax.scan(one_block, start_state, (key_piece, value_piece, reach))
    cache_keys, cache_values = shifted((key_tok, value_tok), "tm", -1)
    accum, totals, highest = state
    attended_head = (accum / totals[..., None]).reshape(row_count, local_width).astype(jnp.bfloat16)
    attended = lax.all_to_all(attended_head, "seq", split_axis=0, concat_axis=1, tiled=True)
    gate_row = lax.dynamic_index_in_dim(gate_table, noise_step[0], 0, keepdims=False)
    updated = (
        hidden[0].astype(jnp.float32) + gate_row[None, :] * attended.astype(jnp.float32)
    ).astype(jnp.bfloat16)
    moved = shifted(updated, "tm", -1)
    advanced = jnp.where(group_index == final_index, fresh_latent, moved)[None]
    next_cache = jnp.stack([cache_keys, cache_values], axis=0)[None]
    return (advanced, next_cache)


def body(queries, *others):
    tm_count, seq_count = lax.axis_size("tm"), lax.axis_size("seq")
    _, tok, width = queries.shape
    count = tm_count * seq_count
    even = width % (count * HD) == 0 and tok % 8 == 0 and seq_count % 4 == 0
    return (spread_body if even else gather_body)(queries, *others)


def solution(mesh):
    placed = (
        P("tm", "seq", None),
        P("tm", "seq", None),
        P("tm", "seq", None),
        P("tm", "seq", None),
        P("seq", None),
        P(),
        P("tm"),
        P(),
    )
    return jax.shard_map(
        body,
        mesh=mesh,
        in_specs=placed,
        out_specs=(P("tm", "seq", None), P("tm", None, None, "seq")),
        check_vma=False,
    )
```

```python
import functools
import math

import jax
import jax.numpy as jnp
from jax import lax
from jax.experimental import pallas as pl
from jax.experimental.pallas import tpu as pltpu
from jax.sharding import PartitionSpec as P

HD = 128
BOTH = ("tm", "seq")
VMEM = pltpu.VMEM
SMEM = pltpu.SMEM
HBM = pltpu.HBM


def shifted(block, axis, distance):
    devices = range(lax.axis_size(axis))
    route = [(i - distance, i) for i in devices if i - distance in devices]
    return lax.ppermute(block, axis, route)


def mixed(index, count):
    return (index + count // 2) % count


def pack_kernel(seq_count, halves, q_hbm, k_hbm, v_hbm, out_hbm, held, block, in_sems, out_sems):
    tok, width = held.shape[1:]
    wide = out_hbm.shape[1] // 3
    count = out_hbm.shape[0] // tok
    tm_count = count // seq_count
    span, part = width // halves, seq_count // halves
    copies = []
    for half in range(halves):
        columns = slice(half * span, (half + 1) * span)
        for place, ref in enumerate((q_hbm, k_hbm, v_hbm)):
            copies.append(
                pltpu.make_async_copy(
                    ref.at[0, :, columns], held.at[place, :, columns], in_sems.at[half, place]
                )
            )
            copies[-1].start()
    outs = []
    for half in range(halves):
        for place in range(3):
            copies[3 * half + place].wait()
            for tm in range(tm_count):
                for seq in range(half * part, (half + 1) * part, 2):
                    rows = []
                    for member in (seq, seq + 1):
                        start = (member * tm_count + tm) * wide
                        rows.append(held[place, :, start : start + wide].astype(jnp.float32))
                    first = (tm * seq_count + mixed(seq, seq_count)) * tok
                    block[first : first + 2 * tok, place * wide : (place + 1) * wide] = jnp.concatenate(
                        rows, axis=0
                    ).astype(jnp.bfloat16)
        for tm in range(tm_count):
            first = (tm * seq_count + mixed(half * part, seq_count)) * tok
            rows = slice(first, first + part * tok)
            outs.append(
                pltpu.make_async_copy(block.at[rows], out_hbm.at[rows], out_sems.at[half, tm])
            )
            outs[-1].start()
    for out in outs:
        out.wait()


def residual_kernel(noise_ref, h_ref, gate_ref, after_ref, out_ref):
    gate = gate_ref[pl.ds(noise_ref[0], 1), :]
    high = gate.astype(jnp.bfloat16).astype(jnp.float32)
    middle = (gate - high).astype(jnp.bfloat16).astype(jnp.float32)
    low = gate - high - middle
    parts = jnp.concatenate([high, middle, low, jnp.zeros((5, gate.shape[1]), jnp.float32)], axis=0)
    out_ref[...] = jnp.concatenate([h_ref[0].astype(jnp.float32), parts], axis=0).astype(jnp.bfloat16)


def partner(here, distance, groups):
    return here ^ distance if groups & (groups - 1) == 0 else (here + groups - distance) % groups


def distances(groups):
    return range(groups - 1, 0, -1)


def attend_kernel(groups, pattern_ref, x_ref, after_ref, out_hbm, *refs):
    *hand_refs, held, sems = refs
    wide = held.shape[2]
    rows = held.shape[1]
    across = (groups - 1) * rows
    factor = math.log2(math.e) / math.sqrt(HD)
    here = lax.axis_index("tm")
    lane = lax.broadcasted_iota(jnp.int32, (1, across), 1)
    ends, kept = [], []
    for source in range(groups):
        first = max(source, 1)
        ends.append(min(across, -(-(groups - first) * rows // 128) * 128))
        chosen = jnp.zeros((1, across), jnp.int32)
        for group in range(first, groups):
            start = (groups - 1 - group) * rows
            chosen = jnp.where((lane >= start) & (lane < start + rows), pattern_ref[group, source], chosen)
        kept.append(chosen[:, : ends[-1]] > 0)

    def spread(row, fill):
        rest = across - row.shape[1]
        return jnp.concatenate([row, jnp.full((1, rest), fill, row.dtype)], axis=1) if rest else row

    for head in range(0, wide, HD):
        query = jnp.concatenate(
            [x_ref[group * rows : (group + 1) * rows, head : head + HD] for group in range(groups - 1, 0, -1)],
            axis=0,
        )
        query = jnp.transpose(query)
        value = jnp.transpose(x_ref[:, 2 * wide + head : 2 * wide + head + HD])
        scores, highest = [], None
        for source in range(groups):
            key = x_ref[source * rows : (source + 1) * rows, wide + head : wide + head + HD]
            scores.append(
                jnp.dot(key, query[:, : ends[source]], preferred_element_type=jnp.float32)
            )
            peak = jnp.where(kept[source], jnp.max(scores[-1], axis=0, keepdims=True), -1e30)
            peak = spread(peak, -1e30)
            highest = peak if highest is None else jnp.maximum(highest, peak)
        highest = highest * factor
        total, probs = 0.0, []
        for source in range(groups):
            offset = jnp.where(kept[source], -highest[:, : ends[source]], -1e30)
            raised = jnp.exp2(scores[source] * factor + offset)
            total += spread(jnp.sum(raised, axis=0, keepdims=True), 0.0)
            probs.append(raised.astype(jnp.bfloat16))
        inverse = 1.0 / total
        start, pieces = 0, []
        for source in range(groups - 1, 0, -1):
            stop = ends[source]
            if stop > start:
                numer = jnp.dot(
                    value[:, : (source + 1) * rows],
                    jnp.concatenate([p[:, start:stop] for p in probs[: source + 1]], axis=0),
                    preferred_element_type=jnp.float32,
                )
                pieces.append(numer * inverse[:, start:stop])
                start = stop
        result = jnp.transpose(jnp.concatenate(pieces, axis=1)).astype(jnp.bfloat16)
        for group in range(1, groups):
            start = (groups - 1 - group) * rows
            held[group - 1, :, head : head + HD] = result[start : start + rows]
    copies = [
        pltpu.make_async_copy(
            held.at[min(place, groups - 2)], out_hbm.at[place * rows : (place + 1) * rows], sems.at[place]
        )
        for place in range(groups)
    ]
    for copy in copies:
        copy.start()
    for distance, hand_ref in zip(distances(groups), hand_refs):
        group = lax.rem(partner(here, distance, groups) + 1, groups)
        hand_ref[...] = x_ref[pl.ds(pl.multiple_of(group * rows, rows), rows), wide:]
    for copy in copies:
        copy.wait()


def cache_kernel(seq_count, x_ref, *refs):
    hand_refs, out_ref = refs[:-2], refs[-1]
    groups = len(hand_refs) + 1
    wide = x_ref.shape[1] // 3
    rows = out_ref.shape[2]
    here = lax.axis_index("tm")

    @pl.when(here == groups - 1)
    def clear():
        out_ref[...] = jnp.zeros_like(out_ref)

    @pl.when(here < groups - 1)
    def place():
        own = x_ref[pl.ds(pl.multiple_of((here + 1) * rows, rows), rows), wide:]
        tok = rows // seq_count
        for distance, block in zip((0, *distances(groups)), (own,) + hand_refs):
            source = partner(here, groups - distance if groups & (groups - 1) else distance, groups)
            lanes = pl.ds(pl.multiple_of(source * wide, wide), wide)
            for half in range(2):
                start = half * (rows // 2)
                place = mixed(half * (seq_count // 2), seq_count) * tok
                for kind in range(2):
                    out_ref[0, kind, start : start + rows // 2, lanes] = block[
                        place : place + rows // 2, kind * wide : (kind + 1) * wide
                    ]


def update_kernel(seq_count, tm_count, att_ref, moved_ref, fresh_ref, out_ref):
    tok = out_ref.shape[1]
    wide = att_ref.shape[1]
    count = att_ref.shape[0] // tok
    last = lax.axis_index("tm") == tm_count - 1

    @pl.when(last)
    def take_fresh():
        out_ref[0] = fresh_ref[...]

    @pl.when(jnp.logical_not(last))
    def take_update():
        for pair in range(count // 2):
            rows = att_ref[2 * pair * tok : 2 * (pair + 1) * tok, :].astype(jnp.float32)
            for half in range(2):
                source = 2 * pair + half
                start = (mixed(source % seq_count, seq_count) * tm_count + source // seq_count) * wide
                moved = moved_ref[:, start : start + wide].astype(jnp.float32)
                gate = (moved[tok : tok + 1] + moved[tok + 1 : tok + 2]) + moved[tok + 2 : tok + 3]
                result = moved[:tok] + gate * rows[half * tok : (half + 1) * tok]
                out_ref[0, :, start : start + wide] = result.astype(jnp.bfloat16)


def whole(space=VMEM):
    return pl.BlockSpec(memory_space=space)


def run(kernel, name, outs, specs, operands, flops=0, scratch=()):
    def size(a):
        return math.prod(a.shape) * jnp.dtype(a.dtype).itemsize

    moved = sum(map(size, operands)) + sum(map(size, outs))
    results = pl.pallas_call(
        kernel,
        out_shape=outs,
        in_specs=specs,
        out_specs=[whole(getattr(a, "memory_space", VMEM)) for a in outs],
        scratch_shapes=scratch,
        compiler_params=pltpu.CompilerParams(vmem_limit_bytes=4 * moved + (4 << 20)),
        cost_estimate=pl.CostEstimate(flops=flops, bytes_accessed=moved, transcendentals=0),
        name=name,
    )(*operands)
    return results if len(outs) > 1 else results[0]


def spread_body(queries, keys_proj, values, hidden, fresh_latent, gate_table, noise_step, pattern):
    tm_count, seq_count = lax.axis_size("tm"), lax.axis_size("seq")
    count = tm_count * seq_count
    _, tok, width = queries.shape
    wide = width // count
    group_tok = tok * seq_count
    kind = queries.dtype
    DMA = pltpu.SemaphoreType.DMA
    halves = 2

    packed = run(
        functools.partial(pack_kernel, seq_count, halves),
        "pack",
        [HBM((count * tok, 3 * wide), kind)],
        [whole(HBM)] * 3,
        [pltpu.with_memory_space_constraint(a, HBM) for a in (queries, keys_proj, values)],
        scratch=[
            VMEM((3, tok, width), kind),
            VMEM((count * tok, 3 * wide), kind),
            DMA((halves, 3)),
            DMA((halves, tm_count)),
        ],
    )
    order = [tm * seq_count + mixed(s, seq_count) for tm in range(tm_count) for s in range(seq_count)]
    exchange = functools.partial(
        lax.all_to_all, axis_name=BOTH, split_axis=0, concat_axis=0, tiled=True, axis_index_groups=[order]
    )
    exchanged = exchange(packed)

    residual = run(
        residual_kernel,
        "residual",
        [VMEM((tok + 8, width), kind)],
        [whole(SMEM), whole(), whole(), whole(HBM)],
        (noise_step, hidden, gate_table, pltpu.with_memory_space_constraint(packed, HBM)),
    )
    moved = shifted(residual, "tm", -1)

    attended, *hands = run(
        functools.partial(attend_kernel, tm_count),
        "attend",
        [HBM((count * tok, wide), kind)] + [VMEM((group_tok, 2 * wide), kind)] * (tm_count - 1),
        [whole(SMEM), whole(), whole(pl.ANY)],
        (pattern, exchanged, moved),
        flops=2 * count * tok * count * tok * wide,
        scratch=[VMEM((tm_count - 1, group_tok, wide), kind), DMA((tm_count,))],
    )
    returned = exchange(attended)
    handed = []
    for distance, hand in zip(distances(tm_count), hands):
        route = [(i, partner(i, distance, tm_count)) for i in range(tm_count)]
        handed.append(lax.ppermute(hand, "tm", [(i, j) for i, j in route if j < tm_count - 1]))

    advanced = run(
        functools.partial(update_kernel, seq_count, tm_count),
        "update",
        [jax.ShapeDtypeStruct((1, tok, width), kind)],
        [whole()] * 3,
        (returned, moved, fresh_latent),
    )
    next_cache = run(
        functools.partial(cache_kernel, seq_count),
        "cache",
        [jax.ShapeDtypeStruct((1, 2, group_tok, tm_count * wide), kind)],
        [whole()] * tm_count + [whole(HBM)],
        (exchanged, *handed, pltpu.with_memory_space_constraint(advanced, HBM)),
    )
    return (advanced, next_cache)


def absorb(state, query_heads, key_piece, value_piece, scale_factor):
    accum, totals, highest = state
    row_count, head_count, head_dim = query_heads.shape
    key_heads = key_piece.reshape(key_piece.shape[0], head_count, head_dim)
    value_heads = value_piece.reshape(value_piece.shape[0], head_count, head_dim)
    scores = (
        jnp.einsum("qhd,khd->qhk", query_heads, key_heads, preferred_element_type=jnp.float32)
        * scale_factor
    )
    raised = jnp.maximum(highest, jnp.max(scores, axis=-1))
    fade = jnp.exp(highest - raised)
    weights = jnp.exp(scores - raised[..., None])
    totals = totals * fade + jnp.sum(weights, axis=-1)
    accum = accum * fade[..., None] + jnp.einsum(
        "qhk,khd->qhd",
        weights.astype(jnp.bfloat16),
        value_heads,
        preferred_element_type=jnp.float32,
    )
    return (accum, totals, raised)


def gather_body(queries, keys_proj, values, hidden, fresh_latent, gate_table, noise_step, pattern):
    group_index = lax.axis_index("tm")
    final_index = lax.axis_size("tm") - 1
    query_tok, key_tok, value_tok = (
        lax.all_to_all(queries[0], "seq", split_axis=1, concat_axis=0, tiled=True),
        lax.all_to_all(keys_proj[0], "seq", split_axis=1, concat_axis=0, tiled=True),
        lax.all_to_all(values[0], "seq", split_axis=1, concat_axis=0, tiled=True),
    )
    row_count, local_width = query_tok.shape
    head_count = local_width // HD
    query_heads = query_tok.reshape(row_count, head_count, HD)
    scale_factor = 1.0 / math.sqrt(HD)
    reach = lax.dynamic_index_in_dim(pattern, group_index, 0, keepdims=False)
    start_state = (
        jnp.zeros((row_count, head_count, HD), jnp.float32),
        jnp.zeros((row_count, head_count), jnp.float32),
        jnp.full((row_count, head_count), -1e30, jnp.float32),
    )

    def one_block(current, inputs):
        key_block, value_block, flag = inputs
        return (
            lax.cond(
                flag > 0,
                lambda state: absorb(state, query_heads, key_block, value_block, scale_factor),
                lambda state: state,
                current,
            ),
            None,
        )

    key_piece = lax.all_gather(key_tok, "tm", axis=0, tiled=False)
    value_piece = lax.all_gather(value_tok, "tm", axis=0, tiled=False)
    state, unused = lax.scan(one_block, start_state, (key_piece, value_piece, reach))
    cache_keys, cache_values = shifted((key_tok, value_tok), "tm", -1)
    accum, totals, highest = state
    attended_head = (accum / totals[..., None]).reshape(row_count, local_width).astype(jnp.bfloat16)
    attended = lax.all_to_all(attended_head, "seq", split_axis=0, concat_axis=1, tiled=True)
    gate_row = lax.dynamic_index_in_dim(gate_table, noise_step[0], 0, keepdims=False)
    updated = (
        hidden[0].astype(jnp.float32) + gate_row[None, :] * attended.astype(jnp.float32)
    ).astype(jnp.bfloat16)
    moved = shifted(updated, "tm", -1)
    advanced = jnp.where(group_index == final_index, fresh_latent, moved)[None]
    next_cache = jnp.stack([cache_keys, cache_values], axis=0)[None]
    return (advanced, next_cache)


def body(queries, *others):
    tm_count, seq_count = lax.axis_size("tm"), lax.axis_size("seq")
    _, tok, width = queries.shape
    count = tm_count * seq_count
    even = width % (count * HD) == 0 and tok % 8 == 0 and seq_count % 4 == 0
    return (spread_body if even else gather_body)(queries, *others)


def solution(mesh):
    placed = (
        P("tm", "seq", None),
        P("tm", "seq", None),
        P("tm", "seq", None),
        P("tm", "seq", None),
        P("seq", None),
        P(),
        P("tm"),
        P(),
    )
    return jax.shard_map(
        body,
        mesh=mesh,
        in_specs=placed,
        out_specs=(P("tm", "seq", None), P("tm", None, None, "seq")),
        check_vma=False,
    )
```

```python
import functools
import math

import jax
import jax.numpy as jnp
from jax import lax
from jax.experimental import pallas as pl
from jax.experimental.pallas import tpu as pltpu
from jax.sharding import PartitionSpec as P

HD = 128
BOTH = ("tm", "seq")
VMEM = pltpu.VMEM
SMEM = pltpu.SMEM
HBM = pltpu.HBM


def shifted(block, axis, distance):
    devices = range(lax.axis_size(axis))
    route = [(i - distance, i) for i in devices if i - distance in devices]
    return lax.ppermute(block, axis, route)


def mixed(index, count):
    return (index + count // 2) % count


def pack_kernel(seq_count, halves, q_hbm, k_hbm, v_hbm, out_hbm, held, block, in_sems, out_sems):
    tok, width = held.shape[1:]
    wide = out_hbm.shape[1] // 3
    count = out_hbm.shape[0] // tok
    tm_count = count // seq_count
    span, part = width // halves, seq_count // halves
    copies = []
    for half in range(halves):
        columns = slice(half * span, (half + 1) * span)
        for place, ref in enumerate((q_hbm, k_hbm, v_hbm)):
            copies.append(
                pltpu.make_async_copy(
                    ref.at[0, :, columns], held.at[place, :, columns], in_sems.at[half, place]
                )
            )
            copies[-1].start()
    outs = []
    for half in range(halves):
        for place in range(3):
            copies[3 * half + place].wait()
            for tm in range(tm_count):
                for seq in range(half * part, (half + 1) * part, 2):
                    rows = []
                    for member in (seq, seq + 1):
                        start = (member * tm_count + tm) * wide
                        rows.append(held[place, :, start : start + wide].astype(jnp.float32))
                    first = (tm * seq_count + mixed(seq, seq_count)) * tok
                    block[first : first + 2 * tok, place * wide : (place + 1) * wide] = jnp.concatenate(
                        rows, axis=0
                    ).astype(jnp.bfloat16)
        for tm in range(tm_count):
            first = (tm * seq_count + mixed(half * part, seq_count)) * tok
            rows = slice(first, first + part * tok)
            outs.append(
                pltpu.make_async_copy(block.at[rows], out_hbm.at[rows], out_sems.at[half, tm])
            )
            outs[-1].start()
    for out in outs:
        out.wait()


def residual_kernel(noise_ref, h_ref, gate_ref, after_ref, out_ref):
    gate = gate_ref[pl.ds(noise_ref[0], 1), :]
    high = gate.astype(jnp.bfloat16).astype(jnp.float32)
    middle = (gate - high).astype(jnp.bfloat16).astype(jnp.float32)
    low = gate - high - middle
    parts = jnp.concatenate([high, middle, low, jnp.zeros((5, gate.shape[1]), jnp.float32)], axis=0)
    out_ref[...] = jnp.concatenate([h_ref[0].astype(jnp.float32), parts], axis=0).astype(jnp.bfloat16)


def partner(here, distance, groups):
    return here ^ distance if groups & (groups - 1) == 0 else (here + groups - distance) % groups


def distances(groups):
    return range(groups - 1, 0, -1)


def attend_kernel(groups, pattern_ref, x_ref, after_ref, out_hbm, *refs):
    *hand_refs, held, sems = refs
    wide = held.shape[2]
    rows = held.shape[1]
    across = (groups - 1) * rows
    factor = math.log2(math.e) / math.sqrt(HD)
    here = lax.axis_index("tm")
    lane = lax.broadcasted_iota(jnp.int32, (1, across), 1)
    ends, kept = [], []
    for source in range(groups):
        first = max(source, 1)
        ends.append(min(across, -(-(groups - first) * rows // 128) * 128))
        chosen = jnp.zeros((1, across), jnp.int32)
        for group in range(first, groups):
            start = (groups - 1 - group) * rows
            flag = pattern_ref[group : group + 1, source : source + 1]
            chosen = jnp.where((lane >= start) & (lane < start + rows), flag, chosen)
        kept.append(chosen[:, : ends[-1]] > 0)

    def spread(row, fill):
        rest = across - row.shape[1]
        return jnp.concatenate([row, jnp.full((1, rest), fill, row.dtype)], axis=1) if rest else row

    for head in range(0, wide, HD):
        query = jnp.concatenate(
            [x_ref[group * rows : (group + 1) * rows, head : head + HD] for group in range(groups - 1, 0, -1)],
            axis=0,
        )
        query = jnp.transpose(query)
        value = jnp.transpose(x_ref[:, 2 * wide + head : 2 * wide + head + HD])
        scores, highest = [], None
        for source in range(groups):
            key = x_ref[source * rows : (source + 1) * rows, wide + head : wide + head + HD]
            scores.append(
                jnp.dot(key, query[:, : ends[source]], preferred_element_type=jnp.float32)
            )
            peak = jnp.where(kept[source], jnp.max(scores[-1], axis=0, keepdims=True), -1e30)
            peak = spread(peak, -1e30)
            highest = peak if highest is None else jnp.maximum(highest, peak)
        highest = highest * factor
        total, probs = 0.0, []
        for source in range(groups):
            offset = jnp.where(kept[source], -highest[:, : ends[source]], -1e30)
            raised = jnp.exp2(scores[source] * factor + offset)
            total += spread(jnp.sum(raised, axis=0, keepdims=True), 0.0)
            probs.append(raised.astype(jnp.bfloat16))
        inverse = 1.0 / total
        start, pieces = 0, []
        for source in range(groups - 1, 0, -1):
            stop = ends[source]
            if stop > start:
                numer = jnp.dot(
                    value[:, : (source + 1) * rows],
                    jnp.concatenate([p[:, start:stop] for p in probs[: source + 1]], axis=0),
                    preferred_element_type=jnp.float32,
                )
                pieces.append(numer * inverse[:, start:stop])
                start = stop
        result = jnp.transpose(jnp.concatenate(pieces, axis=1)).astype(jnp.bfloat16)
        for group in range(1, groups):
            start = (groups - 1 - group) * rows
            held[group - 1, :, head : head + HD] = result[start : start + rows]
    copies = [
        pltpu.make_async_copy(
            held.at[min(place, groups - 2)], out_hbm.at[place * rows : (place + 1) * rows], sems.at[place]
        )
        for place in range(groups)
    ]
    for copy in copies:
        copy.start()
    for distance, hand_ref in zip(distances(groups), hand_refs):
        group = lax.rem(partner(here, distance, groups) + 1, groups)
        hand_ref[...] = x_ref[pl.ds(pl.multiple_of(group * rows, rows), rows), wide:]
    for copy in copies:
        copy.wait()


def cache_places(seq_count, groups, rows, wide, distance, here):
    source = partner(here, groups - distance if groups & (groups - 1) else distance, groups)
    lanes = pl.ds(pl.multiple_of(source * wide, wide), wide)
    tok = rows // seq_count
    for half in range(2):
        start = half * (rows // 2)
        place = mixed(half * (seq_count // 2), seq_count) * tok
        yield slice(start, start + rows // 2), lanes, slice(place, place + rows // 2)


def cache_kernel(seq_count, groups, x_ref, hand_ref, out_ref):
    wide = x_ref.shape[1] // 3
    rows = out_ref.shape[2]
    here = lax.axis_index("tm")
    out_ref[...] = jnp.zeros_like(out_ref)

    @pl.when(here < groups - 1)
    def place():
        own = x_ref[pl.ds(pl.multiple_of((here + 1) * rows, rows), rows), wide:]
        for distance, block in ((0, own), (distances(groups)[0], hand_ref)):
            for to, lanes, at in cache_places(seq_count, groups, rows, wide, distance, here):
                for kind in range(2):
                    out_ref[0, kind, to, lanes] = block[at, kind * wide : (kind + 1) * wide]


def cache_rest_kernel(seq_count, groups, begun_hbm, after_ref, *refs):
    *hand_refs, out_hbm, sems = refs
    wide = hand_refs[0].shape[1] // 2
    rows = out_hbm.shape[2]
    here = lax.axis_index("tm")

    @pl.when(here < groups - 1)
    def place():
        copies = []
        for distance, block in zip(distances(groups)[1:], hand_refs):
            for to, lanes, at in cache_places(seq_count, groups, rows, wide, distance, here):
                for kind in range(2):
                    copies.append(
                        pltpu.make_async_copy(
                            block.at[at, kind * wide : (kind + 1) * wide],
                            out_hbm.at[0, kind, to, lanes],
                            sems.at[len(copies)],
                        )
                    )
                    copies[-1].start()
        for copy in copies:
            copy.wait()


def update_kernel(seq_count, tm_count, att_ref, moved_ref, fresh_ref, after_ref, out_ref):
    tok = out_ref.shape[1]
    wide = att_ref.shape[1]
    count = att_ref.shape[0] // tok
    last = lax.axis_index("tm") == tm_count - 1

    @pl.when(last)
    def take_fresh():
        out_ref[0] = fresh_ref[...]

    @pl.when(jnp.logical_not(last))
    def take_update():
        for pair in range(count // 2):
            rows = att_ref[2 * pair * tok : 2 * (pair + 1) * tok, :].astype(jnp.float32)
            for half in range(2):
                source = 2 * pair + half
                start = (mixed(source % seq_count, seq_count) * tm_count + source // seq_count) * wide
                moved = moved_ref[:, start : start + wide].astype(jnp.float32)
                gate = (moved[tok : tok + 1] + moved[tok + 1 : tok + 2]) + moved[tok + 2 : tok + 3]
                result = moved[:tok] + gate * rows[half * tok : (half + 1) * tok]
                out_ref[0, :, start : start + wide] = result.astype(jnp.bfloat16)


def whole(space=VMEM):
    return pl.BlockSpec(memory_space=space)


def run(kernel, name, outs, specs, operands, flops=0, scratch=(), aliases={}):
    def size(a):
        return math.prod(a.shape) * jnp.dtype(a.dtype).itemsize

    moved = sum(map(size, operands)) + sum(map(size, outs))
    results = pl.pallas_call(
        kernel,
        out_shape=outs,
        in_specs=specs,
        out_specs=[whole(getattr(a, "memory_space", VMEM)) for a in outs],
        scratch_shapes=scratch,
        input_output_aliases=aliases,
        compiler_params=pltpu.CompilerParams(vmem_limit_bytes=4 * moved + (4 << 20)),
        cost_estimate=pl.CostEstimate(flops=flops, bytes_accessed=moved, transcendentals=0),
        name=name,
    )(*operands)
    return results if len(outs) > 1 else results[0]


def spread_body(queries, keys_proj, values, hidden, fresh_latent, gate_table, noise_step, pattern):
    tm_count, seq_count = lax.axis_size("tm"), lax.axis_size("seq")
    count = tm_count * seq_count
    _, tok, width = queries.shape
    wide = width // count
    group_tok = tok * seq_count
    kind = queries.dtype
    DMA = pltpu.SemaphoreType.DMA
    halves = 2

    packed = run(
        functools.partial(pack_kernel, seq_count, halves),
        "pack",
        [HBM((count * tok, 3 * wide), kind)],
        [whole(HBM)] * 3,
        [pltpu.with_memory_space_constraint(a, HBM) for a in (queries, keys_proj, values)],
        scratch=[
            VMEM((3, tok, width), kind),
            VMEM((count * tok, 3 * wide), kind),
            DMA((halves, 3)),
            DMA((halves, tm_count)),
        ],
    )
    order = [tm * seq_count + mixed(s, seq_count) for tm in range(tm_count) for s in range(seq_count)]
    exchange = functools.partial(
        lax.all_to_all, axis_name=BOTH, split_axis=0, concat_axis=0, tiled=True, axis_index_groups=[order]
    )
    exchanged = exchange(packed)

    residual = run(
        residual_kernel,
        "residual",
        [VMEM((tok + 8, width), kind)],
        [whole(SMEM), whole(), whole(), whole(HBM)],
        (noise_step, hidden, gate_table, pltpu.with_memory_space_constraint(packed, HBM)),
    )
    moved = shifted(residual, "tm", -1)

    attended, *hands = run(
        functools.partial(attend_kernel, tm_count),
        "attend",
        [HBM((count * tok, wide), kind)] + [VMEM((group_tok, 2 * wide), kind)] * (tm_count - 1),
        [whole(), whole(), whole(pl.ANY)],
        (pattern, exchanged, moved),
        flops=2 * count * tok * count * tok * wide,
        scratch=[VMEM((tm_count - 1, group_tok, wide), kind), DMA((tm_count,))],
    )
    returned = exchange(attended)
    handed = []
    for distance, hand in zip(distances(tm_count), hands):
        route = [(i, partner(i, distance, tm_count)) for i in range(tm_count)]
        handed.append(lax.ppermute(hand, "tm", [(i, j) for i, j in route if j < tm_count - 1]))

    first, *rest = handed
    begun = run(
        functools.partial(cache_kernel, seq_count, tm_count),
        "cache",
        [jax.ShapeDtypeStruct((1, 2, group_tok, tm_count * wide), kind)],
        [whole()] * 2,
        (exchanged, first),
    )
    begun = pltpu.with_memory_space_constraint(begun, HBM)
    advanced = run(
        functools.partial(update_kernel, seq_count, tm_count),
        "update",
        [jax.ShapeDtypeStruct((1, tok, width), kind)],
        [whole()] * 3 + [whole(HBM)],
        (returned, moved, fresh_latent, begun),
    )
    next_cache = run(
        functools.partial(cache_rest_kernel, seq_count, tm_count),
        "cache_rest",
        [HBM(begun.shape, kind)],
        [whole(HBM)] * 2 + [whole()] * len(rest),
        (begun, pltpu.with_memory_space_constraint(advanced, HBM), *rest),
        scratch=[DMA((4 * len(rest),))],
        aliases={0: 0},
    )
    return (advanced, next_cache)


def absorb(state, query_heads, key_piece, value_piece, scale_factor):
    accum, totals, highest = state
    row_count, head_count, head_dim = query_heads.shape
    key_heads = key_piece.reshape(key_piece.shape[0], head_count, head_dim)
    value_heads = value_piece.reshape(value_piece.shape[0], head_count, head_dim)
    scores = (
        jnp.einsum("qhd,khd->qhk", query_heads, key_heads, preferred_element_type=jnp.float32)
        * scale_factor
    )
    raised = jnp.maximum(highest, jnp.max(scores, axis=-1))
    fade = jnp.exp(highest - raised)
    weights = jnp.exp(scores - raised[..., None])
    totals = totals * fade + jnp.sum(weights, axis=-1)
    accum = accum * fade[..., None] + jnp.einsum(
        "qhk,khd->qhd",
        weights.astype(jnp.bfloat16),
        value_heads,
        preferred_element_type=jnp.float32,
    )
    return (accum, totals, raised)


def gather_body(queries, keys_proj, values, hidden, fresh_latent, gate_table, noise_step, pattern):
    group_index = lax.axis_index("tm")
    final_index = lax.axis_size("tm") - 1
    query_tok, key_tok, value_tok = (
        lax.all_to_all(queries[0], "seq", split_axis=1, concat_axis=0, tiled=True),
        lax.all_to_all(keys_proj[0], "seq", split_axis=1, concat_axis=0, tiled=True),
        lax.all_to_all(values[0], "seq", split_axis=1, concat_axis=0, tiled=True),
    )
    row_count, local_width = query_tok.shape
    head_count = local_width // HD
    query_heads = query_tok.reshape(row_count, head_count, HD)
    scale_factor = 1.0 / math.sqrt(HD)
    reach = lax.dynamic_index_in_dim(pattern, group_index, 0, keepdims=False)
    start_state = (
        jnp.zeros((row_count, head_count, HD), jnp.float32),
        jnp.zeros((row_count, head_count), jnp.float32),
        jnp.full((row_count, head_count), -1e30, jnp.float32),
    )

    def one_block(current, inputs):
        key_block, value_block, flag = inputs
        return (
            lax.cond(
                flag > 0,
                lambda state: absorb(state, query_heads, key_block, value_block, scale_factor),
                lambda state: state,
                current,
            ),
            None,
        )

    key_piece = lax.all_gather(key_tok, "tm", axis=0, tiled=False)
    value_piece = lax.all_gather(value_tok, "tm", axis=0, tiled=False)
    state, unused = lax.scan(one_block, start_state, (key_piece, value_piece, reach))
    cache_keys, cache_values = shifted((key_tok, value_tok), "tm", -1)
    accum, totals, highest = state
    attended_head = (accum / totals[..., None]).reshape(row_count, local_width).astype(jnp.bfloat16)
    attended = lax.all_to_all(attended_head, "seq", split_axis=0, concat_axis=1, tiled=True)
    gate_row = lax.dynamic_index_in_dim(gate_table, noise_step[0], 0, keepdims=False)
    updated = (
        hidden[0].astype(jnp.float32) + gate_row[None, :] * attended.astype(jnp.float32)
    ).astype(jnp.bfloat16)
    moved = shifted(updated, "tm", -1)
    advanced = jnp.where(group_index == final_index, fresh_latent, moved)[None]
    next_cache = jnp.stack([cache_keys, cache_values], axis=0)[None]
    return (advanced, next_cache)


def body(queries, *others):
    tm_count, seq_count = lax.axis_size("tm"), lax.axis_size("seq")
    _, tok, width = queries.shape
    count = tm_count * seq_count
    even = width % (count * HD) == 0 and tok % 8 == 0 and seq_count % 4 == 0 and tm_count > 2
    return (spread_body if even else gather_body)(queries, *others)


def solution(mesh):
    placed = (
        P("tm", "seq", None),
        P("tm", "seq", None),
        P("tm", "seq", None),
        P("tm", "seq", None),
        P("seq", None),
        P(),
        P("tm"),
        P(),
    )
    return jax.shard_map(
        body,
        mesh=mesh,
        in_specs=placed,
        out_specs=(P("tm", "seq", None), P("tm", None, None, "seq")),
        check_vma=False,
    )
```

```python
import functools
import math

import jax
import jax.numpy as jnp
from jax import lax
from jax.experimental import pallas as pl
from jax.experimental.pallas import tpu as pltpu
from jax.sharding import PartitionSpec as P

HD = 128
BOTH = ("tm", "seq")
VMEM = pltpu.VMEM
SMEM = pltpu.SMEM
HBM = pltpu.HBM


def shifted(block, axis, distance):
    devices = range(lax.axis_size(axis))
    route = [(i - distance, i) for i in devices if i - distance in devices]
    return lax.ppermute(block, axis, route)


def mixed(index, count):
    return (index + count // 2) % count


def pack_kernel(seq_count, parts, q_hbm, k_hbm, v_hbm, out_hbm, held, block, in_sems, out_sems):
    tok, width = held.shape[1:]
    wide = out_hbm.shape[1] // 3
    count = out_hbm.shape[0] // tok
    tm_count = count // seq_count
    span, members = width // parts, seq_count // parts
    copies = []
    for part in range(parts):
        columns = slice(part * span, (part + 1) * span)
        for place, ref in enumerate((q_hbm, k_hbm, v_hbm)):
            copies.append(
                pltpu.make_async_copy(
                    ref.at[0, :, columns], held.at[place, :, columns], in_sems.at[part, place]
                )
            )
            copies[-1].start()
    outs = []
    for part in range(parts):
        for place in range(3):
            copies[3 * part + place].wait()
        for tm in range(tm_count):
            for seq in range(part * members, (part + 1) * members, 2):
                first = (tm * seq_count + mixed(seq, seq_count)) * tok
                for place in range(3):
                    rows = []
                    for member in (seq, seq + 1):
                        start = (member * tm_count + tm) * wide
                        rows.append(held[place, :, start : start + wide].astype(jnp.float32))
                    block[first : first + 2 * tok, place * wide : (place + 1) * wide] = jnp.concatenate(
                        rows, axis=0
                    ).astype(jnp.bfloat16)
            first = (tm * seq_count + mixed(part * members, seq_count)) * tok
            rows = slice(first, first + members * tok)
            outs.append(
                pltpu.make_async_copy(block.at[rows], out_hbm.at[rows], out_sems.at[part, tm])
            )
            outs[-1].start()
    for out in outs:
        out.wait()


def residual_kernel(noise_ref, h_ref, gate_ref, after_ref, out_ref):
    gate = gate_ref[pl.ds(noise_ref[0], 1), :]
    high = gate.astype(jnp.bfloat16).astype(jnp.float32)
    middle = (gate - high).astype(jnp.bfloat16).astype(jnp.float32)
    low = gate - high - middle
    parts = jnp.concatenate([high, middle, low, jnp.zeros((5, gate.shape[1]), jnp.float32)], axis=0)
    out_ref[...] = jnp.concatenate([h_ref[0].astype(jnp.float32), parts], axis=0).astype(jnp.bfloat16)


def partner(here, distance, groups):
    return here ^ distance if groups & (groups - 1) == 0 else (here + groups - distance) % groups


def distances(groups):
    return range(groups - 1, 0, -1)


def attend_kernel(groups, pattern_ref, x_ref, after_ref, out_hbm, *refs):
    *hand_refs, held, sems = refs
    wide = held.shape[2]
    rows = held.shape[1]
    across = (groups - 1) * rows
    factor = math.log2(math.e) / math.sqrt(HD)
    here = lax.axis_index("tm")
    lane = lax.broadcasted_iota(jnp.int32, (1, across), 1)
    ends, kept = [], []
    for source in range(groups):
        first = max(source, 1)
        ends.append(min(across, -(-(groups - first) * rows // 128) * 128))
        chosen = jnp.zeros((1, across), jnp.int32)
        for group in range(first, groups):
            start = (groups - 1 - group) * rows
            flag = pattern_ref[group : group + 1, source : source + 1]
            chosen = jnp.where((lane >= start) & (lane < start + rows), flag, chosen)
        kept.append(chosen[:, : ends[-1]] > 0)

    def spread(row, fill):
        rest = across - row.shape[1]
        return jnp.concatenate([row, jnp.full((1, rest), fill, row.dtype)], axis=1) if rest else row

    for head in range(0, wide, HD):
        query = jnp.concatenate(
            [x_ref[group * rows : (group + 1) * rows, head : head + HD] for group in range(groups - 1, 0, -1)],
            axis=0,
        )
        query = jnp.transpose(query)
        value = jnp.transpose(x_ref[:, 2 * wide + head : 2 * wide + head + HD])
        scores, highest = [], None
        for source in range(groups):
            key = x_ref[source * rows : (source + 1) * rows, wide + head : wide + head + HD]
            scores.append(
                jnp.dot(key, query[:, : ends[source]], preferred_element_type=jnp.float32)
            )
            peak = jnp.where(kept[source], jnp.max(scores[-1], axis=0, keepdims=True), -1e30)
            peak = spread(peak, -1e30)
            highest = peak if highest is None else jnp.maximum(highest, peak)
        highest = highest * factor
        total, probs = 0.0, []
        for source in range(groups):
            offset = jnp.where(kept[source], -highest[:, : ends[source]], -1e30)
            raised = jnp.exp2(scores[source] * factor + offset)
            total += spread(jnp.sum(raised, axis=0, keepdims=True), 0.0)
            probs.append(raised.astype(jnp.bfloat16))
        inverse = 1.0 / total
        start, pieces = 0, []
        for source in range(groups - 1, 0, -1):
            stop = ends[source]
            if stop > start:
                numer = jnp.dot(
                    value[:, : (source + 1) * rows],
                    jnp.concatenate([p[:, start:stop] for p in probs[: source + 1]], axis=0),
                    preferred_element_type=jnp.float32,
                )
                pieces.append(numer * inverse[:, start:stop])
                start = stop
        result = jnp.transpose(jnp.concatenate(pieces, axis=1)).astype(jnp.bfloat16)
        for group in range(1, groups):
            start = (groups - 1 - group) * rows
            held[group - 1, :, head : head + HD] = result[start : start + rows]
    copies = [
        pltpu.make_async_copy(
            held.at[min(place, groups - 2)], out_hbm.at[place * rows : (place + 1) * rows], sems.at[place]
        )
        for place in range(groups)
    ]
    for copy in copies:
        copy.start()
    for distance, hand_ref in zip(distances(groups), hand_refs):
        group = lax.rem(partner(here, distance, groups) + 1, groups)
        hand_ref[...] = x_ref[pl.ds(pl.multiple_of(group * rows, rows), rows), wide:]
    for copy in copies:
        copy.wait()


def cache_places(seq_count, groups, rows, wide, distance, here):
    source = partner(here, groups - distance if groups & (groups - 1) else distance, groups)
    lanes = pl.ds(pl.multiple_of(source * wide, wide), wide)
    tok = rows // seq_count
    for half in range(2):
        start = half * (rows // 2)
        place = mixed(half * (seq_count // 2), seq_count) * tok
        yield slice(start, start + rows // 2), lanes, slice(place, place + rows // 2)


def cache_kernel(seq_count, groups, x_ref, hand_ref, out_ref):
    wide = x_ref.shape[1] // 3
    rows = out_ref.shape[2]
    here = lax.axis_index("tm")
    out_ref[...] = jnp.zeros_like(out_ref)

    @pl.when(here < groups - 1)
    def place():
        own = x_ref[pl.ds(pl.multiple_of((here + 1) * rows, rows), rows), wide:]
        for distance, block in ((0, own), (distances(groups)[0], hand_ref)):
            for to, lanes, at in cache_places(seq_count, groups, rows, wide, distance, here):
                for kind in range(2):
                    out_ref[0, kind, to, lanes] = block[at, kind * wide : (kind + 1) * wide]


def cache_rest_kernel(seq_count, groups, begun_hbm, after_ref, *refs):
    *hand_refs, out_hbm, sems = refs
    wide = hand_refs[0].shape[1] // 2
    rows = out_hbm.shape[2]
    here = lax.axis_index("tm")

    @pl.when(here < groups - 1)
    def place():
        copies = []
        for distance, block in zip(distances(groups)[1:], hand_refs):
            for to, lanes, at in cache_places(seq_count, groups, rows, wide, distance, here):
                for kind in range(2):
                    copies.append(
                        pltpu.make_async_copy(
                            block.at[at, kind * wide : (kind + 1) * wide],
                            out_hbm.at[0, kind, to, lanes],
                            sems.at[len(copies)],
                        )
                    )
                    copies[-1].start()
        for copy in copies:
            copy.wait()


def update_kernel(seq_count, tm_count, att_ref, moved_ref, fresh_ref, after_ref, out_ref):
    tok = out_ref.shape[1]
    wide = att_ref.shape[1]
    count = att_ref.shape[0] // tok
    last = lax.axis_index("tm") == tm_count - 1

    @pl.when(last)
    def take_fresh():
        out_ref[0] = fresh_ref[...]

    @pl.when(jnp.logical_not(last))
    def take_update():
        for pair in range(count // 2):
            rows = att_ref[2 * pair * tok : 2 * (pair + 1) * tok, :].astype(jnp.float32)
            for half in range(2):
                source = 2 * pair + half
                start = (mixed(source % seq_count, seq_count) * tm_count + source // seq_count) * wide
                moved = moved_ref[:, start : start + wide].astype(jnp.float32)
                gate = (moved[tok : tok + 1] + moved[tok + 1 : tok + 2]) + moved[tok + 2 : tok + 3]
                result = moved[:tok] + gate * rows[half * tok : (half + 1) * tok]
                out_ref[0, :, start : start + wide] = result.astype(jnp.bfloat16)


def whole(space=VMEM):
    return pl.BlockSpec(memory_space=space)


def run(kernel, name, outs, specs, operands, flops=0, scratch=(), aliases={}):
    def size(a):
        return math.prod(a.shape) * jnp.dtype(a.dtype).itemsize

    moved = sum(map(size, operands)) + sum(map(size, outs))
    results = pl.pallas_call(
        kernel,
        out_shape=outs,
        in_specs=specs,
        out_specs=[whole(getattr(a, "memory_space", VMEM)) for a in outs],
        scratch_shapes=scratch,
        input_output_aliases=aliases,
        compiler_params=pltpu.CompilerParams(vmem_limit_bytes=4 * moved + (4 << 20)),
        cost_estimate=pl.CostEstimate(flops=flops, bytes_accessed=moved, transcendentals=0),
        name=name,
    )(*operands)
    return results if len(outs) > 1 else results[0]


def spread_body(queries, keys_proj, values, hidden, fresh_latent, gate_table, noise_step, pattern):
    tm_count, seq_count = lax.axis_size("tm"), lax.axis_size("seq")
    count = tm_count * seq_count
    _, tok, width = queries.shape
    wide = width // count
    group_tok = tok * seq_count
    kind = queries.dtype
    DMA = pltpu.SemaphoreType.DMA
    parts = 4 if seq_count % 8 == 0 else 2

    packed = run(
        functools.partial(pack_kernel, seq_count, parts),
        "pack",
        [HBM((count * tok, 3 * wide), kind)],
        [whole(HBM)] * 3,
        [pltpu.with_memory_space_constraint(a, HBM) for a in (queries, keys_proj, values)],
        scratch=[
            VMEM((3, tok, width), kind),
            VMEM((count * tok, 3 * wide), kind),
            DMA((parts, 3)),
            DMA((parts, tm_count)),
        ],
    )
    order = [tm * seq_count + mixed(s, seq_count) for tm in range(tm_count) for s in range(seq_count)]
    exchange = functools.partial(
        lax.all_to_all, axis_name=BOTH, split_axis=0, concat_axis=0, tiled=True, axis_index_groups=[order]
    )
    exchanged = exchange(packed)

    residual = run(
        residual_kernel,
        "residual",
        [VMEM((tok + 8, width), kind)],
        [whole(SMEM), whole(), whole(), whole(HBM)],
        (noise_step, hidden, gate_table, pltpu.with_memory_space_constraint(packed, HBM)),
    )
    moved = shifted(residual, "tm", -1)

    attended, *hands = run(
        functools.partial(attend_kernel, tm_count),
        "attend",
        [HBM((count * tok, wide), kind)] + [VMEM((group_tok, 2 * wide), kind)] * (tm_count - 1),
        [whole(), whole(), whole(pl.ANY)],
        (pattern, exchanged, moved),
        flops=2 * count * tok * count * tok * wide,
        scratch=[VMEM((tm_count - 1, group_tok, wide), kind), DMA((tm_count,))],
    )
    returned = exchange(attended)
    handed = []
    for distance, hand in zip(distances(tm_count), hands):
        route = [(i, partner(i, distance, tm_count)) for i in range(tm_count)]
        handed.append(lax.ppermute(hand, "tm", [(i, j) for i, j in route if j < tm_count - 1]))

    first, *rest = handed
    begun = run(
        functools.partial(cache_kernel, seq_count, tm_count),
        "cache",
        [jax.ShapeDtypeStruct((1, 2, group_tok, tm_count * wide), kind)],
        [whole()] * 2,
        (exchanged, first),
    )
    begun = pltpu.with_memory_space_constraint(begun, HBM)
    advanced = run(
        functools.partial(update_kernel, seq_count, tm_count),
        "update",
        [jax.ShapeDtypeStruct((1, tok, width), kind)],
        [whole()] * 3 + [whole(HBM)],
        (returned, moved, fresh_latent, begun),
    )
    next_cache = run(
        functools.partial(cache_rest_kernel, seq_count, tm_count),
        "cache_rest",
        [HBM(begun.shape, kind)],
        [whole(HBM)] * 2 + [whole()] * len(rest),
        (begun, pltpu.with_memory_space_constraint(advanced, HBM), *rest),
        scratch=[DMA((4 * len(rest),))],
        aliases={0: 0},
    )
    return (advanced, next_cache)


def absorb(state, query_heads, key_piece, value_piece, scale_factor):
    accum, totals, highest = state
    row_count, head_count, head_dim = query_heads.shape
    key_heads = key_piece.reshape(key_piece.shape[0], head_count, head_dim)
    value_heads = value_piece.reshape(value_piece.shape[0], head_count, head_dim)
    scores = (
        jnp.einsum("qhd,khd->qhk", query_heads, key_heads, preferred_element_type=jnp.float32)
        * scale_factor
    )
    raised = jnp.maximum(highest, jnp.max(scores, axis=-1))
    fade = jnp.exp(highest - raised)
    weights = jnp.exp(scores - raised[..., None])
    totals = totals * fade + jnp.sum(weights, axis=-1)
    accum = accum * fade[..., None] + jnp.einsum(
        "qhk,khd->qhd",
        weights.astype(jnp.bfloat16),
        value_heads,
        preferred_element_type=jnp.float32,
    )
    return (accum, totals, raised)


def gather_body(queries, keys_proj, values, hidden, fresh_latent, gate_table, noise_step, pattern):
    group_index = lax.axis_index("tm")
    final_index = lax.axis_size("tm") - 1
    query_tok, key_tok, value_tok = (
        lax.all_to_all(queries[0], "seq", split_axis=1, concat_axis=0, tiled=True),
        lax.all_to_all(keys_proj[0], "seq", split_axis=1, concat_axis=0, tiled=True),
        lax.all_to_all(values[0], "seq", split_axis=1, concat_axis=0, tiled=True),
    )
    row_count, local_width = query_tok.shape
    head_count = local_width // HD
    query_heads = query_tok.reshape(row_count, head_count, HD)
    scale_factor = 1.0 / math.sqrt(HD)
    reach = lax.dynamic_index_in_dim(pattern, group_index, 0, keepdims=False)
    start_state = (
        jnp.zeros((row_count, head_count, HD), jnp.float32),
        jnp.zeros((row_count, head_count), jnp.float32),
        jnp.full((row_count, head_count), -1e30, jnp.float32),
    )

    def one_block(current, inputs):
        key_block, value_block, flag = inputs
        return (
            lax.cond(
                flag > 0,
                lambda state: absorb(state, query_heads, key_block, value_block, scale_factor),
                lambda state: state,
                current,
            ),
            None,
        )

    key_piece = lax.all_gather(key_tok, "tm", axis=0, tiled=False)
    value_piece = lax.all_gather(value_tok, "tm", axis=0, tiled=False)
    state, unused = lax.scan(one_block, start_state, (key_piece, value_piece, reach))
    cache_keys, cache_values = shifted((key_tok, value_tok), "tm", -1)
    accum, totals, highest = state
    attended_head = (accum / totals[..., None]).reshape(row_count, local_width).astype(jnp.bfloat16)
    attended = lax.all_to_all(attended_head, "seq", split_axis=0, concat_axis=1, tiled=True)
    gate_row = lax.dynamic_index_in_dim(gate_table, noise_step[0], 0, keepdims=False)
    updated = (
        hidden[0].astype(jnp.float32) + gate_row[None, :] * attended.astype(jnp.float32)
    ).astype(jnp.bfloat16)
    moved = shifted(updated, "tm", -1)
    advanced = jnp.where(group_index == final_index, fresh_latent, moved)[None]
    next_cache = jnp.stack([cache_keys, cache_values], axis=0)[None]
    return (advanced, next_cache)


def body(queries, *others):
    tm_count, seq_count = lax.axis_size("tm"), lax.axis_size("seq")
    _, tok, width = queries.shape
    count = tm_count * seq_count
    even = width % (count * HD) == 0 and tok % 8 == 0 and seq_count % 4 == 0 and tm_count > 2
    return (spread_body if even else gather_body)(queries, *others)


def solution(mesh):
    placed = (
        P("tm", "seq", None),
        P("tm", "seq", None),
        P("tm", "seq", None),
        P("tm", "seq", None),
        P("seq", None),
        P(),
        P("tm"),
        P(),
    )
    return jax.shard_map(
        body,
        mesh=mesh,
        in_specs=placed,
        out_specs=(P("tm", "seq", None), P("tm", None, None, "seq")),
        check_vma=False,
    )
```

```python
import functools
import math

import jax
import jax.numpy as jnp
from jax import lax
from jax.experimental import pallas as pl
from jax.experimental.pallas import tpu as pltpu
from jax.sharding import PartitionSpec as P

HD = 128
BOTH = ("tm", "seq")
VMEM = pltpu.VMEM
SMEM = pltpu.SMEM
HBM = pltpu.HBM


def shifted(block, axis, distance):
    devices = range(lax.axis_size(axis))
    route = [(i - distance, i) for i in devices if i - distance in devices]
    return lax.ppermute(block, axis, route)


def mixed(index, count):
    return (index + count // 2) % count


def pack_kernel(seq_count, parts, q_hbm, k_hbm, v_hbm, out_hbm, held, block, in_sems, out_sems):
    tok, width = held.shape[1:]
    wide = out_hbm.shape[1] // 3
    count = out_hbm.shape[0] // tok
    tm_count = count // seq_count
    span, members = width // parts, seq_count // parts
    copies = []
    for part in range(parts):
        columns = slice(part * span, (part + 1) * span)
        for place, ref in enumerate((q_hbm, k_hbm, v_hbm)):
            copies.append(
                pltpu.make_async_copy(
                    ref.at[0, :, columns], held.at[place, :, columns], in_sems.at[part, place]
                )
            )
            copies[-1].start()
    outs = []
    for part in range(parts):
        for place in range(3):
            copies[3 * part + place].wait()
        for tm in range(tm_count):
            for seq in range(part * members, (part + 1) * members, 2):
                first = (tm * seq_count + mixed(seq, seq_count)) * tok
                for place in range(3):
                    rows = []
                    for member in (seq, seq + 1):
                        start = (member * tm_count + tm) * wide
                        rows.append(held[place, :, start : start + wide].astype(jnp.float32))
                    block[first : first + 2 * tok, place * wide : (place + 1) * wide] = jnp.concatenate(
                        rows, axis=0
                    ).astype(jnp.bfloat16)
            first = (tm * seq_count + mixed(part * members, seq_count)) * tok
            rows = slice(first, first + members * tok)
            outs.append(
                pltpu.make_async_copy(block.at[rows], out_hbm.at[rows], out_sems.at[part, tm])
            )
            outs[-1].start()
    for out in outs:
        out.wait()


def residual_kernel(noise_ref, h_ref, gate_hbm, after_ref, out_ref, held, sem):
    step = noise_ref[0]
    steps = gate_hbm.shape[0]
    whole_tiles = steps // 8 * 8
    first = step // 8 * 8

    @pl.when(step < whole_tiles)
    def take_tile():
        rows = pl.ds(pl.multiple_of(first, 8), 8)
        copy = pltpu.make_async_copy(gate_hbm.at[rows], held, sem)
        copy.start()
        copy.wait()

    if steps > whole_tiles:

        @pl.when(step >= whole_tiles)
        def take_rest():
            copy = pltpu.make_async_copy(
                gate_hbm.at[whole_tiles:steps], held.at[0 : steps - whole_tiles], sem
            )
            copy.start()
            copy.wait()

    gate = held[pl.ds(step - first, 1), :]
    high = gate.astype(jnp.bfloat16).astype(jnp.float32)
    middle = (gate - high).astype(jnp.bfloat16).astype(jnp.float32)
    low = gate - high - middle
    parts = jnp.concatenate([high, middle, low, jnp.zeros((5, gate.shape[1]), jnp.float32)], axis=0)
    out_ref[...] = jnp.concatenate([h_ref[0].astype(jnp.float32), parts], axis=0).astype(jnp.bfloat16)


def partner(here, distance, groups):
    return here ^ distance if groups & (groups - 1) == 0 else (here + groups - distance) % groups


def distances(groups):
    return range(groups - 1, 0, -1)


def attend_kernel(groups, pattern_ref, x_ref, after_ref, out_hbm, *refs):
    *hand_refs, held, sems = refs
    wide = held.shape[2]
    rows = held.shape[1]
    across = (groups - 1) * rows
    factor = math.log2(math.e) / math.sqrt(HD)
    here = lax.axis_index("tm")
    lane = lax.broadcasted_iota(jnp.int32, (1, across), 1)
    ends, kept = [], []
    for source in range(groups):
        first = max(source, 1)
        ends.append(min(across, -(-(groups - first) * rows // 128) * 128))
        chosen = jnp.zeros((1, across), jnp.int32)
        for group in range(first, groups):
            start = (groups - 1 - group) * rows
            flag = pattern_ref[group : group + 1, source : source + 1]
            chosen = jnp.where((lane >= start) & (lane < start + rows), flag, chosen)
        kept.append(chosen[:, : ends[-1]] > 0)

    def spread(row, fill):
        rest = across - row.shape[1]
        return jnp.concatenate([row, jnp.full((1, rest), fill, row.dtype)], axis=1) if rest else row

    for head in range(0, wide, HD):
        query = jnp.concatenate(
            [x_ref[group * rows : (group + 1) * rows, head : head + HD] for group in range(groups - 1, 0, -1)],
            axis=0,
        )
        query = jnp.transpose(query)
        value = jnp.transpose(x_ref[:, 2 * wide + head : 2 * wide + head + HD])
        scores, highest = [], None
        for source in range(groups):
            key = x_ref[source * rows : (source + 1) * rows, wide + head : wide + head + HD]
            scores.append(
                jnp.dot(key, query[:, : ends[source]], preferred_element_type=jnp.float32)
            )
            peak = jnp.where(kept[source], jnp.max(scores[-1], axis=0, keepdims=True), -1e30)
            peak = spread(peak, -1e30)
            highest = peak if highest is None else jnp.maximum(highest, peak)
        highest = highest * factor
        total, probs = 0.0, []
        for source in range(groups):
            offset = jnp.where(kept[source], -highest[:, : ends[source]], -1e30)
            raised = jnp.exp2(scores[source] * factor + offset)
            total += spread(jnp.sum(raised, axis=0, keepdims=True), 0.0)
            probs.append(raised.astype(jnp.bfloat16))
        inverse = 1.0 / total
        start, pieces = 0, []
        for source in range(groups - 1, 0, -1):
            stop = ends[source]
            if stop > start:
                numer = jnp.dot(
                    value[:, : (source + 1) * rows],
                    jnp.concatenate([p[:, start:stop] for p in probs[: source + 1]], axis=0),
                    preferred_element_type=jnp.float32,
                )
                pieces.append(numer * inverse[:, start:stop])
                start = stop
        result = jnp.transpose(jnp.concatenate(pieces, axis=1)).astype(jnp.bfloat16)
        for group in range(1, groups):
            start = (groups - 1 - group) * rows
            held[group - 1, :, head : head + HD] = result[start : start + rows]
    copies = [
        pltpu.make_async_copy(
            held.at[min(place, groups - 2)], out_hbm.at[place * rows : (place + 1) * rows], sems.at[place]
        )
        for place in range(groups)
    ]
    for copy in copies:
        copy.start()
    for distance, hand_ref in zip(distances(groups), hand_refs):
        group = lax.rem(partner(here, distance, groups) + 1, groups)
        hand_ref[...] = x_ref[pl.ds(pl.multiple_of(group * rows, rows), rows), wide:]
    for copy in copies:
        copy.wait()


def cache_places(seq_count, groups, rows, wide, distance, here):
    source = partner(here, groups - distance if groups & (groups - 1) else distance, groups)
    lanes = pl.ds(pl.multiple_of(source * wide, wide), wide)
    tok = rows // seq_count
    for half in range(2):
        start = half * (rows // 2)
        place = mixed(half * (seq_count // 2), seq_count) * tok
        yield slice(start, start + rows // 2), lanes, slice(place, place + rows // 2)


def cache_kernel(seq_count, groups, x_ref, hand_ref, out_ref):
    wide = x_ref.shape[1] // 3
    rows = out_ref.shape[2]
    here = lax.axis_index("tm")
    out_ref[...] = jnp.zeros_like(out_ref)

    @pl.when(here < groups - 1)
    def place():
        own = x_ref[pl.ds(pl.multiple_of((here + 1) * rows, rows), rows), wide:]
        for distance, block in ((0, own), (distances(groups)[0], hand_ref)):
            for to, lanes, at in cache_places(seq_count, groups, rows, wide, distance, here):
                for kind in range(2):
                    out_ref[0, kind, to, lanes] = block[at, kind * wide : (kind + 1) * wide]


def cache_rest_kernel(seq_count, groups, begun_hbm, after_ref, *refs):
    *hand_refs, out_hbm, sems = refs
    wide = hand_refs[0].shape[1] // 2
    rows = out_hbm.shape[2]
    here = lax.axis_index("tm")

    @pl.when(here < groups - 1)
    def place():
        copies = []
        for distance, block in zip(distances(groups)[1:], hand_refs):
            for to, lanes, at in cache_places(seq_count, groups, rows, wide, distance, here):
                for kind in range(2):
                    copies.append(
                        pltpu.make_async_copy(
                            block.at[at, kind * wide : (kind + 1) * wide],
                            out_hbm.at[0, kind, to, lanes],
                            sems.at[len(copies)],
                        )
                    )
                    copies[-1].start()
        for copy in copies:
            copy.wait()


def update_kernel(seq_count, tm_count, att_ref, moved_ref, fresh_ref, after_ref, out_ref):
    tok = out_ref.shape[1]
    wide = att_ref.shape[1]
    count = att_ref.shape[0] // tok
    last = lax.axis_index("tm") == tm_count - 1

    @pl.when(last)
    def take_fresh():
        out_ref[0] = fresh_ref[...]

    @pl.when(jnp.logical_not(last))
    def take_update():
        for pair in range(count // 2):
            rows = att_ref[2 * pair * tok : 2 * (pair + 1) * tok, :].astype(jnp.float32)
            for half in range(2):
                source = 2 * pair + half
                start = (mixed(source % seq_count, seq_count) * tm_count + source // seq_count) * wide
                moved = moved_ref[:, start : start + wide].astype(jnp.float32)
                gate = (moved[tok : tok + 1] + moved[tok + 1 : tok + 2]) + moved[tok + 2 : tok + 3]
                result = moved[:tok] + gate * rows[half * tok : (half + 1) * tok]
                out_ref[0, :, start : start + wide] = result.astype(jnp.bfloat16)


def whole(space=VMEM):
    return pl.BlockSpec(memory_space=space)


def run(kernel, name, outs, specs, operands, flops=0, scratch=(), aliases={}):
    def size(a):
        return math.prod(a.shape) * jnp.dtype(a.dtype).itemsize

    moved = sum(map(size, operands)) + sum(map(size, outs))
    results = pl.pallas_call(
        kernel,
        out_shape=outs,
        in_specs=specs,
        out_specs=[whole(getattr(a, "memory_space", VMEM)) for a in outs],
        scratch_shapes=scratch,
        input_output_aliases=aliases,
        compiler_params=pltpu.CompilerParams(vmem_limit_bytes=4 * moved + (4 << 20)),
        cost_estimate=pl.CostEstimate(flops=flops, bytes_accessed=moved, transcendentals=0),
        name=name,
    )(*operands)
    return results if len(outs) > 1 else results[0]


def spread_body(queries, keys_proj, values, hidden, fresh_latent, gate_table, noise_step, pattern):
    tm_count, seq_count = lax.axis_size("tm"), lax.axis_size("seq")
    count = tm_count * seq_count
    _, tok, width = queries.shape
    wide = width // count
    group_tok = tok * seq_count
    kind = queries.dtype
    DMA = pltpu.SemaphoreType.DMA
    parts = 4 if seq_count % 8 == 0 else 2

    packed = run(
        functools.partial(pack_kernel, seq_count, parts),
        "pack",
        [HBM((count * tok, 3 * wide), kind)],
        [whole(HBM)] * 3,
        [pltpu.with_memory_space_constraint(a, HBM) for a in (queries, keys_proj, values)],
        scratch=[
            VMEM((3, tok, width), kind),
            VMEM((count * tok, 3 * wide), kind),
            DMA((parts, 3)),
            DMA((parts, tm_count)),
        ],
    )
    order = [tm * seq_count + mixed(s, seq_count) for tm in range(tm_count) for s in range(seq_count)]
    exchange = functools.partial(
        lax.all_to_all, axis_name=BOTH, split_axis=0, concat_axis=0, tiled=True, axis_index_groups=[order]
    )
    exchanged = exchange(packed)

    residual = run(
        residual_kernel,
        "residual",
        [VMEM((tok + 8, width), kind)],
        [whole(SMEM), whole(), whole(HBM), whole(HBM)],
        (
            noise_step,
            hidden,
            pltpu.with_memory_space_constraint(gate_table, HBM),
            pltpu.with_memory_space_constraint(packed, HBM),
        ),
        scratch=[VMEM((8, width), jnp.float32), DMA],
    )
    moved = shifted(residual, "tm", -1)

    attended, *hands = run(
        functools.partial(attend_kernel, tm_count),
        "attend",
        [HBM((count * tok, wide), kind)] + [VMEM((group_tok, 2 * wide), kind)] * (tm_count - 1),
        [whole(), whole(), whole(pl.ANY)],
        (pattern, exchanged, moved),
        flops=2 * count * tok * count * tok * wide,
        scratch=[VMEM((tm_count - 1, group_tok, wide), kind), DMA((tm_count,))],
    )
    returned = exchange(attended)
    handed = []
    for distance, hand in zip(distances(tm_count), hands):
        route = [(i, partner(i, distance, tm_count)) for i in range(tm_count)]
        handed.append(lax.ppermute(hand, "tm", [(i, j) for i, j in route if j < tm_count - 1]))

    first, *rest = handed
    begun = run(
        functools.partial(cache_kernel, seq_count, tm_count),
        "cache",
        [jax.ShapeDtypeStruct((1, 2, group_tok, tm_count * wide), kind)],
        [whole()] * 2,
        (exchanged, first),
    )
    begun = pltpu.with_memory_space_constraint(begun, HBM)
    advanced = run(
        functools.partial(update_kernel, seq_count, tm_count),
        "update",
        [jax.ShapeDtypeStruct((1, tok, width), kind)],
        [whole()] * 3 + [whole(HBM)],
        (returned, moved, fresh_latent, begun),
    )
    next_cache = run(
        functools.partial(cache_rest_kernel, seq_count, tm_count),
        "cache_rest",
        [HBM(begun.shape, kind)],
        [whole(HBM)] * 2 + [whole()] * len(rest),
        (begun, pltpu.with_memory_space_constraint(advanced, HBM), *rest),
        scratch=[DMA((4 * len(rest),))],
        aliases={0: 0},
    )
    return (advanced, next_cache)


def absorb(state, query_heads, key_piece, value_piece, scale_factor):
    accum, totals, highest = state
    row_count, head_count, head_dim = query_heads.shape
    key_heads = key_piece.reshape(key_piece.shape[0], head_count, head_dim)
    value_heads = value_piece.reshape(value_piece.shape[0], head_count, head_dim)
    scores = (
        jnp.einsum("qhd,khd->qhk", query_heads, key_heads, preferred_element_type=jnp.float32)
        * scale_factor
    )
    raised = jnp.maximum(highest, jnp.max(scores, axis=-1))
    fade = jnp.exp(highest - raised)
    weights = jnp.exp(scores - raised[..., None])
    totals = totals * fade + jnp.sum(weights, axis=-1)
    accum = accum * fade[..., None] + jnp.einsum(
        "qhk,khd->qhd",
        weights.astype(jnp.bfloat16),
        value_heads,
        preferred_element_type=jnp.float32,
    )
    return (accum, totals, raised)


def gather_body(queries, keys_proj, values, hidden, fresh_latent, gate_table, noise_step, pattern):
    group_index = lax.axis_index("tm")
    final_index = lax.axis_size("tm") - 1
    query_tok, key_tok, value_tok = (
        lax.all_to_all(queries[0], "seq", split_axis=1, concat_axis=0, tiled=True),
        lax.all_to_all(keys_proj[0], "seq", split_axis=1, concat_axis=0, tiled=True),
        lax.all_to_all(values[0], "seq", split_axis=1, concat_axis=0, tiled=True),
    )
    row_count, local_width = query_tok.shape
    head_count = local_width // HD
    query_heads = query_tok.reshape(row_count, head_count, HD)
    scale_factor = 1.0 / math.sqrt(HD)
    reach = lax.dynamic_index_in_dim(pattern, group_index, 0, keepdims=False)
    start_state = (
        jnp.zeros((row_count, head_count, HD), jnp.float32),
        jnp.zeros((row_count, head_count), jnp.float32),
        jnp.full((row_count, head_count), -1e30, jnp.float32),
    )

    def one_block(current, inputs):
        key_block, value_block, flag = inputs
        return (
            lax.cond(
                flag > 0,
                lambda state: absorb(state, query_heads, key_block, value_block, scale_factor),
                lambda state: state,
                current,
            ),
            None,
        )

    key_piece = lax.all_gather(key_tok, "tm", axis=0, tiled=False)
    value_piece = lax.all_gather(value_tok, "tm", axis=0, tiled=False)
    state, unused = lax.scan(one_block, start_state, (key_piece, value_piece, reach))
    cache_keys, cache_values = shifted((key_tok, value_tok), "tm", -1)
    accum, totals, highest = state
    attended_head = (accum / totals[..., None]).reshape(row_count, local_width).astype(jnp.bfloat16)
    attended = lax.all_to_all(attended_head, "seq", split_axis=0, concat_axis=1, tiled=True)
    gate_row = lax.dynamic_index_in_dim(gate_table, noise_step[0], 0, keepdims=False)
    updated = (
        hidden[0].astype(jnp.float32) + gate_row[None, :] * attended.astype(jnp.float32)
    ).astype(jnp.bfloat16)
    moved = shifted(updated, "tm", -1)
    advanced = jnp.where(group_index == final_index, fresh_latent, moved)[None]
    next_cache = jnp.stack([cache_keys, cache_values], axis=0)[None]
    return (advanced, next_cache)


def body(queries, *others):
    tm_count, seq_count = lax.axis_size("tm"), lax.axis_size("seq")
    _, tok, width = queries.shape
    count = tm_count * seq_count
    even = width % (count * HD) == 0 and tok % 8 == 0 and seq_count % 4 == 0 and tm_count > 2
    return (spread_body if even else gather_body)(queries, *others)


def solution(mesh):
    placed = (
        P("tm", "seq", None),
        P("tm", "seq", None),
        P("tm", "seq", None),
        P("tm", "seq", None),
        P("seq", None),
        P(),
        P("tm"),
        P(),
    )
    return jax.shard_map(
        body,
        mesh=mesh,
        in_specs=placed,
        out_specs=(P("tm", "seq", None), P("tm", None, None, "seq")),
        check_vma=False,
    )
```

```python
import functools
import math

import jax
import jax.numpy as jnp
from jax import lax
from jax.experimental import pallas as pl
from jax.experimental.pallas import tpu as pltpu
from jax.sharding import PartitionSpec as P

HD = 128
BOTH = ("tm", "seq")
VMEM = pltpu.VMEM
SMEM = pltpu.SMEM
HBM = pltpu.HBM


def shifted(block, axis, distance):
    devices = range(lax.axis_size(axis))
    route = [(i - distance, i) for i in devices if i - distance in devices]
    return lax.ppermute(block, axis, route)


def mixed(index, count):
    return (index + count // 2) % count


def pack_kernel(seq_count, parts, q_hbm, k_hbm, v_hbm, out_hbm, held, block, in_sems, out_sems):
    tok, width = held.shape[1:]
    wide = out_hbm.shape[1] // 3
    count = out_hbm.shape[0] // tok
    tm_count = count // seq_count
    span, members = width // parts, seq_count // parts
    copies = []
    for part in range(parts):
        columns = slice(part * span, (part + 1) * span)
        for place, ref in enumerate((q_hbm, k_hbm, v_hbm)):
            copies.append(
                pltpu.make_async_copy(
                    ref.at[0, :, columns], held.at[place, :, columns], in_sems.at[part, place]
                )
            )
            copies[-1].start()
    outs = []
    for part in range(parts):
        for place in range(3):
            copies[3 * part + place].wait()
        for tm in range(tm_count):
            for seq in range(part * members, (part + 1) * members, 2):
                first = (tm * seq_count + mixed(seq, seq_count)) * tok
                for place in range(3):
                    rows = []
                    for member in (seq, seq + 1):
                        start = (member * tm_count + tm) * wide
                        rows.append(held[place, :, start : start + wide].astype(jnp.float32))
                    block[first : first + 2 * tok, place * wide : (place + 1) * wide] = jnp.concatenate(
                        rows, axis=0
                    ).astype(jnp.bfloat16)
            first = (tm * seq_count + mixed(part * members, seq_count)) * tok
            rows = slice(first, first + members * tok)
            outs.append(
                pltpu.make_async_copy(block.at[rows], out_hbm.at[rows], out_sems.at[part, tm])
            )
            outs[-1].start()
    for out in outs:
        out.wait()


def residual_kernel(noise_ref, h_ref, gate_hbm, after_ref, out_ref, held, sem):
    step = noise_ref[0]
    steps = gate_hbm.shape[0]
    whole_tiles = steps // 8 * 8
    first = step // 8 * 8

    @pl.when(step < whole_tiles)
    def take_tile():
        rows = pl.ds(pl.multiple_of(first, 8), 8)
        copy = pltpu.make_async_copy(gate_hbm.at[rows], held, sem)
        copy.start()
        copy.wait()

    if steps > whole_tiles:

        @pl.when(step >= whole_tiles)
        def take_rest():
            copy = pltpu.make_async_copy(
                gate_hbm.at[whole_tiles:steps], held.at[0 : steps - whole_tiles], sem
            )
            copy.start()
            copy.wait()

    gate = held[pl.ds(step - first, 1), :]
    high = gate.astype(jnp.bfloat16).astype(jnp.float32)
    middle = (gate - high).astype(jnp.bfloat16).astype(jnp.float32)
    low = gate - high - middle
    parts = jnp.concatenate([high, middle, low, jnp.zeros((5, gate.shape[1]), jnp.float32)], axis=0)
    out_ref[...] = jnp.concatenate([h_ref[0].astype(jnp.float32), parts], axis=0).astype(jnp.bfloat16)


def partner(here, distance, groups):
    return here ^ distance if groups & (groups - 1) == 0 else (here + groups - distance) % groups


def distances(groups):
    return range(groups - 1, 0, -1)


def attend_kernel(groups, pattern_ref, x_ref, after_ref, out_hbm, *refs):
    *hand_refs, held, sems = refs
    wide = held.shape[2]
    rows = held.shape[1]
    across = (groups - 1) * rows
    factor = math.log2(math.e) / math.sqrt(HD)
    here = lax.axis_index("tm")
    lane = lax.broadcasted_iota(jnp.int32, (1, across), 1)
    ends, kept = [], []
    for source in range(groups):
        first = max(source, 1)
        ends.append(min(across, -(-(groups - first) * rows // 128) * 128))
        chosen = jnp.zeros((1, across), jnp.int32)
        for group in range(first, groups):
            start = (groups - 1 - group) * rows
            flag = pattern_ref[group : group + 1, source : source + 1]
            chosen = jnp.where((lane >= start) & (lane < start + rows), flag, chosen)
        kept.append(chosen[:, : ends[-1]] > 0)

    def spread(row, fill):
        rest = across - row.shape[1]
        return jnp.concatenate([row, jnp.full((1, rest), fill, row.dtype)], axis=1) if rest else row

    for head in range(0, wide, HD):
        query = jnp.concatenate(
            [x_ref[group * rows : (group + 1) * rows, head : head + HD] for group in range(groups - 1, 0, -1)],
            axis=0,
        )
        query = jnp.transpose(query)
        value = jnp.transpose(x_ref[:, 2 * wide + head : 2 * wide + head + HD])
        scores, highest = [], None
        for source in range(groups):
            key = x_ref[source * rows : (source + 1) * rows, wide + head : wide + head + HD]
            scores.append(
                jnp.dot(key, query[:, : ends[source]], preferred_element_type=jnp.float32)
            )
            peak = jnp.where(kept[source], jnp.max(scores[-1], axis=0, keepdims=True), -1e30)
            peak = spread(peak, -1e30)
            highest = peak if highest is None else jnp.maximum(highest, peak)
        highest = highest * factor
        total, probs = 0.0, []
        for source in range(groups):
            offset = jnp.where(kept[source], -highest[:, : ends[source]], -1e30)
            raised = jnp.exp2(scores[source] * factor + offset)
            total += spread(jnp.sum(raised, axis=0, keepdims=True), 0.0)
            probs.append(raised.astype(jnp.bfloat16))
        inverse = 1.0 / total
        start, pieces = 0, []
        for source in range(groups - 1, 0, -1):
            stop = ends[source]
            if stop > start:
                numer = jnp.dot(
                    value[:, : (source + 1) * rows],
                    jnp.concatenate([p[:, start:stop] for p in probs[: source + 1]], axis=0),
                    preferred_element_type=jnp.float32,
                )
                pieces.append(numer * inverse[:, start:stop])
                start = stop
        result = jnp.transpose(jnp.concatenate(pieces, axis=1)).astype(jnp.bfloat16)
        for group in range(1, groups):
            start = (groups - 1 - group) * rows
            held[group - 1, :, head : head + HD] = result[start : start + rows]
    copies = []
    half = rows // 2
    for place in range(groups):
        for part in range(2):
            at = mixed(part, 2) * half
            to = place * rows + part * half
            copies.append(
                pltpu.make_async_copy(
                    held.at[min(place, groups - 2), at : at + half],
                    out_hbm.at[to : to + half],
                    sems.at[place, part],
                )
            )
            copies[-1].start()
    for distance, hand_ref in zip(distances(groups), hand_refs):
        group = lax.rem(partner(here, distance, groups) + 1, groups)
        hand_ref[...] = x_ref[pl.ds(pl.multiple_of(group * rows, rows), rows), wide:]
    for copy in copies:
        copy.wait()


def cache_places(seq_count, groups, rows, wide, distance, here):
    source = partner(here, groups - distance if groups & (groups - 1) else distance, groups)
    lanes = pl.ds(pl.multiple_of(source * wide, wide), wide)
    tok = rows // seq_count
    for half in range(2):
        start = half * (rows // 2)
        place = mixed(half * (seq_count // 2), seq_count) * tok
        yield slice(start, start + rows // 2), lanes, slice(place, place + rows // 2)


def cache_kernel(seq_count, groups, x_ref, hand_ref, out_ref):
    wide = x_ref.shape[1] // 3
    rows = out_ref.shape[2]
    here = lax.axis_index("tm")
    out_ref[...] = jnp.zeros_like(out_ref)

    @pl.when(here < groups - 1)
    def place():
        own = x_ref[pl.ds(pl.multiple_of((here + 1) * rows, rows), rows), wide:]
        for distance, block in ((0, own), (distances(groups)[0], hand_ref)):
            for to, lanes, at in cache_places(seq_count, groups, rows, wide, distance, here):
                for kind in range(2):
                    out_ref[0, kind, to, lanes] = block[at, kind * wide : (kind + 1) * wide]


def cache_rest_kernel(seq_count, groups, begun_hbm, after_ref, *refs):
    *hand_refs, out_hbm, sems = refs
    wide = hand_refs[0].shape[1] // 2
    rows = out_hbm.shape[2]
    here = lax.axis_index("tm")

    @pl.when(here < groups - 1)
    def place():
        copies = []
        for distance, block in zip(distances(groups)[1:], hand_refs):
            for to, lanes, at in cache_places(seq_count, groups, rows, wide, distance, here):
                for kind in range(2):
                    copies.append(
                        pltpu.make_async_copy(
                            block.at[at, kind * wide : (kind + 1) * wide],
                            out_hbm.at[0, kind, to, lanes],
                            sems.at[len(copies)],
                        )
                    )
                    copies[-1].start()
        for copy in copies:
            copy.wait()


def update_kernel(seq_count, tm_count, att_ref, moved_ref, fresh_ref, after_ref, out_ref):
    tok = out_ref.shape[1]
    wide = att_ref.shape[1]
    count = att_ref.shape[0] // tok
    last = lax.axis_index("tm") == tm_count - 1

    @pl.when(last)
    def take_fresh():
        out_ref[0] = fresh_ref[...]

    @pl.when(jnp.logical_not(last))
    def take_update():
        for pair in range(count // 2):
            rows = att_ref[2 * pair * tok : 2 * (pair + 1) * tok, :].astype(jnp.float32)
            for half in range(2):
                source = 2 * pair + half
                start = ((source % seq_count) * tm_count + source // seq_count) * wide
                moved = moved_ref[:, start : start + wide].astype(jnp.float32)
                gate = (moved[tok : tok + 1] + moved[tok + 1 : tok + 2]) + moved[tok + 2 : tok + 3]
                result = moved[:tok] + gate * rows[half * tok : (half + 1) * tok]
                out_ref[0, :, start : start + wide] = result.astype(jnp.bfloat16)


def whole(space=VMEM):
    return pl.BlockSpec(memory_space=space)


def run(kernel, name, outs, specs, operands, flops=0, scratch=(), aliases={}):
    def size(a):
        return math.prod(a.shape) * jnp.dtype(a.dtype).itemsize

    moved = sum(map(size, operands)) + sum(map(size, outs))
    results = pl.pallas_call(
        kernel,
        out_shape=outs,
        in_specs=specs,
        out_specs=[whole(getattr(a, "memory_space", VMEM)) for a in outs],
        scratch_shapes=scratch,
        input_output_aliases=aliases,
        compiler_params=pltpu.CompilerParams(vmem_limit_bytes=4 * moved + (4 << 20)),
        cost_estimate=pl.CostEstimate(flops=flops, bytes_accessed=moved, transcendentals=0),
        name=name,
    )(*operands)
    return results if len(outs) > 1 else results[0]


def spread_body(queries, keys_proj, values, hidden, fresh_latent, gate_table, noise_step, pattern):
    tm_count, seq_count = lax.axis_size("tm"), lax.axis_size("seq")
    count = tm_count * seq_count
    _, tok, width = queries.shape
    wide = width // count
    group_tok = tok * seq_count
    kind = queries.dtype
    DMA = pltpu.SemaphoreType.DMA
    parts = 4 if seq_count % 8 == 0 else 2

    packed = run(
        functools.partial(pack_kernel, seq_count, parts),
        "pack",
        [HBM((count * tok, 3 * wide), kind)],
        [whole(HBM)] * 3,
        [pltpu.with_memory_space_constraint(a, HBM) for a in (queries, keys_proj, values)],
        scratch=[
            VMEM((3, tok, width), kind),
            VMEM((count * tok, 3 * wide), kind),
            DMA((parts, 3)),
            DMA((parts, tm_count)),
        ],
    )
    order = [tm * seq_count + mixed(s, seq_count) for tm in range(tm_count) for s in range(seq_count)]
    exchange = functools.partial(
        lax.all_to_all, axis_name=BOTH, split_axis=0, concat_axis=0, tiled=True
    )
    exchanged = exchange(packed, axis_index_groups=[order])

    residual = run(
        residual_kernel,
        "residual",
        [VMEM((tok + 8, width), kind)],
        [whole(SMEM), whole(), whole(HBM), whole(HBM)],
        (
            noise_step,
            hidden,
            pltpu.with_memory_space_constraint(gate_table, HBM),
            pltpu.with_memory_space_constraint(packed, HBM),
        ),
        scratch=[VMEM((8, width), jnp.float32), DMA],
    )
    moved = shifted(residual, "tm", -1)

    attended, *hands = run(
        functools.partial(attend_kernel, tm_count),
        "attend",
        [HBM((count * tok, wide), kind)] + [VMEM((group_tok, 2 * wide), kind)] * (tm_count - 1),
        [whole(), whole(), whole(pl.ANY)],
        (pattern, exchanged, moved),
        flops=2 * count * tok * count * tok * wide,
        scratch=[VMEM((tm_count - 1, group_tok, wide), kind), DMA((tm_count, 2))],
    )
    returned = exchange(attended)
    handed = []
    for distance, hand in zip(distances(tm_count), hands):
        route = [(i, partner(i, distance, tm_count)) for i in range(tm_count)]
        handed.append(lax.ppermute(hand, "tm", [(i, j) for i, j in route if j < tm_count - 1]))

    first, *rest = handed
    begun = run(
        functools.partial(cache_kernel, seq_count, tm_count),
        "cache",
        [jax.ShapeDtypeStruct((1, 2, group_tok, tm_count * wide), kind)],
        [whole()] * 2,
        (exchanged, first),
    )
    begun = pltpu.with_memory_space_constraint(begun, HBM)
    advanced = run(
        functools.partial(update_kernel, seq_count, tm_count),
        "update",
        [jax.ShapeDtypeStruct((1, tok, width), kind)],
        [whole()] * 3 + [whole(HBM)],
        (returned, moved, fresh_latent, begun),
    )
    next_cache = run(
        functools.partial(cache_rest_kernel, seq_count, tm_count),
        "cache_rest",
        [HBM(begun.shape, kind)],
        [whole(HBM)] * 2 + [whole()] * len(rest),
        (begun, pltpu.with_memory_space_constraint(advanced, HBM), *rest),
        scratch=[DMA((4 * len(rest),))],
        aliases={0: 0},
    )
    return (advanced, next_cache)


def absorb(state, query_heads, key_piece, value_piece, scale_factor):
    accum, totals, highest = state
    row_count, head_count, head_dim = query_heads.shape
    key_heads = key_piece.reshape(key_piece.shape[0], head_count, head_dim)
    value_heads = value_piece.reshape(value_piece.shape[0], head_count, head_dim)
    scores = (
        jnp.einsum("qhd,khd->qhk", query_heads, key_heads, preferred_element_type=jnp.float32)
        * scale_factor
    )
    raised = jnp.maximum(highest, jnp.max(scores, axis=-1))
    fade = jnp.exp(highest - raised)
    weights = jnp.exp(scores - raised[..., None])
    totals = totals * fade + jnp.sum(weights, axis=-1)
    accum = accum * fade[..., None] + jnp.einsum(
        "qhk,khd->qhd",
        weights.astype(jnp.bfloat16),
        value_heads,
        preferred_element_type=jnp.float32,
    )
    return (accum, totals, raised)


def gather_body(queries, keys_proj, values, hidden, fresh_latent, gate_table, noise_step, pattern):
    group_index = lax.axis_index("tm")
    final_index = lax.axis_size("tm") - 1
    query_tok, key_tok, value_tok = (
        lax.all_to_all(queries[0], "seq", split_axis=1, concat_axis=0, tiled=True),
        lax.all_to_all(keys_proj[0], "seq", split_axis=1, concat_axis=0, tiled=True),
        lax.all_to_all(values[0], "seq", split_axis=1, concat_axis=0, tiled=True),
    )
    row_count, local_width = query_tok.shape
    head_count = local_width // HD
    query_heads = query_tok.reshape(row_count, head_count, HD)
    scale_factor = 1.0 / math.sqrt(HD)
    reach = lax.dynamic_index_in_dim(pattern, group_index, 0, keepdims=False)
    start_state = (
        jnp.zeros((row_count, head_count, HD), jnp.float32),
        jnp.zeros((row_count, head_count), jnp.float32),
        jnp.full((row_count, head_count), -1e30, jnp.float32),
    )

    def one_block(current, inputs):
        key_block, value_block, flag = inputs
        return (
            lax.cond(
                flag > 0,
                lambda state: absorb(state, query_heads, key_block, value_block, scale_factor),
                lambda state: state,
                current,
            ),
            None,
        )

    key_piece = lax.all_gather(key_tok, "tm", axis=0, tiled=False)
    value_piece = lax.all_gather(value_tok, "tm", axis=0, tiled=False)
    state, unused = lax.scan(one_block, start_state, (key_piece, value_piece, reach))
    cache_keys, cache_values = shifted((key_tok, value_tok), "tm", -1)
    accum, totals, highest = state
    attended_head = (accum / totals[..., None]).reshape(row_count, local_width).astype(jnp.bfloat16)
    attended = lax.all_to_all(attended_head, "seq", split_axis=0, concat_axis=1, tiled=True)
    gate_row = lax.dynamic_index_in_dim(gate_table, noise_step[0], 0, keepdims=False)
    updated = (
        hidden[0].astype(jnp.float32) + gate_row[None, :] * attended.astype(jnp.float32)
    ).astype(jnp.bfloat16)
    moved = shifted(updated, "tm", -1)
    advanced = jnp.where(group_index == final_index, fresh_latent, moved)[None]
    next_cache = jnp.stack([cache_keys, cache_values], axis=0)[None]
    return (advanced, next_cache)


def body(queries, *others):
    tm_count, seq_count = lax.axis_size("tm"), lax.axis_size("seq")
    _, tok, width = queries.shape
    count = tm_count * seq_count
    even = width % (count * HD) == 0 and tok % 8 == 0 and seq_count % 4 == 0 and tm_count > 2
    return (spread_body if even else gather_body)(queries, *others)


def solution(mesh):
    placed = (
        P("tm", "seq", None),
        P("tm", "seq", None),
        P("tm", "seq", None),
        P("tm", "seq", None),
        P("seq", None),
        P(),
        P("tm"),
        P(),
    )
    return jax.shard_map(
        body,
        mesh=mesh,
        in_specs=placed,
        out_specs=(P("tm", "seq", None), P("tm", None, None, "seq")),
        check_vma=False,
    )
```

```python
import functools
import math

import jax
import jax.numpy as jnp
from jax import lax
from jax.experimental import pallas as pl
from jax.experimental.pallas import tpu as pltpu
from jax.sharding import PartitionSpec as P

HD = 128
BOTH = ("tm", "seq")
VMEM = pltpu.VMEM
SMEM = pltpu.SMEM
HBM = pltpu.HBM


def shifted(block, axis, distance):
    devices = range(lax.axis_size(axis))
    route = [(i - distance, i) for i in devices if i - distance in devices]
    return lax.ppermute(block, axis, route)


def mixed(index, count):
    return (index + 2) % count


def runs(count):
    found = []
    for index in range(count):
        if found and found[-1][1] + found[-1][2] == mixed(index, count):
            found[-1][2] += 1
        else:
            found.append([index, mixed(index, count), 1])
    return found


def pack_kernel(seq_count, parts, q_hbm, k_hbm, v_hbm, out_hbm, held, block, in_sems, out_sems):
    tok, width = held.shape[1:]
    wide = out_hbm.shape[1] // 3
    count = out_hbm.shape[0] // tok
    tm_count = count // seq_count
    span, members = width // parts, seq_count // parts
    copies = []
    for part in range(parts):
        columns = slice(part * span, (part + 1) * span)
        for place, ref in enumerate((q_hbm, k_hbm, v_hbm)):
            copies.append(
                pltpu.make_async_copy(
                    ref.at[0, :, columns], held.at[place, :, columns], in_sems.at[part, place]
                )
            )
            copies[-1].start()
    outs = []
    for part in range(parts):
        for place in range(3):
            copies[3 * part + place].wait()
        for tm in range(tm_count):
            for seq in range(part * members, (part + 1) * members, 2):
                first = (tm * seq_count + mixed(seq, seq_count)) * tok
                for place in range(3):
                    rows = []
                    for member in (seq, seq + 1):
                        start = (member * tm_count + tm) * wide
                        rows.append(held[place, :, start : start + wide].astype(jnp.float32))
                    block[first : first + 2 * tok, place * wide : (place + 1) * wide] = jnp.concatenate(
                        rows, axis=0
                    ).astype(jnp.bfloat16)
            first = (tm * seq_count + mixed(part * members, seq_count)) * tok
            rows = slice(first, first + members * tok)
            outs.append(
                pltpu.make_async_copy(block.at[rows], out_hbm.at[rows], out_sems.at[part, tm])
            )
            outs[-1].start()
    for out in outs:
        out.wait()


def residual_kernel(noise_ref, h_ref, gate_hbm, after_ref, out_ref, held, sem):
    step = noise_ref[0]
    steps = gate_hbm.shape[0]
    whole_tiles = steps // 8 * 8
    first = step // 8 * 8

    @pl.when(step < whole_tiles)
    def take_tile():
        rows = pl.ds(pl.multiple_of(first, 8), 8)
        copy = pltpu.make_async_copy(gate_hbm.at[rows], held, sem)
        copy.start()
        copy.wait()

    if steps > whole_tiles:

        @pl.when(step >= whole_tiles)
        def take_rest():
            copy = pltpu.make_async_copy(
                gate_hbm.at[whole_tiles:steps], held.at[0 : steps - whole_tiles], sem
            )
            copy.start()
            copy.wait()

    gate = held[pl.ds(step - first, 1), :]
    high = gate.astype(jnp.bfloat16).astype(jnp.float32)
    middle = (gate - high).astype(jnp.bfloat16).astype(jnp.float32)
    low = gate - high - middle
    parts = jnp.concatenate([high, middle, low, jnp.zeros((5, gate.shape[1]), jnp.float32)], axis=0)
    out_ref[...] = jnp.concatenate([h_ref[0].astype(jnp.float32), parts], axis=0).astype(jnp.bfloat16)


def partner(here, distance, groups):
    return here ^ distance if groups & (groups - 1) == 0 else (here + groups - distance) % groups


def distances(groups):
    return range(groups - 1, 0, -1)


def attend_kernel(groups, pattern_ref, x_ref, after_ref, out_hbm, *refs):
    *hand_refs, held, sems = refs
    wide = held.shape[2]
    rows = held.shape[1]
    across = (groups - 1) * rows
    factor = math.log2(math.e) / math.sqrt(HD)
    here = lax.axis_index("tm")
    lane = lax.broadcasted_iota(jnp.int32, (1, across), 1)
    ends, kept = [], []
    for source in range(groups):
        first = max(source, 1)
        ends.append(min(across, -(-(groups - first) * rows // 128) * 128))
        chosen = jnp.zeros((1, across), jnp.int32)
        for group in range(first, groups):
            start = (groups - 1 - group) * rows
            flag = pattern_ref[group : group + 1, source : source + 1]
            chosen = jnp.where((lane >= start) & (lane < start + rows), flag, chosen)
        kept.append(chosen[:, : ends[-1]] > 0)

    def spread(row, fill):
        rest = across - row.shape[1]
        return jnp.concatenate([row, jnp.full((1, rest), fill, row.dtype)], axis=1) if rest else row

    for head in range(0, wide, HD):
        query = jnp.concatenate(
            [x_ref[group * rows : (group + 1) * rows, head : head + HD] for group in range(groups - 1, 0, -1)],
            axis=0,
        )
        query = jnp.transpose(query)
        value = jnp.transpose(x_ref[:, 2 * wide + head : 2 * wide + head + HD])
        scores, highest = [], None
        for source in range(groups):
            key = x_ref[source * rows : (source + 1) * rows, wide + head : wide + head + HD]
            scores.append(
                jnp.dot(key, query[:, : ends[source]], preferred_element_type=jnp.float32)
            )
            peak = jnp.where(kept[source], jnp.max(scores[-1], axis=0, keepdims=True), -1e30)
            peak = spread(peak, -1e30)
            highest = peak if highest is None else jnp.maximum(highest, peak)
        highest = highest * factor
        total, probs = 0.0, []
        for source in range(groups):
            offset = jnp.where(kept[source], -highest[:, : ends[source]], -1e30)
            raised = jnp.exp2(scores[source] * factor + offset)
            total += spread(jnp.sum(raised, axis=0, keepdims=True), 0.0)
            probs.append(raised.astype(jnp.bfloat16))
        inverse = 1.0 / total
        start, pieces = 0, []
        for source in range(groups - 1, 0, -1):
            stop = ends[source]
            if stop > start:
                numer = jnp.dot(
                    value[:, : (source + 1) * rows],
                    jnp.concatenate([p[:, start:stop] for p in probs[: source + 1]], axis=0),
                    preferred_element_type=jnp.float32,
                )
                pieces.append(numer * inverse[:, start:stop])
                start = stop
        result = jnp.transpose(jnp.concatenate(pieces, axis=1)).astype(jnp.bfloat16)
        for group in range(1, groups):
            start = (groups - 1 - group) * rows
            held[group - 1, :, head : head + HD] = result[start : start + rows]
    copies = [
        pltpu.make_async_copy(
            held.at[min(place, groups - 2)], out_hbm.at[place * rows : (place + 1) * rows], sems.at[place]
        )
        for place in range(groups)
    ]
    for copy in copies:
        copy.start()
    for distance, hand_ref in zip(distances(groups), hand_refs):
        group = lax.rem(partner(here, distance, groups) + 1, groups)
        hand_ref[...] = x_ref[pl.ds(pl.multiple_of(group * rows, rows), rows), wide:]
    for copy in copies:
        copy.wait()


def cache_places(seq_count, groups, rows, wide, distance, here):
    source = partner(here, groups - distance if groups & (groups - 1) else distance, groups)
    lanes = pl.ds(pl.multiple_of(source * wide, wide), wide)
    tok = rows // seq_count
    for index, place, length in runs(seq_count):
        yield (
            slice(index * tok, (index + length) * tok),
            lanes,
            slice(place * tok, (place + length) * tok),
        )


def cache_kernel(seq_count, groups, x_ref, hand_ref, out_ref):
    wide = x_ref.shape[1] // 3
    rows = out_ref.shape[2]
    here = lax.axis_index("tm")
    out_ref[...] = jnp.zeros_like(out_ref)

    @pl.when(here < groups - 1)
    def place():
        own = x_ref[pl.ds(pl.multiple_of((here + 1) * rows, rows), rows), wide:]
        for distance, block in ((0, own), (distances(groups)[0], hand_ref)):
            for to, lanes, at in cache_places(seq_count, groups, rows, wide, distance, here):
                for kind in range(2):
                    out_ref[0, kind, to, lanes] = block[at, kind * wide : (kind + 1) * wide]


def cache_rest_kernel(seq_count, groups, begun_hbm, after_ref, *refs):
    *hand_refs, out_hbm, sems = refs
    wide = hand_refs[0].shape[1] // 2
    rows = out_hbm.shape[2]
    here = lax.axis_index("tm")

    @pl.when(here < groups - 1)
    def place():
        copies = []
        for distance, block in zip(distances(groups)[1:], hand_refs):
            for to, lanes, at in cache_places(seq_count, groups, rows, wide, distance, here):
                for kind in range(2):
                    copies.append(
                        pltpu.make_async_copy(
                            block.at[at, kind * wide : (kind + 1) * wide],
                            out_hbm.at[0, kind, to, lanes],
                            sems.at[len(copies)],
                        )
                    )
                    copies[-1].start()
        for copy in copies:
            copy.wait()


def update_kernel(seq_count, tm_count, att_ref, moved_ref, fresh_ref, after_ref, out_ref):
    tok = out_ref.shape[1]
    wide = att_ref.shape[1]
    count = att_ref.shape[0] // tok
    ordered = sorted(range(seq_count), key=lambda index: mixed(index, seq_count))
    last = lax.axis_index("tm") == tm_count - 1

    @pl.when(last)
    def take_fresh():
        out_ref[0] = fresh_ref[...]

    @pl.when(jnp.logical_not(last))
    def take_update():
        for pair in range(count // 2):
            rows = att_ref[2 * pair * tok : 2 * (pair + 1) * tok, :].astype(jnp.float32)
            for half in range(2):
                source = 2 * pair + half
                start = (ordered[source % seq_count] * tm_count + source // seq_count) * wide
                moved = moved_ref[:, start : start + wide].astype(jnp.float32)
                gate = (moved[tok : tok + 1] + moved[tok + 1 : tok + 2]) + moved[tok + 2 : tok + 3]
                result = moved[:tok] + gate * rows[half * tok : (half + 1) * tok]
                out_ref[0, :, start : start + wide] = result.astype(jnp.bfloat16)


def whole(space=VMEM):
    return pl.BlockSpec(memory_space=space)


def run(kernel, name, outs, specs, operands, flops=0, scratch=(), aliases={}):
    def size(a):
        return math.prod(a.shape) * jnp.dtype(a.dtype).itemsize

    moved = sum(map(size, operands)) + sum(map(size, outs))
    results = pl.pallas_call(
        kernel,
        out_shape=outs,
        in_specs=specs,
        out_specs=[whole(getattr(a, "memory_space", VMEM)) for a in outs],
        scratch_shapes=scratch,
        input_output_aliases=aliases,
        compiler_params=pltpu.CompilerParams(vmem_limit_bytes=4 * moved + (4 << 20)),
        cost_estimate=pl.CostEstimate(flops=flops, bytes_accessed=moved, transcendentals=0),
        name=name,
    )(*operands)
    return results if len(outs) > 1 else results[0]


def spread_body(queries, keys_proj, values, hidden, fresh_latent, gate_table, noise_step, pattern):
    tm_count, seq_count = lax.axis_size("tm"), lax.axis_size("seq")
    count = tm_count * seq_count
    _, tok, width = queries.shape
    wide = width // count
    group_tok = tok * seq_count
    kind = queries.dtype
    DMA = pltpu.SemaphoreType.DMA
    parts = seq_count // 2

    packed = run(
        functools.partial(pack_kernel, seq_count, parts),
        "pack",
        [HBM((count * tok, 3 * wide), kind)],
        [whole(HBM)] * 3,
        [pltpu.with_memory_space_constraint(a, HBM) for a in (queries, keys_proj, values)],
        scratch=[
            VMEM((3, tok, width), kind),
            VMEM((count * tok, 3 * wide), kind),
            DMA((parts, 3)),
            DMA((parts, tm_count)),
        ],
    )
    ordered = sorted(range(seq_count), key=lambda index: mixed(index, seq_count))
    order = [tm * seq_count + index for tm in range(tm_count) for index in ordered]
    exchange = functools.partial(
        lax.all_to_all, axis_name=BOTH, split_axis=0, concat_axis=0, tiled=True, axis_index_groups=[order]
    )
    exchanged = exchange(packed)

    residual = run(
        residual_kernel,
        "residual",
        [VMEM((tok + 8, width), kind)],
        [whole(SMEM), whole(), whole(HBM), whole(HBM)],
        (
            noise_step,
            hidden,
            pltpu.with_memory_space_constraint(gate_table, HBM),
            pltpu.with_memory_space_constraint(packed, HBM),
        ),
        scratch=[VMEM((8, width), jnp.float32), DMA],
    )
    moved = shifted(residual, "tm", -1)

    attended, *hands = run(
        functools.partial(attend_kernel, tm_count),
        "attend",
        [HBM((count * tok, wide), kind)] + [VMEM((group_tok, 2 * wide), kind)] * (tm_count - 1),
        [whole(), whole(), whole(pl.ANY)],
        (pattern, exchanged, moved),
        flops=2 * count * tok * count * tok * wide,
        scratch=[VMEM((tm_count - 1, group_tok, wide), kind), DMA((tm_count,))],
    )
    returned = exchange(attended)
    handed = []
    for distance, hand in zip(distances(tm_count), hands):
        route = [(i, partner(i, distance, tm_count)) for i in range(tm_count)]
        handed.append(lax.ppermute(hand, "tm", [(i, j) for i, j in route if j < tm_count - 1]))

    first, *rest = handed
    begun = run(
        functools.partial(cache_kernel, seq_count, tm_count),
        "cache",
        [jax.ShapeDtypeStruct((1, 2, group_tok, tm_count * wide), kind)],
        [whole()] * 2,
        (exchanged, first),
    )
    begun = pltpu.with_memory_space_constraint(begun, HBM)
    advanced = run(
        functools.partial(update_kernel, seq_count, tm_count),
        "update",
        [jax.ShapeDtypeStruct((1, tok, width), kind)],
        [whole()] * 3 + [whole(HBM)],
        (returned, moved, fresh_latent, begun),
    )
    next_cache = run(
        functools.partial(cache_rest_kernel, seq_count, tm_count),
        "cache_rest",
        [HBM(begun.shape, kind)],
        [whole(HBM)] * 2 + [whole()] * len(rest),
        (begun, pltpu.with_memory_space_constraint(advanced, HBM), *rest),
        scratch=[DMA((2 * len(runs(seq_count)) * len(rest),))],
        aliases={0: 0},
    )
    return (advanced, next_cache)


def absorb(state, query_heads, key_piece, value_piece, scale_factor):
    accum, totals, highest = state
    row_count, head_count, head_dim = query_heads.shape
    key_heads = key_piece.reshape(key_piece.shape[0], head_count, head_dim)
    value_heads = value_piece.reshape(value_piece.shape[0], head_count, head_dim)
    scores = (
        jnp.einsum("qhd,khd->qhk", query_heads, key_heads, preferred_element_type=jnp.float32)
        * scale_factor
    )
    raised = jnp.maximum(highest, jnp.max(scores, axis=-1))
    fade = jnp.exp(highest - raised)
    weights = jnp.exp(scores - raised[..., None])
    totals = totals * fade + jnp.sum(weights, axis=-1)
    accum = accum * fade[..., None] + jnp.einsum(
        "qhk,khd->qhd",
        weights.astype(jnp.bfloat16),
        value_heads,
        preferred_element_type=jnp.float32,
    )
    return (accum, totals, raised)


def gather_body(queries, keys_proj, values, hidden, fresh_latent, gate_table, noise_step, pattern):
    group_index = lax.axis_index("tm")
    final_index = lax.axis_size("tm") - 1
    query_tok, key_tok, value_tok = (
        lax.all_to_all(queries[0], "seq", split_axis=1, concat_axis=0, tiled=True),
        lax.all_to_all(keys_proj[0], "seq", split_axis=1, concat_axis=0, tiled=True),
        lax.all_to_all(values[0], "seq", split_axis=1, concat_axis=0, tiled=True),
    )
    row_count, local_width = query_tok.shape
    head_count = local_width // HD
    query_heads = query_tok.reshape(row_count, head_count, HD)
    scale_factor = 1.0 / math.sqrt(HD)
    reach = lax.dynamic_index_in_dim(pattern, group_index, 0, keepdims=False)
    start_state = (
        jnp.zeros((row_count, head_count, HD), jnp.float32),
        jnp.zeros((row_count, head_count), jnp.float32),
        jnp.full((row_count, head_count), -1e30, jnp.float32),
    )

    def one_block(current, inputs):
        key_block, value_block, flag = inputs
        return (
            lax.cond(
                flag > 0,
                lambda state: absorb(state, query_heads, key_block, value_block, scale_factor),
                lambda state: state,
                current,
            ),
            None,
        )

    key_piece = lax.all_gather(key_tok, "tm", axis=0, tiled=False)
    value_piece = lax.all_gather(value_tok, "tm", axis=0, tiled=False)
    state, unused = lax.scan(one_block, start_state, (key_piece, value_piece, reach))
    cache_keys, cache_values = shifted((key_tok, value_tok), "tm", -1)
    accum, totals, highest = state
    attended_head = (accum / totals[..., None]).reshape(row_count, local_width).astype(jnp.bfloat16)
    attended = lax.all_to_all(attended_head, "seq", split_axis=0, concat_axis=1, tiled=True)
    gate_row = lax.dynamic_index_in_dim(gate_table, noise_step[0], 0, keepdims=False)
    updated = (
        hidden[0].astype(jnp.float32) + gate_row[None, :] * attended.astype(jnp.float32)
    ).astype(jnp.bfloat16)
    moved = shifted(updated, "tm", -1)
    advanced = jnp.where(group_index == final_index, fresh_latent, moved)[None]
    next_cache = jnp.stack([cache_keys, cache_values], axis=0)[None]
    return (advanced, next_cache)


def body(queries, *others):
    tm_count, seq_count = lax.axis_size("tm"), lax.axis_size("seq")
    _, tok, width = queries.shape
    count = tm_count * seq_count
    even = width % (count * HD) == 0 and tok % 8 == 0 and seq_count % 2 == 0 and tm_count > 2
    return (spread_body if even else gather_body)(queries, *others)


def solution(mesh):
    placed = (
        P("tm", "seq", None),
        P("tm", "seq", None),
        P("tm", "seq", None),
        P("tm", "seq", None),
        P("seq", None),
        P(),
        P("tm"),
        P(),
    )
    return jax.shard_map(
        body,
        mesh=mesh,
        in_specs=placed,
        out_specs=(P("tm", "seq", None), P("tm", None, None, "seq")),
        check_vma=False,
    )
```

```python
import functools
import math

import jax
import jax.numpy as jnp
from jax import lax
from jax.experimental import pallas as pl
from jax.experimental.pallas import tpu as pltpu
from jax.sharding import PartitionSpec as P

HD = 128
BOTH = ("tm", "seq")
VMEM = pltpu.VMEM
SMEM = pltpu.SMEM
HBM = pltpu.HBM


def shifted(block, axis, distance):
    devices = range(lax.axis_size(axis))
    route = [(i - distance, i) for i in devices if i - distance in devices]
    return lax.ppermute(block, axis, route)


def mixed(index, count):
    return (index + count // 2) % count


def pack_kernel(seq_count, parts, q_hbm, k_hbm, v_hbm, out_hbm, held, block, in_sems, out_sems):
    tok, width = held.shape[1:]
    wide = out_hbm.shape[1] // 3
    count = out_hbm.shape[0] // tok
    tm_count = count // seq_count
    span, members = width // parts, seq_count // parts
    copies = []
    for part in range(parts):
        columns = slice(part * span, (part + 1) * span)
        for place, ref in enumerate((q_hbm, k_hbm, v_hbm)):
            copies.append(
                pltpu.make_async_copy(
                    ref.at[0, :, columns], held.at[place, :, columns], in_sems.at[part, place]
                )
            )
            copies[-1].start()
    outs = []
    for part in range(parts):
        for place in range(3):
            copies[3 * part + place].wait()
        for tm in range(tm_count):
            for seq in range(part * members, (part + 1) * members, 2):
                first = (tm * seq_count + mixed(seq, seq_count)) * tok
                for place in range(3):
                    rows = []
                    for member in (seq, seq + 1):
                        start = (member * tm_count + tm) * wide
                        rows.append(held[place, :, start : start + wide].astype(jnp.float32))
                    block[first : first + 2 * tok, place * wide : (place + 1) * wide] = jnp.concatenate(
                        rows, axis=0
                    ).astype(jnp.bfloat16)
            first = (tm * seq_count + mixed(part * members, seq_count)) * tok
            rows = slice(first, first + members * tok)
            outs.append(
                pltpu.make_async_copy(block.at[rows], out_hbm.at[rows], out_sems.at[part, tm])
            )
            outs[-1].start()
    for out in outs:
        out.wait()


def residual_kernel(noise_ref, h_ref, gate_hbm, after_ref, out_ref, held, sem):
    step = noise_ref[0]
    steps = gate_hbm.shape[0]
    whole_tiles = steps // 8 * 8
    first = step // 8 * 8

    @pl.when(step < whole_tiles)
    def take_tile():
        rows = pl.ds(pl.multiple_of(first, 8), 8)
        copy = pltpu.make_async_copy(gate_hbm.at[rows], held, sem)
        copy.start()
        copy.wait()

    if steps > whole_tiles:

        @pl.when(step >= whole_tiles)
        def take_rest():
            copy = pltpu.make_async_copy(
                gate_hbm.at[whole_tiles:steps], held.at[0 : steps - whole_tiles], sem
            )
            copy.start()
            copy.wait()

    gate = held[pl.ds(step - first, 1), :]
    high = gate.astype(jnp.bfloat16).astype(jnp.float32)
    middle = (gate - high).astype(jnp.bfloat16).astype(jnp.float32)
    low = gate - high - middle
    parts = jnp.concatenate([high, middle, low, jnp.zeros((5, gate.shape[1]), jnp.float32)], axis=0)
    out_ref[...] = jnp.concatenate([h_ref[0].astype(jnp.float32), parts], axis=0).astype(jnp.bfloat16)


def partner(here, distance, groups):
    return here ^ distance if groups & (groups - 1) == 0 else (here + groups - distance) % groups


def distances(groups):
    return range(groups - 1, 0, -1)


def hand_over(group, x_ref, out_ref, lanes=slice(None)):
    wide = x_ref.shape[1] // 3
    rows = out_ref.shape[1]
    half = rows // 2
    for part in range(2):
        first = pl.multiple_of(group * rows + mixed(part, 2) * half, half)
        for kind in range(2):
            out_ref[kind, part * half : (part + 1) * half, lanes] = x_ref[
                pl.ds(first, half), (kind + 1) * wide : (kind + 2) * wide
            ]


def attend_kernel(groups, pattern_ref, x_ref, after_ref, out_hbm, *refs):
    *hand_refs, held, sems = refs
    wide = held.shape[2]
    rows = held.shape[1]
    across = (groups - 1) * rows
    factor = math.log2(math.e) / math.sqrt(HD)
    here = lax.axis_index("tm")
    lane = lax.broadcasted_iota(jnp.int32, (1, across), 1)
    ends, kept = [], []
    for source in range(groups):
        first = max(source, 1)
        ends.append(min(across, -(-(groups - first) * rows // 128) * 128))
        chosen = jnp.zeros((1, across), jnp.int32)
        for group in range(first, groups):
            start = (groups - 1 - group) * rows
            flag = pattern_ref[group : group + 1, source : source + 1]
            chosen = jnp.where((lane >= start) & (lane < start + rows), flag, chosen)
        kept.append(chosen[:, : ends[-1]] > 0)

    copies = []

    def send(group):
        for place in (group - 1, groups - 1) if group == groups - 1 else (group - 1,):
            copies.append(
                pltpu.make_async_copy(
                    held.at[group - 1], out_hbm.at[place * rows : (place + 1) * rows], sems.at[place]
                )
            )
            copies[-1].start()

    def spread(row, fill):
        rest = across - row.shape[1]
        return jnp.concatenate([row, jnp.full((1, rest), fill, row.dtype)], axis=1) if rest else row

    for head in range(0, wide, HD):
        query = jnp.concatenate(
            [x_ref[group * rows : (group + 1) * rows, head : head + HD] for group in range(groups - 1, 0, -1)],
            axis=0,
        )
        query = jnp.transpose(query)
        value = jnp.transpose(x_ref[:, 2 * wide + head : 2 * wide + head + HD])
        scores, highest = [], None
        for source in range(groups):
            key = x_ref[source * rows : (source + 1) * rows, wide + head : wide + head + HD]
            scores.append(
                jnp.dot(key, query[:, : ends[source]], preferred_element_type=jnp.float32)
            )
            peak = jnp.where(kept[source], jnp.max(scores[-1], axis=0, keepdims=True), -1e30)
            peak = spread(peak, -1e30)
            highest = peak if highest is None else jnp.maximum(highest, peak)
        highest = highest * factor
        total, probs = 0.0, []
        for source in range(groups):
            offset = jnp.where(kept[source], -highest[:, : ends[source]], -1e30)
            raised = jnp.exp2(scores[source] * factor + offset)
            total += spread(jnp.sum(raised, axis=0, keepdims=True), 0.0)
            probs.append(raised.astype(jnp.bfloat16))
        inverse = 1.0 / total
        last = head + HD == wide
        start, left, waiting = 0, None, groups - 1
        for source in range(groups - 1, 0, -1):
            stop = ends[source]
            if stop > start:
                numer = jnp.dot(
                    value[:, : (source + 1) * rows],
                    jnp.concatenate([p[:, start:stop] for p in probs[: source + 1]], axis=0),
                    preferred_element_type=jnp.float32,
                )
                result = jnp.transpose(numer * inverse[:, start:stop])
                left = result if left is None else jnp.concatenate([left, result], axis=0)
                start = stop
            while left is not None and left.shape[0] >= rows:
                held[waiting - 1, :, head : head + HD] = left[:rows].astype(jnp.bfloat16)
                left = left[rows:] if left.shape[0] > rows else None
                if last:
                    send(waiting)
                waiting -= 1
    for distance, hand_ref in zip(distances(groups), hand_refs):
        hand_over(lax.rem(partner(here, distance, groups) + 1, groups), x_ref, hand_ref)
    for copy in copies:
        copy.wait()


def lanes_of(distance, groups, here, wide):
    source = partner(here, groups - distance if groups & (groups - 1) else distance, groups)
    return pl.ds(pl.multiple_of(source * wide, wide), wide)


def cache_kernel(groups, x_ref, hand_ref, out_ref):
    wide = x_ref.shape[1] // 3
    here = lax.axis_index("tm")
    out_ref[...] = jnp.zeros_like(out_ref)

    @pl.when(here < groups - 1)
    def place():
        hand_over(here + 1, x_ref, out_ref.at[0], lanes_of(0, groups, here, wide))
        out_ref[0, :, :, lanes_of(distances(groups)[0], groups, here, wide)] = hand_ref[...]


def cache_rest_kernel(groups, begun_hbm, after_ref, *refs):
    *hand_refs, out_hbm, sems = refs
    here = lax.axis_index("tm")

    @pl.when(here < groups - 1)
    def place():
        copies = [
            pltpu.make_async_copy(
                block, out_hbm.at[0, :, :, lanes_of(distance, groups, here, block.shape[2])], sems.at[index]
            )
            for index, (distance, block) in enumerate(zip(distances(groups)[1:], hand_refs))
        ]
        for copy in copies:
            copy.start()
        for copy in copies:
            copy.wait()


def update_kernel(seq_count, tm_count, att_ref, moved_ref, fresh_ref, after_ref, out_ref):
    tok = out_ref.shape[1]
    wide = att_ref.shape[1]
    count = att_ref.shape[0] // tok
    last = lax.axis_index("tm") == tm_count - 1

    @pl.when(last)
    def take_fresh():
        out_ref[0] = fresh_ref[...]

    @pl.when(jnp.logical_not(last))
    def take_update():
        for pair in range(count // 2):
            rows = att_ref[2 * pair * tok : 2 * (pair + 1) * tok, :].astype(jnp.float32)
            for half in range(2):
                source = 2 * pair + half
                start = (mixed(source % seq_count, seq_count) * tm_count + source // seq_count) * wide
                moved = moved_ref[:, start : start + wide].astype(jnp.float32)
                gate = (moved[tok : tok + 1] + moved[tok + 1 : tok + 2]) + moved[tok + 2 : tok + 3]
                result = moved[:tok] + gate * rows[half * tok : (half + 1) * tok]
                out_ref[0, :, start : start + wide] = result.astype(jnp.bfloat16)


def whole(space=VMEM):
    return pl.BlockSpec(memory_space=space)


def run(kernel, name, outs, specs, operands, flops=0, scratch=(), aliases={}):
    def size(a):
        return math.prod(a.shape) * jnp.dtype(a.dtype).itemsize

    moved = sum(map(size, operands)) + sum(map(size, outs))
    results = pl.pallas_call(
        kernel,
        out_shape=outs,
        in_specs=specs,
        out_specs=[whole(getattr(a, "memory_space", VMEM)) for a in outs],
        scratch_shapes=scratch,
        input_output_aliases=aliases,
        compiler_params=pltpu.CompilerParams(vmem_limit_bytes=4 * moved + (4 << 20)),
        cost_estimate=pl.CostEstimate(flops=flops, bytes_accessed=moved, transcendentals=0),
        name=name,
    )(*operands)
    return results if len(outs) > 1 else results[0]


def spread_body(queries, keys_proj, values, hidden, fresh_latent, gate_table, noise_step, pattern):
    tm_count, seq_count = lax.axis_size("tm"), lax.axis_size("seq")
    count = tm_count * seq_count
    _, tok, width = queries.shape
    wide = width // count
    group_tok = tok * seq_count
    kind = queries.dtype
    DMA = pltpu.SemaphoreType.DMA
    parts = 4 if seq_count % 8 == 0 else 2

    packed = run(
        functools.partial(pack_kernel, seq_count, parts),
        "pack",
        [HBM((count * tok, 3 * wide), kind)],
        [whole(HBM)] * 3,
        [pltpu.with_memory_space_constraint(a, HBM) for a in (queries, keys_proj, values)],
        scratch=[
            VMEM((3, tok, width), kind),
            VMEM((count * tok, 3 * wide), kind),
            DMA((parts, 3)),
            DMA((parts, tm_count)),
        ],
    )
    order = [tm * seq_count + mixed(s, seq_count) for tm in range(tm_count) for s in range(seq_count)]
    exchange = functools.partial(
        lax.all_to_all, axis_name=BOTH, split_axis=0, concat_axis=0, tiled=True, axis_index_groups=[order]
    )
    exchanged = exchange(packed)

    residual = run(
        residual_kernel,
        "residual",
        [VMEM((tok + 8, width), kind)],
        [whole(SMEM), whole(), whole(HBM), whole(HBM)],
        (
            noise_step,
            hidden,
            pltpu.with_memory_space_constraint(gate_table, HBM),
            pltpu.with_memory_space_constraint(packed, HBM),
        ),
        scratch=[VMEM((8, width), jnp.float32), DMA],
    )
    moved = shifted(residual, "tm", -1)

    attended, *hands = run(
        functools.partial(attend_kernel, tm_count),
        "attend",
        [HBM((count * tok, wide), kind)] + [VMEM((2, group_tok, wide), kind)] * (tm_count - 1),
        [whole(), whole(), whole(pl.ANY)],
        (pattern, exchanged, moved),
        flops=2 * count * tok * count * tok * wide,
        scratch=[VMEM((tm_count - 1, group_tok, wide), kind), DMA((tm_count,))],
    )
    returned = exchange(attended)
    handed = []
    for distance, hand in zip(distances(tm_count), hands):
        route = [(i, partner(i, distance, tm_count)) for i in range(tm_count)]
        handed.append(lax.ppermute(hand, "tm", [(i, j) for i, j in route if j < tm_count - 1]))

    first, *rest = handed
    begun = run(
        functools.partial(cache_kernel, tm_count),
        "cache",
        [jax.ShapeDtypeStruct((1, 2, group_tok, tm_count * wide), kind)],
        [whole()] * 2,
        (exchanged, first),
    )
    begun = pltpu.with_memory_space_constraint(begun, HBM)
    advanced = run(
        functools.partial(update_kernel, seq_count, tm_count),
        "update",
        [jax.ShapeDtypeStruct((1, tok, width), kind)],
        [whole()] * 3 + [whole(HBM)],
        (returned, moved, fresh_latent, begun),
    )
    next_cache = run(
        functools.partial(cache_rest_kernel, tm_count),
        "cache_rest",
        [HBM(begun.shape, kind)],
        [whole(HBM)] * 2 + [whole()] * len(rest),
        (begun, pltpu.with_memory_space_constraint(advanced, HBM), *rest),
        scratch=[DMA((len(rest),))],
        aliases={0: 0},
    )
    return (advanced, next_cache)


def absorb(state, query_heads, key_piece, value_piece, scale_factor):
    accum, totals, highest = state
    row_count, head_count, head_dim = query_heads.shape
    key_heads = key_piece.reshape(key_piece.shape[0], head_count, head_dim)
    value_heads = value_piece.reshape(value_piece.shape[0], head_count, head_dim)
    scores = (
        jnp.einsum("qhd,khd->qhk", query_heads, key_heads, preferred_element_type=jnp.float32)
        * scale_factor
    )
    raised = jnp.maximum(highest, jnp.max(scores, axis=-1))
    fade = jnp.exp(highest - raised)
    weights = jnp.exp(scores - raised[..., None])
    totals = totals * fade + jnp.sum(weights, axis=-1)
    accum = accum * fade[..., None] + jnp.einsum(
        "qhk,khd->qhd",
        weights.astype(jnp.bfloat16),
        value_heads,
        preferred_element_type=jnp.float32,
    )
    return (accum, totals, raised)


def gather_body(queries, keys_proj, values, hidden, fresh_latent, gate_table, noise_step, pattern):
    group_index = lax.axis_index("tm")
    final_index = lax.axis_size("tm") - 1
    query_tok, key_tok, value_tok = (
        lax.all_to_all(queries[0], "seq", split_axis=1, concat_axis=0, tiled=True),
        lax.all_to_all(keys_proj[0], "seq", split_axis=1, concat_axis=0, tiled=True),
        lax.all_to_all(values[0], "seq", split_axis=1, concat_axis=0, tiled=True),
    )
    row_count, local_width = query_tok.shape
    head_count = local_width // HD
    query_heads = query_tok.reshape(row_count, head_count, HD)
    scale_factor = 1.0 / math.sqrt(HD)
    reach = lax.dynamic_index_in_dim(pattern, group_index, 0, keepdims=False)
    start_state = (
        jnp.zeros((row_count, head_count, HD), jnp.float32),
        jnp.zeros((row_count, head_count), jnp.float32),
        jnp.full((row_count, head_count), -1e30, jnp.float32),
    )

    def one_block(current, inputs):
        key_block, value_block, flag = inputs
        return (
            lax.cond(
                flag > 0,
                lambda state: absorb(state, query_heads, key_block, value_block, scale_factor),
                lambda state: state,
                current,
            ),
            None,
        )

    key_piece = lax.all_gather(key_tok, "tm", axis=0, tiled=False)
    value_piece = lax.all_gather(value_tok, "tm", axis=0, tiled=False)
    state, unused = lax.scan(one_block, start_state, (key_piece, value_piece, reach))
    cache_keys, cache_values = shifted((key_tok, value_tok), "tm", -1)
    accum, totals, highest = state
    attended_head = (accum / totals[..., None]).reshape(row_count, local_width).astype(jnp.bfloat16)
    attended = lax.all_to_all(attended_head, "seq", split_axis=0, concat_axis=1, tiled=True)
    gate_row = lax.dynamic_index_in_dim(gate_table, noise_step[0], 0, keepdims=False)
    updated = (
        hidden[0].astype(jnp.float32) + gate_row[None, :] * attended.astype(jnp.float32)
    ).astype(jnp.bfloat16)
    moved = shifted(updated, "tm", -1)
    advanced = jnp.where(group_index == final_index, fresh_latent, moved)[None]
    next_cache = jnp.stack([cache_keys, cache_values], axis=0)[None]
    return (advanced, next_cache)


def body(queries, *others):
    tm_count, seq_count = lax.axis_size("tm"), lax.axis_size("seq")
    _, tok, width = queries.shape
    count = tm_count * seq_count
    even = width % (count * HD) == 0 and tok % 8 == 0 and seq_count % 4 == 0 and tm_count > 2
    return (spread_body if even else gather_body)(queries, *others)


def solution(mesh):
    placed = (
        P("tm", "seq", None),
        P("tm", "seq", None),
        P("tm", "seq", None),
        P("tm", "seq", None),
        P("seq", None),
        P(),
        P("tm"),
        P(),
    )
    return jax.shard_map(
        body,
        mesh=mesh,
        in_specs=placed,
        out_specs=(P("tm", "seq", None), P("tm", None, None, "seq")),
        check_vma=False,
    )
```

```python
import functools
import math

import jax
import jax.numpy as jnp
from jax import lax
from jax.experimental import pallas as pl
from jax.experimental.pallas import tpu as pltpu
from jax.sharding import PartitionSpec as P

HD = 128
BOTH = ("tm", "seq")
VMEM = pltpu.VMEM
SMEM = pltpu.SMEM
HBM = pltpu.HBM


def shifted(block, axis, distance):
    devices = range(lax.axis_size(axis))
    route = [(i - distance, i) for i in devices if i - distance in devices]
    return lax.ppermute(block, axis, route)


def mixed(index, count):
    return (index + count // 2) % count


def back_order(tm_count, seq_count):
    ordered = sorted(range(seq_count), key=lambda index: mixed(index, seq_count))
    half = tm_count // 2
    return [
        (high * half + low, ordered[pair + member])
        for low in range(half)
        for pair in range(0, seq_count, 2)
        for high in range(tm_count // half)
        for member in range(2)
    ]


def pack_kernel(seq_count, parts, q_hbm, k_hbm, v_hbm, out_hbm, held, block, in_sems, out_sems):
    tok, width = held.shape[1:]
    wide = out_hbm.shape[1] // 3
    count = out_hbm.shape[0] // tok
    tm_count = count // seq_count
    span, members = width // parts, seq_count // parts
    copies = []
    for part in range(parts):
        columns = slice(part * span, (part + 1) * span)
        for place, ref in enumerate((q_hbm, k_hbm, v_hbm)):
            copies.append(
                pltpu.make_async_copy(
                    ref.at[0, :, columns], held.at[place, :, columns], in_sems.at[part, place]
                )
            )
            copies[-1].start()
    outs = []
    for part in range(parts):
        for place in range(3):
            copies[3 * part + place].wait()
        for tm in range(tm_count):
            for seq in range(part * members, (part + 1) * members, 2):
                first = (tm * seq_count + mixed(seq, seq_count)) * tok
                for place in range(3):
                    rows = []
                    for member in (seq, seq + 1):
                        start = (member * tm_count + tm) * wide
                        rows.append(held[place, :, start : start + wide].astype(jnp.float32))
                    block[first : first + 2 * tok, place * wide : (place + 1) * wide] = jnp.concatenate(
                        rows, axis=0
                    ).astype(jnp.bfloat16)
            first = (tm * seq_count + mixed(part * members, seq_count)) * tok
            rows = slice(first, first + members * tok)
            outs.append(
                pltpu.make_async_copy(block.at[rows], out_hbm.at[rows], out_sems.at[part, tm])
            )
            outs[-1].start()
    for out in outs:
        out.wait()


def residual_kernel(noise_ref, h_ref, gate_hbm, after_ref, out_ref, held, sem):
    step = noise_ref[0]
    steps = gate_hbm.shape[0]
    whole_tiles = steps // 8 * 8
    first = step // 8 * 8

    @pl.when(step < whole_tiles)
    def take_tile():
        rows = pl.ds(pl.multiple_of(first, 8), 8)
        copy = pltpu.make_async_copy(gate_hbm.at[rows], held, sem)
        copy.start()
        copy.wait()

    if steps > whole_tiles:

        @pl.when(step >= whole_tiles)
        def take_rest():
            copy = pltpu.make_async_copy(
                gate_hbm.at[whole_tiles:steps], held.at[0 : steps - whole_tiles], sem
            )
            copy.start()
            copy.wait()

    gate = held[pl.ds(step - first, 1), :]
    high = gate.astype(jnp.bfloat16).astype(jnp.float32)
    middle = (gate - high).astype(jnp.bfloat16).astype(jnp.float32)
    low = gate - high - middle
    parts = jnp.concatenate([high, middle, low, jnp.zeros((5, gate.shape[1]), jnp.float32)], axis=0)
    out_ref[...] = jnp.concatenate([h_ref[0].astype(jnp.float32), parts], axis=0).astype(jnp.bfloat16)


def partner(here, distance, groups):
    return here ^ distance if groups & (groups - 1) == 0 else (here + groups - distance) % groups


def distances(groups):
    return range(groups - 1, 0, -1)


def hand_over(group, x_ref, out_ref, lanes=slice(None)):
    wide = x_ref.shape[1] // 3
    rows = out_ref.shape[1]
    half = rows // 2
    for part in range(2):
        first = pl.multiple_of(group * rows + mixed(part, 2) * half, half)
        for kind in range(2):
            out_ref[kind, part * half : (part + 1) * half, lanes] = x_ref[
                pl.ds(first, half), (kind + 1) * wide : (kind + 2) * wide
            ]


def attend_kernel(groups, seq_count, pattern_ref, x_ref, after_ref, out_hbm, *refs):
    *hand_refs, held, sems = refs
    wide = held.shape[1]
    rows = held.shape[0] // groups
    across = (groups - 1) * rows
    factor = math.log2(math.e) / math.sqrt(HD)
    here = lax.axis_index("tm")
    lane = lax.broadcasted_iota(jnp.int32, (1, across), 1)
    ends, kept = [], []
    for source in range(groups):
        first = max(source, 1)
        ends.append(min(across, -(-(groups - first) * rows // 128) * 128))
        chosen = jnp.zeros((1, across), jnp.int32)
        for group in range(first, groups):
            start = (groups - 1 - group) * rows
            flag = pattern_ref[group : group + 1, source : source + 1]
            chosen = jnp.where((lane >= start) & (lane < start + rows), flag, chosen)
        kept.append(chosen[:, : ends[-1]] > 0)

    halves = groups // (groups // 2)
    pairs = seq_count // 2
    step = rows // pairs

    def keep(group, head, result):
        for place in (group - 1, groups - 1) if group == groups - 1 else (group - 1,):
            low, high = place % (groups // 2), place // (groups // 2)
            for pair in range(pairs):
                to = ((low * pairs + pair) * halves + high) * step
                held[to : to + step, head : head + HD] = result[pair * step : (pair + 1) * step]

    def spread(row, fill):
        rest = across - row.shape[1]
        return jnp.concatenate([row, jnp.full((1, rest), fill, row.dtype)], axis=1) if rest else row

    for head in range(0, wide, HD):
        query = jnp.concatenate(
            [x_ref[group * rows : (group + 1) * rows, head : head + HD] for group in range(groups - 1, 0, -1)],
            axis=0,
        )
        query = jnp.transpose(query)
        value = jnp.transpose(x_ref[:, 2 * wide + head : 2 * wide + head + HD])
        scores, highest = [], None
        for source in range(groups):
            key = x_ref[source * rows : (source + 1) * rows, wide + head : wide + head + HD]
            scores.append(
                jnp.dot(key, query[:, : ends[source]], preferred_element_type=jnp.float32)
            )
            peak = jnp.where(kept[source], jnp.max(scores[-1], axis=0, keepdims=True), -1e30)
            peak = spread(peak, -1e30)
            highest = peak if highest is None else jnp.maximum(highest, peak)
        highest = highest * factor
        total, probs = 0.0, []
        for source in range(groups):
            offset = jnp.where(kept[source], -highest[:, : ends[source]], -1e30)
            raised = jnp.exp2(scores[source] * factor + offset)
            total += spread(jnp.sum(raised, axis=0, keepdims=True), 0.0)
            probs.append(raised.astype(jnp.bfloat16))
        inverse = 1.0 / total
        start, left, waiting = 0, None, groups - 1
        for source in range(groups - 1, 0, -1):
            stop = ends[source]
            if stop > start:
                numer = jnp.dot(
                    value[:, : (source + 1) * rows],
                    jnp.concatenate([p[:, start:stop] for p in probs[: source + 1]], axis=0),
                    preferred_element_type=jnp.float32,
                )
                result = jnp.transpose(numer * inverse[:, start:stop])
                left = result if left is None else jnp.concatenate([left, result], axis=0)
                start = stop
            while left is not None and left.shape[0] >= rows:
                keep(waiting, head, left[:rows].astype(jnp.bfloat16))
                left = left[rows:] if left.shape[0] > rows else None
                waiting -= 1
    copies = [
        pltpu.make_async_copy(
            held.at[place * rows : (place + 1) * rows], out_hbm.at[place * rows : (place + 1) * rows], sems.at[place]
        )
        for place in range(groups)
    ]
    for copy in copies:
        copy.start()
    for distance, hand_ref in zip(distances(groups), hand_refs):
        hand_over(lax.rem(partner(here, distance, groups) + 1, groups), x_ref, hand_ref)
    for copy in copies:
        copy.wait()


def lanes_of(distance, groups, here, wide):
    source = partner(here, groups - distance if groups & (groups - 1) else distance, groups)
    return pl.ds(pl.multiple_of(source * wide, wide), wide)


def cache_kernel(groups, x_ref, hand_ref, out_ref):
    wide = x_ref.shape[1] // 3
    here = lax.axis_index("tm")
    out_ref[...] = jnp.zeros_like(out_ref)

    @pl.when(here < groups - 1)
    def place():
        hand_over(here + 1, x_ref, out_ref.at[0], lanes_of(0, groups, here, wide))
        out_ref[0, :, :, lanes_of(distances(groups)[0], groups, here, wide)] = hand_ref[...]


def cache_rest_kernel(groups, begun_hbm, after_ref, *refs):
    *hand_refs, out_hbm, sems = refs
    here = lax.axis_index("tm")

    @pl.when(here < groups - 1)
    def place():
        copies = [
            pltpu.make_async_copy(
                block, out_hbm.at[0, :, :, lanes_of(distance, groups, here, block.shape[2])], sems.at[index]
            )
            for index, (distance, block) in enumerate(zip(distances(groups)[1:], hand_refs))
        ]
        for copy in copies:
            copy.start()
        for copy in copies:
            copy.wait()


def update_kernel(seq_count, tm_count, att_ref, moved_ref, fresh_ref, after_ref, out_ref):
    tok = out_ref.shape[1]
    wide = att_ref.shape[1]
    count = att_ref.shape[0] // tok
    order = back_order(tm_count, seq_count)
    last = lax.axis_index("tm") == tm_count - 1

    @pl.when(last)
    def take_fresh():
        out_ref[0] = fresh_ref[...]

    @pl.when(jnp.logical_not(last))
    def take_update():
        for pair in range(count // 2):
            rows = att_ref[2 * pair * tok : 2 * (pair + 1) * tok, :].astype(jnp.float32)
            for half in range(2):
                source = 2 * pair + half
                start = (order[source][1] * tm_count + order[source][0]) * wide
                moved = moved_ref[:, start : start + wide].astype(jnp.float32)
                gate = (moved[tok : tok + 1] + moved[tok + 1 : tok + 2]) + moved[tok + 2 : tok + 3]
                result = moved[:tok] + gate * rows[half * tok : (half + 1) * tok]
                out_ref[0, :, start : start + wide] = result.astype(jnp.bfloat16)


def whole(space=VMEM):
    return pl.BlockSpec(memory_space=space)


def run(kernel, name, outs, specs, operands, flops=0, scratch=(), aliases={}):
    def size(a):
        return math.prod(a.shape) * jnp.dtype(a.dtype).itemsize

    moved = sum(map(size, operands)) + sum(map(size, outs))
    results = pl.pallas_call(
        kernel,
        out_shape=outs,
        in_specs=specs,
        out_specs=[whole(getattr(a, "memory_space", VMEM)) for a in outs],
        scratch_shapes=scratch,
        input_output_aliases=aliases,
        compiler_params=pltpu.CompilerParams(vmem_limit_bytes=4 * moved + (4 << 20)),
        cost_estimate=pl.CostEstimate(flops=flops, bytes_accessed=moved, transcendentals=0),
        name=name,
    )(*operands)
    return results if len(outs) > 1 else results[0]


def spread_body(queries, keys_proj, values, hidden, fresh_latent, gate_table, noise_step, pattern):
    tm_count, seq_count = lax.axis_size("tm"), lax.axis_size("seq")
    count = tm_count * seq_count
    _, tok, width = queries.shape
    wide = width // count
    group_tok = tok * seq_count
    kind = queries.dtype
    DMA = pltpu.SemaphoreType.DMA
    parts = 4 if seq_count % 8 == 0 else 2

    packed = run(
        functools.partial(pack_kernel, seq_count, parts),
        "pack",
        [HBM((count * tok, 3 * wide), kind)],
        [whole(HBM)] * 3,
        [pltpu.with_memory_space_constraint(a, HBM) for a in (queries, keys_proj, values)],
        scratch=[
            VMEM((3, tok, width), kind),
            VMEM((count * tok, 3 * wide), kind),
            DMA((parts, 3)),
            DMA((parts, tm_count)),
        ],
    )
    order = [tm * seq_count + mixed(s, seq_count) for tm in range(tm_count) for s in range(seq_count)]
    back = [tm * seq_count + index for tm, index in back_order(tm_count, seq_count)]
    exchange = functools.partial(
        lax.all_to_all, axis_name=BOTH, split_axis=0, concat_axis=0, tiled=True
    )
    exchanged = exchange(packed, axis_index_groups=[order])

    residual = run(
        residual_kernel,
        "residual",
        [VMEM((tok + 8, width), kind)],
        [whole(SMEM), whole(), whole(HBM), whole(HBM)],
        (
            noise_step,
            hidden,
            pltpu.with_memory_space_constraint(gate_table, HBM),
            pltpu.with_memory_space_constraint(packed, HBM),
        ),
        scratch=[VMEM((8, width), jnp.float32), DMA],
    )
    moved = shifted(residual, "tm", -1)

    attended, *hands = run(
        functools.partial(attend_kernel, tm_count, seq_count),
        "attend",
        [HBM((count * tok, wide), kind)] + [VMEM((2, group_tok, wide), kind)] * (tm_count - 1),
        [whole(), whole(), whole(pl.ANY)],
        (pattern, exchanged, moved),
        flops=2 * count * tok * count * tok * wide,
        scratch=[VMEM((count * tok, wide), kind), DMA((tm_count,))],
    )
    returned = exchange(attended, axis_index_groups=[back])
    handed = []
    for distance, hand in zip(distances(tm_count), hands):
        route = [(i, partner(i, distance, tm_count)) for i in range(tm_count)]
        handed.append(lax.ppermute(hand, "tm", [(i, j) for i, j in route if j < tm_count - 1]))

    first, *rest = handed
    begun = run(
        functools.partial(cache_kernel, tm_count),
        "cache",
        [jax.ShapeDtypeStruct((1, 2, group_tok, tm_count * wide), kind)],
        [whole()] * 2,
        (exchanged, first),
    )
    begun = pltpu.with_memory_space_constraint(begun, HBM)
    advanced = run(
        functools.partial(update_kernel, seq_count, tm_count),
        "update",
        [jax.ShapeDtypeStruct((1, tok, width), kind)],
        [whole()] * 3 + [whole(HBM)],
        (returned, moved, fresh_latent, begun),
    )
    next_cache = run(
        functools.partial(cache_rest_kernel, tm_count),
        "cache_rest",
        [HBM(begun.shape, kind)],
        [whole(HBM)] * 2 + [whole()] * len(rest),
        (begun, pltpu.with_memory_space_constraint(advanced, HBM), *rest),
        scratch=[DMA((len(rest),))],
        aliases={0: 0},
    )
    return (advanced, next_cache)


def absorb(state, query_heads, key_piece, value_piece, scale_factor):
    accum, totals, highest = state
    row_count, head_count, head_dim = query_heads.shape
    key_heads = key_piece.reshape(key_piece.shape[0], head_count, head_dim)
    value_heads = value_piece.reshape(value_piece.shape[0], head_count, head_dim)
    scores = (
        jnp.einsum("qhd,khd->qhk", query_heads, key_heads, preferred_element_type=jnp.float32)
        * scale_factor
    )
    raised = jnp.maximum(highest, jnp.max(scores, axis=-1))
    fade = jnp.exp(highest - raised)
    weights = jnp.exp(scores - raised[..., None])
    totals = totals * fade + jnp.sum(weights, axis=-1)
    accum = accum * fade[..., None] + jnp.einsum(
        "qhk,khd->qhd",
        weights.astype(jnp.bfloat16),
        value_heads,
        preferred_element_type=jnp.float32,
    )
    return (accum, totals, raised)


def gather_body(queries, keys_proj, values, hidden, fresh_latent, gate_table, noise_step, pattern):
    group_index = lax.axis_index("tm")
    final_index = lax.axis_size("tm") - 1
    query_tok, key_tok, value_tok = (
        lax.all_to_all(queries[0], "seq", split_axis=1, concat_axis=0, tiled=True),
        lax.all_to_all(keys_proj[0], "seq", split_axis=1, concat_axis=0, tiled=True),
        lax.all_to_all(values[0], "seq", split_axis=1, concat_axis=0, tiled=True),
    )
    row_count, local_width = query_tok.shape
    head_count = local_width // HD
    query_heads = query_tok.reshape(row_count, head_count, HD)
    scale_factor = 1.0 / math.sqrt(HD)
    reach = lax.dynamic_index_in_dim(pattern, group_index, 0, keepdims=False)
    start_state = (
        jnp.zeros((row_count, head_count, HD), jnp.float32),
        jnp.zeros((row_count, head_count), jnp.float32),
        jnp.full((row_count, head_count), -1e30, jnp.float32),
    )

    def one_block(current, inputs):
        key_block, value_block, flag = inputs
        return (
            lax.cond(
                flag > 0,
                lambda state: absorb(state, query_heads, key_block, value_block, scale_factor),
                lambda state: state,
                current,
            ),
            None,
        )

    key_piece = lax.all_gather(key_tok, "tm", axis=0, tiled=False)
    value_piece = lax.all_gather(value_tok, "tm", axis=0, tiled=False)
    state, unused = lax.scan(one_block, start_state, (key_piece, value_piece, reach))
    cache_keys, cache_values = shifted((key_tok, value_tok), "tm", -1)
    accum, totals, highest = state
    attended_head = (accum / totals[..., None]).reshape(row_count, local_width).astype(jnp.bfloat16)
    attended = lax.all_to_all(attended_head, "seq", split_axis=0, concat_axis=1, tiled=True)
    gate_row = lax.dynamic_index_in_dim(gate_table, noise_step[0], 0, keepdims=False)
    updated = (
        hidden[0].astype(jnp.float32) + gate_row[None, :] * attended.astype(jnp.float32)
    ).astype(jnp.bfloat16)
    moved = shifted(updated, "tm", -1)
    advanced = jnp.where(group_index == final_index, fresh_latent, moved)[None]
    next_cache = jnp.stack([cache_keys, cache_values], axis=0)[None]
    return (advanced, next_cache)


def body(queries, *others):
    tm_count, seq_count = lax.axis_size("tm"), lax.axis_size("seq")
    _, tok, width = queries.shape
    count = tm_count * seq_count
    even = width % (count * HD) == 0 and tok % 8 == 0 and seq_count % 4 == 0 and tm_count > 2 and tm_count % 2 == 0
    return (spread_body if even else gather_body)(queries, *others)


def solution(mesh):
    placed = (
        P("tm", "seq", None),
        P("tm", "seq", None),
        P("tm", "seq", None),
        P("tm", "seq", None),
        P("seq", None),
        P(),
        P("tm"),
        P(),
    )
    return jax.shard_map(
        body,
        mesh=mesh,
        in_specs=placed,
        out_specs=(P("tm", "seq", None), P("tm", None, None, "seq")),
        check_vma=False,
    )
```

```python
import functools
import math

import jax
import jax.numpy as jnp
from jax import lax
from jax.experimental import pallas as pl
from jax.experimental.pallas import tpu as pltpu
from jax.sharding import PartitionSpec as P

HD = 128
BOTH = ("tm", "seq")
VMEM = pltpu.VMEM
SMEM = pltpu.SMEM
HBM = pltpu.HBM


def shifted(block, axis, distance):
    devices = range(lax.axis_size(axis))
    route = [(i - distance, i) for i in devices if i - distance in devices]
    return lax.ppermute(block, axis, route)


def mixed(index, count):
    return (index + count // 2) % count


def out_order(tm_count, seq_count):
    ordered = sorted(range(seq_count), key=lambda index: mixed(index, seq_count))
    half = tm_count // 2
    return [
        (high * half + low, ordered[pair + member])
        for low in range(half)
        for pair in range(0, seq_count, 2)
        for high in range(tm_count // half)
        for member in range(2)
    ]


def back_order(tm_count, seq_count):
    ordered = sorted(range(seq_count), key=lambda index: mixed(index, seq_count))
    return [(tm, index) for tm in range(tm_count) for index in ordered]


def piece(group, pair, groups, pairs, step):
    half = groups // 2
    return ((group % half * pairs + pair) * (groups // half) + group // half) * step


def pack_kernel(seq_count, parts, q_hbm, k_hbm, v_hbm, out_hbm, held, block, in_sems, out_sems):
    tok, width = held.shape[1:]
    wide = out_hbm.shape[1] // 3
    count = out_hbm.shape[0] // tok
    tm_count = count // seq_count
    span, members = width // parts, seq_count // parts
    order = out_order(tm_count, seq_count)
    copies = []
    for part in range(parts):
        columns = slice(part * span, (part + 1) * span)
        for place, ref in enumerate((q_hbm, k_hbm, v_hbm)):
            copies.append(
                pltpu.make_async_copy(
                    ref.at[0, :, columns], held.at[place, :, columns], in_sems.at[part, place]
                )
            )
            copies[-1].start()
    outs = []
    for part in range(parts):
        for place in range(3):
            copies[3 * part + place].wait()
        for tm in range(tm_count):
            for seq in range(part * members, (part + 1) * members, 2):
                first = order.index((tm, seq)) * tok
                for place in range(3):
                    rows = []
                    for member in (seq, seq + 1):
                        start = (member * tm_count + tm) * wide
                        rows.append(held[place, :, start : start + wide].astype(jnp.float32))
                    block[first : first + 2 * tok, place * wide : (place + 1) * wide] = jnp.concatenate(
                        rows, axis=0
                    ).astype(jnp.bfloat16)
            first = order.index((tm, part * members)) * tok
            rows = slice(first, first + members * tok)
            outs.append(
                pltpu.make_async_copy(block.at[rows], out_hbm.at[rows], out_sems.at[part, tm])
            )
            outs[-1].start()
    for out in outs:
        out.wait()


def residual_kernel(noise_ref, h_ref, gate_hbm, after_ref, out_ref, held, sem):
    step = noise_ref[0]
    steps = gate_hbm.shape[0]
    whole_tiles = steps // 8 * 8
    first = step // 8 * 8

    @pl.when(step < whole_tiles)
    def take_tile():
        rows = pl.ds(pl.multiple_of(first, 8), 8)
        copy = pltpu.make_async_copy(gate_hbm.at[rows], held, sem)
        copy.start()
        copy.wait()

    if steps > whole_tiles:

        @pl.when(step >= whole_tiles)
        def take_rest():
            copy = pltpu.make_async_copy(
                gate_hbm.at[whole_tiles:steps], held.at[0 : steps - whole_tiles], sem
            )
            copy.start()
            copy.wait()

    gate = held[pl.ds(step - first, 1), :]
    high = gate.astype(jnp.bfloat16).astype(jnp.float32)
    middle = (gate - high).astype(jnp.bfloat16).astype(jnp.float32)
    low = gate - high - middle
    parts = jnp.concatenate([high, middle, low, jnp.zeros((5, gate.shape[1]), jnp.float32)], axis=0)
    out_ref[...] = jnp.concatenate([h_ref[0].astype(jnp.float32), parts], axis=0).astype(jnp.bfloat16)


def partner(here, distance, groups):
    return here ^ distance if groups & (groups - 1) == 0 else (here + groups - distance) % groups


def distances(groups):
    return range(groups - 1, 0, -1)


def hand_over(group, groups, seq_count, x_ref, out_ref, lanes=slice(None)):
    wide = x_ref.shape[1] // 3
    pairs = seq_count // 2
    step = out_ref.shape[1] // pairs
    for pair in range(pairs):
        first = pl.multiple_of(piece(group, mixed(2 * pair, seq_count) // 2, groups, pairs, step), step)
        for kind in range(2):
            out_ref[kind, pair * step : (pair + 1) * step, lanes] = x_ref[
                pl.ds(first, step), (kind + 1) * wide : (kind + 2) * wide
            ]


def attend_kernel(groups, seq_count, pattern_ref, x_ref, after_ref, out_hbm, *refs):
    *hand_refs, held, sems = refs
    wide = held.shape[1]
    rows = held.shape[0] // groups
    across = (groups - 1) * rows
    factor = math.log2(math.e) / math.sqrt(HD)
    here = lax.axis_index("tm")
    lane = lax.broadcasted_iota(jnp.int32, (1, across), 1)
    ends, kept = [], []
    for source in range(groups):
        first = max(source, 1)
        ends.append(min(across, -(-(groups - first) * rows // 128) * 128))
        chosen = jnp.zeros((1, across), jnp.int32)
        for group in range(first, groups):
            start = (groups - 1 - group) * rows
            flag = pattern_ref[group : group + 1, source : source + 1]
            chosen = jnp.where((lane >= start) & (lane < start + rows), flag, chosen)
        kept.append(chosen[:, : ends[-1]] > 0)

    pairs = seq_count // 2
    step = rows // pairs

    def take(group, first):
        starts = [piece(group, pair, groups, pairs, step) for pair in range(pairs)]
        return jnp.concatenate([x_ref[at : at + step, first : first + HD] for at in starts], axis=0)

    def keep(group, head, result):
        for place in (group - 1, groups - 1) if group == groups - 1 else (group - 1,):
            held[place * rows : (place + 1) * rows, head : head + HD] = result

    def spread(row, fill):
        rest = across - row.shape[1]
        return jnp.concatenate([row, jnp.full((1, rest), fill, row.dtype)], axis=1) if rest else row

    for head in range(0, wide, HD):
        query = jnp.concatenate(
            [take(group, head) for group in range(groups - 1, 0, -1)], axis=0
        )
        query = jnp.transpose(query)
        value = jnp.transpose(
            jnp.concatenate([take(group, 2 * wide + head) for group in range(groups)], axis=0)
        )
        scores, highest = [], None
        for source in range(groups):
            key = take(source, wide + head)
            scores.append(
                jnp.dot(key, query[:, : ends[source]], preferred_element_type=jnp.float32)
            )
            peak = jnp.where(kept[source], jnp.max(scores[-1], axis=0, keepdims=True), -1e30)
            peak = spread(peak, -1e30)
            highest = peak if highest is None else jnp.maximum(highest, peak)
        highest = highest * factor
        total, probs = 0.0, []
        for source in range(groups):
            offset = jnp.where(kept[source], -highest[:, : ends[source]], -1e30)
            raised = jnp.exp2(scores[source] * factor + offset)
            total += spread(jnp.sum(raised, axis=0, keepdims=True), 0.0)
            probs.append(raised.astype(jnp.bfloat16))
        inverse = 1.0 / total
        start, left, waiting = 0, None, groups - 1
        for source in range(groups - 1, 0, -1):
            stop = ends[source]
            if stop > start:
                numer = jnp.dot(
                    value[:, : (source + 1) * rows],
                    jnp.concatenate([p[:, start:stop] for p in probs[: source + 1]], axis=0),
                    preferred_element_type=jnp.float32,
                )
                result = jnp.transpose(numer * inverse[:, start:stop])
                left = result if left is None else jnp.concatenate([left, result], axis=0)
                start = stop
            while left is not None and left.shape[0] >= rows:
                keep(waiting, head, left[:rows].astype(jnp.bfloat16))
                left = left[rows:] if left.shape[0] > rows else None
                waiting -= 1
    copies = [
        pltpu.make_async_copy(
            held.at[place * rows : (place + 1) * rows], out_hbm.at[place * rows : (place + 1) * rows], sems.at[place]
        )
        for place in range(groups)
    ]
    for copy in copies:
        copy.start()
    for distance, hand_ref in zip(distances(groups), hand_refs):
        group = lax.rem(partner(here, distance, groups) + 1, groups)
        hand_over(group, groups, seq_count, x_ref, hand_ref)
    for copy in copies:
        copy.wait()


def lanes_of(distance, groups, here, wide):
    source = partner(here, groups - distance if groups & (groups - 1) else distance, groups)
    return pl.ds(pl.multiple_of(source * wide, wide), wide)


def cache_kernel(groups, seq_count, x_ref, hand_ref, out_ref):
    wide = x_ref.shape[1] // 3
    here = lax.axis_index("tm")
    out_ref[...] = jnp.zeros_like(out_ref)

    @pl.when(here < groups - 1)
    def place():
        hand_over(here + 1, groups, seq_count, x_ref, out_ref.at[0], lanes_of(0, groups, here, wide))
        out_ref[0, :, :, lanes_of(distances(groups)[0], groups, here, wide)] = hand_ref[...]


def cache_rest_kernel(groups, begun_hbm, after_ref, *refs):
    *hand_refs, out_hbm, sems = refs
    here = lax.axis_index("tm")

    @pl.when(here < groups - 1)
    def place():
        copies = [
            pltpu.make_async_copy(
                block, out_hbm.at[0, :, :, lanes_of(distance, groups, here, block.shape[2])], sems.at[index]
            )
            for index, (distance, block) in enumerate(zip(distances(groups)[1:], hand_refs))
        ]
        for copy in copies:
            copy.start()
        for copy in copies:
            copy.wait()


def update_kernel(seq_count, tm_count, att_ref, moved_ref, fresh_ref, after_ref, out_ref):
    tok = out_ref.shape[1]
    wide = att_ref.shape[1]
    count = att_ref.shape[0] // tok
    order = back_order(tm_count, seq_count)
    last = lax.axis_index("tm") == tm_count - 1

    @pl.when(last)
    def take_fresh():
        out_ref[0] = fresh_ref[...]

    @pl.when(jnp.logical_not(last))
    def take_update():
        for pair in range(count // 2):
            rows = att_ref[2 * pair * tok : 2 * (pair + 1) * tok, :].astype(jnp.float32)
            for half in range(2):
                source = 2 * pair + half
                start = (order[source][1] * tm_count + order[source][0]) * wide
                moved = moved_ref[:, start : start + wide].astype(jnp.float32)
                gate = (moved[tok : tok + 1] + moved[tok + 1 : tok + 2]) + moved[tok + 2 : tok + 3]
                result = moved[:tok] + gate * rows[half * tok : (half + 1) * tok]
                out_ref[0, :, start : start + wide] = result.astype(jnp.bfloat16)


def whole(space=VMEM):
    return pl.BlockSpec(memory_space=space)


def run(kernel, name, outs, specs, operands, flops=0, scratch=(), aliases={}):
    def size(a):
        return math.prod(a.shape) * jnp.dtype(a.dtype).itemsize

    moved = sum(map(size, operands)) + sum(map(size, outs))
    results = pl.pallas_call(
        kernel,
        out_shape=outs,
        in_specs=specs,
        out_specs=[whole(getattr(a, "memory_space", VMEM)) for a in outs],
        scratch_shapes=scratch,
        input_output_aliases=aliases,
        compiler_params=pltpu.CompilerParams(vmem_limit_bytes=4 * moved + (4 << 20)),
        cost_estimate=pl.CostEstimate(flops=flops, bytes_accessed=moved, transcendentals=0),
        name=name,
    )(*operands)
    return results if len(outs) > 1 else results[0]


def spread_body(queries, keys_proj, values, hidden, fresh_latent, gate_table, noise_step, pattern):
    tm_count, seq_count = lax.axis_size("tm"), lax.axis_size("seq")
    count = tm_count * seq_count
    _, tok, width = queries.shape
    wide = width // count
    group_tok = tok * seq_count
    kind = queries.dtype
    DMA = pltpu.SemaphoreType.DMA
    parts = seq_count // 2

    packed = run(
        functools.partial(pack_kernel, seq_count, parts),
        "pack",
        [HBM((count * tok, 3 * wide), kind)],
        [whole(HBM)] * 3,
        [pltpu.with_memory_space_constraint(a, HBM) for a in (queries, keys_proj, values)],
        scratch=[
            VMEM((3, tok, width), kind),
            VMEM((count * tok, 3 * wide), kind),
            DMA((parts, 3)),
            DMA((parts, tm_count)),
        ],
    )
    out, back = (
        [tm * seq_count + index for tm, index in order(tm_count, seq_count)]
        for order in (out_order, back_order)
    )
    exchange = functools.partial(
        lax.all_to_all, axis_name=BOTH, split_axis=0, concat_axis=0, tiled=True
    )
    exchanged = exchange(packed, axis_index_groups=[out])

    residual = run(
        residual_kernel,
        "residual",
        [VMEM((tok + 8, width), kind)],
        [whole(SMEM), whole(), whole(HBM), whole(HBM)],
        (
            noise_step,
            hidden,
            pltpu.with_memory_space_constraint(gate_table, HBM),
            pltpu.with_memory_space_constraint(packed, HBM),
        ),
        scratch=[VMEM((8, width), jnp.float32), DMA],
    )
    moved = shifted(residual, "tm", -1)

    attended, *hands = run(
        functools.partial(attend_kernel, tm_count, seq_count),
        "attend",
        [HBM((count * tok, wide), kind)] + [VMEM((2, group_tok, wide), kind)] * (tm_count - 1),
        [whole(), whole(), whole(pl.ANY)],
        (pattern, exchanged, moved),
        flops=2 * count * tok * count * tok * wide,
        scratch=[VMEM((count * tok, wide), kind), DMA((tm_count,))],
    )
    returned = exchange(attended, axis_index_groups=[back])
    handed = []
    for distance, hand in zip(distances(tm_count), hands):
        route = [(i, partner(i, distance, tm_count)) for i in range(tm_count)]
        handed.append(lax.ppermute(hand, "tm", [(i, j) for i, j in route if j < tm_count - 1]))

    first, *rest = handed
    begun = run(
        functools.partial(cache_kernel, tm_count, seq_count),
        "cache",
        [jax.ShapeDtypeStruct((1, 2, group_tok, tm_count * wide), kind)],
        [whole()] * 2,
        (exchanged, first),
    )
    begun = pltpu.with_memory_space_constraint(begun, HBM)
    advanced = run(
        functools.partial(update_kernel, seq_count, tm_count),
        "update",
        [jax.ShapeDtypeStruct((1, tok, width), kind)],
        [whole()] * 3 + [whole(HBM)],
        (returned, moved, fresh_latent, begun),
    )
    next_cache = run(
        functools.partial(cache_rest_kernel, tm_count),
        "cache_rest",
        [HBM(begun.shape, kind)],
        [whole(HBM)] * 2 + [whole()] * len(rest),
        (begun, pltpu.with_memory_space_constraint(advanced, HBM), *rest),
        scratch=[DMA((len(rest),))],
        aliases={0: 0},
    )
    return (advanced, next_cache)


def absorb(state, query_heads, key_piece, value_piece, scale_factor):
    accum, totals, highest = state
    row_count, head_count, head_dim = query_heads.shape
    key_heads = key_piece.reshape(key_piece.shape[0], head_count, head_dim)
    value_heads = value_piece.reshape(value_piece.shape[0], head_count, head_dim)
    scores = (
        jnp.einsum("qhd,khd->qhk", query_heads, key_heads, preferred_element_type=jnp.float32)
        * scale_factor
    )
    raised = jnp.maximum(highest, jnp.max(scores, axis=-1))
    fade = jnp.exp(highest - raised)
    weights = jnp.exp(scores - raised[..., None])
    totals = totals * fade + jnp.sum(weights, axis=-1)
    accum = accum * fade[..., None] + jnp.einsum(
        "qhk,khd->qhd",
        weights.astype(jnp.bfloat16),
        value_heads,
        preferred_element_type=jnp.float32,
    )
    return (accum, totals, raised)


def gather_body(queries, keys_proj, values, hidden, fresh_latent, gate_table, noise_step, pattern):
    group_index = lax.axis_index("tm")
    final_index = lax.axis_size("tm") - 1
    query_tok, key_tok, value_tok = (
        lax.all_to_all(queries[0], "seq", split_axis=1, concat_axis=0, tiled=True),
        lax.all_to_all(keys_proj[0], "seq", split_axis=1, concat_axis=0, tiled=True),
        lax.all_to_all(values[0], "seq", split_axis=1, concat_axis=0, tiled=True),
    )
    row_count, local_width = query_tok.shape
    head_count = local_width // HD
    query_heads = query_tok.reshape(row_count, head_count, HD)
    scale_factor = 1.0 / math.sqrt(HD)
    reach = lax.dynamic_index_in_dim(pattern, group_index, 0, keepdims=False)
    start_state = (
        jnp.zeros((row_count, head_count, HD), jnp.float32),
        jnp.zeros((row_count, head_count), jnp.float32),
        jnp.full((row_count, head_count), -1e30, jnp.float32),
    )

    def one_block(current, inputs):
        key_block, value_block, flag = inputs
        return (
            lax.cond(
                flag > 0,
                lambda state: absorb(state, query_heads, key_block, value_block, scale_factor),
                lambda state: state,
                current,
            ),
            None,
        )

    key_piece = lax.all_gather(key_tok, "tm", axis=0, tiled=False)
    value_piece = lax.all_gather(value_tok, "tm", axis=0, tiled=False)
    state, unused = lax.scan(one_block, start_state, (key_piece, value_piece, reach))
    cache_keys, cache_values = shifted((key_tok, value_tok), "tm", -1)
    accum, totals, highest = state
    attended_head = (accum / totals[..., None]).reshape(row_count, local_width).astype(jnp.bfloat16)
    attended = lax.all_to_all(attended_head, "seq", split_axis=0, concat_axis=1, tiled=True)
    gate_row = lax.dynamic_index_in_dim(gate_table, noise_step[0], 0, keepdims=False)
    updated = (
        hidden[0].astype(jnp.float32) + gate_row[None, :] * attended.astype(jnp.float32)
    ).astype(jnp.bfloat16)
    moved = shifted(updated, "tm", -1)
    advanced = jnp.where(group_index == final_index, fresh_latent, moved)[None]
    next_cache = jnp.stack([cache_keys, cache_values], axis=0)[None]
    return (advanced, next_cache)


def body(queries, *others):
    tm_count, seq_count = lax.axis_size("tm"), lax.axis_size("seq")
    _, tok, width = queries.shape
    count = tm_count * seq_count
    even = width % (count * HD) == 0 and tok % 8 == 0 and seq_count % 4 == 0 and tm_count > 2 and tm_count % 2 == 0
    return (spread_body if even else gather_body)(queries, *others)


def solution(mesh):
    placed = (
        P("tm", "seq", None),
        P("tm", "seq", None),
        P("tm", "seq", None),
        P("tm", "seq", None),
        P("seq", None),
        P(),
        P("tm"),
        P(),
    )
    return jax.shard_map(
        body,
        mesh=mesh,
        in_specs=placed,
        out_specs=(P("tm", "seq", None), P("tm", None, None, "seq")),
        check_vma=False,
    )
```

```python
import functools
import math

import jax
import jax.numpy as jnp
from jax import lax
from jax.experimental import pallas as pl
from jax.experimental.pallas import tpu as pltpu
from jax.sharding import PartitionSpec as P

HD = 128
BOTH = ("tm", "seq")
VMEM = pltpu.VMEM
SMEM = pltpu.SMEM
HBM = pltpu.HBM


def shifted(block, axis, distance):
    devices = range(lax.axis_size(axis))
    route = [(i - distance, i) for i in devices if i - distance in devices]
    return lax.ppermute(block, axis, route)


def mixed(index, count):
    return (index + count // 2) % count


def pack_kernel(seq_count, parts, q_hbm, k_hbm, v_hbm, out_hbm, held, block, in_sems, out_sems):
    tok, width = held.shape[1:]
    wide = out_hbm.shape[1] // 3
    count = out_hbm.shape[0] // tok
    tm_count = count // seq_count
    span, members = width // parts, seq_count // parts
    copies = []
    for part in range(parts):
        columns = slice(part * span, (part + 1) * span)
        for place, ref in enumerate((q_hbm, k_hbm, v_hbm)):
            copies.append(
                pltpu.make_async_copy(
                    ref.at[0, :, columns], held.at[place, :, columns], in_sems.at[part, place]
                )
            )
            copies[-1].start()
    outs = []
    for part in range(parts):
        for place in range(3):
            copies[3 * part + place].wait()
        for tm in range(tm_count):
            for seq in range(part * members, (part + 1) * members, 2):
                first = (tm * seq_count + mixed(seq, seq_count)) * tok
                for place in range(3):
                    rows = []
                    for member in (seq, seq + 1):
                        start = (member * tm_count + tm) * wide
                        rows.append(held[place, :, start : start + wide].astype(jnp.float32))
                    block[first : first + 2 * tok, place * wide : (place + 1) * wide] = jnp.concatenate(
                        rows, axis=0
                    ).astype(jnp.bfloat16)
            first = (tm * seq_count + mixed(part * members, seq_count)) * tok
            rows = slice(first, first + members * tok)
            outs.append(
                pltpu.make_async_copy(block.at[rows], out_hbm.at[rows], out_sems.at[part, tm])
            )
            outs[-1].start()
    for out in outs:
        out.wait()


def residual_kernel(noise_ref, h_ref, gate_hbm, after_ref, out_ref, held, sem):
    step = noise_ref[0]
    steps = gate_hbm.shape[0]
    whole_tiles = steps // 8 * 8
    first = step // 8 * 8

    @pl.when(step < whole_tiles)
    def take_tile():
        rows = pl.ds(pl.multiple_of(first, 8), 8)
        copy = pltpu.make_async_copy(gate_hbm.at[rows], held, sem)
        copy.start()
        copy.wait()

    if steps > whole_tiles:

        @pl.when(step >= whole_tiles)
        def take_rest():
            copy = pltpu.make_async_copy(
                gate_hbm.at[whole_tiles:steps], held.at[0 : steps - whole_tiles], sem
            )
            copy.start()
            copy.wait()

    gate = held[pl.ds(step - first, 1), :]
    high = gate.astype(jnp.bfloat16).astype(jnp.float32)
    middle = (gate - high).astype(jnp.bfloat16).astype(jnp.float32)
    low = gate - high - middle
    parts = jnp.concatenate([high, middle, low, jnp.zeros((5, gate.shape[1]), jnp.float32)], axis=0)
    out_ref[...] = jnp.concatenate([h_ref[0].astype(jnp.float32), parts], axis=0).astype(jnp.bfloat16)


def partner(here, distance, groups):
    return here ^ distance if groups & (groups - 1) == 0 else (here + groups - distance) % groups


def distances(groups):
    return sorted(range(1, groups), key=lambda distance: (distance < groups // 2, distance))


def hand_over(group, x_ref, out_ref, lanes=slice(None)):
    wide = x_ref.shape[1] // 3
    rows = out_ref.shape[1]
    half = rows // 2
    for part in range(2):
        first = pl.multiple_of(group * rows + mixed(part, 2) * half, half)
        for kind in range(2):
            out_ref[kind, part * half : (part + 1) * half, lanes] = x_ref[
                pl.ds(first, half), (kind + 1) * wide : (kind + 2) * wide
            ]


def attend_kernel(groups, pattern_ref, x_ref, after_ref, out_hbm, *refs):
    *hand_refs, held, sems = refs
    wide = held.shape[2]
    rows = held.shape[1]
    across = (groups - 1) * rows
    factor = math.log2(math.e) / math.sqrt(HD)
    here = lax.axis_index("tm")
    lane = lax.broadcasted_iota(jnp.int32, (1, across), 1)
    ends, kept = [], []
    for source in range(groups):
        first = max(source, 1)
        ends.append(min(across, -(-(groups - first) * rows // 128) * 128))
        chosen = jnp.zeros((1, across), jnp.int32)
        for group in range(first, groups):
            start = (groups - 1 - group) * rows
            flag = pattern_ref[group : group + 1, source : source + 1]
            chosen = jnp.where((lane >= start) & (lane < start + rows), flag, chosen)
        kept.append(chosen[:, : ends[-1]] > 0)

    copies = []

    def send(group):
        for place in (group - 1, groups - 1) if group == groups - 1 else (group - 1,):
            copies.append(
                pltpu.make_async_copy(
                    held.at[group - 1], out_hbm.at[place * rows : (place + 1) * rows], sems.at[place]
                )
            )
            copies[-1].start()

    def spread(row, fill):
        rest = across - row.shape[1]
        return jnp.concatenate([row, jnp.full((1, rest), fill, row.dtype)], axis=1) if rest else row

    for head in range(0, wide, HD):
        query = jnp.concatenate(
            [x_ref[group * rows : (group + 1) * rows, head : head + HD] for group in range(groups - 1, 0, -1)],
            axis=0,
        )
        query = jnp.transpose(query)
        value = jnp.transpose(x_ref[:, 2 * wide + head : 2 * wide + head + HD])
        scores, highest = [], None
        for source in range(groups):
            key = x_ref[source * rows : (source + 1) * rows, wide + head : wide + head + HD]
            scores.append(
                jnp.dot(key, query[:, : ends[source]], preferred_element_type=jnp.float32)
            )
            peak = jnp.where(kept[source], jnp.max(scores[-1], axis=0, keepdims=True), -1e30)
            peak = spread(peak, -1e30)
            highest = peak if highest is None else jnp.maximum(highest, peak)
        highest = highest * factor
        total, probs = 0.0, []
        for source in range(groups):
            offset = jnp.where(kept[source], -highest[:, : ends[source]], -1e30)
            raised = jnp.exp2(scores[source] * factor + offset)
            total += spread(jnp.sum(raised, axis=0, keepdims=True), 0.0)
            probs.append(raised.astype(jnp.bfloat16))
        inverse = 1.0 / total
        last = head + HD == wide
        start, left, waiting = 0, None, groups - 1
        for source in range(groups - 1, 0, -1):
            stop = ends[source]
            if stop > start:
                numer = jnp.dot(
                    value[:, : (source + 1) * rows],
                    jnp.concatenate([p[:, start:stop] for p in probs[: source + 1]], axis=0),
                    preferred_element_type=jnp.float32,
                )
                result = jnp.transpose(numer * inverse[:, start:stop])
                left = result if left is None else jnp.concatenate([left, result], axis=0)
                start = stop
            while left is not None and left.shape[0] >= rows:
                held[waiting - 1, :, head : head + HD] = left[:rows].astype(jnp.bfloat16)
                left = left[rows:] if left.shape[0] > rows else None
                if last:
                    send(waiting)
                waiting -= 1
    for distance, hand_ref in zip(distances(groups), hand_refs):
        hand_over(lax.rem(partner(here, distance, groups) + 1, groups), x_ref, hand_ref)
    for copy in copies:
        copy.wait()


def lanes_of(distance, groups, here, wide):
    source = partner(here, groups - distance if groups & (groups - 1) else distance, groups)
    return pl.ds(pl.multiple_of(source * wide, wide), wide)


def cache_kernel(groups, x_ref, hand_ref, out_ref):
    wide = x_ref.shape[1] // 3
    here = lax.axis_index("tm")
    out_ref[...] = jnp.zeros_like(out_ref)

    @pl.when(here < groups - 1)
    def place():
        hand_over(here + 1, x_ref, out_ref.at[0], lanes_of(0, groups, here, wide))
        out_ref[0, :, :, lanes_of(distances(groups)[0], groups, here, wide)] = hand_ref[...]


def cache_rest_kernel(groups, begun_hbm, after_ref, *refs):
    *hand_refs, out_hbm, sems = refs
    here = lax.axis_index("tm")

    @pl.when(here < groups - 1)
    def place():
        copies = [
            pltpu.make_async_copy(
                block, out_hbm.at[0, :, :, lanes_of(distance, groups, here, block.shape[2])], sems.at[index]
            )
            for index, (distance, block) in enumerate(zip(distances(groups)[1:], hand_refs))
        ]
        for copy in copies:
            copy.start()
        for copy in copies:
            copy.wait()


def update_kernel(seq_count, tm_count, att_ref, moved_ref, fresh_ref, after_ref, out_ref):
    tok = out_ref.shape[1]
    wide = att_ref.shape[1]
    count = att_ref.shape[0] // tok
    last = lax.axis_index("tm") == tm_count - 1

    @pl.when(last)
    def take_fresh():
        out_ref[0] = fresh_ref[...]

    @pl.when(jnp.logical_not(last))
    def take_update():
        for pair in range(count // 2):
            rows = att_ref[2 * pair * tok : 2 * (pair + 1) * tok, :].astype(jnp.float32)
            for half in range(2):
                source = 2 * pair + half
                start = (mixed(source % seq_count, seq_count) * tm_count + source // seq_count) * wide
                moved = moved_ref[:, start : start + wide].astype(jnp.float32)
                gate = (moved[tok : tok + 1] + moved[tok + 1 : tok + 2]) + moved[tok + 2 : tok + 3]
                result = moved[:tok] + gate * rows[half * tok : (half + 1) * tok]
                out_ref[0, :, start : start + wide] = result.astype(jnp.bfloat16)


def whole(space=VMEM):
    return pl.BlockSpec(memory_space=space)


def run(kernel, name, outs, specs, operands, flops=0, scratch=(), aliases={}):
    def size(a):
        return math.prod(a.shape) * jnp.dtype(a.dtype).itemsize

    moved = sum(map(size, operands)) + sum(map(size, outs))
    results = pl.pallas_call(
        kernel,
        out_shape=outs,
        in_specs=specs,
        out_specs=[whole(getattr(a, "memory_space", VMEM)) for a in outs],
        scratch_shapes=scratch,
        input_output_aliases=aliases,
        compiler_params=pltpu.CompilerParams(vmem_limit_bytes=4 * moved + (4 << 20)),
        cost_estimate=pl.CostEstimate(flops=flops, bytes_accessed=moved, transcendentals=0),
        name=name,
    )(*operands)
    return results if len(outs) > 1 else results[0]


def spread_body(queries, keys_proj, values, hidden, fresh_latent, gate_table, noise_step, pattern):
    tm_count, seq_count = lax.axis_size("tm"), lax.axis_size("seq")
    count = tm_count * seq_count
    _, tok, width = queries.shape
    wide = width // count
    group_tok = tok * seq_count
    kind = queries.dtype
    DMA = pltpu.SemaphoreType.DMA
    parts = 4 if seq_count % 8 == 0 else 2

    packed = run(
        functools.partial(pack_kernel, seq_count, parts),
        "pack",
        [HBM((count * tok, 3 * wide), kind)],
        [whole(HBM)] * 3,
        [pltpu.with_memory_space_constraint(a, HBM) for a in (queries, keys_proj, values)],
        scratch=[
            VMEM((3, tok, width), kind),
            VMEM((count * tok, 3 * wide), kind),
            DMA((parts, 3)),
            DMA((parts, tm_count)),
        ],
    )
    order = [tm * seq_count + mixed(s, seq_count) for tm in range(tm_count) for s in range(seq_count)]
    exchange = functools.partial(
        lax.all_to_all, axis_name=BOTH, split_axis=0, concat_axis=0, tiled=True, axis_index_groups=[order]
    )
    exchanged = exchange(packed)

    residual = run(
        residual_kernel,
        "residual",
        [VMEM((tok + 8, width), kind)],
        [whole(SMEM), whole(), whole(HBM), whole(HBM)],
        (
            noise_step,
            hidden,
            pltpu.with_memory_space_constraint(gate_table, HBM),
            pltpu.with_memory_space_constraint(packed, HBM),
        ),
        scratch=[VMEM((8, width), jnp.float32), DMA],
    )
    moved = shifted(residual, "tm", -1)

    attended, *hands = run(
        functools.partial(attend_kernel, tm_count),
        "attend",
        [HBM((count * tok, wide), kind)] + [VMEM((2, group_tok, wide), kind)] * (tm_count - 1),
        [whole(), whole(), whole(pl.ANY)],
        (pattern, exchanged, moved),
        flops=2 * count * tok * count * tok * wide,
        scratch=[VMEM((tm_count - 1, group_tok, wide), kind), DMA((tm_count,))],
    )
    returned = exchange(attended)
    handed = []
    for distance, hand in zip(distances(tm_count), hands):
        route = [(i, partner(i, distance, tm_count)) for i in range(tm_count)]
        handed.append(lax.ppermute(hand, "tm", [(i, j) for i, j in route if j < tm_count - 1]))

    first, *rest = handed
    begun = run(
        functools.partial(cache_kernel, tm_count),
        "cache",
        [jax.ShapeDtypeStruct((1, 2, group_tok, tm_count * wide), kind)],
        [whole()] * 2,
        (exchanged, first),
    )
    begun = pltpu.with_memory_space_constraint(begun, HBM)
    advanced = run(
        functools.partial(update_kernel, seq_count, tm_count),
        "update",
        [jax.ShapeDtypeStruct((1, tok, width), kind)],
        [whole()] * 3 + [whole(HBM)],
        (returned, moved, fresh_latent, begun),
    )
    next_cache = run(
        functools.partial(cache_rest_kernel, tm_count),
        "cache_rest",
        [HBM(begun.shape, kind)],
        [whole(HBM)] * 2 + [whole()] * len(rest),
        (begun, pltpu.with_memory_space_constraint(advanced, HBM), *rest),
        scratch=[DMA((len(rest),))],
        aliases={0: 0},
    )
    return (advanced, next_cache)


def absorb(state, query_heads, key_piece, value_piece, scale_factor):
    accum, totals, highest = state
    row_count, head_count, head_dim = query_heads.shape
    key_heads = key_piece.reshape(key_piece.shape[0], head_count, head_dim)
    value_heads = value_piece.reshape(value_piece.shape[0], head_count, head_dim)
    scores = (
        jnp.einsum("qhd,khd->qhk", query_heads, key_heads, preferred_element_type=jnp.float32)
        * scale_factor
    )
    raised = jnp.maximum(highest, jnp.max(scores, axis=-1))
    fade = jnp.exp(highest - raised)
    weights = jnp.exp(scores - raised[..., None])
    totals = totals * fade + jnp.sum(weights, axis=-1)
    accum = accum * fade[..., None] + jnp.einsum(
        "qhk,khd->qhd",
        weights.astype(jnp.bfloat16),
        value_heads,
        preferred_element_type=jnp.float32,
    )
    return (accum, totals, raised)


def gather_body(queries, keys_proj, values, hidden, fresh_latent, gate_table, noise_step, pattern):
    group_index = lax.axis_index("tm")
    final_index = lax.axis_size("tm") - 1
    query_tok, key_tok, value_tok = (
        lax.all_to_all(queries[0], "seq", split_axis=1, concat_axis=0, tiled=True),
        lax.all_to_all(keys_proj[0], "seq", split_axis=1, concat_axis=0, tiled=True),
        lax.all_to_all(values[0], "seq", split_axis=1, concat_axis=0, tiled=True),
    )
    row_count, local_width = query_tok.shape
    head_count = local_width // HD
    query_heads = query_tok.reshape(row_count, head_count, HD)
    scale_factor = 1.0 / math.sqrt(HD)
    reach = lax.dynamic_index_in_dim(pattern, group_index, 0, keepdims=False)
    start_state = (
        jnp.zeros((row_count, head_count, HD), jnp.float32),
        jnp.zeros((row_count, head_count), jnp.float32),
        jnp.full((row_count, head_count), -1e30, jnp.float32),
    )

    def one_block(current, inputs):
        key_block, value_block, flag = inputs
        return (
            lax.cond(
                flag > 0,
                lambda state: absorb(state, query_heads, key_block, value_block, scale_factor),
                lambda state: state,
                current,
            ),
            None,
        )

    key_piece = lax.all_gather(key_tok, "tm", axis=0, tiled=False)
    value_piece = lax.all_gather(value_tok, "tm", axis=0, tiled=False)
    state, unused = lax.scan(one_block, start_state, (key_piece, value_piece, reach))
    cache_keys, cache_values = shifted((key_tok, value_tok), "tm", -1)
    accum, totals, highest = state
    attended_head = (accum / totals[..., None]).reshape(row_count, local_width).astype(jnp.bfloat16)
    attended = lax.all_to_all(attended_head, "seq", split_axis=0, concat_axis=1, tiled=True)
    gate_row = lax.dynamic_index_in_dim(gate_table, noise_step[0], 0, keepdims=False)
    updated = (
        hidden[0].astype(jnp.float32) + gate_row[None, :] * attended.astype(jnp.float32)
    ).astype(jnp.bfloat16)
    moved = shifted(updated, "tm", -1)
    advanced = jnp.where(group_index == final_index, fresh_latent, moved)[None]
    next_cache = jnp.stack([cache_keys, cache_values], axis=0)[None]
    return (advanced, next_cache)


def body(queries, *others):
    tm_count, seq_count = lax.axis_size("tm"), lax.axis_size("seq")
    _, tok, width = queries.shape
    count = tm_count * seq_count
    even = width % (count * HD) == 0 and tok % 8 == 0 and seq_count % 4 == 0 and tm_count > 2
    return (spread_body if even else gather_body)(queries, *others)


def solution(mesh):
    placed = (
        P("tm", "seq", None),
        P("tm", "seq", None),
        P("tm", "seq", None),
        P("tm", "seq", None),
        P("seq", None),
        P(),
        P("tm"),
        P(),
    )
    return jax.shard_map(
        body,
        mesh=mesh,
        in_specs=placed,
        out_specs=(P("tm", "seq", None), P("tm", None, None, "seq")),
        check_vma=False,
    )
```

```python
import functools
import math

import jax
import jax.numpy as jnp
from jax import lax
from jax.experimental import pallas as pl
from jax.experimental.pallas import tpu as pltpu
from jax.sharding import PartitionSpec as P

HD = 128
BOTH = ("tm", "seq")
VMEM = pltpu.VMEM
SMEM = pltpu.SMEM
HBM = pltpu.HBM


def shifted(block, axis, distance):
    devices = range(lax.axis_size(axis))
    route = [(i - distance, i) for i in devices if i - distance in devices]
    return lax.ppermute(block, axis, route)


def mixed(index, count):
    return (index + count // 2) % count


def pack_kernel(seq_count, parts, q_hbm, k_hbm, v_hbm, out_hbm, held, block, in_sems, out_sems):
    tok, width = held.shape[1:]
    wide = out_hbm.shape[1] // 3
    count = out_hbm.shape[0] // tok
    tm_count = count // seq_count
    span, members = width // parts, seq_count // parts
    copies = []
    for part in range(parts):
        columns = slice(part * span, (part + 1) * span)
        for place, ref in enumerate((q_hbm, k_hbm, v_hbm)):
            copies.append(
                pltpu.make_async_copy(
                    ref.at[0, :, columns], held.at[place, :, columns], in_sems.at[part, place]
                )
            )
            copies[-1].start()
    outs = []
    for part in range(parts):
        for place in range(3):
            copies[3 * part + place].wait()
        for tm in range(tm_count):
            for seq in range(part * members, (part + 1) * members, 2):
                first = (tm * seq_count + mixed(seq, seq_count)) * tok
                for place in range(3):
                    rows = []
                    for member in (seq, seq + 1):
                        start = (member * tm_count + tm) * wide
                        rows.append(held[place, :, start : start + wide].astype(jnp.float32))
                    block[first : first + 2 * tok, place * wide : (place + 1) * wide] = jnp.concatenate(
                        rows, axis=0
                    ).astype(jnp.bfloat16)
            first = (tm * seq_count + mixed(part * members, seq_count)) * tok
            rows = slice(first, first + members * tok)
            outs.append(
                pltpu.make_async_copy(block.at[rows], out_hbm.at[rows], out_sems.at[part, tm])
            )
            outs[-1].start()
    for out in outs:
        out.wait()


def residual_kernel(noise_ref, h_ref, gate_hbm, after_ref, out_ref, held, sem):
    step = noise_ref[0]
    steps = gate_hbm.shape[0]
    whole_tiles = steps // 8 * 8
    first = step // 8 * 8

    @pl.when(step < whole_tiles)
    def take_tile():
        rows = pl.ds(pl.multiple_of(first, 8), 8)
        copy = pltpu.make_async_copy(gate_hbm.at[rows], held, sem)
        copy.start()
        copy.wait()

    if steps > whole_tiles:

        @pl.when(step >= whole_tiles)
        def take_rest():
            copy = pltpu.make_async_copy(
                gate_hbm.at[whole_tiles:steps], held.at[0 : steps - whole_tiles], sem
            )
            copy.start()
            copy.wait()

    gate = held[pl.ds(step - first, 1), :]
    high = gate.astype(jnp.bfloat16).astype(jnp.float32)
    middle = (gate - high).astype(jnp.bfloat16).astype(jnp.float32)
    low = gate - high - middle
    parts = jnp.concatenate([high, middle, low, jnp.zeros((5, gate.shape[1]), jnp.float32)], axis=0)
    out_ref[...] = jnp.concatenate([h_ref[0].astype(jnp.float32), parts], axis=0).astype(jnp.bfloat16)


def rounds(groups):
    half = groups // 2
    far, near = range(half, groups), range(1, half)
    upper, lower, every = range(half, groups), range(half), range(groups)
    plan = [(d, upper) for d in far] + [(d, every) for d in near] + [(d, lower) for d in far]
    return [(d, [(t, t ^ d) for t in senders if t ^ d < groups - 1]) for d, senders in plan]


def hand_over(group, x_ref, out_ref, lanes=slice(None)):
    wide = x_ref.shape[1] // 3
    rows = out_ref.shape[1]
    half = rows // 2
    for part in range(2):
        first = pl.multiple_of(group * rows + mixed(part, 2) * half, half)
        for kind in range(2):
            out_ref[kind, part * half : (part + 1) * half, lanes] = x_ref[
                pl.ds(first, half), (kind + 1) * wide : (kind + 2) * wide
            ]


def attend_kernel(groups, pattern_ref, x_ref, after_ref, out_hbm, *refs):
    *hand_refs, held, sems = refs
    wide = held.shape[2]
    rows = held.shape[1]
    across = (groups - 1) * rows
    factor = math.log2(math.e) / math.sqrt(HD)
    here = lax.axis_index("tm")
    lane = lax.broadcasted_iota(jnp.int32, (1, across), 1)
    ends, kept = [], []
    for source in range(groups):
        first = max(source, 1)
        ends.append(min(across, -(-(groups - first) * rows // 128) * 128))
        chosen = jnp.zeros((1, across), jnp.int32)
        for group in range(first, groups):
            start = (groups - 1 - group) * rows
            flag = pattern_ref[group : group + 1, source : source + 1]
            chosen = jnp.where((lane >= start) & (lane < start + rows), flag, chosen)
        kept.append(chosen[:, : ends[-1]] > 0)

    copies = []

    def send(group):
        for place in (group - 1, groups - 1) if group == groups - 1 else (group - 1,):
            copies.append(
                pltpu.make_async_copy(
                    held.at[group - 1], out_hbm.at[place * rows : (place + 1) * rows], sems.at[place]
                )
            )
            copies[-1].start()

    def spread(row, fill):
        rest = across - row.shape[1]
        return jnp.concatenate([row, jnp.full((1, rest), fill, row.dtype)], axis=1) if rest else row

    for head in range(0, wide, HD):
        query = jnp.concatenate(
            [x_ref[group * rows : (group + 1) * rows, head : head + HD] for group in range(groups - 1, 0, -1)],
            axis=0,
        )
        query = jnp.transpose(query)
        value = jnp.transpose(x_ref[:, 2 * wide + head : 2 * wide + head + HD])
        scores, highest = [], None
        for source in range(groups):
            key = x_ref[source * rows : (source + 1) * rows, wide + head : wide + head + HD]
            scores.append(
                jnp.dot(key, query[:, : ends[source]], preferred_element_type=jnp.float32)
            )
            peak = jnp.where(kept[source], jnp.max(scores[-1], axis=0, keepdims=True), -1e30)
            peak = spread(peak, -1e30)
            highest = peak if highest is None else jnp.maximum(highest, peak)
        highest = highest * factor
        total, probs = 0.0, []
        for source in range(groups):
            offset = jnp.where(kept[source], -highest[:, : ends[source]], -1e30)
            raised = jnp.exp2(scores[source] * factor + offset)
            total += spread(jnp.sum(raised, axis=0, keepdims=True), 0.0)
            probs.append(raised.astype(jnp.bfloat16))
        inverse = 1.0 / total
        last = head + HD == wide
        start, left, waiting = 0, None, groups - 1
        for source in range(groups - 1, 0, -1):
            stop = ends[source]
            if stop > start:
                numer = jnp.dot(
                    value[:, : (source + 1) * rows],
                    jnp.concatenate([p[:, start:stop] for p in probs[: source + 1]], axis=0),
                    preferred_element_type=jnp.float32,
                )
                result = jnp.transpose(numer * inverse[:, start:stop])
                left = result if left is None else jnp.concatenate([left, result], axis=0)
                start = stop
            while left is not None and left.shape[0] >= rows:
                held[waiting - 1, :, head : head + HD] = left[:rows].astype(jnp.bfloat16)
                left = left[rows:] if left.shape[0] > rows else None
                if last:
                    send(waiting)
                waiting -= 1
    for distance, hand_ref in enumerate(hand_refs, 1):
        hand_over(lax.rem((here ^ distance) + 1, groups), x_ref, hand_ref)
    for copy in copies:
        copy.wait()


def lanes_of(source, wide):
    return pl.ds(pl.multiple_of(source * wide, wide), wide)


def taking(here, sends):
    return functools.reduce(jnp.logical_or, [here == target for _, target in sends])


def cache_kernel(groups, x_ref, hand_ref, out_ref):
    wide = x_ref.shape[1] // 3
    here = lax.axis_index("tm")
    distance, sends = rounds(groups)[0]
    out_ref[...] = jnp.zeros_like(out_ref)

    @pl.when(here < groups - 1)
    def place_own():
        hand_over(here + 1, x_ref, out_ref.at[0], lanes_of(here, wide))

    @pl.when(taking(here, sends))
    def place_first():
        out_ref[0, :, :, lanes_of(here ^ distance, wide)] = hand_ref[...]


def cache_rest_kernel(groups, begun_hbm, after_ref, *refs):
    *hand_refs, out_hbm, sems = refs
    here = lax.axis_index("tm")
    copies = [
        (
            taking(here, sends),
            pltpu.make_async_copy(
                block, out_hbm.at[0, :, :, lanes_of(here ^ distance, block.shape[2])], sems.at[index]
            ),
        )
        for index, ((distance, sends), block) in enumerate(zip(rounds(groups)[1:], hand_refs))
    ]
    for taken, copy in copies:
        pl.when(taken)(copy.start)
    for taken, copy in copies:
        pl.when(taken)(copy.wait)


def update_kernel(seq_count, tm_count, att_ref, moved_ref, fresh_ref, after_ref, out_ref):
    tok = out_ref.shape[1]
    wide = att_ref.shape[1]
    count = att_ref.shape[0] // tok
    last = lax.axis_index("tm") == tm_count - 1

    @pl.when(last)
    def take_fresh():
        out_ref[0] = fresh_ref[...]

    @pl.when(jnp.logical_not(last))
    def take_update():
        for pair in range(count // 2):
            rows = att_ref[2 * pair * tok : 2 * (pair + 1) * tok, :].astype(jnp.float32)
            for half in range(2):
                source = 2 * pair + half
                start = (mixed(source % seq_count, seq_count) * tm_count + source // seq_count) * wide
                moved = moved_ref[:, start : start + wide].astype(jnp.float32)
                gate = (moved[tok : tok + 1] + moved[tok + 1 : tok + 2]) + moved[tok + 2 : tok + 3]
                result = moved[:tok] + gate * rows[half * tok : (half + 1) * tok]
                out_ref[0, :, start : start + wide] = result.astype(jnp.bfloat16)


def whole(space=VMEM):
    return pl.BlockSpec(memory_space=space)


def run(kernel, name, outs, specs, operands, flops=0, scratch=(), aliases={}):
    def size(a):
        return math.prod(a.shape) * jnp.dtype(a.dtype).itemsize

    moved = sum(map(size, operands)) + sum(map(size, outs))
    results = pl.pallas_call(
        kernel,
        out_shape=outs,
        in_specs=specs,
        out_specs=[whole(getattr(a, "memory_space", VMEM)) for a in outs],
        scratch_shapes=scratch,
        input_output_aliases=aliases,
        compiler_params=pltpu.CompilerParams(vmem_limit_bytes=4 * moved + (4 << 20)),
        cost_estimate=pl.CostEstimate(flops=flops, bytes_accessed=moved, transcendentals=0),
        name=name,
    )(*operands)
    return results if len(outs) > 1 else results[0]


def spread_body(queries, keys_proj, values, hidden, fresh_latent, gate_table, noise_step, pattern):
    tm_count, seq_count = lax.axis_size("tm"), lax.axis_size("seq")
    count = tm_count * seq_count
    _, tok, width = queries.shape
    wide = width // count
    group_tok = tok * seq_count
    kind = queries.dtype
    DMA = pltpu.SemaphoreType.DMA
    parts = 4 if seq_count % 8 == 0 else 2

    packed = run(
        functools.partial(pack_kernel, seq_count, parts),
        "pack",
        [HBM((count * tok, 3 * wide), kind)],
        [whole(HBM)] * 3,
        [pltpu.with_memory_space_constraint(a, HBM) for a in (queries, keys_proj, values)],
        scratch=[
            VMEM((3, tok, width), kind),
            VMEM((count * tok, 3 * wide), kind),
            DMA((parts, 3)),
            DMA((parts, tm_count)),
        ],
    )
    order = [tm * seq_count + mixed(s, seq_count) for tm in range(tm_count) for s in range(seq_count)]
    exchange = functools.partial(
        lax.all_to_all, axis_name=BOTH, split_axis=0, concat_axis=0, tiled=True, axis_index_groups=[order]
    )
    exchanged = exchange(packed)

    residual = run(
        residual_kernel,
        "residual",
        [VMEM((tok + 8, width), kind)],
        [whole(SMEM), whole(), whole(HBM), whole(HBM)],
        (
            noise_step,
            hidden,
            pltpu.with_memory_space_constraint(gate_table, HBM),
            pltpu.with_memory_space_constraint(packed, HBM),
        ),
        scratch=[VMEM((8, width), jnp.float32), DMA],
    )
    moved = shifted(residual, "tm", -1)

    attended, *hands = run(
        functools.partial(attend_kernel, tm_count),
        "attend",
        [HBM((count * tok, wide), kind)] + [VMEM((2, group_tok, wide), kind)] * (tm_count - 1),
        [whole(), whole(), whole(pl.ANY)],
        (pattern, exchanged, moved),
        flops=2 * count * tok * count * tok * wide,
        scratch=[VMEM((tm_count - 1, group_tok, wide), kind), DMA((tm_count,))],
    )
    returned = exchange(attended)
    handed = [lax.ppermute(hands[distance - 1], "tm", sends) for distance, sends in rounds(tm_count)]

    first, *rest = handed
    begun = run(
        functools.partial(cache_kernel, tm_count),
        "cache",
        [jax.ShapeDtypeStruct((1, 2, group_tok, tm_count * wide), kind)],
        [whole()] * 2,
        (exchanged, first),
    )
    begun = pltpu.with_memory_space_constraint(begun, HBM)
    advanced = run(
        functools.partial(update_kernel, seq_count, tm_count),
        "update",
        [jax.ShapeDtypeStruct((1, tok, width), kind)],
        [whole()] * 3 + [whole(HBM)],
        (returned, moved, fresh_latent, begun),
    )
    next_cache = run(
        functools.partial(cache_rest_kernel, tm_count),
        "cache_rest",
        [HBM(begun.shape, kind)],
        [whole(HBM)] * 2 + [whole()] * len(rest),
        (begun, pltpu.with_memory_space_constraint(advanced, HBM), *rest),
        scratch=[DMA((len(rest),))],
        aliases={0: 0},
    )
    return (advanced, next_cache)


def absorb(state, query_heads, key_piece, value_piece, scale_factor):
    accum, totals, highest = state
    row_count, head_count, head_dim = query_heads.shape
    key_heads = key_piece.reshape(key_piece.shape[0], head_count, head_dim)
    value_heads = value_piece.reshape(value_piece.shape[0], head_count, head_dim)
    scores = (
        jnp.einsum("qhd,khd->qhk", query_heads, key_heads, preferred_element_type=jnp.float32)
        * scale_factor
    )
    raised = jnp.maximum(highest, jnp.max(scores, axis=-1))
    fade = jnp.exp(highest - raised)
    weights = jnp.exp(scores - raised[..., None])
    totals = totals * fade + jnp.sum(weights, axis=-1)
    accum = accum * fade[..., None] + jnp.einsum(
        "qhk,khd->qhd",
        weights.astype(jnp.bfloat16),
        value_heads,
        preferred_element_type=jnp.float32,
    )
    return (accum, totals, raised)


def gather_body(queries, keys_proj, values, hidden, fresh_latent, gate_table, noise_step, pattern):
    group_index = lax.axis_index("tm")
    final_index = lax.axis_size("tm") - 1
    query_tok, key_tok, value_tok = (
        lax.all_to_all(queries[0], "seq", split_axis=1, concat_axis=0, tiled=True),
        lax.all_to_all(keys_proj[0], "seq", split_axis=1, concat_axis=0, tiled=True),
        lax.all_to_all(values[0], "seq", split_axis=1, concat_axis=0, tiled=True),
    )
    row_count, local_width = query_tok.shape
    head_count = local_width // HD
    query_heads = query_tok.reshape(row_count, head_count, HD)
    scale_factor = 1.0 / math.sqrt(HD)
    reach = lax.dynamic_index_in_dim(pattern, group_index, 0, keepdims=False)
    start_state = (
        jnp.zeros((row_count, head_count, HD), jnp.float32),
        jnp.zeros((row_count, head_count), jnp.float32),
        jnp.full((row_count, head_count), -1e30, jnp.float32),
    )

    def one_block(current, inputs):
        key_block, value_block, flag = inputs
        return (
            lax.cond(
                flag > 0,
                lambda state: absorb(state, query_heads, key_block, value_block, scale_factor),
                lambda state: state,
                current,
            ),
            None,
        )

    key_piece = lax.all_gather(key_tok, "tm", axis=0, tiled=False)
    value_piece = lax.all_gather(value_tok, "tm", axis=0, tiled=False)
    state, unused = lax.scan(one_block, start_state, (key_piece, value_piece, reach))
    cache_keys, cache_values = shifted((key_tok, value_tok), "tm", -1)
    accum, totals, highest = state
    attended_head = (accum / totals[..., None]).reshape(row_count, local_width).astype(jnp.bfloat16)
    attended = lax.all_to_all(attended_head, "seq", split_axis=0, concat_axis=1, tiled=True)
    gate_row = lax.dynamic_index_in_dim(gate_table, noise_step[0], 0, keepdims=False)
    updated = (
        hidden[0].astype(jnp.float32) + gate_row[None, :] * attended.astype(jnp.float32)
    ).astype(jnp.bfloat16)
    moved = shifted(updated, "tm", -1)
    advanced = jnp.where(group_index == final_index, fresh_latent, moved)[None]
    next_cache = jnp.stack([cache_keys, cache_values], axis=0)[None]
    return (advanced, next_cache)


def body(queries, *others):
    tm_count, seq_count = lax.axis_size("tm"), lax.axis_size("seq")
    _, tok, width = queries.shape
    count = tm_count * seq_count
    even = width % (count * HD) == 0 and tok % 8 == 0 and seq_count % 4 == 0 and tm_count > 2 and tm_count & (tm_count - 1) == 0
    return (spread_body if even else gather_body)(queries, *others)


def solution(mesh):
    placed = (
        P("tm", "seq", None),
        P("tm", "seq", None),
        P("tm", "seq", None),
        P("tm", "seq", None),
        P("seq", None),
        P(),
        P("tm"),
        P(),
    )
    return jax.shard_map(
        body,
        mesh=mesh,
        in_specs=placed,
        out_specs=(P("tm", "seq", None), P("tm", None, None, "seq")),
        check_vma=False,
    )
```

```python
import functools
import math

import jax
import jax.numpy as jnp
from jax import lax
from jax.experimental import pallas as pl
from jax.experimental.pallas import tpu as pltpu
from jax.sharding import PartitionSpec as P

HD = 128
BOTH = ("tm", "seq")
VMEM = pltpu.VMEM
SMEM = pltpu.SMEM
HBM = pltpu.HBM


def shifted(block, axis, distance):
    devices = range(lax.axis_size(axis))
    route = [(i - distance, i) for i in devices if i - distance in devices]
    return lax.ppermute(block, axis, route)


def mixed(index, count):
    return (index + count // 2) % count


def pack_kernel(seq_count, parts, q_hbm, k_hbm, v_hbm, out_hbm, held, block, in_sems, out_sems):
    tok, width = held.shape[1:]
    wide = out_hbm.shape[1] // 3
    count = out_hbm.shape[0] // tok
    tm_count = count // seq_count
    span, members = width // parts, seq_count // parts
    copies = []
    for part in range(parts):
        columns = slice(part * span, (part + 1) * span)
        for place, ref in enumerate((q_hbm, k_hbm, v_hbm)):
            copies.append(
                pltpu.make_async_copy(
                    ref.at[0, :, columns], held.at[place, :, columns], in_sems.at[part, place]
                )
            )
            copies[-1].start(priority=(len(copies) - 1) % 2)
    outs = []
    for part in range(parts):
        for place in range(3):
            copies[3 * part + place].wait()
        for tm in range(tm_count):
            for seq in range(part * members, (part + 1) * members, 2):
                first = (tm * seq_count + mixed(seq, seq_count)) * tok
                for place in range(3):
                    rows = []
                    for member in (seq, seq + 1):
                        start = (member * tm_count + tm) * wide
                        rows.append(held[place, :, start : start + wide].astype(jnp.float32))
                    block[first : first + 2 * tok, place * wide : (place + 1) * wide] = jnp.concatenate(
                        rows, axis=0
                    ).astype(jnp.bfloat16)
            first = (tm * seq_count + mixed(part * members, seq_count)) * tok
            rows = slice(first, first + members * tok)
            outs.append(
                pltpu.make_async_copy(block.at[rows], out_hbm.at[rows], out_sems.at[part, tm])
            )
            outs[-1].start(priority=(len(outs) - 1) % 2)
    for out in outs:
        out.wait()


def residual_kernel(noise_ref, h_ref, gate_hbm, after_ref, out_ref, held, sem):
    step = noise_ref[0]
    steps = gate_hbm.shape[0]
    whole_tiles = steps // 8 * 8
    first = step // 8 * 8

    @pl.when(step < whole_tiles)
    def take_tile():
        rows = pl.ds(pl.multiple_of(first, 8), 8)
        copy = pltpu.make_async_copy(gate_hbm.at[rows], held, sem)
        copy.start()
        copy.wait()

    if steps > whole_tiles:

        @pl.when(step >= whole_tiles)
        def take_rest():
            copy = pltpu.make_async_copy(
                gate_hbm.at[whole_tiles:steps], held.at[0 : steps - whole_tiles], sem
            )
            copy.start()
            copy.wait()

    gate = held[pl.ds(step - first, 1), :]
    high = gate.astype(jnp.bfloat16).astype(jnp.float32)
    middle = (gate - high).astype(jnp.bfloat16).astype(jnp.float32)
    low = gate - high - middle
    parts = jnp.concatenate([high, middle, low, jnp.zeros((5, gate.shape[1]), jnp.float32)], axis=0)
    out_ref[...] = jnp.concatenate([h_ref[0].astype(jnp.float32), parts], axis=0).astype(jnp.bfloat16)


def partner(here, distance, groups):
    return here ^ distance if groups & (groups - 1) == 0 else (here + groups - distance) % groups


def distances(groups):
    return range(groups - 1, 0, -1)


def hand_over(group, x_ref, out_ref, lanes=slice(None)):
    wide = x_ref.shape[1] // 3
    rows = out_ref.shape[1]
    half = rows // 2
    for part in range(2):
        first = pl.multiple_of(group * rows + mixed(part, 2) * half, half)
        for kind in range(2):
            out_ref[kind, part * half : (part + 1) * half, lanes] = x_ref[
                pl.ds(first, half), (kind + 1) * wide : (kind + 2) * wide
            ]


def attend_kernel(groups, pattern_ref, x_ref, after_ref, out_hbm, *refs):
    *hand_refs, held, sems = refs
    wide = held.shape[2]
    rows = held.shape[1]
    across = (groups - 1) * rows
    factor = math.log2(math.e) / math.sqrt(HD)
    here = lax.axis_index("tm")
    lane = lax.broadcasted_iota(jnp.int32, (1, across), 1)
    ends, kept = [], []
    for source in range(groups):
        first = max(source, 1)
        ends.append(min(across, -(-(groups - first) * rows // 128) * 128))
        chosen = jnp.zeros((1, across), jnp.int32)
        for group in range(first, groups):
            start = (groups - 1 - group) * rows
            flag = pattern_ref[group : group + 1, source : source + 1]
            chosen = jnp.where((lane >= start) & (lane < start + rows), flag, chosen)
        kept.append(chosen[:, : ends[-1]] > 0)

    copies = []

    def send(group):
        for place in (group - 1, groups - 1) if group == groups - 1 else (group - 1,):
            copies.append(
                pltpu.make_async_copy(
                    held.at[group - 1], out_hbm.at[place * rows : (place + 1) * rows], sems.at[place]
                )
            )
            copies[-1].start(priority=place % 2)

    def spread(row, fill):
        rest = across - row.shape[1]
        return jnp.concatenate([row, jnp.full((1, rest), fill, row.dtype)], axis=1) if rest else row

    for head in range(0, wide, HD):
        query = jnp.concatenate(
            [x_ref[group * rows : (group + 1) * rows, head : head + HD] for group in range(groups - 1, 0, -1)],
            axis=0,
        )
        query = jnp.transpose(query)
        value = jnp.transpose(x_ref[:, 2 * wide + head : 2 * wide + head + HD])
        scores, highest = [], None
        for source in range(groups):
            key = x_ref[source * rows : (source + 1) * rows, wide + head : wide + head + HD]
            scores.append(
                jnp.dot(key, query[:, : ends[source]], preferred_element_type=jnp.float32)
            )
            peak = jnp.where(kept[source], jnp.max(scores[-1], axis=0, keepdims=True), -1e30)
            peak = spread(peak, -1e30)
            highest = peak if highest is None else jnp.maximum(highest, peak)
        highest = highest * factor
        total, probs = 0.0, []
        for source in range(groups):
            offset = jnp.where(kept[source], -highest[:, : ends[source]], -1e30)
            raised = jnp.exp2(scores[source] * factor + offset)
            total += spread(jnp.sum(raised, axis=0, keepdims=True), 0.0)
            probs.append(raised.astype(jnp.bfloat16))
        inverse = 1.0 / total
        last = head + HD == wide
        start, left, waiting = 0, None, groups - 1
        for source in range(groups - 1, 0, -1):
            stop = ends[source]
            if stop > start:
                numer = jnp.dot(
                    value[:, : (source + 1) * rows],
                    jnp.concatenate([p[:, start:stop] for p in probs[: source + 1]], axis=0),
                    preferred_element_type=jnp.float32,
                )
                result = jnp.transpose(numer * inverse[:, start:stop])
                left = result if left is None else jnp.concatenate([left, result], axis=0)
                start = stop
            while left is not None and left.shape[0] >= rows:
                held[waiting - 1, :, head : head + HD] = left[:rows].astype(jnp.bfloat16)
                left = left[rows:] if left.shape[0] > rows else None
                if last:
                    send(waiting)
                waiting -= 1
    for distance, hand_ref in zip(distances(groups), hand_refs):
        hand_over(lax.rem(partner(here, distance, groups) + 1, groups), x_ref, hand_ref)
    for copy in copies:
        copy.wait()


def lanes_of(distance, groups, here, wide):
    source = partner(here, groups - distance if groups & (groups - 1) else distance, groups)
    return pl.ds(pl.multiple_of(source * wide, wide), wide)


def cache_kernel(groups, x_ref, hand_ref, out_ref):
    wide = x_ref.shape[1] // 3
    here = lax.axis_index("tm")
    out_ref[...] = jnp.zeros_like(out_ref)

    @pl.when(here < groups - 1)
    def place():
        hand_over(here + 1, x_ref, out_ref.at[0], lanes_of(0, groups, here, wide))
        out_ref[0, :, :, lanes_of(distances(groups)[0], groups, here, wide)] = hand_ref[...]


def cache_rest_kernel(groups, begun_hbm, after_ref, *refs):
    *hand_refs, out_hbm, sems = refs
    here = lax.axis_index("tm")

    @pl.when(here < groups - 1)
    def place():
        copies = [
            pltpu.make_async_copy(
                block, out_hbm.at[0, :, :, lanes_of(distance, groups, here, block.shape[2])], sems.at[index]
            )
            for index, (distance, block) in enumerate(zip(distances(groups)[1:], hand_refs))
        ]
        for index, copy in enumerate(copies):
            copy.start(priority=index % 2)
        for copy in copies:
            copy.wait()


def update_kernel(seq_count, tm_count, att_ref, moved_ref, fresh_ref, after_ref, out_ref):
    tok = out_ref.shape[1]
    wide = att_ref.shape[1]
    count = att_ref.shape[0] // tok
    last = lax.axis_index("tm") == tm_count - 1

    @pl.when(last)
    def take_fresh():
        out_ref[0] = fresh_ref[...]

    @pl.when(jnp.logical_not(last))
    def take_update():
        for pair in range(count // 2):
            rows = att_ref[2 * pair * tok : 2 * (pair + 1) * tok, :].astype(jnp.float32)
            for half in range(2):
                source = 2 * pair + half
                start = (mixed(source % seq_count, seq_count) * tm_count + source // seq_count) * wide
                moved = moved_ref[:, start : start + wide].astype(jnp.float32)
                gate = (moved[tok : tok + 1] + moved[tok + 1 : tok + 2]) + moved[tok + 2 : tok + 3]
                result = moved[:tok] + gate * rows[half * tok : (half + 1) * tok]
                out_ref[0, :, start : start + wide] = result.astype(jnp.bfloat16)


def whole(space=VMEM):
    return pl.BlockSpec(memory_space=space)


def run(kernel, name, outs, specs, operands, flops=0, scratch=(), aliases={}):
    def size(a):
        return math.prod(a.shape) * jnp.dtype(a.dtype).itemsize

    moved = sum(map(size, operands)) + sum(map(size, outs))
    results = pl.pallas_call(
        kernel,
        out_shape=outs,
        in_specs=specs,
        out_specs=[whole(getattr(a, "memory_space", VMEM)) for a in outs],
        scratch_shapes=scratch,
        input_output_aliases=aliases,
        compiler_params=pltpu.CompilerParams(vmem_limit_bytes=4 * moved + (4 << 20)),
        cost_estimate=pl.CostEstimate(flops=flops, bytes_accessed=moved, transcendentals=0),
        name=name,
    )(*operands)
    return results if len(outs) > 1 else results[0]


def spread_body(queries, keys_proj, values, hidden, fresh_latent, gate_table, noise_step, pattern):
    tm_count, seq_count = lax.axis_size("tm"), lax.axis_size("seq")
    count = tm_count * seq_count
    _, tok, width = queries.shape
    wide = width // count
    group_tok = tok * seq_count
    kind = queries.dtype
    DMA = pltpu.SemaphoreType.DMA
    parts = 4 if seq_count % 8 == 0 else 2

    packed = run(
        functools.partial(pack_kernel, seq_count, parts),
        "pack",
        [HBM((count * tok, 3 * wide), kind)],
        [whole(HBM)] * 3,
        [pltpu.with_memory_space_constraint(a, HBM) for a in (queries, keys_proj, values)],
        scratch=[
            VMEM((3, tok, width), kind),
            VMEM((count * tok, 3 * wide), kind),
            DMA((parts, 3)),
            DMA((parts, tm_count)),
        ],
    )
    order = [tm * seq_count + mixed(s, seq_count) for tm in range(tm_count) for s in range(seq_count)]
    exchange = functools.partial(
        lax.all_to_all, axis_name=BOTH, split_axis=0, concat_axis=0, tiled=True, axis_index_groups=[order]
    )
    exchanged = exchange(packed)

    residual = run(
        residual_kernel,
        "residual",
        [VMEM((tok + 8, width), kind)],
        [whole(SMEM), whole(), whole(HBM), whole(HBM)],
        (
            noise_step,
            hidden,
            pltpu.with_memory_space_constraint(gate_table, HBM),
            pltpu.with_memory_space_constraint(packed, HBM),
        ),
        scratch=[VMEM((8, width), jnp.float32), DMA],
    )
    moved = shifted(residual, "tm", -1)

    attended, *hands = run(
        functools.partial(attend_kernel, tm_count),
        "attend",
        [HBM((count * tok, wide), kind)] + [VMEM((2, group_tok, wide), kind)] * (tm_count - 1),
        [whole(), whole(), whole(pl.ANY)],
        (pattern, exchanged, moved),
        flops=2 * count * tok * count * tok * wide,
        scratch=[VMEM((tm_count - 1, group_tok, wide), kind), DMA((tm_count,))],
    )
    returned = exchange(attended)
    handed = []
    for distance, hand in zip(distances(tm_count), hands):
        route = [(i, partner(i, distance, tm_count)) for i in range(tm_count)]
        handed.append(lax.ppermute(hand, "tm", [(i, j) for i, j in route if j < tm_count - 1]))

    first, *rest = handed
    begun = run(
        functools.partial(cache_kernel, tm_count),
        "cache",
        [jax.ShapeDtypeStruct((1, 2, group_tok, tm_count * wide), kind)],
        [whole()] * 2,
        (exchanged, first),
    )
    begun = pltpu.with_memory_space_constraint(begun, HBM)
    advanced = run(
        functools.partial(update_kernel, seq_count, tm_count),
        "update",
        [jax.ShapeDtypeStruct((1, tok, width), kind)],
        [whole()] * 3 + [whole(HBM)],
        (returned, moved, fresh_latent, begun),
    )
    next_cache = run(
        functools.partial(cache_rest_kernel, tm_count),
        "cache_rest",
        [HBM(begun.shape, kind)],
        [whole(HBM)] * 2 + [whole()] * len(rest),
        (begun, pltpu.with_memory_space_constraint(advanced, HBM), *rest),
        scratch=[DMA((len(rest),))],
        aliases={0: 0},
    )
    return (advanced, next_cache)


def absorb(state, query_heads, key_piece, value_piece, scale_factor):
    accum, totals, highest = state
    row_count, head_count, head_dim = query_heads.shape
    key_heads = key_piece.reshape(key_piece.shape[0], head_count, head_dim)
    value_heads = value_piece.reshape(value_piece.shape[0], head_count, head_dim)
    scores = (
        jnp.einsum("qhd,khd->qhk", query_heads, key_heads, preferred_element_type=jnp.float32)
        * scale_factor
    )
    raised = jnp.maximum(highest, jnp.max(scores, axis=-1))
    fade = jnp.exp(highest - raised)
    weights = jnp.exp(scores - raised[..., None])
    totals = totals * fade + jnp.sum(weights, axis=-1)
    accum = accum * fade[..., None] + jnp.einsum(
        "qhk,khd->qhd",
        weights.astype(jnp.bfloat16),
        value_heads,
        preferred_element_type=jnp.float32,
    )
    return (accum, totals, raised)


def gather_body(queries, keys_proj, values, hidden, fresh_latent, gate_table, noise_step, pattern):
    group_index = lax.axis_index("tm")
    final_index = lax.axis_size("tm") - 1
    query_tok, key_tok, value_tok = (
        lax.all_to_all(queries[0], "seq", split_axis=1, concat_axis=0, tiled=True),
        lax.all_to_all(keys_proj[0], "seq", split_axis=1, concat_axis=0, tiled=True),
        lax.all_to_all(values[0], "seq", split_axis=1, concat_axis=0, tiled=True),
    )
    row_count, local_width = query_tok.shape
    head_count = local_width // HD
    query_heads = query_tok.reshape(row_count, head_count, HD)
    scale_factor = 1.0 / math.sqrt(HD)
    reach = lax.dynamic_index_in_dim(pattern, group_index, 0, keepdims=False)
    start_state = (
        jnp.zeros((row_count, head_count, HD), jnp.float32),
        jnp.zeros((row_count, head_count), jnp.float32),
        jnp.full((row_count, head_count), -1e30, jnp.float32),
    )

    def one_block(current, inputs):
        key_block, value_block, flag = inputs
        return (
            lax.cond(
                flag > 0,
                lambda state: absorb(state, query_heads, key_block, value_block, scale_factor),
                lambda state: state,
                current,
            ),
            None,
        )

    key_piece = lax.all_gather(key_tok, "tm", axis=0, tiled=False)
    value_piece = lax.all_gather(value_tok, "tm", axis=0, tiled=False)
    state, unused = lax.scan(one_block, start_state, (key_piece, value_piece, reach))
    cache_keys, cache_values = shifted((key_tok, value_tok), "tm", -1)
    accum, totals, highest = state
    attended_head = (accum / totals[..., None]).reshape(row_count, local_width).astype(jnp.bfloat16)
    attended = lax.all_to_all(attended_head, "seq", split_axis=0, concat_axis=1, tiled=True)
    gate_row = lax.dynamic_index_in_dim(gate_table, noise_step[0], 0, keepdims=False)
    updated = (
        hidden[0].astype(jnp.float32) + gate_row[None, :] * attended.astype(jnp.float32)
    ).astype(jnp.bfloat16)
    moved = shifted(updated, "tm", -1)
    advanced = jnp.where(group_index == final_index, fresh_latent, moved)[None]
    next_cache = jnp.stack([cache_keys, cache_values], axis=0)[None]
    return (advanced, next_cache)


def body(queries, *others):
    tm_count, seq_count = lax.axis_size("tm"), lax.axis_size("seq")
    _, tok, width = queries.shape
    count = tm_count * seq_count
    even = width % (count * HD) == 0 and tok % 8 == 0 and seq_count % 4 == 0 and tm_count > 2
    return (spread_body if even else gather_body)(queries, *others)


def solution(mesh):
    placed = (
        P("tm", "seq", None),
        P("tm", "seq", None),
        P("tm", "seq", None),
        P("tm", "seq", None),
        P("seq", None),
        P(),
        P("tm"),
        P(),
    )
    return jax.shard_map(
        body,
        mesh=mesh,
        in_specs=placed,
        out_specs=(P("tm", "seq", None), P("tm", None, None, "seq")),
        check_vma=False,
    )
```

```python
import functools
import math

import jax
import jax.numpy as jnp
from jax import lax
from jax.experimental import pallas as pl
from jax.experimental.pallas import tpu as pltpu
from jax.sharding import PartitionSpec as P

HD = 128
BOTH = ("tm", "seq")
VMEM = pltpu.VMEM
SMEM = pltpu.SMEM
HBM = pltpu.HBM


def shifted(block, axis, distance):
    devices = range(lax.axis_size(axis))
    route = [(i - distance, i) for i in devices if i - distance in devices]
    return lax.ppermute(block, axis, route)


def mixed(index, count):
    return (index + count // 2) % count


def pack_kernel(seq_count, parts, k_hbm, v_hbm, q_hbm, kv_hbm, out_hbm, held, kv_block, q_block, in_sems, out_sems):
    tok, width = held.shape[1:]
    wide = out_hbm.shape[1]
    count = out_hbm.shape[0] // tok
    tm_count = count // seq_count
    span, members = width // parts, seq_count // parts
    copies = []
    for part in range(parts):
        columns = slice(part * span, (part + 1) * span)
        for place, ref in enumerate((k_hbm, v_hbm, q_hbm)):
            copies.append(
                pltpu.make_async_copy(
                    ref.at[0, :, columns], held.at[place, :, columns], in_sems.at[part, place]
                )
            )
            copies[-1].start()
    outs = []
    for part in range(parts):
        for place in range(3):
            copies[3 * part + place].wait()
        for tm in range(tm_count):
            for seq in range(part * members, (part + 1) * members, 2):
                first = (tm * seq_count + mixed(seq, seq_count)) * tok
                for place, (block, lane) in enumerate(((kv_block, 0), (kv_block, wide), (q_block, 0))):
                    rows = []
                    for member in (seq, seq + 1):
                        start = (member * tm_count + tm) * wide
                        rows.append(held[place, :, start : start + wide].astype(jnp.float32))
                    block[first : first + 2 * tok, lane : lane + wide] = jnp.concatenate(
                        rows, axis=0
                    ).astype(jnp.bfloat16)
            first = (tm * seq_count + mixed(part * members, seq_count)) * tok
            rows = slice(first, first + members * tok)
            for index, (block, to) in enumerate(((kv_block, kv_hbm), (q_block, out_hbm))):
                outs.append(
                    pltpu.make_async_copy(block.at[rows], to.at[rows], out_sems.at[part, tm, index])
                )
                outs[-1].start()
    for out in outs:
        out.wait()


def residual_kernel(noise_ref, h_ref, gate_hbm, after_ref, out_ref, held, sem):
    step = noise_ref[0]
    steps = gate_hbm.shape[0]
    whole_tiles = steps // 8 * 8
    first = step // 8 * 8

    @pl.when(step < whole_tiles)
    def take_tile():
        rows = pl.ds(pl.multiple_of(first, 8), 8)
        copy = pltpu.make_async_copy(gate_hbm.at[rows], held, sem)
        copy.start()
        copy.wait()

    if steps > whole_tiles:

        @pl.when(step >= whole_tiles)
        def take_rest():
            copy = pltpu.make_async_copy(
                gate_hbm.at[whole_tiles:steps], held.at[0 : steps - whole_tiles], sem
            )
            copy.start()
            copy.wait()

    gate = held[pl.ds(step - first, 1), :]
    high = gate.astype(jnp.bfloat16).astype(jnp.float32)
    middle = (gate - high).astype(jnp.bfloat16).astype(jnp.float32)
    low = gate - high - middle
    parts = jnp.concatenate([high, middle, low, jnp.zeros((5, gate.shape[1]), jnp.float32)], axis=0)
    out_ref[...] = jnp.concatenate([h_ref[0].astype(jnp.float32), parts], axis=0).astype(jnp.bfloat16)


def partner(here, distance, groups):
    return here ^ distance if groups & (groups - 1) == 0 else (here + groups - distance) % groups


def distances(groups):
    return range(groups - 1, 0, -1)


def hand_over(group, x_ref, out_ref, lanes=slice(None)):
    wide = x_ref.shape[1] // 2
    rows = out_ref.shape[1]
    half = rows // 2
    for part in range(2):
        first = pl.multiple_of(group * rows + mixed(part, 2) * half, half)
        for kind in range(2):
            out_ref[kind, part * half : (part + 1) * half, lanes] = x_ref[
                pl.ds(first, half), kind * wide : (kind + 1) * wide
            ]


def hand_kernel(groups, x_ref, *hand_refs):
    here = lax.axis_index("tm")
    for distance, hand_ref in zip(distances(groups), hand_refs):
        hand_over(lax.rem(partner(here, distance, groups) + 1, groups), x_ref, hand_ref)


def attend_kernel(groups, pattern_ref, x_ref, q_ref, after_ref, out_hbm, held, sems):
    wide = held.shape[2]
    rows = held.shape[1]
    across = (groups - 1) * rows
    factor = math.log2(math.e) / math.sqrt(HD)
    lane = lax.broadcasted_iota(jnp.int32, (1, across), 1)
    ends, kept = [], []
    for source in range(groups):
        first = max(source, 1)
        ends.append(min(across, -(-(groups - first) * rows // 128) * 128))
        chosen = jnp.zeros((1, across), jnp.int32)
        for group in range(first, groups):
            start = (groups - 1 - group) * rows
            flag = pattern_ref[group : group + 1, source : source + 1]
            chosen = jnp.where((lane >= start) & (lane < start + rows), flag, chosen)
        kept.append(chosen[:, : ends[-1]] > 0)

    copies = []

    def send(group):
        for place in (group - 1, groups - 1) if group == groups - 1 else (group - 1,):
            copies.append(
                pltpu.make_async_copy(
                    held.at[group - 1], out_hbm.at[place * rows : (place + 1) * rows], sems.at[place]
                )
            )
            copies[-1].start()

    def spread(row, fill):
        rest = across - row.shape[1]
        return jnp.concatenate([row, jnp.full((1, rest), fill, row.dtype)], axis=1) if rest else row

    for head in range(0, wide, HD):
        query = jnp.concatenate(
            [q_ref[group * rows : (group + 1) * rows, head : head + HD] for group in range(groups - 1, 0, -1)],
            axis=0,
        )
        query = jnp.transpose(query)
        value = jnp.transpose(x_ref[:, wide + head : wide + head + HD])
        scores, highest = [], None
        for source in range(groups):
            key = x_ref[source * rows : (source + 1) * rows, head : head + HD]
            scores.append(
                jnp.dot(key, query[:, : ends[source]], preferred_element_type=jnp.float32)
            )
            peak = jnp.where(kept[source], jnp.max(scores[-1], axis=0, keepdims=True), -1e30)
            peak = spread(peak, -1e30)
            highest = peak if highest is None else jnp.maximum(highest, peak)
        highest = highest * factor
        total, probs = 0.0, []
        for source in range(groups):
            offset = jnp.where(kept[source], -highest[:, : ends[source]], -1e30)
            raised = jnp.exp2(scores[source] * factor + offset)
            total += spread(jnp.sum(raised, axis=0, keepdims=True), 0.0)
            probs.append(raised.astype(jnp.bfloat16))
        inverse = 1.0 / total
        last = head + HD == wide
        start, left, waiting = 0, None, groups - 1
        for source in range(groups - 1, 0, -1):
            stop = ends[source]
            if stop > start:
                numer = jnp.dot(
                    value[:, : (source + 1) * rows],
                    jnp.concatenate([p[:, start:stop] for p in probs[: source + 1]], axis=0),
                    preferred_element_type=jnp.float32,
                )
                result = jnp.transpose(numer * inverse[:, start:stop])
                left = result if left is None else jnp.concatenate([left, result], axis=0)
                start = stop
            while left is not None and left.shape[0] >= rows:
                held[waiting - 1, :, head : head + HD] = left[:rows].astype(jnp.bfloat16)
                left = left[rows:] if left.shape[0] > rows else None
                if last:
                    send(waiting)
                waiting -= 1
    for copy in copies:
        copy.wait()


def lanes_of(distance, groups, here, wide):
    source = partner(here, groups - distance if groups & (groups - 1) else distance, groups)
    return pl.ds(pl.multiple_of(source * wide, wide), wide)


def cache_kernel(groups, x_ref, hand_ref, out_ref):
    wide = x_ref.shape[1] // 2
    here = lax.axis_index("tm")
    out_ref[...] = jnp.zeros_like(out_ref)

    @pl.when(here < groups - 1)
    def place():
        hand_over(here + 1, x_ref, out_ref.at[0], lanes_of(0, groups, here, wide))
        out_ref[0, :, :, lanes_of(distances(groups)[0], groups, here, wide)] = hand_ref[...]


def cache_rest_kernel(groups, begun_hbm, after_ref, *refs):
    *hand_refs, out_hbm, sems = refs
    here = lax.axis_index("tm")

    @pl.when(here < groups - 1)
    def place():
        copies = [
            pltpu.make_async_copy(
                block, out_hbm.at[0, :, :, lanes_of(distance, groups, here, block.shape[2])], sems.at[index]
            )
            for index, (distance, block) in enumerate(zip(distances(groups)[1:], hand_refs))
        ]
        for copy in copies:
            copy.start()
        for copy in copies:
            copy.wait()


def update_kernel(seq_count, tm_count, att_ref, moved_ref, fresh_ref, after_ref, out_ref):
    tok = out_ref.shape[1]
    wide = att_ref.shape[1]
    count = att_ref.shape[0] // tok
    last = lax.axis_index("tm") == tm_count - 1

    @pl.when(last)
    def take_fresh():
        out_ref[0] = fresh_ref[...]

    @pl.when(jnp.logical_not(last))
    def take_update():
        for pair in range(count // 2):
            rows = att_ref[2 * pair * tok : 2 * (pair + 1) * tok, :].astype(jnp.float32)
            for half in range(2):
                source = 2 * pair + half
                start = (mixed(source % seq_count, seq_count) * tm_count + source // seq_count) * wide
                moved = moved_ref[:, start : start + wide].astype(jnp.float32)
                gate = (moved[tok : tok + 1] + moved[tok + 1 : tok + 2]) + moved[tok + 2 : tok + 3]
                result = moved[:tok] + gate * rows[half * tok : (half + 1) * tok]
                out_ref[0, :, start : start + wide] = result.astype(jnp.bfloat16)


def whole(space=VMEM):
    return pl.BlockSpec(memory_space=space)


def run(kernel, name, outs, specs, operands, flops=0, scratch=(), aliases={}):
    def size(a):
        return math.prod(a.shape) * jnp.dtype(a.dtype).itemsize

    moved = sum(map(size, operands)) + sum(map(size, outs))
    results = pl.pallas_call(
        kernel,
        out_shape=outs,
        in_specs=specs,
        out_specs=[whole(getattr(a, "memory_space", VMEM)) for a in outs],
        scratch_shapes=scratch,
        input_output_aliases=aliases,
        compiler_params=pltpu.CompilerParams(vmem_limit_bytes=4 * moved + (4 << 20)),
        cost_estimate=pl.CostEstimate(flops=flops, bytes_accessed=moved, transcendentals=0),
        name=name,
    )(*operands)
    return results if len(outs) > 1 else results[0]


def spread_body(queries, keys_proj, values, hidden, fresh_latent, gate_table, noise_step, pattern):
    tm_count, seq_count = lax.axis_size("tm"), lax.axis_size("seq")
    count = tm_count * seq_count
    _, tok, width = queries.shape
    wide = width // count
    group_tok = tok * seq_count
    kind = queries.dtype
    DMA = pltpu.SemaphoreType.DMA
    parts = 4 if seq_count % 8 == 0 else 2

    packed_kv, packed = run(
        functools.partial(pack_kernel, seq_count, parts),
        "pack",
        [HBM((count * tok, 2 * wide), kind), HBM((count * tok, wide), kind)],
        [whole(HBM)] * 3,
        [pltpu.with_memory_space_constraint(a, HBM) for a in (keys_proj, values, queries)],
        scratch=[
            VMEM((3, tok, width), kind),
            VMEM((count * tok, 2 * wide), kind),
            VMEM((count * tok, wide), kind),
            DMA((parts, 3)),
            DMA((parts, tm_count, 2)),
        ],
    )
    order = [tm * seq_count + mixed(s, seq_count) for tm in range(tm_count) for s in range(seq_count)]
    exchange = functools.partial(
        lax.all_to_all, axis_name=BOTH, split_axis=0, concat_axis=0, tiled=True, axis_index_groups=[order]
    )
    exchanged = exchange(packed_kv)
    asked = exchange(packed)

    residual = run(
        residual_kernel,
        "residual",
        [VMEM((tok + 8, width), kind)],
        [whole(SMEM), whole(), whole(HBM), whole(HBM)],
        (
            noise_step,
            hidden,
            pltpu.with_memory_space_constraint(gate_table, HBM),
            pltpu.with_memory_space_constraint(packed, HBM),
        ),
        scratch=[VMEM((8, width), jnp.float32), DMA],
    )
    moved = shifted(residual, "tm", -1)

    hands = run(
        functools.partial(hand_kernel, tm_count),
        "hand",
        [VMEM((2, group_tok, wide), kind)] * (tm_count - 1),
        [whole()],
        (exchanged,),
    )
    attended = run(
        functools.partial(attend_kernel, tm_count),
        "attend",
        [HBM((count * tok, wide), kind)],
        [whole(), whole(), whole(), whole(pl.ANY)],
        (pattern, exchanged, asked, moved),
        flops=2 * count * tok * count * tok * wide,
        scratch=[VMEM((tm_count - 1, group_tok, wide), kind), DMA((tm_count,))],
    )
    returned = exchange(attended)
    handed = []
    for distance, hand in zip(distances(tm_count), hands):
        route = [(i, partner(i, distance, tm_count)) for i in range(tm_count)]
        handed.append(lax.ppermute(hand, "tm", [(i, j) for i, j in route if j < tm_count - 1]))

    first, *rest = handed
    begun = run(
        functools.partial(cache_kernel, tm_count),
        "cache",
        [jax.ShapeDtypeStruct((1, 2, group_tok, tm_count * wide), kind)],
        [whole()] * 2,
        (exchanged, first),
    )
    begun = pltpu.with_memory_space_constraint(begun, HBM)
    advanced = run(
        functools.partial(update_kernel, seq_count, tm_count),
        "update",
        [jax.ShapeDtypeStruct((1, tok, width), kind)],
        [whole()] * 3 + [whole(HBM)],
        (returned, moved, fresh_latent, begun),
    )
    next_cache = run(
        functools.partial(cache_rest_kernel, tm_count),
        "cache_rest",
        [HBM(begun.shape, kind)],
        [whole(HBM)] * 2 + [whole()] * len(rest),
        (begun, pltpu.with_memory_space_constraint(advanced, HBM), *rest),
        scratch=[DMA((len(rest),))],
        aliases={0: 0},
    )
    return (advanced, next_cache)


def absorb(state, query_heads, key_piece, value_piece, scale_factor):
    accum, totals, highest = state
    row_count, head_count, head_dim = query_heads.shape
    key_heads = key_piece.reshape(key_piece.shape[0], head_count, head_dim)
    value_heads = value_piece.reshape(value_piece.shape[0], head_count, head_dim)
    scores = (
        jnp.einsum("qhd,khd->qhk", query_heads, key_heads, preferred_element_type=jnp.float32)
        * scale_factor
    )
    raised = jnp.maximum(highest, jnp.max(scores, axis=-1))
    fade = jnp.exp(highest - raised)
    weights = jnp.exp(scores - raised[..., None])
    totals = totals * fade + jnp.sum(weights, axis=-1)
    accum = accum * fade[..., None] + jnp.einsum(
        "qhk,khd->qhd",
        weights.astype(jnp.bfloat16),
        value_heads,
        preferred_element_type=jnp.float32,
    )
    return (accum, totals, raised)


def gather_body(queries, keys_proj, values, hidden, fresh_latent, gate_table, noise_step, pattern):
    group_index = lax.axis_index("tm")
    final_index = lax.axis_size("tm") - 1
    query_tok, key_tok, value_tok = (
        lax.all_to_all(queries[0], "seq", split_axis=1, concat_axis=0, tiled=True),
        lax.all_to_all(keys_proj[0], "seq", split_axis=1, concat_axis=0, tiled=True),
        lax.all_to_all(values[0], "seq", split_axis=1, concat_axis=0, tiled=True),
    )
    row_count, local_width = query_tok.shape
    head_count = local_width // HD
    query_heads = query_tok.reshape(row_count, head_count, HD)
    scale_factor = 1.0 / math.sqrt(HD)
    reach = lax.dynamic_index_in_dim(pattern, group_index, 0, keepdims=False)
    start_state = (
        jnp.zeros((row_count, head_count, HD), jnp.float32),
        jnp.zeros((row_count, head_count), jnp.float32),
        jnp.full((row_count, head_count), -1e30, jnp.float32),
    )

    def one_block(current, inputs):
        key_block, value_block, flag = inputs
        return (
            lax.cond(
                flag > 0,
                lambda state: absorb(state, query_heads, key_block, value_block, scale_factor),
                lambda state: state,
                current,
            ),
            None,
        )

    key_piece = lax.all_gather(key_tok, "tm", axis=0, tiled=False)
    value_piece = lax.all_gather(value_tok, "tm", axis=0, tiled=False)
    state, unused = lax.scan(one_block, start_state, (key_piece, value_piece, reach))
    cache_keys, cache_values = shifted((key_tok, value_tok), "tm", -1)
    accum, totals, highest = state
    attended_head = (accum / totals[..., None]).reshape(row_count, local_width).astype(jnp.bfloat16)
    attended = lax.all_to_all(attended_head, "seq", split_axis=0, concat_axis=1, tiled=True)
    gate_row = lax.dynamic_index_in_dim(gate_table, noise_step[0], 0, keepdims=False)
    updated = (
        hidden[0].astype(jnp.float32) + gate_row[None, :] * attended.astype(jnp.float32)
    ).astype(jnp.bfloat16)
    moved = shifted(updated, "tm", -1)
    advanced = jnp.where(group_index == final_index, fresh_latent, moved)[None]
    next_cache = jnp.stack([cache_keys, cache_values], axis=0)[None]
    return (advanced, next_cache)


def body(queries, *others):
    tm_count, seq_count = lax.axis_size("tm"), lax.axis_size("seq")
    _, tok, width = queries.shape
    count = tm_count * seq_count
    even = width % (count * HD) == 0 and tok % 8 == 0 and seq_count % 4 == 0 and tm_count > 2
    return (spread_body if even else gather_body)(queries, *others)


def solution(mesh):
    placed = (
        P("tm", "seq", None),
        P("tm", "seq", None),
        P("tm", "seq", None),
        P("tm", "seq", None),
        P("seq", None),
        P(),
        P("tm"),
        P(),
    )
    return jax.shard_map(
        body,
        mesh=mesh,
        in_specs=placed,
        out_specs=(P("tm", "seq", None), P("tm", None, None, "seq")),
        check_vma=False,
    )
```

```python
import functools
import math

import jax
import jax.numpy as jnp
from jax import lax
from jax.experimental import pallas as pl
from jax.experimental.pallas import tpu as pltpu
from jax.sharding import PartitionSpec as P

HD = 128
BOTH = ("tm", "seq")
VMEM = pltpu.VMEM
SMEM = pltpu.SMEM
HBM = pltpu.HBM


def shifted(block, axis, distance):
    devices = range(lax.axis_size(axis))
    route = [(i - distance, i) for i in devices if i - distance in devices]
    return lax.ppermute(block, axis, route)


def mixed(index, count):
    return (index + count // 2) % count


def pack_kernel(seq_count, parts, q_hbm, k_hbm, v_hbm, out_hbm, held, block, in_sems, out_sems):
    tok, width = held.shape[1:]
    wide = out_hbm.shape[1] // 3
    count = out_hbm.shape[0] // tok
    tm_count = count // seq_count
    span, members = width // parts, seq_count // parts
    copies = []
    for part in range(parts):
        columns = slice(part * span, (part + 1) * span)
        for place, ref in enumerate((q_hbm, k_hbm, v_hbm)):
            copies.append(
                pltpu.make_async_copy(
                    ref.at[0, :, columns], held.at[place, :, columns], in_sems.at[part, place]
                )
            )
            copies[-1].start()
    outs = []
    for part in range(parts):
        for place in range(3):
            copies[3 * part + place].wait()
        for tm in range(tm_count):
            for seq in range(part * members, (part + 1) * members, 2):
                first = (tm * seq_count + mixed(seq, seq_count)) * tok
                for place in range(3):
                    rows = []
                    for member in (seq, seq + 1):
                        start = (member * tm_count + tm) * wide
                        rows.append(held[place, :, start : start + wide].astype(jnp.float32))
                    block[first : first + 2 * tok, place * wide : (place + 1) * wide] = jnp.concatenate(
                        rows, axis=0
                    ).astype(jnp.bfloat16)
            first = (tm * seq_count + mixed(part * members, seq_count)) * tok
            rows = slice(first, first + members * tok)
            outs.append(
                pltpu.make_async_copy(block.at[rows], out_hbm.at[rows], out_sems.at[part, tm])
            )
            outs[-1].start()
    for out in outs:
        out.wait()


def residual_kernel(noise_ref, h_ref, gate_hbm, after_ref, out_ref, held, sem):
    step = noise_ref[0]
    steps = gate_hbm.shape[0]
    whole_tiles = steps // 8 * 8
    first = step // 8 * 8

    @pl.when(step < whole_tiles)
    def take_tile():
        rows = pl.ds(pl.multiple_of(first, 8), 8)
        copy = pltpu.make_async_copy(gate_hbm.at[rows], held, sem)
        copy.start()
        copy.wait()

    if steps > whole_tiles:

        @pl.when(step >= whole_tiles)
        def take_rest():
            copy = pltpu.make_async_copy(
                gate_hbm.at[whole_tiles:steps], held.at[0 : steps - whole_tiles], sem
            )
            copy.start()
            copy.wait()

    gate = held[pl.ds(step - first, 1), :]
    high = gate.astype(jnp.bfloat16).astype(jnp.float32)
    middle = (gate - high).astype(jnp.bfloat16).astype(jnp.float32)
    low = gate - high - middle
    parts = jnp.concatenate([high, middle, low, jnp.zeros((5, gate.shape[1]), jnp.float32)], axis=0)
    out_ref[...] = jnp.concatenate([h_ref[0].astype(jnp.float32), parts], axis=0).astype(jnp.bfloat16)


def partner(here, distance, groups):
    return here ^ distance if groups & (groups - 1) == 0 else (here + groups - distance) % groups


def distances(groups):
    return range(groups - 1, 0, -1)


def hand_over(group, x_ref, out_ref, lanes=slice(None)):
    wide = x_ref.shape[1] // 3
    rows = out_ref.shape[1]
    half = rows // 2
    for part in range(2):
        first = pl.multiple_of(group * rows + mixed(part, 2) * half, half)
        for kind in range(2):
            out_ref[kind, part * half : (part + 1) * half, lanes] = x_ref[
                pl.ds(first, half), (kind + 1) * wide : (kind + 2) * wide
            ]


def attend_kernel(groups, pattern_ref, x_ref, after_ref, out_hbm, *refs):
    *hand_refs, held, sems = refs
    wide = held.shape[2]
    rows = held.shape[1]
    across = (groups - 1) * rows
    factor = math.log2(math.e) / math.sqrt(HD)
    here = lax.axis_index("tm")
    lane = lax.broadcasted_iota(jnp.int32, (1, across), 1)
    ends, kept = [], []
    for source in range(groups):
        first = max(source, 1)
        ends.append(min(across, -(-(groups - first) * rows // 128) * 128))
        chosen = jnp.zeros((1, across), jnp.int32)
        for group in range(first, groups):
            start = (groups - 1 - group) * rows
            flag = pattern_ref[group : group + 1, source : source + 1]
            chosen = jnp.where((lane >= start) & (lane < start + rows), flag, chosen)
        kept.append(chosen[:, : ends[-1]] > 0)

    copies = []

    def send(group):
        for place in (group - 1, groups - 1) if group == groups - 1 else (group - 1,):
            copies.append(
                pltpu.make_async_copy(
                    held.at[group - 1], out_hbm.at[place * rows : (place + 1) * rows], sems.at[place]
                )
            )
            copies[-1].start()

    def spread(row, fill):
        rest = across - row.shape[1]
        return jnp.concatenate([row, jnp.full((1, rest), fill, row.dtype)], axis=1) if rest else row

    for head in range(0, wide, HD):
        query = jnp.concatenate(
            [x_ref[group * rows : (group + 1) * rows, head : head + HD] for group in range(groups - 1, 0, -1)],
            axis=0,
        )
        value = jnp.transpose(x_ref[:, 2 * wide + head : 2 * wide + head + HD])
        scores, highest = [], None
        for source in range(groups):
            key = x_ref[source * rows : (source + 1) * rows, wide + head : wide + head + HD]
            scores.append(
                lax.dot_general(
                    key,
                    query[: ends[source]],
                    (((1,), (1,)), ((), ())),
                    preferred_element_type=jnp.float32,
                )
            )
            peak = jnp.where(kept[source], jnp.max(scores[-1], axis=0, keepdims=True), -1e30)
            peak = spread(peak, -1e30)
            highest = peak if highest is None else jnp.maximum(highest, peak)
        highest = highest * factor
        total, probs = 0.0, []
        for source in range(groups):
            offset = jnp.where(kept[source], -highest[:, : ends[source]], -1e30)
            raised = jnp.exp2(scores[source] * factor + offset)
            total += spread(jnp.sum(raised, axis=0, keepdims=True), 0.0)
            probs.append(raised.astype(jnp.bfloat16))
        inverse = 1.0 / total
        last = head + HD == wide
        start, left, waiting = 0, None, groups - 1
        for source in range(groups - 1, 0, -1):
            stop = ends[source]
            if stop > start:
                numer = jnp.dot(
                    value[:, : (source + 1) * rows],
                    jnp.concatenate([p[:, start:stop] for p in probs[: source + 1]], axis=0),
                    preferred_element_type=jnp.float32,
                )
                result = jnp.transpose(numer * inverse[:, start:stop])
                left = result if left is None else jnp.concatenate([left, result], axis=0)
                start = stop
            while left is not None and left.shape[0] >= rows:
                held[waiting - 1, :, head : head + HD] = left[:rows].astype(jnp.bfloat16)
                left = left[rows:] if left.shape[0] > rows else None
                if last:
                    send(waiting)
                waiting -= 1
    for distance, hand_ref in zip(distances(groups), hand_refs):
        hand_over(lax.rem(partner(here, distance, groups) + 1, groups), x_ref, hand_ref)
    for copy in copies:
        copy.wait()


def lanes_of(distance, groups, here, wide):
    source = partner(here, groups - distance if groups & (groups - 1) else distance, groups)
    return pl.ds(pl.multiple_of(source * wide, wide), wide)


def cache_kernel(groups, x_ref, hand_ref, out_ref):
    wide = x_ref.shape[1] // 3
    here = lax.axis_index("tm")
    out_ref[...] = jnp.zeros_like(out_ref)

    @pl.when(here < groups - 1)
    def place():
        hand_over(here + 1, x_ref, out_ref.at[0], lanes_of(0, groups, here, wide))
        out_ref[0, :, :, lanes_of(distances(groups)[0], groups, here, wide)] = hand_ref[...]


def cache_rest_kernel(groups, begun_hbm, after_ref, *refs):
    *hand_refs, out_hbm, sems = refs
    here = lax.axis_index("tm")

    @pl.when(here < groups - 1)
    def place():
        copies = [
            pltpu.make_async_copy(
                block, out_hbm.at[0, :, :, lanes_of(distance, groups, here, block.shape[2])], sems.at[index]
            )
            for index, (distance, block) in enumerate(zip(distances(groups)[1:], hand_refs))
        ]
        for copy in copies:
            copy.start()
        for copy in copies:
            copy.wait()


def update_kernel(seq_count, tm_count, att_ref, moved_ref, fresh_ref, after_ref, out_ref):
    tok = out_ref.shape[1]
    wide = att_ref.shape[1]
    count = att_ref.shape[0] // tok
    last = lax.axis_index("tm") == tm_count - 1

    @pl.when(last)
    def take_fresh():
        out_ref[0] = fresh_ref[...]

    @pl.when(jnp.logical_not(last))
    def take_update():
        for pair in range(count // 2):
            rows = att_ref[2 * pair * tok : 2 * (pair + 1) * tok, :].astype(jnp.float32)
            for half in range(2):
                source = 2 * pair + half
                start = (mixed(source % seq_count, seq_count) * tm_count + source // seq_count) * wide
                moved = moved_ref[:, start : start + wide].astype(jnp.float32)
                gate = (moved[tok : tok + 1] + moved[tok + 1 : tok + 2]) + moved[tok + 2 : tok + 3]
                result = moved[:tok] + gate * rows[half * tok : (half + 1) * tok]
                out_ref[0, :, start : start + wide] = result.astype(jnp.bfloat16)


def whole(space=VMEM):
    return pl.BlockSpec(memory_space=space)


def run(kernel, name, outs, specs, operands, flops=0, scratch=(), aliases={}):
    def size(a):
        return math.prod(a.shape) * jnp.dtype(a.dtype).itemsize

    moved = sum(map(size, operands)) + sum(map(size, outs))
    results = pl.pallas_call(
        kernel,
        out_shape=outs,
        in_specs=specs,
        out_specs=[whole(getattr(a, "memory_space", VMEM)) for a in outs],
        scratch_shapes=scratch,
        input_output_aliases=aliases,
        compiler_params=pltpu.CompilerParams(vmem_limit_bytes=4 * moved + (4 << 20)),
        cost_estimate=pl.CostEstimate(flops=flops, bytes_accessed=moved, transcendentals=0),
        name=name,
    )(*operands)
    return results if len(outs) > 1 else results[0]


def spread_body(queries, keys_proj, values, hidden, fresh_latent, gate_table, noise_step, pattern):
    tm_count, seq_count = lax.axis_size("tm"), lax.axis_size("seq")
    count = tm_count * seq_count
    _, tok, width = queries.shape
    wide = width // count
    group_tok = tok * seq_count
    kind = queries.dtype
    DMA = pltpu.SemaphoreType.DMA
    parts = 4 if seq_count % 8 == 0 else 2

    packed = run(
        functools.partial(pack_kernel, seq_count, parts),
        "pack",
        [HBM((count * tok, 3 * wide), kind)],
        [whole(HBM)] * 3,
        [pltpu.with_memory_space_constraint(a, HBM) for a in (queries, keys_proj, values)],
        scratch=[
            VMEM((3, tok, width), kind),
            VMEM((count * tok, 3 * wide), kind),
            DMA((parts, 3)),
            DMA((parts, tm_count)),
        ],
    )
    order = [tm * seq_count + mixed(s, seq_count) for tm in range(tm_count) for s in range(seq_count)]
    exchange = functools.partial(
        lax.all_to_all, axis_name=BOTH, split_axis=0, concat_axis=0, tiled=True, axis_index_groups=[order]
    )
    exchanged = exchange(packed)

    residual = run(
        residual_kernel,
        "residual",
        [VMEM((tok + 8, width), kind)],
        [whole(SMEM), whole(), whole(HBM), whole(HBM)],
        (
            noise_step,
            hidden,
            pltpu.with_memory_space_constraint(gate_table, HBM),
            pltpu.with_memory_space_constraint(packed, HBM),
        ),
        scratch=[VMEM((8, width), jnp.float32), DMA],
    )
    moved = shifted(residual, "tm", -1)

    attended, *hands = run(
        functools.partial(attend_kernel, tm_count),
        "attend",
        [HBM((count * tok, wide), kind)] + [VMEM((2, group_tok, wide), kind)] * (tm_count - 1),
        [whole(), whole(), whole(pl.ANY)],
        (pattern, exchanged, moved),
        flops=2 * count * tok * count * tok * wide,
        scratch=[VMEM((tm_count - 1, group_tok, wide), kind), DMA((tm_count,))],
    )
    returned = exchange(attended)
    handed = []
    for distance, hand in zip(distances(tm_count), hands):
        route = [(i, partner(i, distance, tm_count)) for i in range(tm_count)]
        handed.append(lax.ppermute(hand, "tm", [(i, j) for i, j in route if j < tm_count - 1]))

    first, *rest = handed
    begun = run(
        functools.partial(cache_kernel, tm_count),
        "cache",
        [jax.ShapeDtypeStruct((1, 2, group_tok, tm_count * wide), kind)],
        [whole()] * 2,
        (exchanged, first),
    )
    begun = pltpu.with_memory_space_constraint(begun, HBM)
    advanced = run(
        functools.partial(update_kernel, seq_count, tm_count),
        "update",
        [jax.ShapeDtypeStruct((1, tok, width), kind)],
        [whole()] * 3 + [whole(HBM)],
        (returned, moved, fresh_latent, begun),
    )
    next_cache = run(
        functools.partial(cache_rest_kernel, tm_count),
        "cache_rest",
        [HBM(begun.shape, kind)],
        [whole(HBM)] * 2 + [whole()] * len(rest),
        (begun, pltpu.with_memory_space_constraint(advanced, HBM), *rest),
        scratch=[DMA((len(rest),))],
        aliases={0: 0},
    )
    return (advanced, next_cache)


def absorb(state, query_heads, key_piece, value_piece, scale_factor):
    accum, totals, highest = state
    row_count, head_count, head_dim = query_heads.shape
    key_heads = key_piece.reshape(key_piece.shape[0], head_count, head_dim)
    value_heads = value_piece.reshape(value_piece.shape[0], head_count, head_dim)
    scores = (
        jnp.einsum("qhd,khd->qhk", query_heads, key_heads, preferred_element_type=jnp.float32)
        * scale_factor
    )
    raised = jnp.maximum(highest, jnp.max(scores, axis=-1))
    fade = jnp.exp(highest - raised)
    weights = jnp.exp(scores - raised[..., None])
    totals = totals * fade + jnp.sum(weights, axis=-1)
    accum = accum * fade[..., None] + jnp.einsum(
        "qhk,khd->qhd",
        weights.astype(jnp.bfloat16),
        value_heads,
        preferred_element_type=jnp.float32,
    )
    return (accum, totals, raised)


def gather_body(queries, keys_proj, values, hidden, fresh_latent, gate_table, noise_step, pattern):
    group_index = lax.axis_index("tm")
    final_index = lax.axis_size("tm") - 1
    query_tok, key_tok, value_tok = (
        lax.all_to_all(queries[0], "seq", split_axis=1, concat_axis=0, tiled=True),
        lax.all_to_all(keys_proj[0], "seq", split_axis=1, concat_axis=0, tiled=True),
        lax.all_to_all(values[0], "seq", split_axis=1, concat_axis=0, tiled=True),
    )
    row_count, local_width = query_tok.shape
    head_count = local_width // HD
    query_heads = query_tok.reshape(row_count, head_count, HD)
    scale_factor = 1.0 / math.sqrt(HD)
    reach = lax.dynamic_index_in_dim(pattern, group_index, 0, keepdims=False)
    start_state = (
        jnp.zeros((row_count, head_count, HD), jnp.float32),
        jnp.zeros((row_count, head_count), jnp.float32),
        jnp.full((row_count, head_count), -1e30, jnp.float32),
    )

    def one_block(current, inputs):
        key_block, value_block, flag = inputs
        return (
            lax.cond(
                flag > 0,
                lambda state: absorb(state, query_heads, key_block, value_block, scale_factor),
                lambda state: state,
                current,
            ),
            None,
        )

    key_piece = lax.all_gather(key_tok, "tm", axis=0, tiled=False)
    value_piece = lax.all_gather(value_tok, "tm", axis=0, tiled=False)
    state, unused = lax.scan(one_block, start_state, (key_piece, value_piece, reach))
    cache_keys, cache_values = shifted((key_tok, value_tok), "tm", -1)
    accum, totals, highest = state
    attended_head = (accum / totals[..., None]).reshape(row_count, local_width).astype(jnp.bfloat16)
    attended = lax.all_to_all(attended_head, "seq", split_axis=0, concat_axis=1, tiled=True)
    gate_row = lax.dynamic_index_in_dim(gate_table, noise_step[0], 0, keepdims=False)
    updated = (
        hidden[0].astype(jnp.float32) + gate_row[None, :] * attended.astype(jnp.float32)
    ).astype(jnp.bfloat16)
    moved = shifted(updated, "tm", -1)
    advanced = jnp.where(group_index == final_index, fresh_latent, moved)[None]
    next_cache = jnp.stack([cache_keys, cache_values], axis=0)[None]
    return (advanced, next_cache)


def body(queries, *others):
    tm_count, seq_count = lax.axis_size("tm"), lax.axis_size("seq")
    _, tok, width = queries.shape
    count = tm_count * seq_count
    even = width % (count * HD) == 0 and tok % 8 == 0 and seq_count % 4 == 0 and tm_count > 2
    return (spread_body if even else gather_body)(queries, *others)


def solution(mesh):
    placed = (
        P("tm", "seq", None),
        P("tm", "seq", None),
        P("tm", "seq", None),
        P("tm", "seq", None),
        P("seq", None),
        P(),
        P("tm"),
        P(),
    )
    return jax.shard_map(
        body,
        mesh=mesh,
        in_specs=placed,
        out_specs=(P("tm", "seq", None), P("tm", None, None, "seq")),
        check_vma=False,
    )
```

```python
import functools
import math

import jax
import jax.numpy as jnp
from jax import lax
from jax.experimental import pallas as pl
from jax.experimental.pallas import tpu as pltpu
from jax.sharding import PartitionSpec as P

HD = 128
BOTH = ("tm", "seq")
VMEM = pltpu.VMEM
SMEM = pltpu.SMEM
HBM = pltpu.HBM


def shifted(block, axis, distance):
    devices = range(lax.axis_size(axis))
    route = [(i - distance, i) for i in devices if i - distance in devices]
    return lax.ppermute(block, axis, route)


def mixed(index, count):
    return count - 2 - index + 2 * (index % 2)


def runs(count):
    found = []
    for index in range(count):
        if found and found[-1][1] + found[-1][2] == mixed(index, count):
            found[-1][2] += 1
        else:
            found.append([index, mixed(index, count), 1])
    return found


def pack_kernel(seq_count, parts, q_hbm, k_hbm, v_hbm, out_hbm, held, block, in_sems, out_sems):
    tok, width = held.shape[1:]
    wide = out_hbm.shape[1] // 3
    count = out_hbm.shape[0] // tok
    tm_count = count // seq_count
    span, members = width // parts, seq_count // parts
    copies = []
    for part in range(parts):
        columns = slice(part * span, (part + 1) * span)
        for place, ref in enumerate((q_hbm, k_hbm, v_hbm)):
            copies.append(
                pltpu.make_async_copy(
                    ref.at[0, :, columns], held.at[place, :, columns], in_sems.at[part, place]
                )
            )
            copies[-1].start()
    outs = []
    for part in range(parts):
        for place in range(3):
            copies[3 * part + place].wait()
        for tm in range(tm_count):
            for seq in range(part * members, (part + 1) * members, 2):
                first = (tm * seq_count + mixed(seq, seq_count)) * tok
                for place in range(3):
                    rows = []
                    for member in (seq, seq + 1):
                        start = (member * tm_count + tm) * wide
                        rows.append(held[place, :, start : start + wide].astype(jnp.float32))
                    block[first : first + 2 * tok, place * wide : (place + 1) * wide] = jnp.concatenate(
                        rows, axis=0
                    ).astype(jnp.bfloat16)
            first = (tm * seq_count + mixed(part * members, seq_count)) * tok
            rows = slice(first, first + members * tok)
            outs.append(
                pltpu.make_async_copy(block.at[rows], out_hbm.at[rows], out_sems.at[part, tm])
            )
            outs[-1].start()
    for out in outs:
        out.wait()


def residual_kernel(noise_ref, h_ref, gate_hbm, after_ref, out_ref, held, sem):
    step = noise_ref[0]
    steps = gate_hbm.shape[0]
    whole_tiles = steps // 8 * 8
    first = step // 8 * 8

    @pl.when(step < whole_tiles)
    def take_tile():
        rows = pl.ds(pl.multiple_of(first, 8), 8)
        copy = pltpu.make_async_copy(gate_hbm.at[rows], held, sem)
        copy.start()
        copy.wait()

    if steps > whole_tiles:

        @pl.when(step >= whole_tiles)
        def take_rest():
            copy = pltpu.make_async_copy(
                gate_hbm.at[whole_tiles:steps], held.at[0 : steps - whole_tiles], sem
            )
            copy.start()
            copy.wait()

    gate = held[pl.ds(step - first, 1), :]
    high = gate.astype(jnp.bfloat16).astype(jnp.float32)
    middle = (gate - high).astype(jnp.bfloat16).astype(jnp.float32)
    low = gate - high - middle
    parts = jnp.concatenate([high, middle, low, jnp.zeros((5, gate.shape[1]), jnp.float32)], axis=0)
    out_ref[...] = jnp.concatenate([h_ref[0].astype(jnp.float32), parts], axis=0).astype(jnp.bfloat16)


def partner(here, distance, groups):
    return here ^ distance if groups & (groups - 1) == 0 else (here + groups - distance) % groups


def distances(groups):
    return range(groups - 1, 0, -1)


def attend_kernel(groups, pattern_ref, x_ref, after_ref, out_hbm, *refs):
    *hand_refs, held, sems = refs
    wide = held.shape[2]
    rows = held.shape[1]
    across = (groups - 1) * rows
    factor = math.log2(math.e) / math.sqrt(HD)
    here = lax.axis_index("tm")
    lane = lax.broadcasted_iota(jnp.int32, (1, across), 1)
    ends, kept = [], []
    for source in range(groups):
        first = max(source, 1)
        ends.append(min(across, -(-(groups - first) * rows // 128) * 128))
        chosen = jnp.zeros((1, across), jnp.int32)
        for group in range(first, groups):
            start = (groups - 1 - group) * rows
            flag = pattern_ref[group : group + 1, source : source + 1]
            chosen = jnp.where((lane >= start) & (lane < start + rows), flag, chosen)
        kept.append(chosen[:, : ends[-1]] > 0)

    def spread(row, fill):
        rest = across - row.shape[1]
        return jnp.concatenate([row, jnp.full((1, rest), fill, row.dtype)], axis=1) if rest else row

    for head in range(0, wide, HD):
        query = jnp.concatenate(
            [x_ref[group * rows : (group + 1) * rows, head : head + HD] for group in range(groups - 1, 0, -1)],
            axis=0,
        )
        query = jnp.transpose(query)
        value = jnp.transpose(x_ref[:, 2 * wide + head : 2 * wide + head + HD])
        scores, highest = [], None
        for source in range(groups):
            key = x_ref[source * rows : (source + 1) * rows, wide + head : wide + head + HD]
            scores.append(
                jnp.dot(key, query[:, : ends[source]], preferred_element_type=jnp.float32)
            )
            peak = jnp.where(kept[source], jnp.max(scores[-1], axis=0, keepdims=True), -1e30)
            peak = spread(peak, -1e30)
            highest = peak if highest is None else jnp.maximum(highest, peak)
        highest = highest * factor
        total, probs = 0.0, []
        for source in range(groups):
            offset = jnp.where(kept[source], -highest[:, : ends[source]], -1e30)
            raised = jnp.exp2(scores[source] * factor + offset)
            total += spread(jnp.sum(raised, axis=0, keepdims=True), 0.0)
            probs.append(raised.astype(jnp.bfloat16))
        inverse = 1.0 / total
        start, pieces = 0, []
        for source in range(groups - 1, 0, -1):
            stop = ends[source]
            if stop > start:
                numer = jnp.dot(
                    value[:, : (source + 1) * rows],
                    jnp.concatenate([p[:, start:stop] for p in probs[: source + 1]], axis=0),
                    preferred_element_type=jnp.float32,
                )
                pieces.append(numer * inverse[:, start:stop])
                start = stop
        result = jnp.transpose(jnp.concatenate(pieces, axis=1)).astype(jnp.bfloat16)
        for group in range(1, groups):
            start = (groups - 1 - group) * rows
            held[group - 1, :, head : head + HD] = result[start : start + rows]
    copies = [
        pltpu.make_async_copy(
            held.at[min(place, groups - 2)], out_hbm.at[place * rows : (place + 1) * rows], sems.at[place]
        )
        for place in range(groups)
    ]
    for copy in copies:
        copy.start()
    for distance, hand_ref in zip(distances(groups), hand_refs):
        group = lax.rem(partner(here, distance, groups) + 1, groups)
        hand_ref[...] = x_ref[pl.ds(pl.multiple_of(group * rows, rows), rows), wide:]
    for copy in copies:
        copy.wait()


def cache_places(seq_count, groups, rows, wide, distance, here):
    source = partner(here, groups - distance if groups & (groups - 1) else distance, groups)
    lanes = pl.ds(pl.multiple_of(source * wide, wide), wide)
    tok = rows // seq_count
    for index, place, length in runs(seq_count):
        yield (
            slice(index * tok, (index + length) * tok),
            lanes,
            slice(place * tok, (place + length) * tok),
        )


def cache_kernel(seq_count, groups, x_ref, hand_ref, out_ref):
    wide = x_ref.shape[1] // 3
    rows = out_ref.shape[2]
    here = lax.axis_index("tm")
    out_ref[...] = jnp.zeros_like(out_ref)

    @pl.when(here < groups - 1)
    def place():
        own = x_ref[pl.ds(pl.multiple_of((here + 1) * rows, rows), rows), wide:]
        for distance, block in ((0, own), (distances(groups)[0], hand_ref)):
            for to, lanes, at in cache_places(seq_count, groups, rows, wide, distance, here):
                for kind in range(2):
                    out_ref[0, kind, to, lanes] = block[at, kind * wide : (kind + 1) * wide]


def cache_rest_kernel(seq_count, groups, begun_hbm, after_ref, *refs):
    *hand_refs, out_hbm, sems = refs
    wide = hand_refs[0].shape[1] // 2
    rows = out_hbm.shape[2]
    here = lax.axis_index("tm")

    @pl.when(here < groups - 1)
    def place():
        copies = []
        for distance, block in zip(distances(groups)[1:], hand_refs):
            for to, lanes, at in cache_places(seq_count, groups, rows, wide, distance, here):
                for kind in range(2):
                    copies.append(
                        pltpu.make_async_copy(
                            block.at[at, kind * wide : (kind + 1) * wide],
                            out_hbm.at[0, kind, to, lanes],
                            sems.at[len(copies)],
                        )
                    )
                    copies[-1].start()
        for copy in copies:
            copy.wait()


def update_kernel(seq_count, tm_count, att_ref, moved_ref, fresh_ref, after_ref, out_ref):
    tok = out_ref.shape[1]
    wide = att_ref.shape[1]
    count = att_ref.shape[0] // tok
    ordered = sorted(range(seq_count), key=lambda index: mixed(index, seq_count))
    last = lax.axis_index("tm") == tm_count - 1

    @pl.when(last)
    def take_fresh():
        out_ref[0] = fresh_ref[...]

    @pl.when(jnp.logical_not(last))
    def take_update():
        for pair in range(count // 2):
            rows = att_ref[2 * pair * tok : 2 * (pair + 1) * tok, :].astype(jnp.float32)
            for half in range(2):
                source = 2 * pair + half
                start = (ordered[source % seq_count] * tm_count + source // seq_count) * wide
                moved = moved_ref[:, start : start + wide].astype(jnp.float32)
                gate = (moved[tok : tok + 1] + moved[tok + 1 : tok + 2]) + moved[tok + 2 : tok + 3]
                result = moved[:tok] + gate * rows[half * tok : (half + 1) * tok]
                out_ref[0, :, start : start + wide] = result.astype(jnp.bfloat16)


def whole(space=VMEM):
    return pl.BlockSpec(memory_space=space)


def run(kernel, name, outs, specs, operands, flops=0, scratch=(), aliases={}):
    def size(a):
        return math.prod(a.shape) * jnp.dtype(a.dtype).itemsize

    moved = sum(map(size, operands)) + sum(map(size, outs))
    results = pl.pallas_call(
        kernel,
        out_shape=outs,
        in_specs=specs,
        out_specs=[whole(getattr(a, "memory_space", VMEM)) for a in outs],
        scratch_shapes=scratch,
        input_output_aliases=aliases,
        compiler_params=pltpu.CompilerParams(vmem_limit_bytes=4 * moved + (4 << 20)),
        cost_estimate=pl.CostEstimate(flops=flops, bytes_accessed=moved, transcendentals=0),
        name=name,
    )(*operands)
    return results if len(outs) > 1 else results[0]


def spread_body(queries, keys_proj, values, hidden, fresh_latent, gate_table, noise_step, pattern):
    tm_count, seq_count = lax.axis_size("tm"), lax.axis_size("seq")
    count = tm_count * seq_count
    _, tok, width = queries.shape
    wide = width // count
    group_tok = tok * seq_count
    kind = queries.dtype
    DMA = pltpu.SemaphoreType.DMA
    parts = seq_count // 2

    packed = run(
        functools.partial(pack_kernel, seq_count, parts),
        "pack",
        [HBM((count * tok, 3 * wide), kind)],
        [whole(HBM)] * 3,
        [pltpu.with_memory_space_constraint(a, HBM) for a in (queries, keys_proj, values)],
        scratch=[
            VMEM((3, tok, width), kind),
            VMEM((count * tok, 3 * wide), kind),
            DMA((parts, 3)),
            DMA((parts, tm_count)),
        ],
    )
    ordered = sorted(range(seq_count), key=lambda index: mixed(index, seq_count))
    order = [tm * seq_count + index for tm in range(tm_count) for index in ordered]
    exchange = functools.partial(
        lax.all_to_all, axis_name=BOTH, split_axis=0, concat_axis=0, tiled=True, axis_index_groups=[order]
    )
    exchanged = exchange(packed)

    residual = run(
        residual_kernel,
        "residual",
        [VMEM((tok + 8, width), kind)],
        [whole(SMEM), whole(), whole(HBM), whole(HBM)],
        (
            noise_step,
            hidden,
            pltpu.with_memory_space_constraint(gate_table, HBM),
            pltpu.with_memory_space_constraint(packed, HBM),
        ),
        scratch=[VMEM((8, width), jnp.float32), DMA],
    )
    moved = shifted(residual, "tm", -1)

    attended, *hands = run(
        functools.partial(attend_kernel, tm_count),
        "attend",
        [HBM((count * tok, wide), kind)] + [VMEM((group_tok, 2 * wide), kind)] * (tm_count - 1),
        [whole(), whole(), whole(pl.ANY)],
        (pattern, exchanged, moved),
        flops=2 * count * tok * count * tok * wide,
        scratch=[VMEM((tm_count - 1, group_tok, wide), kind), DMA((tm_count,))],
    )
    returned = exchange(attended)
    handed = []
    for distance, hand in zip(distances(tm_count), hands):
        route = [(i, partner(i, distance, tm_count)) for i in range(tm_count)]
        handed.append(lax.ppermute(hand, "tm", [(i, j) for i, j in route if j < tm_count - 1]))

    first, *rest = handed
    begun = run(
        functools.partial(cache_kernel, seq_count, tm_count),
        "cache",
        [jax.ShapeDtypeStruct((1, 2, group_tok, tm_count * wide), kind)],
        [whole()] * 2,
        (exchanged, first),
    )
    begun = pltpu.with_memory_space_constraint(begun, HBM)
    advanced = run(
        functools.partial(update_kernel, seq_count, tm_count),
        "update",
        [jax.ShapeDtypeStruct((1, tok, width), kind)],
        [whole()] * 3 + [whole(HBM)],
        (returned, moved, fresh_latent, begun),
    )
    next_cache = run(
        functools.partial(cache_rest_kernel, seq_count, tm_count),
        "cache_rest",
        [HBM(begun.shape, kind)],
        [whole(HBM)] * 2 + [whole()] * len(rest),
        (begun, pltpu.with_memory_space_constraint(advanced, HBM), *rest),
        scratch=[DMA((2 * len(runs(seq_count)) * len(rest),))],
        aliases={0: 0},
    )
    return (advanced, next_cache)


def absorb(state, query_heads, key_piece, value_piece, scale_factor):
    accum, totals, highest = state
    row_count, head_count, head_dim = query_heads.shape
    key_heads = key_piece.reshape(key_piece.shape[0], head_count, head_dim)
    value_heads = value_piece.reshape(value_piece.shape[0], head_count, head_dim)
    scores = (
        jnp.einsum("qhd,khd->qhk", query_heads, key_heads, preferred_element_type=jnp.float32)
        * scale_factor
    )
    raised = jnp.maximum(highest, jnp.max(scores, axis=-1))
    fade = jnp.exp(highest - raised)
    weights = jnp.exp(scores - raised[..., None])
    totals = totals * fade + jnp.sum(weights, axis=-1)
    accum = accum * fade[..., None] + jnp.einsum(
        "qhk,khd->qhd",
        weights.astype(jnp.bfloat16),
        value_heads,
        preferred_element_type=jnp.float32,
    )
    return (accum, totals, raised)


def gather_body(queries, keys_proj, values, hidden, fresh_latent, gate_table, noise_step, pattern):
    group_index = lax.axis_index("tm")
    final_index = lax.axis_size("tm") - 1
    query_tok, key_tok, value_tok = (
        lax.all_to_all(queries[0], "seq", split_axis=1, concat_axis=0, tiled=True),
        lax.all_to_all(keys_proj[0], "seq", split_axis=1, concat_axis=0, tiled=True),
        lax.all_to_all(values[0], "seq", split_axis=1, concat_axis=0, tiled=True),
    )
    row_count, local_width = query_tok.shape
    head_count = local_width // HD
    query_heads = query_tok.reshape(row_count, head_count, HD)
    scale_factor = 1.0 / math.sqrt(HD)
    reach = lax.dynamic_index_in_dim(pattern, group_index, 0, keepdims=False)
    start_state = (
        jnp.zeros((row_count, head_count, HD), jnp.float32),
        jnp.zeros((row_count, head_count), jnp.float32),
        jnp.full((row_count, head_count), -1e30, jnp.float32),
    )

    def one_block(current, inputs):
        key_block, value_block, flag = inputs
        return (
            lax.cond(
                flag > 0,
                lambda state: absorb(state, query_heads, key_block, value_block, scale_factor),
                lambda state: state,
                current,
            ),
            None,
        )

    key_piece = lax.all_gather(key_tok, "tm", axis=0, tiled=False)
    value_piece = lax.all_gather(value_tok, "tm", axis=0, tiled=False)
    state, unused = lax.scan(one_block, start_state, (key_piece, value_piece, reach))
    cache_keys, cache_values = shifted((key_tok, value_tok), "tm", -1)
    accum, totals, highest = state
    attended_head = (accum / totals[..., None]).reshape(row_count, local_width).astype(jnp.bfloat16)
    attended = lax.all_to_all(attended_head, "seq", split_axis=0, concat_axis=1, tiled=True)
    gate_row = lax.dynamic_index_in_dim(gate_table, noise_step[0], 0, keepdims=False)
    updated = (
        hidden[0].astype(jnp.float32) + gate_row[None, :] * attended.astype(jnp.float32)
    ).astype(jnp.bfloat16)
    moved = shifted(updated, "tm", -1)
    advanced = jnp.where(group_index == final_index, fresh_latent, moved)[None]
    next_cache = jnp.stack([cache_keys, cache_values], axis=0)[None]
    return (advanced, next_cache)


def body(queries, *others):
    tm_count, seq_count = lax.axis_size("tm"), lax.axis_size("seq")
    _, tok, width = queries.shape
    count = tm_count * seq_count
    even = width % (count * HD) == 0 and tok % 8 == 0 and seq_count % 2 == 0 and tm_count > 2
    return (spread_body if even else gather_body)(queries, *others)


def solution(mesh):
    placed = (
        P("tm", "seq", None),
        P("tm", "seq", None),
        P("tm", "seq", None),
        P("tm", "seq", None),
        P("seq", None),
        P(),
        P("tm"),
        P(),
    )
    return jax.shard_map(
        body,
        mesh=mesh,
        in_specs=placed,
        out_specs=(P("tm", "seq", None), P("tm", None, None, "seq")),
        check_vma=False,
    )
```

```python
import functools
import math

import jax
import jax.numpy as jnp
from jax import lax
from jax.experimental import pallas as pl
from jax.experimental.pallas import tpu as pltpu
from jax.sharding import PartitionSpec as P

HD = 128
BOTH = ("tm", "seq")
VMEM = pltpu.VMEM
SMEM = pltpu.SMEM
HBM = pltpu.HBM


def shifted(block, axis, distance):
    devices = range(lax.axis_size(axis))
    route = [(i - distance, i) for i in devices if i - distance in devices]
    return lax.ppermute(block, axis, route)


def mixed(index, count):
    return (index + count // 2) % count


def back_place(pair, pairs):
    return pairs - 1 - pair


def back_order(tm_count, seq_count):
    pairs = seq_count // 2
    ordered = sorted(range(pairs), key=lambda pair: back_place(pair, pairs))
    return [(tm, 2 * pair + member) for tm in range(tm_count) for pair in ordered for member in range(2)]


def pack_kernel(seq_count, parts, q_hbm, k_hbm, v_hbm, out_hbm, held, block, in_sems, out_sems):
    tok, width = held.shape[1:]
    wide = out_hbm.shape[1] // 3
    count = out_hbm.shape[0] // tok
    tm_count = count // seq_count
    span, members = width // parts, seq_count // parts
    copies = []
    for part in range(parts):
        columns = slice(part * span, (part + 1) * span)
        for place, ref in enumerate((q_hbm, k_hbm, v_hbm)):
            copies.append(
                pltpu.make_async_copy(
                    ref.at[0, :, columns], held.at[place, :, columns], in_sems.at[part, place]
                )
            )
            copies[-1].start()
    outs = []
    for part in range(parts):
        for place in range(3):
            copies[3 * part + place].wait()
        for tm in range(tm_count):
            for seq in range(part * members, (part + 1) * members, 2):
                first = (tm * seq_count + mixed(seq, seq_count)) * tok
                for place in range(3):
                    rows = []
                    for member in (seq, seq + 1):
                        start = (member * tm_count + tm) * wide
                        rows.append(held[place, :, start : start + wide].astype(jnp.float32))
                    block[first : first + 2 * tok, place * wide : (place + 1) * wide] = jnp.concatenate(
                        rows, axis=0
                    ).astype(jnp.bfloat16)
            first = (tm * seq_count + mixed(part * members, seq_count)) * tok
            rows = slice(first, first + members * tok)
            outs.append(
                pltpu.make_async_copy(block.at[rows], out_hbm.at[rows], out_sems.at[part, tm])
            )
            outs[-1].start()
    for out in outs:
        out.wait()


def residual_kernel(noise_ref, h_ref, gate_hbm, after_ref, out_ref, held, sem):
    step = noise_ref[0]
    steps = gate_hbm.shape[0]
    whole_tiles = steps // 8 * 8
    first = step // 8 * 8

    @pl.when(step < whole_tiles)
    def take_tile():
        rows = pl.ds(pl.multiple_of(first, 8), 8)
        copy = pltpu.make_async_copy(gate_hbm.at[rows], held, sem)
        copy.start()
        copy.wait()

    if steps > whole_tiles:

        @pl.when(step >= whole_tiles)
        def take_rest():
            copy = pltpu.make_async_copy(
                gate_hbm.at[whole_tiles:steps], held.at[0 : steps - whole_tiles], sem
            )
            copy.start()
            copy.wait()

    gate = held[pl.ds(step - first, 1), :]
    high = gate.astype(jnp.bfloat16).astype(jnp.float32)
    middle = (gate - high).astype(jnp.bfloat16).astype(jnp.float32)
    low = gate - high - middle
    parts = jnp.concatenate([high, middle, low, jnp.zeros((5, gate.shape[1]), jnp.float32)], axis=0)
    out_ref[...] = jnp.concatenate([h_ref[0].astype(jnp.float32), parts], axis=0).astype(jnp.bfloat16)


def partner(here, distance, groups):
    return here ^ distance if groups & (groups - 1) == 0 else (here + groups - distance) % groups


def distances(groups):
    return range(groups - 1, 0, -1)


def hand_over(group, x_ref, out_ref, lanes=slice(None)):
    wide = x_ref.shape[1] // 3
    rows = out_ref.shape[1]
    half = rows // 2
    for part in range(2):
        first = pl.multiple_of(group * rows + mixed(part, 2) * half, half)
        for kind in range(2):
            out_ref[kind, part * half : (part + 1) * half, lanes] = x_ref[
                pl.ds(first, half), (kind + 1) * wide : (kind + 2) * wide
            ]


def attend_kernel(groups, seq_count, pattern_ref, x_ref, after_ref, out_hbm, *refs):
    *hand_refs, held, sems = refs
    wide = held.shape[1]
    rows = held.shape[0] // groups
    across = (groups - 1) * rows
    factor = math.log2(math.e) / math.sqrt(HD)
    here = lax.axis_index("tm")
    lane = lax.broadcasted_iota(jnp.int32, (1, across), 1)
    ends, kept = [], []
    for source in range(groups):
        first = max(source, 1)
        ends.append(min(across, -(-(groups - first) * rows // 128) * 128))
        chosen = jnp.zeros((1, across), jnp.int32)
        for group in range(first, groups):
            start = (groups - 1 - group) * rows
            flag = pattern_ref[group : group + 1, source : source + 1]
            chosen = jnp.where((lane >= start) & (lane < start + rows), flag, chosen)
        kept.append(chosen[:, : ends[-1]] > 0)

    pairs = seq_count // 2
    step = rows // pairs

    def keep(group, head, result):
        for place in (group - 1, groups - 1) if group == groups - 1 else (group - 1,):
            for pair in range(pairs):
                at = mixed(2 * pair, seq_count) // 2 * step
                to = place * rows + back_place(pair, pairs) * step
                held[to : to + step, head : head + HD] = result[at : at + step]

    def spread(row, fill):
        rest = across - row.shape[1]
        return jnp.concatenate([row, jnp.full((1, rest), fill, row.dtype)], axis=1) if rest else row

    for head in range(0, wide, HD):
        query = jnp.concatenate(
            [x_ref[group * rows : (group + 1) * rows, head : head + HD] for group in range(groups - 1, 0, -1)],
            axis=0,
        )
        query = jnp.transpose(query)
        value = jnp.transpose(x_ref[:, 2 * wide + head : 2 * wide + head + HD])
        scores, highest = [], None
        for source in range(groups):
            key = x_ref[source * rows : (source + 1) * rows, wide + head : wide + head + HD]
            scores.append(
                jnp.dot(key, query[:, : ends[source]], preferred_element_type=jnp.float32)
            )
            peak = jnp.where(kept[source], jnp.max(scores[-1], axis=0, keepdims=True), -1e30)
            peak = spread(peak, -1e30)
            highest = peak if highest is None else jnp.maximum(highest, peak)
        highest = highest * factor
        total, probs = 0.0, []
        for source in range(groups):
            offset = jnp.where(kept[source], -highest[:, : ends[source]], -1e30)
            raised = jnp.exp2(scores[source] * factor + offset)
            total += spread(jnp.sum(raised, axis=0, keepdims=True), 0.0)
            probs.append(raised.astype(jnp.bfloat16))
        inverse = 1.0 / total
        start, left, waiting = 0, None, groups - 1
        for source in range(groups - 1, 0, -1):
            stop = ends[source]
            if stop > start:
                numer = jnp.dot(
                    value[:, : (source + 1) * rows],
                    jnp.concatenate([p[:, start:stop] for p in probs[: source + 1]], axis=0),
                    preferred_element_type=jnp.float32,
                )
                result = jnp.transpose(numer * inverse[:, start:stop])
                left = result if left is None else jnp.concatenate([left, result], axis=0)
                start = stop
            while left is not None and left.shape[0] >= rows:
                keep(waiting, head, left[:rows].astype(jnp.bfloat16))
                left = left[rows:] if left.shape[0] > rows else None
                waiting -= 1
    copies = [
        pltpu.make_async_copy(
            held.at[place * rows : (place + 1) * rows], out_hbm.at[place * rows : (place + 1) * rows], sems.at[place]
        )
        for place in range(groups)
    ]
    for copy in copies:
        copy.start()
    for distance, hand_ref in zip(distances(groups), hand_refs):
        hand_over(lax.rem(partner(here, distance, groups) + 1, groups), x_ref, hand_ref)
    for copy in copies:
        copy.wait()


def lanes_of(distance, groups, here, wide):
    source = partner(here, groups - distance if groups & (groups - 1) else distance, groups)
    return pl.ds(pl.multiple_of(source * wide, wide), wide)


def cache_kernel(groups, x_ref, hand_ref, out_ref):
    wide = x_ref.shape[1] // 3
    here = lax.axis_index("tm")
    out_ref[...] = jnp.zeros_like(out_ref)

    @pl.when(here < groups - 1)
    def place():
        hand_over(here + 1, x_ref, out_ref.at[0], lanes_of(0, groups, here, wide))
        out_ref[0, :, :, lanes_of(distances(groups)[0], groups, here, wide)] = hand_ref[...]


def finish_kernel(seq_count, tm_count, att_ref, moved_ref, fresh_ref, begun_hbm, *refs):
    *hand_refs, out_hbm, cache_hbm, held, sem, sems = refs
    tok = held.shape[1]
    wide = att_ref.shape[1]
    count = att_ref.shape[0] // tok
    order = back_order(tm_count, seq_count)
    here = lax.axis_index("tm")
    last = here == tm_count - 1
    copies = [
        pltpu.make_async_copy(
            block, cache_hbm.at[0, :, :, lanes_of(distance, tm_count, here, block.shape[2])], sems.at[index]
        )
        for index, (distance, block) in enumerate(zip(distances(tm_count)[1:], hand_refs))
    ]

    @pl.when(last)
    def take_fresh():
        copy = pltpu.make_async_copy(fresh_ref, out_hbm.at[0], sem)
        copy.start()
        copy.wait()

    @pl.when(jnp.logical_not(last))
    def take_update():
        for copy in copies:
            copy.start()
        for pair in range(count // 2):
            rows = att_ref[2 * pair * tok : 2 * (pair + 1) * tok, :].astype(jnp.float32)
            for half in range(2):
                tm, seq = order[2 * pair + half]
                start = (seq * tm_count + tm) * wide
                moved = moved_ref[:, start : start + wide].astype(jnp.float32)
                gate = (moved[tok : tok + 1] + moved[tok + 1 : tok + 2]) + moved[tok + 2 : tok + 3]
                result = moved[:tok] + gate * rows[half * tok : (half + 1) * tok]
                held[0, :, start : start + wide] = result.astype(jnp.bfloat16)
        copy = pltpu.make_async_copy(held, out_hbm, sem)
        copy.start()
        copy.wait()
        for copy in copies:
            copy.wait()


def whole(space=VMEM):
    return pl.BlockSpec(memory_space=space)


def run(kernel, name, outs, specs, operands, flops=0, scratch=(), aliases={}):
    def size(a):
        return math.prod(a.shape) * jnp.dtype(a.dtype).itemsize

    moved = sum(map(size, operands)) + sum(map(size, outs))
    results = pl.pallas_call(
        kernel,
        out_shape=outs,
        in_specs=specs,
        out_specs=[whole(getattr(a, "memory_space", VMEM)) for a in outs],
        scratch_shapes=scratch,
        input_output_aliases=aliases,
        compiler_params=pltpu.CompilerParams(vmem_limit_bytes=4 * moved + (4 << 20)),
        cost_estimate=pl.CostEstimate(flops=flops, bytes_accessed=moved, transcendentals=0),
        name=name,
    )(*operands)
    return results if len(outs) > 1 else results[0]


def spread_body(queries, keys_proj, values, hidden, fresh_latent, gate_table, noise_step, pattern):
    tm_count, seq_count = lax.axis_size("tm"), lax.axis_size("seq")
    count = tm_count * seq_count
    _, tok, width = queries.shape
    wide = width // count
    group_tok = tok * seq_count
    kind = queries.dtype
    DMA = pltpu.SemaphoreType.DMA
    parts = 4 if seq_count % 8 == 0 else 2

    packed = run(
        functools.partial(pack_kernel, seq_count, parts),
        "pack",
        [HBM((count * tok, 3 * wide), kind)],
        [whole(HBM)] * 3,
        [pltpu.with_memory_space_constraint(a, HBM) for a in (queries, keys_proj, values)],
        scratch=[
            VMEM((3, tok, width), kind),
            VMEM((count * tok, 3 * wide), kind),
            DMA((parts, 3)),
            DMA((parts, tm_count)),
        ],
    )
    order = [tm * seq_count + mixed(s, seq_count) for tm in range(tm_count) for s in range(seq_count)]
    back = [tm * seq_count + index for tm, index in back_order(tm_count, seq_count)]
    exchange = functools.partial(
        lax.all_to_all, axis_name=BOTH, split_axis=0, concat_axis=0, tiled=True
    )
    exchanged = exchange(packed, axis_index_groups=[order])

    residual = run(
        residual_kernel,
        "residual",
        [VMEM((tok + 8, width), kind)],
        [whole(SMEM), whole(), whole(HBM), whole(HBM)],
        (
            noise_step,
            hidden,
            pltpu.with_memory_space_constraint(gate_table, HBM),
            pltpu.with_memory_space_constraint(packed, HBM),
        ),
        scratch=[VMEM((8, width), jnp.float32), DMA],
    )
    moved = shifted(residual, "tm", -1)

    attended, *hands = run(
        functools.partial(attend_kernel, tm_count, seq_count),
        "attend",
        [HBM((count * tok, wide), kind)] + [VMEM((2, group_tok, wide), kind)] * (tm_count - 1),
        [whole(), whole(), whole(pl.ANY)],
        (pattern, exchanged, moved),
        flops=2 * count * tok * count * tok * wide,
        scratch=[VMEM((count * tok, wide), kind), DMA((tm_count,))],
    )
    returned = exchange(attended, axis_index_groups=[back])
    handed = []
    for distance, hand in zip(distances(tm_count), hands):
        route = [(i, partner(i, distance, tm_count)) for i in range(tm_count)]
        handed.append(lax.ppermute(hand, "tm", [(i, j) for i, j in route if j < tm_count - 1]))

    first, *rest = handed
    begun = run(
        functools.partial(cache_kernel, tm_count),
        "cache",
        [jax.ShapeDtypeStruct((1, 2, group_tok, tm_count * wide), kind)],
        [whole()] * 2,
        (exchanged, first),
    )
    begun = pltpu.with_memory_space_constraint(begun, HBM)
    advanced, next_cache = run(
        functools.partial(finish_kernel, seq_count, tm_count),
        "finish",
        [HBM((1, tok, width), kind), HBM(begun.shape, kind)],
        [whole()] * 3 + [whole(HBM)] + [whole()] * len(rest),
        (returned, moved, fresh_latent, begun, *rest),
        scratch=[VMEM((1, tok, width), kind), DMA, DMA((len(rest),))],
        aliases={3: 1},
    )
    return (advanced, next_cache)


def absorb(state, query_heads, key_piece, value_piece, scale_factor):
    accum, totals, highest = state
    row_count, head_count, head_dim = query_heads.shape
    key_heads = key_piece.reshape(key_piece.shape[0], head_count, head_dim)
    value_heads = value_piece.reshape(value_piece.shape[0], head_count, head_dim)
    scores = (
        jnp.einsum("qhd,khd->qhk", query_heads, key_heads, preferred_element_type=jnp.float32)
        * scale_factor
    )
    raised = jnp.maximum(highest, jnp.max(scores, axis=-1))
    fade = jnp.exp(highest - raised)
    weights = jnp.exp(scores - raised[..., None])
    totals = totals * fade + jnp.sum(weights, axis=-1)
    accum = accum * fade[..., None] + jnp.einsum(
        "qhk,khd->qhd",
        weights.astype(jnp.bfloat16),
        value_heads,
        preferred_element_type=jnp.float32,
    )
    return (accum, totals, raised)


def gather_body(queries, keys_proj, values, hidden, fresh_latent, gate_table, noise_step, pattern):
    group_index = lax.axis_index("tm")
    final_index = lax.axis_size("tm") - 1
    query_tok, key_tok, value_tok = (
        lax.all_to_all(queries[0], "seq", split_axis=1, concat_axis=0, tiled=True),
        lax.all_to_all(keys_proj[0], "seq", split_axis=1, concat_axis=0, tiled=True),
        lax.all_to_all(values[0], "seq", split_axis=1, concat_axis=0, tiled=True),
    )
    row_count, local_width = query_tok.shape
    head_count = local_width // HD
    query_heads = query_tok.reshape(row_count, head_count, HD)
    scale_factor = 1.0 / math.sqrt(HD)
    reach = lax.dynamic_index_in_dim(pattern, group_index, 0, keepdims=False)
    start_state = (
        jnp.zeros((row_count, head_count, HD), jnp.float32),
        jnp.zeros((row_count, head_count), jnp.float32),
        jnp.full((row_count, head_count), -1e30, jnp.float32),
    )

    def one_block(current, inputs):
        key_block, value_block, flag = inputs
        return (
            lax.cond(
                flag > 0,
                lambda state: absorb(state, query_heads, key_block, value_block, scale_factor),
                lambda state: state,
                current,
            ),
            None,
        )

    key_piece = lax.all_gather(key_tok, "tm", axis=0, tiled=False)
    value_piece = lax.all_gather(value_tok, "tm", axis=0, tiled=False)
    state, unused = lax.scan(one_block, start_state, (key_piece, value_piece, reach))
    cache_keys, cache_values = shifted((key_tok, value_tok), "tm", -1)
    accum, totals, highest = state
    attended_head = (accum / totals[..., None]).reshape(row_count, local_width).astype(jnp.bfloat16)
    attended = lax.all_to_all(attended_head, "seq", split_axis=0, concat_axis=1, tiled=True)
    gate_row = lax.dynamic_index_in_dim(gate_table, noise_step[0], 0, keepdims=False)
    updated = (
        hidden[0].astype(jnp.float32) + gate_row[None, :] * attended.astype(jnp.float32)
    ).astype(jnp.bfloat16)
    moved = shifted(updated, "tm", -1)
    advanced = jnp.where(group_index == final_index, fresh_latent, moved)[None]
    next_cache = jnp.stack([cache_keys, cache_values], axis=0)[None]
    return (advanced, next_cache)


def body(queries, *others):
    tm_count, seq_count = lax.axis_size("tm"), lax.axis_size("seq")
    _, tok, width = queries.shape
    count = tm_count * seq_count
    even = width % (count * HD) == 0 and tok % 8 == 0 and seq_count % 4 == 0 and tm_count > 2 and tm_count % 2 == 0
    return (spread_body if even else gather_body)(queries, *others)


def solution(mesh):
    placed = (
        P("tm", "seq", None),
        P("tm", "seq", None),
        P("tm", "seq", None),
        P("tm", "seq", None),
        P("seq", None),
        P(),
        P("tm"),
        P(),
    )
    return jax.shard_map(
        body,
        mesh=mesh,
        in_specs=placed,
        out_specs=(P("tm", "seq", None), P("tm", None, None, "seq")),
        check_vma=False,
    )
```

```python
import functools
import math

import jax
import jax.numpy as jnp
from jax import lax
from jax.experimental import pallas as pl
from jax.experimental.pallas import tpu as pltpu
from jax.sharding import PartitionSpec as P

HD = 128
BOTH = ("tm", "seq")
VMEM = pltpu.VMEM
SMEM = pltpu.SMEM
HBM = pltpu.HBM


def shifted(block, axis, distance):
    devices = range(lax.axis_size(axis))
    route = [(i - distance, i) for i in devices if i - distance in devices]
    return lax.ppermute(block, axis, route)


def mixed(index, count):
    return (index + count // 2) % count


def turned(group, groups):
    return (group + groups // 2) % groups


def pack_kernel(seq_count, parts, q_hbm, k_hbm, v_hbm, out_hbm, held, block, in_sems, out_sems):
    tok, width = held.shape[1:]
    wide = out_hbm.shape[1] // 3
    count = out_hbm.shape[0] // tok
    tm_count = count // seq_count
    span, members = width // parts, seq_count // parts
    copies = []
    for part in range(parts):
        columns = slice(part * span, (part + 1) * span)
        for place, ref in enumerate((q_hbm, k_hbm, v_hbm)):
            copies.append(
                pltpu.make_async_copy(
                    ref.at[0, :, columns], held.at[place, :, columns], in_sems.at[part, place]
                )
            )
            copies[-1].start()
    outs = []
    for part in range(parts):
        for place in range(3):
            copies[3 * part + place].wait()
        for tm in range(tm_count):
            for seq in range(part * members, (part + 1) * members, 2):
                first = (turned(tm, tm_count) * seq_count + mixed(seq, seq_count)) * tok
                for place in range(3):
                    rows = []
                    for member in (seq, seq + 1):
                        start = (member * tm_count + tm) * wide
                        rows.append(held[place, :, start : start + wide].astype(jnp.float32))
                    block[first : first + 2 * tok, place * wide : (place + 1) * wide] = jnp.concatenate(
                        rows, axis=0
                    ).astype(jnp.bfloat16)
            first = (turned(tm, tm_count) * seq_count + mixed(part * members, seq_count)) * tok
            rows = slice(first, first + members * tok)
            outs.append(
                pltpu.make_async_copy(block.at[rows], out_hbm.at[rows], out_sems.at[part, tm])
            )
            outs[-1].start()
    for out in outs:
        out.wait()


def residual_kernel(noise_ref, h_ref, gate_hbm, after_ref, out_ref, held, sem):
    step = noise_ref[0]
    steps = gate_hbm.shape[0]
    whole_tiles = steps // 8 * 8
    first = step // 8 * 8

    @pl.when(step < whole_tiles)
    def take_tile():
        rows = pl.ds(pl.multiple_of(first, 8), 8)
        copy = pltpu.make_async_copy(gate_hbm.at[rows], held, sem)
        copy.start()
        copy.wait()

    if steps > whole_tiles:

        @pl.when(step >= whole_tiles)
        def take_rest():
            copy = pltpu.make_async_copy(
                gate_hbm.at[whole_tiles:steps], held.at[0 : steps - whole_tiles], sem
            )
            copy.start()
            copy.wait()

    gate = held[pl.ds(step - first, 1), :]
    high = gate.astype(jnp.bfloat16).astype(jnp.float32)
    middle = (gate - high).astype(jnp.bfloat16).astype(jnp.float32)
    low = gate - high - middle
    parts = jnp.concatenate([high, middle, low, jnp.zeros((5, gate.shape[1]), jnp.float32)], axis=0)
    out_ref[...] = jnp.concatenate([h_ref[0].astype(jnp.float32), parts], axis=0).astype(jnp.bfloat16)


def partner(here, distance, groups):
    return here ^ distance if groups & (groups - 1) == 0 else (here + groups - distance) % groups


def distances(groups):
    return range(groups - 1, 0, -1)


def hand_over(group, groups, x_ref, out_ref, lanes=slice(None)):
    wide = x_ref.shape[1] // 3
    rows = out_ref.shape[1]
    half = rows // 2
    for part in range(2):
        first = pl.multiple_of(turned(group, groups) * rows + mixed(part, 2) * half, half)
        for kind in range(2):
            out_ref[kind, part * half : (part + 1) * half, lanes] = x_ref[
                pl.ds(first, half), (kind + 1) * wide : (kind + 2) * wide
            ]


def attend_kernel(groups, pattern_ref, x_ref, after_ref, out_hbm, *refs):
    *hand_refs, held, sems = refs
    wide = held.shape[2]
    rows = held.shape[1]
    across = (groups - 1) * rows
    factor = math.log2(math.e) / math.sqrt(HD)
    here = lax.axis_index("tm")
    lane = lax.broadcasted_iota(jnp.int32, (1, across), 1)
    ends, kept = [], []
    for source in range(groups):
        first = max(source, 1)
        ends.append(min(across, -(-(groups - first) * rows // 128) * 128))
        chosen = jnp.zeros((1, across), jnp.int32)
        for group in range(first, groups):
            start = (groups - 1 - group) * rows
            flag = pattern_ref[group : group + 1, source : source + 1]
            chosen = jnp.where((lane >= start) & (lane < start + rows), flag, chosen)
        kept.append(chosen[:, : ends[-1]] > 0)

    def take(group, first):
        start = turned(group, groups) * rows
        return x_ref[start : start + rows, first : first + HD]

    copies = []

    def send(group):
        for place in (group - 1, groups - 1) if group == groups - 1 else (group - 1,):
            copies.append(
                pltpu.make_async_copy(
                    held.at[group - 1], out_hbm.at[place * rows : (place + 1) * rows], sems.at[place]
                )
            )
            copies[-1].start()

    def spread(row, fill):
        rest = across - row.shape[1]
        return jnp.concatenate([row, jnp.full((1, rest), fill, row.dtype)], axis=1) if rest else row

    for head in range(0, wide, HD):
        query = jnp.concatenate(
            [take(group, head) for group in range(groups - 1, 0, -1)], axis=0
        )
        query = jnp.transpose(query)
        value = jnp.transpose(
            jnp.concatenate([take(group, 2 * wide + head) for group in range(groups)], axis=0)
        )
        scores, highest = [], None
        for source in range(groups):
            key = take(source, wide + head)
            scores.append(
                jnp.dot(key, query[:, : ends[source]], preferred_element_type=jnp.float32)
            )
            peak = jnp.where(kept[source], jnp.max(scores[-1], axis=0, keepdims=True), -1e30)
            peak = spread(peak, -1e30)
            highest = peak if highest is None else jnp.maximum(highest, peak)
        highest = highest * factor
        total, probs = 0.0, []
        for source in range(groups):
            offset = jnp.where(kept[source], -highest[:, : ends[source]], -1e30)
            raised = jnp.exp2(scores[source] * factor + offset)
            total += spread(jnp.sum(raised, axis=0, keepdims=True), 0.0)
            probs.append(raised.astype(jnp.bfloat16))
        inverse = 1.0 / total
        last = head + HD == wide
        start, left, waiting = 0, None, groups - 1
        for source in range(groups - 1, 0, -1):
            stop = ends[source]
            if stop > start:
                numer = jnp.dot(
                    value[:, : (source + 1) * rows],
                    jnp.concatenate([p[:, start:stop] for p in probs[: source + 1]], axis=0),
                    preferred_element_type=jnp.float32,
                )
                result = jnp.transpose(numer * inverse[:, start:stop])
                left = result if left is None else jnp.concatenate([left, result], axis=0)
                start = stop
            while left is not None and left.shape[0] >= rows:
                held[waiting - 1, :, head : head + HD] = left[:rows].astype(jnp.bfloat16)
                left = left[rows:] if left.shape[0] > rows else None
                if last:
                    send(waiting)
                waiting -= 1
    for distance, hand_ref in zip(distances(groups), hand_refs):
        hand_over(lax.rem(partner(here, distance, groups) + 1, groups), groups, x_ref, hand_ref)
    for copy in copies:
        copy.wait()


def lanes_of(distance, groups, here, wide):
    source = partner(here, groups - distance if groups & (groups - 1) else distance, groups)
    return pl.ds(pl.multiple_of(source * wide, wide), wide)


def cache_kernel(groups, x_ref, hand_ref, out_ref):
    wide = x_ref.shape[1] // 3
    here = lax.axis_index("tm")
    out_ref[...] = jnp.zeros_like(out_ref)

    @pl.when(here < groups - 1)
    def place():
        hand_over(here + 1, groups, x_ref, out_ref.at[0], lanes_of(0, groups, here, wide))
        out_ref[0, :, :, lanes_of(distances(groups)[0], groups, here, wide)] = hand_ref[...]


def cache_rest_kernel(groups, begun_hbm, after_ref, *refs):
    *hand_refs, out_hbm, sems = refs
    here = lax.axis_index("tm")

    @pl.when(here < groups - 1)
    def place():
        copies = [
            pltpu.make_async_copy(
                block, out_hbm.at[0, :, :, lanes_of(distance, groups, here, block.shape[2])], sems.at[index]
            )
            for index, (distance, block) in enumerate(zip(distances(groups)[1:], hand_refs))
        ]
        for copy in copies:
            copy.start()
        for copy in copies:
            copy.wait()


def update_kernel(seq_count, tm_count, att_ref, moved_ref, fresh_ref, after_ref, out_ref):
    tok = out_ref.shape[1]
    wide = att_ref.shape[1]
    count = att_ref.shape[0] // tok
    last = lax.axis_index("tm") == tm_count - 1

    @pl.when(last)
    def take_fresh():
        out_ref[0] = fresh_ref[...]

    @pl.when(jnp.logical_not(last))
    def take_update():
        for pair in range(count // 2):
            rows = att_ref[2 * pair * tok : 2 * (pair + 1) * tok, :].astype(jnp.float32)
            for half in range(2):
                source = 2 * pair + half
                start = (mixed(source % seq_count, seq_count) * tm_count + source // seq_count) * wide
                moved = moved_ref[:, start : start + wide].astype(jnp.float32)
                gate = (moved[tok : tok + 1] + moved[tok + 1 : tok + 2]) + moved[tok + 2 : tok + 3]
                result = moved[:tok] + gate * rows[half * tok : (half + 1) * tok]
                out_ref[0, :, start : start + wide] = result.astype(jnp.bfloat16)


def whole(space=VMEM):
    return pl.BlockSpec(memory_space=space)


def run(kernel, name, outs, specs, operands, flops=0, scratch=(), aliases={}):
    def size(a):
        return math.prod(a.shape) * jnp.dtype(a.dtype).itemsize

    moved = sum(map(size, operands)) + sum(map(size, outs))
    results = pl.pallas_call(
        kernel,
        out_shape=outs,
        in_specs=specs,
        out_specs=[whole(getattr(a, "memory_space", VMEM)) for a in outs],
        scratch_shapes=scratch,
        input_output_aliases=aliases,
        compiler_params=pltpu.CompilerParams(vmem_limit_bytes=4 * moved + (4 << 20)),
        cost_estimate=pl.CostEstimate(flops=flops, bytes_accessed=moved, transcendentals=0),
        name=name,
    )(*operands)
    return results if len(outs) > 1 else results[0]


def spread_body(queries, keys_proj, values, hidden, fresh_latent, gate_table, noise_step, pattern):
    tm_count, seq_count = lax.axis_size("tm"), lax.axis_size("seq")
    count = tm_count * seq_count
    _, tok, width = queries.shape
    wide = width // count
    group_tok = tok * seq_count
    kind = queries.dtype
    DMA = pltpu.SemaphoreType.DMA
    parts = 4 if seq_count % 8 == 0 else 2

    packed = run(
        functools.partial(pack_kernel, seq_count, parts),
        "pack",
        [HBM((count * tok, 3 * wide), kind)],
        [whole(HBM)] * 3,
        [pltpu.with_memory_space_constraint(a, HBM) for a in (queries, keys_proj, values)],
        scratch=[
            VMEM((3, tok, width), kind),
            VMEM((count * tok, 3 * wide), kind),
            DMA((parts, 3)),
            DMA((parts, tm_count)),
        ],
    )
    back = [tm * seq_count + mixed(s, seq_count) for tm in range(tm_count) for s in range(seq_count)]
    half = len(back) // 2
    exchange = functools.partial(
        lax.all_to_all, axis_name=BOTH, split_axis=0, concat_axis=0, tiled=True
    )
    exchanged = exchange(packed, axis_index_groups=[back[half:] + back[:half]])

    residual = run(
        residual_kernel,
        "residual",
        [VMEM((tok + 8, width), kind)],
        [whole(SMEM), whole(), whole(HBM), whole(HBM)],
        (
            noise_step,
            hidden,
            pltpu.with_memory_space_constraint(gate_table, HBM),
            pltpu.with_memory_space_constraint(packed, HBM),
        ),
        scratch=[VMEM((8, width), jnp.float32), DMA],
    )
    moved = shifted(residual, "tm", -1)

    attended, *hands = run(
        functools.partial(attend_kernel, tm_count),
        "attend",
        [HBM((count * tok, wide), kind)] + [VMEM((2, group_tok, wide), kind)] * (tm_count - 1),
        [whole(), whole(), whole(pl.ANY)],
        (pattern, exchanged, moved),
        flops=2 * count * tok * count * tok * wide,
        scratch=[VMEM((tm_count - 1, group_tok, wide), kind), DMA((tm_count,))],
    )
    returned = exchange(attended, axis_index_groups=[back])
    handed = []
    for distance, hand in zip(distances(tm_count), hands):
        route = [(i, partner(i, distance, tm_count)) for i in range(tm_count)]
        handed.append(lax.ppermute(hand, "tm", [(i, j) for i, j in route if j < tm_count - 1]))

    first, *rest = handed
    begun = run(
        functools.partial(cache_kernel, tm_count),
        "cache",
        [jax.ShapeDtypeStruct((1, 2, group_tok, tm_count * wide), kind)],
        [whole()] * 2,
        (exchanged, first),
    )
    begun = pltpu.with_memory_space_constraint(begun, HBM)
    advanced = run(
        functools.partial(update_kernel, seq_count, tm_count),
        "update",
        [jax.ShapeDtypeStruct((1, tok, width), kind)],
        [whole()] * 3 + [whole(HBM)],
        (returned, moved, fresh_latent, begun),
    )
    next_cache = run(
        functools.partial(cache_rest_kernel, tm_count),
        "cache_rest",
        [HBM(begun.shape, kind)],
        [whole(HBM)] * 2 + [whole()] * len(rest),
        (begun, pltpu.with_memory_space_constraint(advanced, HBM), *rest),
        scratch=[DMA((len(rest),))],
        aliases={0: 0},
    )
    return (advanced, next_cache)


def absorb(state, query_heads, key_piece, value_piece, scale_factor):
    accum, totals, highest = state
    row_count, head_count, head_dim = query_heads.shape
    key_heads = key_piece.reshape(key_piece.shape[0], head_count, head_dim)
    value_heads = value_piece.reshape(value_piece.shape[0], head_count, head_dim)
    scores = (
        jnp.einsum("qhd,khd->qhk", query_heads, key_heads, preferred_element_type=jnp.float32)
        * scale_factor
    )
    raised = jnp.maximum(highest, jnp.max(scores, axis=-1))
    fade = jnp.exp(highest - raised)
    weights = jnp.exp(scores - raised[..., None])
    totals = totals * fade + jnp.sum(weights, axis=-1)
    accum = accum * fade[..., None] + jnp.einsum(
        "qhk,khd->qhd",
        weights.astype(jnp.bfloat16),
        value_heads,
        preferred_element_type=jnp.float32,
    )
    return (accum, totals, raised)


def gather_body(queries, keys_proj, values, hidden, fresh_latent, gate_table, noise_step, pattern):
    group_index = lax.axis_index("tm")
    final_index = lax.axis_size("tm") - 1
    query_tok, key_tok, value_tok = (
        lax.all_to_all(queries[0], "seq", split_axis=1, concat_axis=0, tiled=True),
        lax.all_to_all(keys_proj[0], "seq", split_axis=1, concat_axis=0, tiled=True),
        lax.all_to_all(values[0], "seq", split_axis=1, concat_axis=0, tiled=True),
    )
    row_count, local_width = query_tok.shape
    head_count = local_width // HD
    query_heads = query_tok.reshape(row_count, head_count, HD)
    scale_factor = 1.0 / math.sqrt(HD)
    reach = lax.dynamic_index_in_dim(pattern, group_index, 0, keepdims=False)
    start_state = (
        jnp.zeros((row_count, head_count, HD), jnp.float32),
        jnp.zeros((row_count, head_count), jnp.float32),
        jnp.full((row_count, head_count), -1e30, jnp.float32),
    )

    def one_block(current, inputs):
        key_block, value_block, flag = inputs
        return (
            lax.cond(
                flag > 0,
                lambda state: absorb(state, query_heads, key_block, value_block, scale_factor),
                lambda state: state,
                current,
            ),
            None,
        )

    key_piece = lax.all_gather(key_tok, "tm", axis=0, tiled=False)
    value_piece = lax.all_gather(value_tok, "tm", axis=0, tiled=False)
    state, unused = lax.scan(one_block, start_state, (key_piece, value_piece, reach))
    cache_keys, cache_values = shifted((key_tok, value_tok), "tm", -1)
    accum, totals, highest = state
    attended_head = (accum / totals[..., None]).reshape(row_count, local_width).astype(jnp.bfloat16)
    attended = lax.all_to_all(attended_head, "seq", split_axis=0, concat_axis=1, tiled=True)
    gate_row = lax.dynamic_index_in_dim(gate_table, noise_step[0], 0, keepdims=False)
    updated = (
        hidden[0].astype(jnp.float32) + gate_row[None, :] * attended.astype(jnp.float32)
    ).astype(jnp.bfloat16)
    moved = shifted(updated, "tm", -1)
    advanced = jnp.where(group_index == final_index, fresh_latent, moved)[None]
    next_cache = jnp.stack([cache_keys, cache_values], axis=0)[None]
    return (advanced, next_cache)


def body(queries, *others):
    tm_count, seq_count = lax.axis_size("tm"), lax.axis_size("seq")
    _, tok, width = queries.shape
    count = tm_count * seq_count
    even = width % (count * HD) == 0 and tok % 8 == 0 and seq_count % 4 == 0 and tm_count > 2 and tm_count % 2 == 0
    return (spread_body if even else gather_body)(queries, *others)


def solution(mesh):
    placed = (
        P("tm", "seq", None),
        P("tm", "seq", None),
        P("tm", "seq", None),
        P("tm", "seq", None),
        P("seq", None),
        P(),
        P("tm"),
        P(),
    )
    return jax.shard_map(
        body,
        mesh=mesh,
        in_specs=placed,
        out_specs=(P("tm", "seq", None), P("tm", None, None, "seq")),
        check_vma=False,
    )
```

```python
import functools
import math

import jax
import jax.numpy as jnp
from jax import lax
from jax.experimental import pallas as pl
from jax.experimental.pallas import tpu as pltpu
from jax.sharding import PartitionSpec as P

HD = 128
BOTH = ("tm", "seq")
VMEM = pltpu.VMEM
SMEM = pltpu.SMEM
HBM = pltpu.HBM


def shifted(block, axis, distance):
    devices = range(lax.axis_size(axis))
    route = [(i - distance, i) for i in devices if i - distance in devices]
    return lax.ppermute(block, axis, route)


def mixed(index, count):
    return (index + count // 2) % count


def pair_place(group, pair, pairs):
    return pair + group % 2 * (pairs - 1 - 2 * pair)


def out_order(tm_count, seq_count):
    pairs = seq_count // 2
    return [
        (tm, 2 * pair_place(tm, pair, pairs) + member)
        for tm in range(tm_count)
        for pair in range(pairs)
        for member in range(2)
    ]


def pack_kernel(seq_count, parts, q_hbm, k_hbm, v_hbm, out_hbm, held, block, in_sems, out_sems):
    tok, width = held.shape[1:]
    wide = out_hbm.shape[1] // 3
    count = out_hbm.shape[0] // tok
    tm_count = count // seq_count
    span, members = width // parts, seq_count // parts
    order = out_order(tm_count, seq_count)
    copies = []
    for part in range(parts):
        columns = slice(part * span, (part + 1) * span)
        for place, ref in enumerate((q_hbm, k_hbm, v_hbm)):
            copies.append(
                pltpu.make_async_copy(
                    ref.at[0, :, columns], held.at[place, :, columns], in_sems.at[part, place]
                )
            )
            copies[-1].start()
    outs = []
    for part in range(parts):
        for place in range(3):
            copies[3 * part + place].wait()
        for tm in range(tm_count):
            for seq in range(part * members, (part + 1) * members, 2):
                first = order.index((tm, seq)) * tok
                for place in range(3):
                    rows = []
                    for member in (seq, seq + 1):
                        start = (member * tm_count + tm) * wide
                        rows.append(held[place, :, start : start + wide].astype(jnp.float32))
                    block[first : first + 2 * tok, place * wide : (place + 1) * wide] = jnp.concatenate(
                        rows, axis=0
                    ).astype(jnp.bfloat16)
            first = order.index((tm, part * members)) * tok
            rows = slice(first, first + members * tok)
            outs.append(
                pltpu.make_async_copy(block.at[rows], out_hbm.at[rows], out_sems.at[part, tm])
            )
            outs[-1].start()
    for out in outs:
        out.wait()


def residual_kernel(noise_ref, h_ref, gate_hbm, after_ref, out_ref, held, sem):
    step = noise_ref[0]
    steps = gate_hbm.shape[0]
    whole_tiles = steps // 8 * 8
    first = step // 8 * 8

    @pl.when(step < whole_tiles)
    def take_tile():
        rows = pl.ds(pl.multiple_of(first, 8), 8)
        copy = pltpu.make_async_copy(gate_hbm.at[rows], held, sem)
        copy.start()
        copy.wait()

    if steps > whole_tiles:

        @pl.when(step >= whole_tiles)
        def take_rest():
            copy = pltpu.make_async_copy(
                gate_hbm.at[whole_tiles:steps], held.at[0 : steps - whole_tiles], sem
            )
            copy.start()
            copy.wait()

    gate = held[pl.ds(step - first, 1), :]
    high = gate.astype(jnp.bfloat16).astype(jnp.float32)
    middle = (gate - high).astype(jnp.bfloat16).astype(jnp.float32)
    low = gate - high - middle
    parts = jnp.concatenate([high, middle, low, jnp.zeros((5, gate.shape[1]), jnp.float32)], axis=0)
    out_ref[...] = jnp.concatenate([h_ref[0].astype(jnp.float32), parts], axis=0).astype(jnp.bfloat16)


def partner(here, distance, groups):
    return here ^ distance if groups & (groups - 1) == 0 else (here + groups - distance) % groups


def distances(groups):
    return range(groups - 1, 0, -1)


def hand_over(group, seq_count, x_ref, out_ref, lanes=slice(None)):
    wide = x_ref.shape[1] // 3
    pairs = seq_count // 2
    step = out_ref.shape[1] // pairs
    for pair in range(pairs):
        first = pl.multiple_of((group * pairs + pair_place(group, pair, pairs)) * step, step)
        for kind in range(2):
            out_ref[kind, pair * step : (pair + 1) * step, lanes] = x_ref[
                pl.ds(first, step), (kind + 1) * wide : (kind + 2) * wide
            ]


def attend_kernel(groups, seq_count, pattern_ref, x_ref, after_ref, out_hbm, *refs):
    *hand_refs, held, sems = refs
    wide = held.shape[2]
    rows = held.shape[1]
    pairs = seq_count // 2
    step = rows // pairs
    across = (groups - 1) * rows
    factor = math.log2(math.e) / math.sqrt(HD)
    here = lax.axis_index("tm")
    lane = lax.broadcasted_iota(jnp.int32, (1, across), 1)
    ends, kept = [], []
    for source in range(groups):
        first = max(source, 1)
        ends.append(min(across, -(-(groups - first) * rows // 128) * 128))
        chosen = jnp.zeros((1, across), jnp.int32)
        for group in range(first, groups):
            start = (groups - 1 - group) * rows
            flag = pattern_ref[group : group + 1, source : source + 1]
            chosen = jnp.where((lane >= start) & (lane < start + rows), flag, chosen)
        kept.append(chosen[:, : ends[-1]] > 0)

    def take(group, first):
        return x_ref[group * rows : (group + 1) * rows, first : first + HD]

    copies = []

    def send(group):
        for place in (group - 1, groups - 1) if group == groups - 1 else (group - 1,):
            copies.append(
                pltpu.make_async_copy(
                    held.at[group - 1], out_hbm.at[place * rows : (place + 1) * rows], sems.at[place]
                )
            )
            copies[-1].start()

    def spread(row, fill):
        rest = across - row.shape[1]
        return jnp.concatenate([row, jnp.full((1, rest), fill, row.dtype)], axis=1) if rest else row

    for head in range(0, wide, HD):
        query = jnp.concatenate(
            [take(group, head) for group in range(groups - 1, 0, -1)], axis=0
        )
        query = jnp.transpose(query)
        value = jnp.transpose(
            jnp.concatenate([take(group, 2 * wide + head) for group in range(groups)], axis=0)
        )
        scores, highest = [], None
        for source in range(groups):
            key = take(source, wide + head)
            scores.append(
                jnp.dot(key, query[:, : ends[source]], preferred_element_type=jnp.float32)
            )
            peak = jnp.where(kept[source], jnp.max(scores[-1], axis=0, keepdims=True), -1e30)
            peak = spread(peak, -1e30)
            highest = peak if highest is None else jnp.maximum(highest, peak)
        highest = highest * factor
        total, probs = 0.0, []
        for source in range(groups):
            offset = jnp.where(kept[source], -highest[:, : ends[source]], -1e30)
            raised = jnp.exp2(scores[source] * factor + offset)
            total += spread(jnp.sum(raised, axis=0, keepdims=True), 0.0)
            probs.append(raised.astype(jnp.bfloat16))
        inverse = 1.0 / total
        last = head + HD == wide
        start, left, waiting = 0, None, groups - 1
        for source in range(groups - 1, 0, -1):
            stop = ends[source]
            if stop > start:
                numer = jnp.dot(
                    value[:, : (source + 1) * rows],
                    jnp.concatenate([p[:, start:stop] for p in probs[: source + 1]], axis=0),
                    preferred_element_type=jnp.float32,
                )
                result = jnp.transpose(numer * inverse[:, start:stop])
                left = result if left is None else jnp.concatenate([left, result], axis=0)
                start = stop
            while left is not None and left.shape[0] >= rows:
                ready = left[:rows].astype(jnp.bfloat16)
                for pair in range(pairs):
                    at = pair_place(waiting, pair, pairs) * step
                    to = mixed(2 * pair, seq_count) // 2 * step
                    held[waiting - 1, to : to + step, head : head + HD] = ready[at : at + step]
                left = left[rows:] if left.shape[0] > rows else None
                if last:
                    send(waiting)
                waiting -= 1
    for distance, hand_ref in zip(distances(groups), hand_refs):
        hand_over(lax.rem(partner(here, distance, groups) + 1, groups), seq_count, x_ref, hand_ref)
    for copy in copies:
        copy.wait()


def lanes_of(distance, groups, here, wide):
    source = partner(here, groups - distance if groups & (groups - 1) else distance, groups)
    return pl.ds(pl.multiple_of(source * wide, wide), wide)


def cache_kernel(groups, seq_count, x_ref, hand_ref, out_ref):
    wide = x_ref.shape[1] // 3
    here = lax.axis_index("tm")
    out_ref[...] = jnp.zeros_like(out_ref)

    @pl.when(here < groups - 1)
    def place():
        hand_over(here + 1, seq_count, x_ref, out_ref.at[0], lanes_of(0, groups, here, wide))
        out_ref[0, :, :, lanes_of(distances(groups)[0], groups, here, wide)] = hand_ref[...]


def cache_rest_kernel(groups, begun_hbm, after_ref, *refs):
    *hand_refs, out_hbm, sems = refs
    here = lax.axis_index("tm")

    @pl.when(here < groups - 1)
    def place():
        copies = [
            pltpu.make_async_copy(
                block, out_hbm.at[0, :, :, lanes_of(distance, groups, here, block.shape[2])], sems.at[index]
            )
            for index, (distance, block) in enumerate(zip(distances(groups)[1:], hand_refs))
        ]
        for copy in copies:
            copy.start()
        for copy in copies:
            copy.wait()


def update_kernel(seq_count, tm_count, att_ref, moved_ref, fresh_ref, after_ref, out_ref):
    tok = out_ref.shape[1]
    wide = att_ref.shape[1]
    count = att_ref.shape[0] // tok
    last = lax.axis_index("tm") == tm_count - 1

    @pl.when(last)
    def take_fresh():
        out_ref[0] = fresh_ref[...]

    @pl.when(jnp.logical_not(last))
    def take_update():
        for pair in range(count // 2):
            rows = att_ref[2 * pair * tok : 2 * (pair + 1) * tok, :].astype(jnp.float32)
            for half in range(2):
                source = 2 * pair + half
                start = (mixed(source % seq_count, seq_count) * tm_count + source // seq_count) * wide
                moved = moved_ref[:, start : start + wide].astype(jnp.float32)
                gate = (moved[tok : tok + 1] + moved[tok + 1 : tok + 2]) + moved[tok + 2 : tok + 3]
                result = moved[:tok] + gate * rows[half * tok : (half + 1) * tok]
                out_ref[0, :, start : start + wide] = result.astype(jnp.bfloat16)


def whole(space=VMEM):
    return pl.BlockSpec(memory_space=space)


def run(kernel, name, outs, specs, operands, flops=0, scratch=(), aliases={}):
    def size(a):
        return math.prod(a.shape) * jnp.dtype(a.dtype).itemsize

    moved = sum(map(size, operands)) + sum(map(size, outs))
    results = pl.pallas_call(
        kernel,
        out_shape=outs,
        in_specs=specs,
        out_specs=[whole(getattr(a, "memory_space", VMEM)) for a in outs],
        scratch_shapes=scratch,
        input_output_aliases=aliases,
        compiler_params=pltpu.CompilerParams(vmem_limit_bytes=4 * moved + (4 << 20)),
        cost_estimate=pl.CostEstimate(flops=flops, bytes_accessed=moved, transcendentals=0),
        name=name,
    )(*operands)
    return results if len(outs) > 1 else results[0]


def spread_body(queries, keys_proj, values, hidden, fresh_latent, gate_table, noise_step, pattern):
    tm_count, seq_count = lax.axis_size("tm"), lax.axis_size("seq")
    count = tm_count * seq_count
    _, tok, width = queries.shape
    wide = width // count
    group_tok = tok * seq_count
    kind = queries.dtype
    DMA = pltpu.SemaphoreType.DMA
    parts = seq_count // 2

    packed = run(
        functools.partial(pack_kernel, seq_count, parts),
        "pack",
        [HBM((count * tok, 3 * wide), kind)],
        [whole(HBM)] * 3,
        [pltpu.with_memory_space_constraint(a, HBM) for a in (queries, keys_proj, values)],
        scratch=[
            VMEM((3, tok, width), kind),
            VMEM((count * tok, 3 * wide), kind),
            DMA((parts, 3)),
            DMA((parts, tm_count)),
        ],
    )
    back = [tm * seq_count + mixed(s, seq_count) for tm in range(tm_count) for s in range(seq_count)]
    out = [tm * seq_count + index for tm, index in out_order(tm_count, seq_count)]
    exchange = functools.partial(
        lax.all_to_all, axis_name=BOTH, split_axis=0, concat_axis=0, tiled=True
    )
    exchanged = exchange(packed, axis_index_groups=[out])

    residual = run(
        residual_kernel,
        "residual",
        [VMEM((tok + 8, width), kind)],
        [whole(SMEM), whole(), whole(HBM), whole(HBM)],
        (
            noise_step,
            hidden,
            pltpu.with_memory_space_constraint(gate_table, HBM),
            pltpu.with_memory_space_constraint(packed, HBM),
        ),
        scratch=[VMEM((8, width), jnp.float32), DMA],
    )
    moved = shifted(residual, "tm", -1)

    attended, *hands = run(
        functools.partial(attend_kernel, tm_count, seq_count),
        "attend",
        [HBM((count * tok, wide), kind)] + [VMEM((2, group_tok, wide), kind)] * (tm_count - 1),
        [whole(), whole(), whole(pl.ANY)],
        (pattern, exchanged, moved),
        flops=2 * count * tok * count * tok * wide,
        scratch=[VMEM((tm_count - 1, group_tok, wide), kind), DMA((tm_count,))],
    )
    returned = exchange(attended, axis_index_groups=[back])
    handed = []
    for distance, hand in zip(distances(tm_count), hands):
        route = [(i, partner(i, distance, tm_count)) for i in range(tm_count)]
        handed.append(lax.ppermute(hand, "tm", [(i, j) for i, j in route if j < tm_count - 1]))

    first, *rest = handed
    begun = run(
        functools.partial(cache_kernel, tm_count, seq_count),
        "cache",
        [jax.ShapeDtypeStruct((1, 2, group_tok, tm_count * wide), kind)],
        [whole()] * 2,
        (exchanged, first),
    )
    begun = pltpu.with_memory_space_constraint(begun, HBM)
    advanced = run(
        functools.partial(update_kernel, seq_count, tm_count),
        "update",
        [jax.ShapeDtypeStruct((1, tok, width), kind)],
        [whole()] * 3 + [whole(HBM)],
        (returned, moved, fresh_latent, begun),
    )
    next_cache = run(
        functools.partial(cache_rest_kernel, tm_count),
        "cache_rest",
        [HBM(begun.shape, kind)],
        [whole(HBM)] * 2 + [whole()] * len(rest),
        (begun, pltpu.with_memory_space_constraint(advanced, HBM), *rest),
        scratch=[DMA((len(rest),))],
        aliases={0: 0},
    )
    return (advanced, next_cache)


def absorb(state, query_heads, key_piece, value_piece, scale_factor):
    accum, totals, highest = state
    row_count, head_count, head_dim = query_heads.shape
    key_heads = key_piece.reshape(key_piece.shape[0], head_count, head_dim)
    value_heads = value_piece.reshape(value_piece.shape[0], head_count, head_dim)
    scores = (
        jnp.einsum("qhd,khd->qhk", query_heads, key_heads, preferred_element_type=jnp.float32)
        * scale_factor
    )
    raised = jnp.maximum(highest, jnp.max(scores, axis=-1))
    fade = jnp.exp(highest - raised)
    weights = jnp.exp(scores - raised[..., None])
    totals = totals * fade + jnp.sum(weights, axis=-1)
    accum = accum * fade[..., None] + jnp.einsum(
        "qhk,khd->qhd",
        weights.astype(jnp.bfloat16),
        value_heads,
        preferred_element_type=jnp.float32,
    )
    return (accum, totals, raised)


def gather_body(queries, keys_proj, values, hidden, fresh_latent, gate_table, noise_step, pattern):
    group_index = lax.axis_index("tm")
    final_index = lax.axis_size("tm") - 1
    query_tok, key_tok, value_tok = (
        lax.all_to_all(queries[0], "seq", split_axis=1, concat_axis=0, tiled=True),
        lax.all_to_all(keys_proj[0], "seq", split_axis=1, concat_axis=0, tiled=True),
        lax.all_to_all(values[0], "seq", split_axis=1, concat_axis=0, tiled=True),
    )
    row_count, local_width = query_tok.shape
    head_count = local_width // HD
    query_heads = query_tok.reshape(row_count, head_count, HD)
    scale_factor = 1.0 / math.sqrt(HD)
    reach = lax.dynamic_index_in_dim(pattern, group_index, 0, keepdims=False)
    start_state = (
        jnp.zeros((row_count, head_count, HD), jnp.float32),
        jnp.zeros((row_count, head_count), jnp.float32),
        jnp.full((row_count, head_count), -1e30, jnp.float32),
    )

    def one_block(current, inputs):
        key_block, value_block, flag = inputs
        return (
            lax.cond(
                flag > 0,
                lambda state: absorb(state, query_heads, key_block, value_block, scale_factor),
                lambda state: state,
                current,
            ),
            None,
        )

    key_piece = lax.all_gather(key_tok, "tm", axis=0, tiled=False)
    value_piece = lax.all_gather(value_tok, "tm", axis=0, tiled=False)
    state, unused = lax.scan(one_block, start_state, (key_piece, value_piece, reach))
    cache_keys, cache_values = shifted((key_tok, value_tok), "tm", -1)
    accum, totals, highest = state
    attended_head = (accum / totals[..., None]).reshape(row_count, local_width).astype(jnp.bfloat16)
    attended = lax.all_to_all(attended_head, "seq", split_axis=0, concat_axis=1, tiled=True)
    gate_row = lax.dynamic_index_in_dim(gate_table, noise_step[0], 0, keepdims=False)
    updated = (
        hidden[0].astype(jnp.float32) + gate_row[None, :] * attended.astype(jnp.float32)
    ).astype(jnp.bfloat16)
    moved = shifted(updated, "tm", -1)
    advanced = jnp.where(group_index == final_index, fresh_latent, moved)[None]
    next_cache = jnp.stack([cache_keys, cache_values], axis=0)[None]
    return (advanced, next_cache)


def body(queries, *others):
    tm_count, seq_count = lax.axis_size("tm"), lax.axis_size("seq")
    _, tok, width = queries.shape
    count = tm_count * seq_count
    even = width % (count * HD) == 0 and tok % 8 == 0 and seq_count % 4 == 0 and tm_count > 2 and tm_count % 2 == 0
    return (spread_body if even else gather_body)(queries, *others)


def solution(mesh):
    placed = (
        P("tm", "seq", None),
        P("tm", "seq", None),
        P("tm", "seq", None),
        P("tm", "seq", None),
        P("seq", None),
        P(),
        P("tm"),
        P(),
    )
    return jax.shard_map(
        body,
        mesh=mesh,
        in_specs=placed,
        out_specs=(P("tm", "seq", None), P("tm", None, None, "seq")),
        check_vma=False,
    )
```

```python
import functools
import math

import jax
import jax.numpy as jnp
from jax import lax
from jax.experimental import pallas as pl
from jax.experimental.pallas import tpu as pltpu
from jax.sharding import PartitionSpec as P

HD = 128
BOTH = ("tm", "seq")
VMEM = pltpu.VMEM
SMEM = pltpu.SMEM
HBM = pltpu.HBM


def shifted(block, axis, distance):
    devices = range(lax.axis_size(axis))
    route = [(i - distance, i) for i in devices if i - distance in devices]
    return lax.ppermute(block, axis, route)


def mixed(index, count):
    return (index + count // 2) % count


def pair_place(group, pair, pairs):
    place = (pair + pairs // 2) % pairs
    return place + group % 2 * (pairs - 1 - 2 * place)


def out_order(tm_count, seq_count):
    pairs = seq_count // 2
    return [
        (tm, 2 * pair_place(tm, pair, pairs) + member)
        for tm in range(tm_count)
        for pair in range(pairs)
        for member in range(2)
    ]


def pack_kernel(seq_count, parts, q_hbm, k_hbm, v_hbm, out_hbm, held, block, in_sems, out_sems):
    tok, width = held.shape[1:]
    wide = out_hbm.shape[1] // 3
    count = out_hbm.shape[0] // tok
    tm_count = count // seq_count
    span, members = width // parts, seq_count // parts
    order = out_order(tm_count, seq_count)
    copies = []
    for part in range(parts):
        columns = slice(part * span, (part + 1) * span)
        for place, ref in enumerate((q_hbm, k_hbm, v_hbm)):
            copies.append(
                pltpu.make_async_copy(
                    ref.at[0, :, columns], held.at[place, :, columns], in_sems.at[part, place]
                )
            )
            copies[-1].start()
    outs = []
    for part in range(parts):
        for place in range(3):
            copies[3 * part + place].wait()
        for tm in range(tm_count):
            for seq in range(part * members, (part + 1) * members, 2):
                first = order.index((tm, seq)) * tok
                for place in range(3):
                    rows = []
                    for member in (seq, seq + 1):
                        start = (member * tm_count + tm) * wide
                        rows.append(held[place, :, start : start + wide].astype(jnp.float32))
                    block[first : first + 2 * tok, place * wide : (place + 1) * wide] = jnp.concatenate(
                        rows, axis=0
                    ).astype(jnp.bfloat16)
            first = order.index((tm, part * members)) * tok
            rows = slice(first, first + members * tok)
            outs.append(
                pltpu.make_async_copy(block.at[rows], out_hbm.at[rows], out_sems.at[part, tm])
            )
            outs[-1].start()
    for out in outs:
        out.wait()


def residual_kernel(noise_ref, h_ref, gate_hbm, after_ref, out_ref, held, sem):
    step = noise_ref[0]
    steps = gate_hbm.shape[0]
    whole_tiles = steps // 8 * 8
    first = step // 8 * 8

    @pl.when(step < whole_tiles)
    def take_tile():
        rows = pl.ds(pl.multiple_of(first, 8), 8)
        copy = pltpu.make_async_copy(gate_hbm.at[rows], held, sem)
        copy.start()
        copy.wait()

    if steps > whole_tiles:

        @pl.when(step >= whole_tiles)
        def take_rest():
            copy = pltpu.make_async_copy(
                gate_hbm.at[whole_tiles:steps], held.at[0 : steps - whole_tiles], sem
            )
            copy.start()
            copy.wait()

    gate = held[pl.ds(step - first, 1), :]
    high = gate.astype(jnp.bfloat16).astype(jnp.float32)
    middle = (gate - high).astype(jnp.bfloat16).astype(jnp.float32)
    low = gate - high - middle
    parts = jnp.concatenate([high, middle, low, jnp.zeros((5, gate.shape[1]), jnp.float32)], axis=0)
    out_ref[...] = jnp.concatenate([h_ref[0].astype(jnp.float32), parts], axis=0).astype(jnp.bfloat16)


def partner(here, distance, groups):
    return here ^ distance if groups & (groups - 1) == 0 else (here + groups - distance) % groups


def distances(groups):
    return range(groups - 1, 0, -1)


def hand_over(group, seq_count, x_ref, out_ref, lanes=slice(None)):
    wide = x_ref.shape[1] // 3
    pairs = seq_count // 2
    step = out_ref.shape[1] // pairs
    for pair in range(pairs):
        first = pl.multiple_of((group * pairs + pair_place(group, pair, pairs)) * step, step)
        for kind in range(2):
            out_ref[kind, pair * step : (pair + 1) * step, lanes] = x_ref[
                pl.ds(first, step), (kind + 1) * wide : (kind + 2) * wide
            ]


def attend_kernel(groups, seq_count, pattern_ref, x_ref, after_ref, out_hbm, *refs):
    *hand_refs, held, sems = refs
    wide = held.shape[2]
    rows = held.shape[1]
    pairs = seq_count // 2
    step = rows // pairs
    across = (groups - 1) * rows
    factor = math.log2(math.e) / math.sqrt(HD)
    here = lax.axis_index("tm")
    lane = lax.broadcasted_iota(jnp.int32, (1, across), 1)
    ends, kept = [], []
    for source in range(groups):
        first = max(source, 1)
        ends.append(min(across, -(-(groups - first) * rows // 128) * 128))
        chosen = jnp.zeros((1, across), jnp.int32)
        for group in range(first, groups):
            start = (groups - 1 - group) * rows
            flag = pattern_ref[group : group + 1, source : source + 1]
            chosen = jnp.where((lane >= start) & (lane < start + rows), flag, chosen)
        kept.append(chosen[:, : ends[-1]] > 0)

    def take(group, first):
        return x_ref[group * rows : (group + 1) * rows, first : first + HD]

    copies = []

    def send(group):
        for place in (group - 1, groups - 1) if group == groups - 1 else (group - 1,):
            copies.append(
                pltpu.make_async_copy(
                    held.at[group - 1], out_hbm.at[place * rows : (place + 1) * rows], sems.at[place]
                )
            )
            copies[-1].start()

    def spread(row, fill):
        rest = across - row.shape[1]
        return jnp.concatenate([row, jnp.full((1, rest), fill, row.dtype)], axis=1) if rest else row

    for head in range(0, wide, HD):
        query = jnp.concatenate(
            [take(group, head) for group in range(groups - 1, 0, -1)], axis=0
        )
        query = jnp.transpose(query)
        value = jnp.transpose(
            jnp.concatenate([take(group, 2 * wide + head) for group in range(groups)], axis=0)
        )
        scores, highest = [], None
        for source in range(groups):
            key = take(source, wide + head)
            scores.append(
                jnp.dot(key, query[:, : ends[source]], preferred_element_type=jnp.float32)
            )
            peak = jnp.where(kept[source], jnp.max(scores[-1], axis=0, keepdims=True), -1e30)
            peak = spread(peak, -1e30)
            highest = peak if highest is None else jnp.maximum(highest, peak)
        highest = highest * factor
        total, probs = 0.0, []
        for source in range(groups):
            offset = jnp.where(kept[source], -highest[:, : ends[source]], -1e30)
            raised = jnp.exp2(scores[source] * factor + offset)
            total += spread(jnp.sum(raised, axis=0, keepdims=True), 0.0)
            probs.append(raised.astype(jnp.bfloat16))
        inverse = 1.0 / total
        last = head + HD == wide
        start, left, waiting = 0, None, groups - 1
        for source in range(groups - 1, 0, -1):
            stop = ends[source]
            if stop > start:
                numer = jnp.dot(
                    value[:, : (source + 1) * rows],
                    jnp.concatenate([p[:, start:stop] for p in probs[: source + 1]], axis=0),
                    preferred_element_type=jnp.float32,
                )
                result = jnp.transpose(numer * inverse[:, start:stop])
                left = result if left is None else jnp.concatenate([left, result], axis=0)
                start = stop
            while left is not None and left.shape[0] >= rows:
                ready = left[:rows].astype(jnp.bfloat16)
                for pair in range(pairs):
                    at = pair_place(waiting, pair, pairs) * step
                    to = mixed(2 * pair, seq_count) // 2 * step
                    held[waiting - 1, to : to + step, head : head + HD] = ready[at : at + step]
                left = left[rows:] if left.shape[0] > rows else None
                if last:
                    send(waiting)
                waiting -= 1
    for distance, hand_ref in zip(distances(groups), hand_refs):
        hand_over(lax.rem(partner(here, distance, groups) + 1, groups), seq_count, x_ref, hand_ref)
    for copy in copies:
        copy.wait()


def lanes_of(distance, groups, here, wide):
    source = partner(here, groups - distance if groups & (groups - 1) else distance, groups)
    return pl.ds(pl.multiple_of(source * wide, wide), wide)


def cache_kernel(groups, seq_count, x_ref, hand_ref, out_ref):
    wide = x_ref.shape[1] // 3
    here = lax.axis_index("tm")
    out_ref[...] = jnp.zeros_like(out_ref)

    @pl.when(here < groups - 1)
    def place():
        hand_over(here + 1, seq_count, x_ref, out_ref.at[0], lanes_of(0, groups, here, wide))
        out_ref[0, :, :, lanes_of(distances(groups)[0], groups, here, wide)] = hand_ref[...]


def cache_rest_kernel(groups, begun_hbm, after_ref, *refs):
    *hand_refs, out_hbm, sems = refs
    here = lax.axis_index("tm")

    @pl.when(here < groups - 1)
    def place():
        copies = [
            pltpu.make_async_copy(
                block, out_hbm.at[0, :, :, lanes_of(distance, groups, here, block.shape[2])], sems.at[index]
            )
            for index, (distance, block) in enumerate(zip(distances(groups)[1:], hand_refs))
        ]
        for copy in copies:
            copy.start()
        for copy in copies:
            copy.wait()


def update_kernel(seq_count, tm_count, att_ref, moved_ref, fresh_ref, after_ref, out_ref):
    tok = out_ref.shape[1]
    wide = att_ref.shape[1]
    count = att_ref.shape[0] // tok
    last = lax.axis_index("tm") == tm_count - 1

    @pl.when(last)
    def take_fresh():
        out_ref[0] = fresh_ref[...]

    @pl.when(jnp.logical_not(last))
    def take_update():
        for pair in range(count // 2):
            rows = att_ref[2 * pair * tok : 2 * (pair + 1) * tok, :].astype(jnp.float32)
            for half in range(2):
                source = 2 * pair + half
                start = (mixed(source % seq_count, seq_count) * tm_count + source // seq_count) * wide
                moved = moved_ref[:, start : start + wide].astype(jnp.float32)
                gate = (moved[tok : tok + 1] + moved[tok + 1 : tok + 2]) + moved[tok + 2 : tok + 3]
                result = moved[:tok] + gate * rows[half * tok : (half + 1) * tok]
                out_ref[0, :, start : start + wide] = result.astype(jnp.bfloat16)


def whole(space=VMEM):
    return pl.BlockSpec(memory_space=space)


def run(kernel, name, outs, specs, operands, flops=0, scratch=(), aliases={}):
    def size(a):
        return math.prod(a.shape) * jnp.dtype(a.dtype).itemsize

    moved = sum(map(size, operands)) + sum(map(size, outs))
    results = pl.pallas_call(
        kernel,
        out_shape=outs,
        in_specs=specs,
        out_specs=[whole(getattr(a, "memory_space", VMEM)) for a in outs],
        scratch_shapes=scratch,
        input_output_aliases=aliases,
        compiler_params=pltpu.CompilerParams(vmem_limit_bytes=4 * moved + (4 << 20)),
        cost_estimate=pl.CostEstimate(flops=flops, bytes_accessed=moved, transcendentals=0),
        name=name,
    )(*operands)
    return results if len(outs) > 1 else results[0]


def spread_body(queries, keys_proj, values, hidden, fresh_latent, gate_table, noise_step, pattern):
    tm_count, seq_count = lax.axis_size("tm"), lax.axis_size("seq")
    count = tm_count * seq_count
    _, tok, width = queries.shape
    wide = width // count
    group_tok = tok * seq_count
    kind = queries.dtype
    DMA = pltpu.SemaphoreType.DMA
    parts = seq_count // 2

    packed = run(
        functools.partial(pack_kernel, seq_count, parts),
        "pack",
        [HBM((count * tok, 3 * wide), kind)],
        [whole(HBM)] * 3,
        [pltpu.with_memory_space_constraint(a, HBM) for a in (queries, keys_proj, values)],
        scratch=[
            VMEM((3, tok, width), kind),
            VMEM((count * tok, 3 * wide), kind),
            DMA((parts, 3)),
            DMA((parts, tm_count)),
        ],
    )
    back = [tm * seq_count + mixed(s, seq_count) for tm in range(tm_count) for s in range(seq_count)]
    out = [tm * seq_count + index for tm, index in out_order(tm_count, seq_count)]
    exchange = functools.partial(
        lax.all_to_all, axis_name=BOTH, split_axis=0, concat_axis=0, tiled=True
    )
    exchanged = exchange(packed, axis_index_groups=[out])

    residual = run(
        residual_kernel,
        "residual",
        [VMEM((tok + 8, width), kind)],
        [whole(SMEM), whole(), whole(HBM), whole(HBM)],
        (
            noise_step,
            hidden,
            pltpu.with_memory_space_constraint(gate_table, HBM),
            pltpu.with_memory_space_constraint(packed, HBM),
        ),
        scratch=[VMEM((8, width), jnp.float32), DMA],
    )
    moved = shifted(residual, "tm", -1)

    attended, *hands = run(
        functools.partial(attend_kernel, tm_count, seq_count),
        "attend",
        [HBM((count * tok, wide), kind)] + [VMEM((2, group_tok, wide), kind)] * (tm_count - 1),
        [whole(), whole(), whole(pl.ANY)],
        (pattern, exchanged, moved),
        flops=2 * count * tok * count * tok * wide,
        scratch=[VMEM((tm_count - 1, group_tok, wide), kind), DMA((tm_count,))],
    )
    returned = exchange(attended, axis_index_groups=[back])
    handed = []
    for distance, hand in zip(distances(tm_count), hands):
        route = [(i, partner(i, distance, tm_count)) for i in range(tm_count)]
        handed.append(lax.ppermute(hand, "tm", [(i, j) for i, j in route if j < tm_count - 1]))

    first, *rest = handed
    begun = run(
        functools.partial(cache_kernel, tm_count, seq_count),
        "cache",
        [jax.ShapeDtypeStruct((1, 2, group_tok, tm_count * wide), kind)],
        [whole()] * 2,
        (exchanged, first),
    )
    begun = pltpu.with_memory_space_constraint(begun, HBM)
    advanced = run(
        functools.partial(update_kernel, seq_count, tm_count),
        "update",
        [jax.ShapeDtypeStruct((1, tok, width), kind)],
        [whole()] * 3 + [whole(HBM)],
        (returned, moved, fresh_latent, begun),
    )
    next_cache = run(
        functools.partial(cache_rest_kernel, tm_count),
        "cache_rest",
        [HBM(begun.shape, kind)],
        [whole(HBM)] * 2 + [whole()] * len(rest),
        (begun, pltpu.with_memory_space_constraint(advanced, HBM), *rest),
        scratch=[DMA((len(rest),))],
        aliases={0: 0},
    )
    return (advanced, next_cache)


def absorb(state, query_heads, key_piece, value_piece, scale_factor):
    accum, totals, highest = state
    row_count, head_count, head_dim = query_heads.shape
    key_heads = key_piece.reshape(key_piece.shape[0], head_count, head_dim)
    value_heads = value_piece.reshape(value_piece.shape[0], head_count, head_dim)
    scores = (
        jnp.einsum("qhd,khd->qhk", query_heads, key_heads, preferred_element_type=jnp.float32)
        * scale_factor
    )
    raised = jnp.maximum(highest, jnp.max(scores, axis=-1))
    fade = jnp.exp(highest - raised)
    weights = jnp.exp(scores - raised[..., None])
    totals = totals * fade + jnp.sum(weights, axis=-1)
    accum = accum * fade[..., None] + jnp.einsum(
        "qhk,khd->qhd",
        weights.astype(jnp.bfloat16),
        value_heads,
        preferred_element_type=jnp.float32,
    )
    return (accum, totals, raised)


def gather_body(queries, keys_proj, values, hidden, fresh_latent, gate_table, noise_step, pattern):
    group_index = lax.axis_index("tm")
    final_index = lax.axis_size("tm") - 1
    query_tok, key_tok, value_tok = (
        lax.all_to_all(queries[0], "seq", split_axis=1, concat_axis=0, tiled=True),
        lax.all_to_all(keys_proj[0], "seq", split_axis=1, concat_axis=0, tiled=True),
        lax.all_to_all(values[0], "seq", split_axis=1, concat_axis=0, tiled=True),
    )
    row_count, local_width = query_tok.shape
    head_count = local_width // HD
    query_heads = query_tok.reshape(row_count, head_count, HD)
    scale_factor = 1.0 / math.sqrt(HD)
    reach = lax.dynamic_index_in_dim(pattern, group_index, 0, keepdims=False)
    start_state = (
        jnp.zeros((row_count, head_count, HD), jnp.float32),
        jnp.zeros((row_count, head_count), jnp.float32),
        jnp.full((row_count, head_count), -1e30, jnp.float32),
    )

    def one_block(current, inputs):
        key_block, value_block, flag = inputs
        return (
            lax.cond(
                flag > 0,
                lambda state: absorb(state, query_heads, key_block, value_block, scale_factor),
                lambda state: state,
                current,
            ),
            None,
        )

    key_piece = lax.all_gather(key_tok, "tm", axis=0, tiled=False)
    value_piece = lax.all_gather(value_tok, "tm", axis=0, tiled=False)
    state, unused = lax.scan(one_block, start_state, (key_piece, value_piece, reach))
    cache_keys, cache_values = shifted((key_tok, value_tok), "tm", -1)
    accum, totals, highest = state
    attended_head = (accum / totals[..., None]).reshape(row_count, local_width).astype(jnp.bfloat16)
    attended = lax.all_to_all(attended_head, "seq", split_axis=0, concat_axis=1, tiled=True)
    gate_row = lax.dynamic_index_in_dim(gate_table, noise_step[0], 0, keepdims=False)
    updated = (
        hidden[0].astype(jnp.float32) + gate_row[None, :] * attended.astype(jnp.float32)
    ).astype(jnp.bfloat16)
    moved = shifted(updated, "tm", -1)
    advanced = jnp.where(group_index == final_index, fresh_latent, moved)[None]
    next_cache = jnp.stack([cache_keys, cache_values], axis=0)[None]
    return (advanced, next_cache)


def body(queries, *others):
    tm_count, seq_count = lax.axis_size("tm"), lax.axis_size("seq")
    _, tok, width = queries.shape
    count = tm_count * seq_count
    even = width % (count * HD) == 0 and tok % 8 == 0 and seq_count % 4 == 0 and tm_count > 2 and tm_count % 2 == 0
    return (spread_body if even else gather_body)(queries, *others)


def solution(mesh):
    placed = (
        P("tm", "seq", None),
        P("tm", "seq", None),
        P("tm", "seq", None),
        P("tm", "seq", None),
        P("seq", None),
        P(),
        P("tm"),
        P(),
    )
    return jax.shard_map(
        body,
        mesh=mesh,
        in_specs=placed,
        out_specs=(P("tm", "seq", None), P("tm", None, None, "seq")),
        check_vma=False,
    )
```

```python
import functools
import math

import jax
import jax.numpy as jnp
from jax import lax
from jax.experimental import pallas as pl
from jax.experimental.pallas import tpu as pltpu
from jax.sharding import PartitionSpec as P

HD = 128
BOTH = ("tm", "seq")
VMEM = pltpu.VMEM
SMEM = pltpu.SMEM
HBM = pltpu.HBM


def shifted(block, axis, distance):
    devices = range(lax.axis_size(axis))
    route = [(i - distance, i) for i in devices if i - distance in devices]
    return lax.ppermute(block, axis, route)


def mixed(index, count):
    return (index + count // 2) % count


def pair_place(group, pair, pairs):
    place = (pair + pairs // 2) % pairs
    return place + group // 2 % 2 * (pairs - 1 - 2 * place)


def out_order(tm_count, seq_count):
    pairs = seq_count // 2
    return [
        (tm, 2 * pair_place(tm, pair, pairs) + member)
        for tm in range(tm_count)
        for pair in range(pairs)
        for member in range(2)
    ]


def pack_kernel(seq_count, parts, q_hbm, k_hbm, v_hbm, out_hbm, held, block, in_sems, out_sems):
    tok, width = held.shape[1:]
    wide = out_hbm.shape[1] // 3
    count = out_hbm.shape[0] // tok
    tm_count = count // seq_count
    span, members = width // parts, seq_count // parts
    order = out_order(tm_count, seq_count)
    copies = []
    for part in range(parts):
        columns = slice(part * span, (part + 1) * span)
        for place, ref in enumerate((q_hbm, k_hbm, v_hbm)):
            copies.append(
                pltpu.make_async_copy(
                    ref.at[0, :, columns], held.at[place, :, columns], in_sems.at[part, place]
                )
            )
            copies[-1].start()
    outs = []
    for part in range(parts):
        for place in range(3):
            copies[3 * part + place].wait()
        for tm in range(tm_count):
            for seq in range(part * members, (part + 1) * members, 2):
                first = order.index((tm, seq)) * tok
                for place in range(3):
                    rows = []
                    for member in (seq, seq + 1):
                        start = (member * tm_count + tm) * wide
                        rows.append(held[place, :, start : start + wide].astype(jnp.float32))
                    block[first : first + 2 * tok, place * wide : (place + 1) * wide] = jnp.concatenate(
                        rows, axis=0
                    ).astype(jnp.bfloat16)
            first = order.index((tm, part * members)) * tok
            rows = slice(first, first + members * tok)
            outs.append(
                pltpu.make_async_copy(block.at[rows], out_hbm.at[rows], out_sems.at[part, tm])
            )
            outs[-1].start()
    for out in outs:
        out.wait()


def residual_kernel(noise_ref, h_ref, gate_hbm, after_ref, out_ref, held, sem):
    step = noise_ref[0]
    steps = gate_hbm.shape[0]
    whole_tiles = steps // 8 * 8
    first = step // 8 * 8

    @pl.when(step < whole_tiles)
    def take_tile():
        rows = pl.ds(pl.multiple_of(first, 8), 8)
        copy = pltpu.make_async_copy(gate_hbm.at[rows], held, sem)
        copy.start()
        copy.wait()

    if steps > whole_tiles:

        @pl.when(step >= whole_tiles)
        def take_rest():
            copy = pltpu.make_async_copy(
                gate_hbm.at[whole_tiles:steps], held.at[0 : steps - whole_tiles], sem
            )
            copy.start()
            copy.wait()

    gate = held[pl.ds(step - first, 1), :]
    high = gate.astype(jnp.bfloat16).astype(jnp.float32)
    middle = (gate - high).astype(jnp.bfloat16).astype(jnp.float32)
    low = gate - high - middle
    parts = jnp.concatenate([high, middle, low, jnp.zeros((5, gate.shape[1]), jnp.float32)], axis=0)
    out_ref[...] = jnp.concatenate([h_ref[0].astype(jnp.float32), parts], axis=0).astype(jnp.bfloat16)


def partner(here, distance, groups):
    return here ^ distance if groups & (groups - 1) == 0 else (here + groups - distance) % groups


def distances(groups):
    return range(groups - 1, 0, -1)


def hand_over(group, seq_count, x_ref, out_ref, lanes=slice(None)):
    wide = x_ref.shape[1] // 3
    pairs = seq_count // 2
    step = out_ref.shape[1] // pairs
    for pair in range(pairs):
        first = pl.multiple_of((group * pairs + pair_place(group, pair, pairs)) * step, step)
        for kind in range(2):
            out_ref[kind, pair * step : (pair + 1) * step, lanes] = x_ref[
                pl.ds(first, step), (kind + 1) * wide : (kind + 2) * wide
            ]


def attend_kernel(groups, seq_count, pattern_ref, x_ref, after_ref, out_hbm, *refs):
    *hand_refs, held, sems = refs
    wide = held.shape[2]
    rows = held.shape[1]
    pairs = seq_count // 2
    step = rows // pairs
    across = (groups - 1) * rows
    factor = math.log2(math.e) / math.sqrt(HD)
    here = lax.axis_index("tm")
    lane = lax.broadcasted_iota(jnp.int32, (1, across), 1)
    ends, kept = [], []
    for source in range(groups):
        first = max(source, 1)
        ends.append(min(across, -(-(groups - first) * rows // 128) * 128))
        chosen = jnp.zeros((1, across), jnp.int32)
        for group in range(first, groups):
            start = (groups - 1 - group) * rows
            flag = pattern_ref[group : group + 1, source : source + 1]
            chosen = jnp.where((lane >= start) & (lane < start + rows), flag, chosen)
        kept.append(chosen[:, : ends[-1]] > 0)

    def take(group, first):
        return x_ref[group * rows : (group + 1) * rows, first : first + HD]

    copies = []

    def send(group):
        for place in (group - 1, groups - 1) if group == groups - 1 else (group - 1,):
            copies.append(
                pltpu.make_async_copy(
                    held.at[group - 1], out_hbm.at[place * rows : (place + 1) * rows], sems.at[place]
                )
            )
            copies[-1].start()

    def spread(row, fill):
        rest = across - row.shape[1]
        return jnp.concatenate([row, jnp.full((1, rest), fill, row.dtype)], axis=1) if rest else row

    for head in range(0, wide, HD):
        query = jnp.concatenate(
            [take(group, head) for group in range(groups - 1, 0, -1)], axis=0
        )
        query = jnp.transpose(query)
        value = jnp.transpose(
            jnp.concatenate([take(group, 2 * wide + head) for group in range(groups)], axis=0)
        )
        scores, highest = [], None
        for source in range(groups):
            key = take(source, wide + head)
            scores.append(
                jnp.dot(key, query[:, : ends[source]], preferred_element_type=jnp.float32)
            )
            peak = jnp.where(kept[source], jnp.max(scores[-1], axis=0, keepdims=True), -1e30)
            peak = spread(peak, -1e30)
            highest = peak if highest is None else jnp.maximum(highest, peak)
        highest = highest * factor
        total, probs = 0.0, []
        for source in range(groups):
            offset = jnp.where(kept[source], -highest[:, : ends[source]], -1e30)
            raised = jnp.exp2(scores[source] * factor + offset)
            total += spread(jnp.sum(raised, axis=0, keepdims=True), 0.0)
            probs.append(raised.astype(jnp.bfloat16))
        inverse = 1.0 / total
        last = head + HD == wide
        start, left, waiting = 0, None, groups - 1
        for source in range(groups - 1, 0, -1):
            stop = ends[source]
            if stop > start:
                numer = jnp.dot(
                    value[:, : (source + 1) * rows],
                    jnp.concatenate([p[:, start:stop] for p in probs[: source + 1]], axis=0),
                    preferred_element_type=jnp.float32,
                )
                result = jnp.transpose(numer * inverse[:, start:stop])
                left = result if left is None else jnp.concatenate([left, result], axis=0)
                start = stop
            while left is not None and left.shape[0] >= rows:
                ready = left[:rows].astype(jnp.bfloat16)
                for pair in range(pairs):
                    at = pair_place(waiting, pair, pairs) * step
                    to = mixed(2 * pair, seq_count) // 2 * step
                    held[waiting - 1, to : to + step, head : head + HD] = ready[at : at + step]
                left = left[rows:] if left.shape[0] > rows else None
                if last:
                    send(waiting)
                waiting -= 1
    for distance, hand_ref in zip(distances(groups), hand_refs):
        hand_over(lax.rem(partner(here, distance, groups) + 1, groups), seq_count, x_ref, hand_ref)
    for copy in copies:
        copy.wait()


def lanes_of(distance, groups, here, wide):
    source = partner(here, groups - distance if groups & (groups - 1) else distance, groups)
    return pl.ds(pl.multiple_of(source * wide, wide), wide)


def cache_kernel(groups, seq_count, x_ref, hand_ref, out_ref):
    wide = x_ref.shape[1] // 3
    here = lax.axis_index("tm")
    out_ref[...] = jnp.zeros_like(out_ref)

    @pl.when(here < groups - 1)
    def place():
        hand_over(here + 1, seq_count, x_ref, out_ref.at[0], lanes_of(0, groups, here, wide))
        out_ref[0, :, :, lanes_of(distances(groups)[0], groups, here, wide)] = hand_ref[...]


def cache_rest_kernel(groups, begun_hbm, after_ref, *refs):
    *hand_refs, out_hbm, sems = refs
    here = lax.axis_index("tm")

    @pl.when(here < groups - 1)
    def place():
        copies = [
            pltpu.make_async_copy(
                block, out_hbm.at[0, :, :, lanes_of(distance, groups, here, block.shape[2])], sems.at[index]
            )
            for index, (distance, block) in enumerate(zip(distances(groups)[1:], hand_refs))
        ]
        for copy in copies:
            copy.start()
        for copy in copies:
            copy.wait()


def update_kernel(seq_count, tm_count, att_ref, moved_ref, fresh_ref, after_ref, out_ref):
    tok = out_ref.shape[1]
    wide = att_ref.shape[1]
    count = att_ref.shape[0] // tok
    last = lax.axis_index("tm") == tm_count - 1

    @pl.when(last)
    def take_fresh():
        out_ref[0] = fresh_ref[...]

    @pl.when(jnp.logical_not(last))
    def take_update():
        for pair in range(count // 2):
            rows = att_ref[2 * pair * tok : 2 * (pair + 1) * tok, :].astype(jnp.float32)
            for half in range(2):
                source = 2 * pair + half
                start = (mixed(source % seq_count, seq_count) * tm_count + source // seq_count) * wide
                moved = moved_ref[:, start : start + wide].astype(jnp.float32)
                gate = (moved[tok : tok + 1] + moved[tok + 1 : tok + 2]) + moved[tok + 2 : tok + 3]
                result = moved[:tok] + gate * rows[half * tok : (half + 1) * tok]
                out_ref[0, :, start : start + wide] = result.astype(jnp.bfloat16)


def whole(space=VMEM):
    return pl.BlockSpec(memory_space=space)


def run(kernel, name, outs, specs, operands, flops=0, scratch=(), aliases={}):
    def size(a):
        return math.prod(a.shape) * jnp.dtype(a.dtype).itemsize

    moved = sum(map(size, operands)) + sum(map(size, outs))
    results = pl.pallas_call(
        kernel,
        out_shape=outs,
        in_specs=specs,
        out_specs=[whole(getattr(a, "memory_space", VMEM)) for a in outs],
        scratch_shapes=scratch,
        input_output_aliases=aliases,
        compiler_params=pltpu.CompilerParams(vmem_limit_bytes=4 * moved + (4 << 20)),
        cost_estimate=pl.CostEstimate(flops=flops, bytes_accessed=moved, transcendentals=0),
        name=name,
    )(*operands)
    return results if len(outs) > 1 else results[0]


def spread_body(queries, keys_proj, values, hidden, fresh_latent, gate_table, noise_step, pattern):
    tm_count, seq_count = lax.axis_size("tm"), lax.axis_size("seq")
    count = tm_count * seq_count
    _, tok, width = queries.shape
    wide = width // count
    group_tok = tok * seq_count
    kind = queries.dtype
    DMA = pltpu.SemaphoreType.DMA
    parts = seq_count // 2

    packed = run(
        functools.partial(pack_kernel, seq_count, parts),
        "pack",
        [HBM((count * tok, 3 * wide), kind)],
        [whole(HBM)] * 3,
        [pltpu.with_memory_space_constraint(a, HBM) for a in (queries, keys_proj, values)],
        scratch=[
            VMEM((3, tok, width), kind),
            VMEM((count * tok, 3 * wide), kind),
            DMA((parts, 3)),
            DMA((parts, tm_count)),
        ],
    )
    back = [tm * seq_count + mixed(s, seq_count) for tm in range(tm_count) for s in range(seq_count)]
    out = [tm * seq_count + index for tm, index in out_order(tm_count, seq_count)]
    exchange = functools.partial(
        lax.all_to_all, axis_name=BOTH, split_axis=0, concat_axis=0, tiled=True
    )
    exchanged = exchange(packed, axis_index_groups=[out])

    residual = run(
        residual_kernel,
        "residual",
        [VMEM((tok + 8, width), kind)],
        [whole(SMEM), whole(), whole(HBM), whole(HBM)],
        (
            noise_step,
            hidden,
            pltpu.with_memory_space_constraint(gate_table, HBM),
            pltpu.with_memory_space_constraint(packed, HBM),
        ),
        scratch=[VMEM((8, width), jnp.float32), DMA],
    )
    moved = shifted(residual, "tm", -1)

    attended, *hands = run(
        functools.partial(attend_kernel, tm_count, seq_count),
        "attend",
        [HBM((count * tok, wide), kind)] + [VMEM((2, group_tok, wide), kind)] * (tm_count - 1),
        [whole(), whole(), whole(pl.ANY)],
        (pattern, exchanged, moved),
        flops=2 * count * tok * count * tok * wide,
        scratch=[VMEM((tm_count - 1, group_tok, wide), kind), DMA((tm_count,))],
    )
    returned = exchange(attended, axis_index_groups=[back])
    handed = []
    for distance, hand in zip(distances(tm_count), hands):
        route = [(i, partner(i, distance, tm_count)) for i in range(tm_count)]
        handed.append(lax.ppermute(hand, "tm", [(i, j) for i, j in route if j < tm_count - 1]))

    first, *rest = handed
    begun = run(
        functools.partial(cache_kernel, tm_count, seq_count),
        "cache",
        [jax.ShapeDtypeStruct((1, 2, group_tok, tm_count * wide), kind)],
        [whole()] * 2,
        (exchanged, first),
    )
    begun = pltpu.with_memory_space_constraint(begun, HBM)
    advanced = run(
        functools.partial(update_kernel, seq_count, tm_count),
        "update",
        [jax.ShapeDtypeStruct((1, tok, width), kind)],
        [whole()] * 3 + [whole(HBM)],
        (returned, moved, fresh_latent, begun),
    )
    next_cache = run(
        functools.partial(cache_rest_kernel, tm_count),
        "cache_rest",
        [HBM(begun.shape, kind)],
        [whole(HBM)] * 2 + [whole()] * len(rest),
        (begun, pltpu.with_memory_space_constraint(advanced, HBM), *rest),
        scratch=[DMA((len(rest),))],
        aliases={0: 0},
    )
    return (advanced, next_cache)


def absorb(state, query_heads, key_piece, value_piece, scale_factor):
    accum, totals, highest = state
    row_count, head_count, head_dim = query_heads.shape
    key_heads = key_piece.reshape(key_piece.shape[0], head_count, head_dim)
    value_heads = value_piece.reshape(value_piece.shape[0], head_count, head_dim)
    scores = (
        jnp.einsum("qhd,khd->qhk", query_heads, key_heads, preferred_element_type=jnp.float32)
        * scale_factor
    )
    raised = jnp.maximum(highest, jnp.max(scores, axis=-1))
    fade = jnp.exp(highest - raised)
    weights = jnp.exp(scores - raised[..., None])
    totals = totals * fade + jnp.sum(weights, axis=-1)
    accum = accum * fade[..., None] + jnp.einsum(
        "qhk,khd->qhd",
        weights.astype(jnp.bfloat16),
        value_heads,
        preferred_element_type=jnp.float32,
    )
    return (accum, totals, raised)


def gather_body(queries, keys_proj, values, hidden, fresh_latent, gate_table, noise_step, pattern):
    group_index = lax.axis_index("tm")
    final_index = lax.axis_size("tm") - 1
    query_tok, key_tok, value_tok = (
        lax.all_to_all(queries[0], "seq", split_axis=1, concat_axis=0, tiled=True),
        lax.all_to_all(keys_proj[0], "seq", split_axis=1, concat_axis=0, tiled=True),
        lax.all_to_all(values[0], "seq", split_axis=1, concat_axis=0, tiled=True),
    )
    row_count, local_width = query_tok.shape
    head_count = local_width // HD
    query_heads = query_tok.reshape(row_count, head_count, HD)
    scale_factor = 1.0 / math.sqrt(HD)
    reach = lax.dynamic_index_in_dim(pattern, group_index, 0, keepdims=False)
    start_state = (
        jnp.zeros((row_count, head_count, HD), jnp.float32),
        jnp.zeros((row_count, head_count), jnp.float32),
        jnp.full((row_count, head_count), -1e30, jnp.float32),
    )

    def one_block(current, inputs):
        key_block, value_block, flag = inputs
        return (
            lax.cond(
                flag > 0,
                lambda state: absorb(state, query_heads, key_block, value_block, scale_factor),
                lambda state: state,
                current,
            ),
            None,
        )

    key_piece = lax.all_gather(key_tok, "tm", axis=0, tiled=False)
    value_piece = lax.all_gather(value_tok, "tm", axis=0, tiled=False)
    state, unused = lax.scan(one_block, start_state, (key_piece, value_piece, reach))
    cache_keys, cache_values = shifted((key_tok, value_tok), "tm", -1)
    accum, totals, highest = state
    attended_head = (accum / totals[..., None]).reshape(row_count, local_width).astype(jnp.bfloat16)
    attended = lax.all_to_all(attended_head, "seq", split_axis=0, concat_axis=1, tiled=True)
    gate_row = lax.dynamic_index_in_dim(gate_table, noise_step[0], 0, keepdims=False)
    updated = (
        hidden[0].astype(jnp.float32) + gate_row[None, :] * attended.astype(jnp.float32)
    ).astype(jnp.bfloat16)
    moved = shifted(updated, "tm", -1)
    advanced = jnp.where(group_index == final_index, fresh_latent, moved)[None]
    next_cache = jnp.stack([cache_keys, cache_values], axis=0)[None]
    return (advanced, next_cache)


def body(queries, *others):
    tm_count, seq_count = lax.axis_size("tm"), lax.axis_size("seq")
    _, tok, width = queries.shape
    count = tm_count * seq_count
    even = width % (count * HD) == 0 and tok % 8 == 0 and seq_count % 4 == 0 and tm_count > 2 and tm_count % 2 == 0
    return (spread_body if even else gather_body)(queries, *others)


def solution(mesh):
    placed = (
        P("tm", "seq", None),
        P("tm", "seq", None),
        P("tm", "seq", None),
        P("tm", "seq", None),
        P("seq", None),
        P(),
        P("tm"),
        P(),
    )
    return jax.shard_map(
        body,
        mesh=mesh,
        in_specs=placed,
        out_specs=(P("tm", "seq", None), P("tm", None, None, "seq")),
        check_vma=False,
    )
```

```python
import functools
import math

import jax
import jax.numpy as jnp
from jax import lax
from jax.experimental import pallas as pl
from jax.experimental.pallas import tpu as pltpu
from jax.sharding import PartitionSpec as P

HD = 128
BOTH = ("tm", "seq")
VMEM = pltpu.VMEM
SMEM = pltpu.SMEM
HBM = pltpu.HBM


def shifted(block, axis, distance):
    devices = range(lax.axis_size(axis))
    route = [(i - distance, i) for i in devices if i - distance in devices]
    return lax.ppermute(block, axis, route)


def pair_place(group, pair, pairs):
    place = (pair + pairs // 2) % pairs
    return place + group // 2 % 2 * (pairs - 1 - 2 * place)


def out_order(tm_count, seq_count):
    pairs = seq_count // 2
    return [
        (tm, 2 * pair_place(tm, pair, pairs) + member)
        for tm in range(tm_count)
        for pair in range(pairs)
        for member in range(2)
    ]


def pack_kernel(seq_count, parts, q_hbm, k_hbm, v_hbm, out_hbm, held, block, in_sems, out_sems):
    tok, width = held.shape[1:]
    wide = out_hbm.shape[1] // 3
    count = out_hbm.shape[0] // tok
    tm_count = count // seq_count
    span, members = width // parts, seq_count // parts
    order = out_order(tm_count, seq_count)
    copies = []
    for part in range(parts):
        columns = slice(part * span, (part + 1) * span)
        for place, ref in enumerate((q_hbm, k_hbm, v_hbm)):
            copies.append(
                pltpu.make_async_copy(
                    ref.at[0, :, columns], held.at[place, :, columns], in_sems.at[part, place]
                )
            )
            copies[-1].start()
    outs = []
    for part in range(parts):
        for place in range(3):
            copies[3 * part + place].wait()
        for tm in range(tm_count):
            for seq in range(part * members, (part + 1) * members, 2):
                first = order.index((tm, seq)) * tok
                for place in range(3):
                    rows = []
                    for member in (seq, seq + 1):
                        start = (member * tm_count + tm) * wide
                        rows.append(held[place, :, start : start + wide].astype(jnp.float32))
                    block[first : first + 2 * tok, place * wide : (place + 1) * wide] = jnp.concatenate(
                        rows, axis=0
                    ).astype(jnp.bfloat16)
            first = order.index((tm, part * members)) * tok
            rows = slice(first, first + members * tok)
            outs.append(
                pltpu.make_async_copy(block.at[rows], out_hbm.at[rows], out_sems.at[part, tm])
            )
            outs[-1].start()
    for out in outs:
        out.wait()


def residual_kernel(noise_ref, h_ref, gate_hbm, after_ref, out_ref, held, sem):
    step = noise_ref[0]
    steps = gate_hbm.shape[0]
    whole_tiles = steps // 8 * 8
    first = step // 8 * 8

    @pl.when(step < whole_tiles)
    def take_tile():
        rows = pl.ds(pl.multiple_of(first, 8), 8)
        copy = pltpu.make_async_copy(gate_hbm.at[rows], held, sem)
        copy.start()
        copy.wait()

    if steps > whole_tiles:

        @pl.when(step >= whole_tiles)
        def take_rest():
            copy = pltpu.make_async_copy(
                gate_hbm.at[whole_tiles:steps], held.at[0 : steps - whole_tiles], sem
            )
            copy.start()
            copy.wait()

    gate = held[pl.ds(step - first, 1), :]
    high = gate.astype(jnp.bfloat16).astype(jnp.float32)
    middle = (gate - high).astype(jnp.bfloat16).astype(jnp.float32)
    low = gate - high - middle
    parts = jnp.concatenate([high, middle, low, jnp.zeros((5, gate.shape[1]), jnp.float32)], axis=0)
    out_ref[...] = jnp.concatenate([h_ref[0].astype(jnp.float32), parts], axis=0).astype(jnp.bfloat16)


def partner(here, distance, groups):
    return here ^ distance if groups & (groups - 1) == 0 else (here + groups - distance) % groups


def distances(groups):
    return range(groups - 1, 0, -1)


def hand_over(group, seq_count, x_ref, out_ref, lanes=slice(None)):
    wide = x_ref.shape[1] // 3
    pairs = seq_count // 2
    step = out_ref.shape[1] // pairs
    for pair in range(pairs):
        first = pl.multiple_of((group * pairs + pair_place(group, pair, pairs)) * step, step)
        for kind in range(2):
            out_ref[kind, pair * step : (pair + 1) * step, lanes] = x_ref[
                pl.ds(first, step), (kind + 1) * wide : (kind + 2) * wide
            ]


def attend_kernel(groups, seq_count, pattern_ref, x_ref, after_ref, out_hbm, *refs):
    *hand_refs, held, sems = refs
    wide = held.shape[2]
    rows = held.shape[1]
    pairs = seq_count // 2
    step = rows // pairs
    across = (groups - 1) * rows
    factor = math.log2(math.e) / math.sqrt(HD)
    here = lax.axis_index("tm")
    lane = lax.broadcasted_iota(jnp.int32, (1, across), 1)
    ends, kept = [], []
    for source in range(groups):
        first = max(source, 1)
        ends.append(min(across, -(-(groups - first) * rows // 128) * 128))
        chosen = jnp.zeros((1, across), jnp.int32)
        for group in range(first, groups):
            start = (groups - 1 - group) * rows
            flag = pattern_ref[group : group + 1, source : source + 1]
            chosen = jnp.where((lane >= start) & (lane < start + rows), flag, chosen)
        kept.append(chosen[:, : ends[-1]] > 0)

    def take(group, first):
        return x_ref[group * rows : (group + 1) * rows, first : first + HD]

    copies = []

    def send(group):
        for place in (group - 1, groups - 1) if group == groups - 1 else (group - 1,):
            copies.append(
                pltpu.make_async_copy(
                    held.at[group - 1], out_hbm.at[place * rows : (place + 1) * rows], sems.at[place]
                )
            )
            copies[-1].start()

    def spread(row, fill):
        rest = across - row.shape[1]
        return jnp.concatenate([row, jnp.full((1, rest), fill, row.dtype)], axis=1) if rest else row

    for head in range(0, wide, HD):
        query = jnp.concatenate(
            [take(group, head) for group in range(groups - 1, 0, -1)], axis=0
        )
        query = jnp.transpose(query)
        value = jnp.transpose(
            jnp.concatenate([take(group, 2 * wide + head) for group in range(groups)], axis=0)
        )
        scores, highest = [], None
        for source in range(groups):
            key = take(source, wide + head)
            scores.append(
                jnp.dot(key, query[:, : ends[source]], preferred_element_type=jnp.float32)
            )
            peak = jnp.where(kept[source], jnp.max(scores[-1], axis=0, keepdims=True), -1e30)
            peak = spread(peak, -1e30)
            highest = peak if highest is None else jnp.maximum(highest, peak)
        highest = highest * factor
        total, probs = 0.0, []
        for source in range(groups):
            offset = jnp.where(kept[source], -highest[:, : ends[source]], -1e30)
            raised = jnp.exp2(scores[source] * factor + offset)
            total += spread(jnp.sum(raised, axis=0, keepdims=True), 0.0)
            probs.append(raised.astype(jnp.bfloat16))
        inverse = 1.0 / total
        last = head + HD == wide
        start, left, waiting = 0, None, groups - 1
        for source in range(groups - 1, 0, -1):
            stop = ends[source]
            if stop > start:
                numer = jnp.dot(
                    value[:, : (source + 1) * rows],
                    jnp.concatenate([p[:, start:stop] for p in probs[: source + 1]], axis=0),
                    preferred_element_type=jnp.float32,
                )
                result = jnp.transpose(numer * inverse[:, start:stop])
                left = result if left is None else jnp.concatenate([left, result], axis=0)
                start = stop
            while left is not None and left.shape[0] >= rows:
                ready = left[:rows].astype(jnp.bfloat16)
                for pair in range(pairs):
                    at = pair_place(waiting, pair, pairs) * step
                    to = pair_place(waiting - 1, pair, pairs) * step
                    held[waiting - 1, to : to + step, head : head + HD] = ready[at : at + step]
                left = left[rows:] if left.shape[0] > rows else None
                if last:
                    send(waiting)
                waiting -= 1
    for distance, hand_ref in zip(distances(groups), hand_refs):
        hand_over(lax.rem(partner(here, distance, groups) + 1, groups), seq_count, x_ref, hand_ref)
    for copy in copies:
        copy.wait()


def lanes_of(distance, groups, here, wide):
    source = partner(here, groups - distance if groups & (groups - 1) else distance, groups)
    return pl.ds(pl.multiple_of(source * wide, wide), wide)


def cache_kernel(groups, seq_count, x_ref, hand_ref, out_ref):
    wide = x_ref.shape[1] // 3
    here = lax.axis_index("tm")
    out_ref[...] = jnp.zeros_like(out_ref)

    @pl.when(here < groups - 1)
    def place():
        hand_over(here + 1, seq_count, x_ref, out_ref.at[0], lanes_of(0, groups, here, wide))
        out_ref[0, :, :, lanes_of(distances(groups)[0], groups, here, wide)] = hand_ref[...]


def cache_rest_kernel(groups, begun_hbm, after_ref, *refs):
    *hand_refs, out_hbm, sems = refs
    here = lax.axis_index("tm")

    @pl.when(here < groups - 1)
    def place():
        copies = [
            pltpu.make_async_copy(
                block, out_hbm.at[0, :, :, lanes_of(distance, groups, here, block.shape[2])], sems.at[index]
            )
            for index, (distance, block) in enumerate(zip(distances(groups)[1:], hand_refs))
        ]
        for copy in copies:
            copy.start()
        for copy in copies:
            copy.wait()


def update_kernel(seq_count, tm_count, att_ref, moved_ref, fresh_ref, after_ref, out_ref):
    tok = out_ref.shape[1]
    wide = att_ref.shape[1]
    count = att_ref.shape[0] // tok
    order = out_order(tm_count, seq_count)
    last = lax.axis_index("tm") == tm_count - 1

    @pl.when(last)
    def take_fresh():
        out_ref[0] = fresh_ref[...]

    @pl.when(jnp.logical_not(last))
    def take_update():
        for pair in range(count // 2):
            rows = att_ref[2 * pair * tok : 2 * (pair + 1) * tok, :].astype(jnp.float32)
            for half in range(2):
                source = 2 * pair + half
                tm, seq = order[source]
                start = (seq * tm_count + tm) * wide
                moved = moved_ref[:, start : start + wide].astype(jnp.float32)
                gate = (moved[tok : tok + 1] + moved[tok + 1 : tok + 2]) + moved[tok + 2 : tok + 3]
                result = moved[:tok] + gate * rows[half * tok : (half + 1) * tok]
                out_ref[0, :, start : start + wide] = result.astype(jnp.bfloat16)


def whole(space=VMEM):
    return pl.BlockSpec(memory_space=space)


def run(kernel, name, outs, specs, operands, flops=0, scratch=(), aliases={}):
    def size(a):
        return math.prod(a.shape) * jnp.dtype(a.dtype).itemsize

    moved = sum(map(size, operands)) + sum(map(size, outs))
    results = pl.pallas_call(
        kernel,
        out_shape=outs,
        in_specs=specs,
        out_specs=[whole(getattr(a, "memory_space", VMEM)) for a in outs],
        scratch_shapes=scratch,
        input_output_aliases=aliases,
        compiler_params=pltpu.CompilerParams(vmem_limit_bytes=4 * moved + (4 << 20)),
        cost_estimate=pl.CostEstimate(flops=flops, bytes_accessed=moved, transcendentals=0),
        name=name,
    )(*operands)
    return results if len(outs) > 1 else results[0]


def spread_body(queries, keys_proj, values, hidden, fresh_latent, gate_table, noise_step, pattern):
    tm_count, seq_count = lax.axis_size("tm"), lax.axis_size("seq")
    count = tm_count * seq_count
    _, tok, width = queries.shape
    wide = width // count
    group_tok = tok * seq_count
    kind = queries.dtype
    DMA = pltpu.SemaphoreType.DMA
    parts = seq_count // 2

    packed = run(
        functools.partial(pack_kernel, seq_count, parts),
        "pack",
        [HBM((count * tok, 3 * wide), kind)],
        [whole(HBM)] * 3,
        [pltpu.with_memory_space_constraint(a, HBM) for a in (queries, keys_proj, values)],
        scratch=[
            VMEM((3, tok, width), kind),
            VMEM((count * tok, 3 * wide), kind),
            DMA((parts, 3)),
            DMA((parts, tm_count)),
        ],
    )
    out = [tm * seq_count + index for tm, index in out_order(tm_count, seq_count)]
    exchange = functools.partial(
        lax.all_to_all, axis_name=BOTH, split_axis=0, concat_axis=0, tiled=True
    )
    exchanged = exchange(packed, axis_index_groups=[out])

    residual = run(
        residual_kernel,
        "residual",
        [VMEM((tok + 8, width), kind)],
        [whole(SMEM), whole(), whole(HBM), whole(HBM)],
        (
            noise_step,
            hidden,
            pltpu.with_memory_space_constraint(gate_table, HBM),
            pltpu.with_memory_space_constraint(packed, HBM),
        ),
        scratch=[VMEM((8, width), jnp.float32), DMA],
    )
    moved = shifted(residual, "tm", -1)

    attended, *hands = run(
        functools.partial(attend_kernel, tm_count, seq_count),
        "attend",
        [HBM((count * tok, wide), kind)] + [VMEM((2, group_tok, wide), kind)] * (tm_count - 1),
        [whole(), whole(), whole(pl.ANY)],
        (pattern, exchanged, moved),
        flops=2 * count * tok * count * tok * wide,
        scratch=[VMEM((tm_count - 1, group_tok, wide), kind), DMA((tm_count,))],
    )
    returned = exchange(attended, axis_index_groups=[out])
    handed = []
    for distance, hand in zip(distances(tm_count), hands):
        route = [(i, partner(i, distance, tm_count)) for i in range(tm_count)]
        handed.append(lax.ppermute(hand, "tm", [(i, j) for i, j in route if j < tm_count - 1]))

    first, *rest = handed
    begun = run(
        functools.partial(cache_kernel, tm_count, seq_count),
        "cache",
        [jax.ShapeDtypeStruct((1, 2, group_tok, tm_count * wide), kind)],
        [whole()] * 2,
        (exchanged, first),
    )
    begun = pltpu.with_memory_space_constraint(begun, HBM)
    advanced = run(
        functools.partial(update_kernel, seq_count, tm_count),
        "update",
        [jax.ShapeDtypeStruct((1, tok, width), kind)],
        [whole()] * 3 + [whole(HBM)],
        (returned, moved, fresh_latent, begun),
    )
    next_cache = run(
        functools.partial(cache_rest_kernel, tm_count),
        "cache_rest",
        [HBM(begun.shape, kind)],
        [whole(HBM)] * 2 + [whole()] * len(rest),
        (begun, pltpu.with_memory_space_constraint(advanced, HBM), *rest),
        scratch=[DMA((len(rest),))],
        aliases={0: 0},
    )
    return (advanced, next_cache)


def absorb(state, query_heads, key_piece, value_piece, scale_factor):
    accum, totals, highest = state
    row_count, head_count, head_dim = query_heads.shape
    key_heads = key_piece.reshape(key_piece.shape[0], head_count, head_dim)
    value_heads = value_piece.reshape(value_piece.shape[0], head_count, head_dim)
    scores = (
        jnp.einsum("qhd,khd->qhk", query_heads, key_heads, preferred_element_type=jnp.float32)
        * scale_factor
    )
    raised = jnp.maximum(highest, jnp.max(scores, axis=-1))
    fade = jnp.exp(highest - raised)
    weights = jnp.exp(scores - raised[..., None])
    totals = totals * fade + jnp.sum(weights, axis=-1)
    accum = accum * fade[..., None] + jnp.einsum(
        "qhk,khd->qhd",
        weights.astype(jnp.bfloat16),
        value_heads,
        preferred_element_type=jnp.float32,
    )
    return (accum, totals, raised)


def gather_body(queries, keys_proj, values, hidden, fresh_latent, gate_table, noise_step, pattern):
    group_index = lax.axis_index("tm")
    final_index = lax.axis_size("tm") - 1
    query_tok, key_tok, value_tok = (
        lax.all_to_all(queries[0], "seq", split_axis=1, concat_axis=0, tiled=True),
        lax.all_to_all(keys_proj[0], "seq", split_axis=1, concat_axis=0, tiled=True),
        lax.all_to_all(values[0], "seq", split_axis=1, concat_axis=0, tiled=True),
    )
    row_count, local_width = query_tok.shape
    head_count = local_width // HD
    query_heads = query_tok.reshape(row_count, head_count, HD)
    scale_factor = 1.0 / math.sqrt(HD)
    reach = lax.dynamic_index_in_dim(pattern, group_index, 0, keepdims=False)
    start_state = (
        jnp.zeros((row_count, head_count, HD), jnp.float32),
        jnp.zeros((row_count, head_count), jnp.float32),
        jnp.full((row_count, head_count), -1e30, jnp.float32),
    )

    def one_block(current, inputs):
        key_block, value_block, flag = inputs
        return (
            lax.cond(
                flag > 0,
                lambda state: absorb(state, query_heads, key_block, value_block, scale_factor),
                lambda state: state,
                current,
            ),
            None,
        )

    key_piece = lax.all_gather(key_tok, "tm", axis=0, tiled=False)
    value_piece = lax.all_gather(value_tok, "tm", axis=0, tiled=False)
    state, unused = lax.scan(one_block, start_state, (key_piece, value_piece, reach))
    cache_keys, cache_values = shifted((key_tok, value_tok), "tm", -1)
    accum, totals, highest = state
    attended_head = (accum / totals[..., None]).reshape(row_count, local_width).astype(jnp.bfloat16)
    attended = lax.all_to_all(attended_head, "seq", split_axis=0, concat_axis=1, tiled=True)
    gate_row = lax.dynamic_index_in_dim(gate_table, noise_step[0], 0, keepdims=False)
    updated = (
        hidden[0].astype(jnp.float32) + gate_row[None, :] * attended.astype(jnp.float32)
    ).astype(jnp.bfloat16)
    moved = shifted(updated, "tm", -1)
    advanced = jnp.where(group_index == final_index, fresh_latent, moved)[None]
    next_cache = jnp.stack([cache_keys, cache_values], axis=0)[None]
    return (advanced, next_cache)


def body(queries, *others):
    tm_count, seq_count = lax.axis_size("tm"), lax.axis_size("seq")
    _, tok, width = queries.shape
    count = tm_count * seq_count
    even = width % (count * HD) == 0 and tok % 8 == 0 and seq_count % 4 == 0 and tm_count > 2 and tm_count % 2 == 0
    return (spread_body if even else gather_body)(queries, *others)


def solution(mesh):
    placed = (
        P("tm", "seq", None),
        P("tm", "seq", None),
        P("tm", "seq", None),
        P("tm", "seq", None),
        P("seq", None),
        P(),
        P("tm"),
        P(),
    )
    return jax.shard_map(
        body,
        mesh=mesh,
        in_specs=placed,
        out_specs=(P("tm", "seq", None), P("tm", None, None, "seq")),
        check_vma=False,
    )
```

```python
import functools
import math

import jax
import jax.numpy as jnp
from jax import lax
from jax.experimental import pallas as pl
from jax.experimental.pallas import tpu as pltpu
from jax.sharding import PartitionSpec as P

HD = 128
BOTH = ("tm", "seq")
VMEM = pltpu.VMEM
SMEM = pltpu.SMEM
HBM = pltpu.HBM


def shifted(block, axis, distance):
    devices = range(lax.axis_size(axis))
    route = [(i - distance, i) for i in devices if i - distance in devices]
    return lax.ppermute(block, axis, route)


def pair_place(group, pair, pairs):
    place = (pair + pairs // 2) % pairs
    return place + group // 2 % 2 * (pairs - 1 - 2 * place)


def out_order(tm_count, seq_count):
    pairs = seq_count // 2
    return [
        (tm, 2 * pair_place(tm, pair, pairs) + member)
        for tm in range(tm_count)
        for pair in range(pairs)
        for member in range(2)
    ]


def pack_kernel(seq_count, parts, q_hbm, k_hbm, v_hbm, out_hbm, held, block, in_sems, out_sems):
    tok, width = held.shape[1:]
    wide = out_hbm.shape[1] // 3
    count = out_hbm.shape[0] // tok
    tm_count = count // seq_count
    span, members = width // parts, seq_count // parts
    order = out_order(tm_count, seq_count)
    copies = []
    for part in range(parts):
        columns = slice(part * span, (part + 1) * span)
        for place, ref in enumerate((q_hbm, k_hbm, v_hbm)):
            copies.append(
                pltpu.make_async_copy(
                    ref.at[0, :, columns], held.at[place, :, columns], in_sems.at[part, place]
                )
            )
            copies[-1].start()
    outs = []
    for part in range(parts):
        for place in range(3):
            copies[3 * part + place].wait()
        for tm in range(tm_count):
            for seq in range(part * members, (part + 1) * members, 2):
                first = order.index((tm, seq)) * tok
                for place in range(3):
                    rows = []
                    for member in (seq, seq + 1):
                        start = (member * tm_count + tm) * wide
                        rows.append(held[place, :, start : start + wide].astype(jnp.float32))
                    block[first : first + 2 * tok, place * wide : (place + 1) * wide] = jnp.concatenate(
                        rows, axis=0
                    ).astype(jnp.bfloat16)
            first = order.index((tm, part * members)) * tok
            rows = slice(first, first + members * tok)
            outs.append(
                pltpu.make_async_copy(block.at[rows], out_hbm.at[rows], out_sems.at[part, tm])
            )
            outs[-1].start()
    for out in outs:
        out.wait()


def residual_kernel(noise_ref, h_ref, gate_hbm, after_ref, out_ref, held, sem):
    step = noise_ref[0]
    steps = gate_hbm.shape[0]
    whole_tiles = steps // 8 * 8
    first = step // 8 * 8

    @pl.when(step < whole_tiles)
    def take_tile():
        rows = pl.ds(pl.multiple_of(first, 8), 8)
        copy = pltpu.make_async_copy(gate_hbm.at[rows], held, sem)
        copy.start()
        copy.wait()

    if steps > whole_tiles:

        @pl.when(step >= whole_tiles)
        def take_rest():
            copy = pltpu.make_async_copy(
                gate_hbm.at[whole_tiles:steps], held.at[0 : steps - whole_tiles], sem
            )
            copy.start()
            copy.wait()

    gate = held[pl.ds(step - first, 1), :]
    high = gate.astype(jnp.bfloat16).astype(jnp.float32)
    middle = (gate - high).astype(jnp.bfloat16).astype(jnp.float32)
    low = gate - high - middle
    parts = jnp.concatenate([high, middle, low, jnp.zeros((5, gate.shape[1]), jnp.float32)], axis=0)
    out_ref[...] = jnp.concatenate([h_ref[0].astype(jnp.float32), parts], axis=0).astype(jnp.bfloat16)


def partner(here, distance, groups):
    return here ^ distance if groups & (groups - 1) == 0 else (here + groups - distance) % groups


def distances(groups):
    return range(groups - 1, 0, -1)


def hand_over(group, seq_count, x_ref, out_ref, lanes=slice(None)):
    wide = x_ref.shape[1] // 3
    pairs = seq_count // 2
    step = out_ref.shape[1] // pairs
    for pair in range(pairs):
        first = pl.multiple_of((group * pairs + pair_place(group, pair, pairs)) * step, step)
        for kind in range(2):
            out_ref[kind, pair * step : (pair + 1) * step, lanes] = x_ref[
                pl.ds(first, step), (kind + 1) * wide : (kind + 2) * wide
            ]


def attend_kernel(groups, seq_count, pattern_ref, x_ref, after_ref, out_hbm, *refs):
    *hand_refs, held, sems = refs
    wide = held.shape[2]
    rows = held.shape[1]
    pairs = seq_count // 2
    step = rows // pairs
    across = (groups - 1) * rows
    factor = math.log2(math.e) / math.sqrt(HD)
    here = lax.axis_index("tm")
    lane = lax.broadcasted_iota(jnp.int32, (1, across), 1)
    ends, kept = [], []
    for source in range(groups):
        first = max(source, 1)
        ends.append(min(across, -(-(groups - first) * rows // 128) * 128))
        chosen = jnp.zeros((1, across), jnp.int32)
        for group in range(first, groups):
            start = (groups - 1 - group) * rows
            flag = pattern_ref[group : group + 1, source : source + 1]
            chosen = jnp.where((lane >= start) & (lane < start + rows), flag, chosen)
        kept.append(chosen[:, : ends[-1]] > 0)

    def take(group, first):
        return x_ref[group * rows : (group + 1) * rows, first : first + HD]

    copies = []

    def send(group):
        for place in (group - 1, groups - 1) if group == groups - 1 else (group - 1,):
            copies.append(
                pltpu.make_async_copy(
                    held.at[group - 1], out_hbm.at[place * rows : (place + 1) * rows], sems.at[place]
                )
            )
            copies[-1].start()

    def spread(row, fill):
        rest = across - row.shape[1]
        return jnp.concatenate([row, jnp.full((1, rest), fill, row.dtype)], axis=1) if rest else row

    for head in range(0, wide, HD):
        query = jnp.concatenate(
            [take(group, head) for group in range(groups - 1, 0, -1)], axis=0
        )
        query = jnp.transpose(query)
        value = jnp.transpose(
            jnp.concatenate([take(group, 2 * wide + head) for group in range(groups)], axis=0)
        )
        scores, highest = [], None
        for source in range(groups):
            key = take(source, wide + head)
            scores.append(
                jnp.dot(key, query[:, : ends[source]], preferred_element_type=jnp.float32)
            )
            peak = jnp.where(kept[source], jnp.max(scores[-1], axis=0, keepdims=True), -1e30)
            peak = spread(peak, -1e30)
            highest = peak if highest is None else jnp.maximum(highest, peak)
        highest = highest * factor
        total, probs = 0.0, []
        for source in range(groups):
            offset = jnp.where(kept[source], -highest[:, : ends[source]], -1e30)
            raised = jnp.exp2(scores[source] * factor + offset)
            total += spread(jnp.sum(raised, axis=0, keepdims=True), 0.0)
            probs.append(raised.astype(jnp.bfloat16))
        inverse = 1.0 / total
        last = head + HD == wide
        start, left, waiting = 0, None, groups - 1
        for source in range(groups - 1, 0, -1):
            stop = ends[source]
            if stop > start:
                numer = jnp.dot(
                    value[:, : (source + 1) * rows],
                    jnp.concatenate([p[:, start:stop] for p in probs[: source + 1]], axis=0),
                    preferred_element_type=jnp.float32,
                )
                result = jnp.transpose(numer * inverse[:, start:stop])
                left = result if left is None else jnp.concatenate([left, result], axis=0)
                start = stop
            while left is not None and left.shape[0] >= rows:
                ready = left[:rows].astype(jnp.bfloat16)
                for pair in range(pairs):
                    at = pair_place(waiting, pair, pairs) * step
                    to = pair_place(waiting - 1, pair, pairs) * step
                    held[waiting - 1, to : to + step, head : head + HD] = ready[at : at + step]
                left = left[rows:] if left.shape[0] > rows else None
                if last:
                    send(waiting)
                waiting -= 1
    for distance, hand_ref in zip(distances(groups), hand_refs):
        hand_over(lax.rem(partner(here, distance, groups) + 1, groups), seq_count, x_ref, hand_ref)
    for copy in copies:
        copy.wait()


def lanes_of(distance, groups, here, wide):
    source = partner(here, groups - distance if groups & (groups - 1) else distance, groups)
    return pl.ds(pl.multiple_of(source * wide, wide), wide)


def cache_kernel(groups, seq_count, x_ref, hand_ref, out_ref):
    wide = x_ref.shape[1] // 3
    here = lax.axis_index("tm")
    out_ref[...] = jnp.zeros_like(out_ref)

    @pl.when(here < groups - 1)
    def place():
        hand_over(here + 1, seq_count, x_ref, out_ref.at[0], lanes_of(0, groups, here, wide))
        out_ref[0, :, :, lanes_of(distances(groups)[0], groups, here, wide)] = hand_ref[...]


def finish_kernel(seq_count, tm_count, att_ref, moved_ref, fresh_ref, begun_hbm, *refs):
    *hand_refs, out_hbm, cache_hbm, held, sem, sems = refs
    tok = held.shape[1]
    wide = att_ref.shape[1]
    count = att_ref.shape[0] // tok
    order = out_order(tm_count, seq_count)
    here = lax.axis_index("tm")
    last = here == tm_count - 1
    copies = [
        pltpu.make_async_copy(
            block, cache_hbm.at[0, :, :, lanes_of(distance, tm_count, here, block.shape[2])], sems.at[index]
        )
        for index, (distance, block) in enumerate(zip(distances(tm_count)[1:], hand_refs))
    ]

    @pl.when(last)
    def take_fresh():
        copy = pltpu.make_async_copy(fresh_ref, out_hbm.at[0], sem)
        copy.start()
        copy.wait()

    @pl.when(jnp.logical_not(last))
    def take_update():
        for copy in copies:
            copy.start()
        for pair in range(count // 2):
            rows = att_ref[2 * pair * tok : 2 * (pair + 1) * tok, :].astype(jnp.float32)
            for half in range(2):
                tm, seq = order[2 * pair + half]
                start = (seq * tm_count + tm) * wide
                moved = moved_ref[:, start : start + wide].astype(jnp.float32)
                gate = (moved[tok : tok + 1] + moved[tok + 1 : tok + 2]) + moved[tok + 2 : tok + 3]
                result = moved[:tok] + gate * rows[half * tok : (half + 1) * tok]
                held[0, :, start : start + wide] = result.astype(jnp.bfloat16)
        copy = pltpu.make_async_copy(held, out_hbm, sem)
        copy.start()
        copy.wait()
        for copy in copies:
            copy.wait()


def whole(space=VMEM):
    return pl.BlockSpec(memory_space=space)


def run(kernel, name, outs, specs, operands, flops=0, scratch=(), aliases={}):
    def size(a):
        return math.prod(a.shape) * jnp.dtype(a.dtype).itemsize

    moved = sum(map(size, operands)) + sum(map(size, outs))
    results = pl.pallas_call(
        kernel,
        out_shape=outs,
        in_specs=specs,
        out_specs=[whole(getattr(a, "memory_space", VMEM)) for a in outs],
        scratch_shapes=scratch,
        input_output_aliases=aliases,
        compiler_params=pltpu.CompilerParams(vmem_limit_bytes=4 * moved + (4 << 20)),
        cost_estimate=pl.CostEstimate(flops=flops, bytes_accessed=moved, transcendentals=0),
        name=name,
    )(*operands)
    return results if len(outs) > 1 else results[0]


def spread_body(queries, keys_proj, values, hidden, fresh_latent, gate_table, noise_step, pattern):
    tm_count, seq_count = lax.axis_size("tm"), lax.axis_size("seq")
    count = tm_count * seq_count
    _, tok, width = queries.shape
    wide = width // count
    group_tok = tok * seq_count
    kind = queries.dtype
    DMA = pltpu.SemaphoreType.DMA
    parts = seq_count // 2

    packed = run(
        functools.partial(pack_kernel, seq_count, parts),
        "pack",
        [HBM((count * tok, 3 * wide), kind)],
        [whole(HBM)] * 3,
        [pltpu.with_memory_space_constraint(a, HBM) for a in (queries, keys_proj, values)],
        scratch=[
            VMEM((3, tok, width), kind),
            VMEM((count * tok, 3 * wide), kind),
            DMA((parts, 3)),
            DMA((parts, tm_count)),
        ],
    )
    out = [tm * seq_count + index for tm, index in out_order(tm_count, seq_count)]
    exchange = functools.partial(
        lax.all_to_all, axis_name=BOTH, split_axis=0, concat_axis=0, tiled=True
    )
    exchanged = exchange(packed, axis_index_groups=[out])

    residual = run(
        residual_kernel,
        "residual",
        [VMEM((tok + 8, width), kind)],
        [whole(SMEM), whole(), whole(HBM), whole(HBM)],
        (
            noise_step,
            hidden,
            pltpu.with_memory_space_constraint(gate_table, HBM),
            pltpu.with_memory_space_constraint(packed, HBM),
        ),
        scratch=[VMEM((8, width), jnp.float32), DMA],
    )
    moved = shifted(residual, "tm", -1)

    attended, *hands = run(
        functools.partial(attend_kernel, tm_count, seq_count),
        "attend",
        [HBM((count * tok, wide), kind)] + [VMEM((2, group_tok, wide), kind)] * (tm_count - 1),
        [whole(), whole(), whole(pl.ANY)],
        (pattern, exchanged, moved),
        flops=2 * count * tok * count * tok * wide,
        scratch=[VMEM((tm_count - 1, group_tok, wide), kind), DMA((tm_count,))],
    )
    returned = exchange(attended, axis_index_groups=[out])
    handed = []
    for distance, hand in zip(distances(tm_count), hands):
        route = [(i, partner(i, distance, tm_count)) for i in range(tm_count)]
        handed.append(lax.ppermute(hand, "tm", [(i, j) for i, j in route if j < tm_count - 1]))

    first, *rest = handed
    begun = run(
        functools.partial(cache_kernel, tm_count, seq_count),
        "cache",
        [jax.ShapeDtypeStruct((1, 2, group_tok, tm_count * wide), kind)],
        [whole()] * 2,
        (exchanged, first),
    )
    begun = pltpu.with_memory_space_constraint(begun, HBM)
    advanced, next_cache = run(
        functools.partial(finish_kernel, seq_count, tm_count),
        "finish",
        [HBM((1, tok, width), kind), HBM(begun.shape, kind)],
        [whole()] * 3 + [whole(HBM)] + [whole()] * len(rest),
        (returned, moved, fresh_latent, begun, *rest),
        scratch=[VMEM((1, tok, width), kind), DMA, DMA((len(rest),))],
        aliases={3: 1},
    )
    return (advanced, next_cache)


def absorb(state, query_heads, key_piece, value_piece, scale_factor):
    accum, totals, highest = state
    row_count, head_count, head_dim = query_heads.shape
    key_heads = key_piece.reshape(key_piece.shape[0], head_count, head_dim)
    value_heads = value_piece.reshape(value_piece.shape[0], head_count, head_dim)
    scores = (
        jnp.einsum("qhd,khd->qhk", query_heads, key_heads, preferred_element_type=jnp.float32)
        * scale_factor
    )
    raised = jnp.maximum(highest, jnp.max(scores, axis=-1))
    fade = jnp.exp(highest - raised)
    weights = jnp.exp(scores - raised[..., None])
    totals = totals * fade + jnp.sum(weights, axis=-1)
    accum = accum * fade[..., None] + jnp.einsum(
        "qhk,khd->qhd",
        weights.astype(jnp.bfloat16),
        value_heads,
        preferred_element_type=jnp.float32,
    )
    return (accum, totals, raised)


def gather_body(queries, keys_proj, values, hidden, fresh_latent, gate_table, noise_step, pattern):
    group_index = lax.axis_index("tm")
    final_index = lax.axis_size("tm") - 1
    query_tok, key_tok, value_tok = (
        lax.all_to_all(queries[0], "seq", split_axis=1, concat_axis=0, tiled=True),
        lax.all_to_all(keys_proj[0], "seq", split_axis=1, concat_axis=0, tiled=True),
        lax.all_to_all(values[0], "seq", split_axis=1, concat_axis=0, tiled=True),
    )
    row_count, local_width = query_tok.shape
    head_count = local_width // HD
    query_heads = query_tok.reshape(row_count, head_count, HD)
    scale_factor = 1.0 / math.sqrt(HD)
    reach = lax.dynamic_index_in_dim(pattern, group_index, 0, keepdims=False)
    start_state = (
        jnp.zeros((row_count, head_count, HD), jnp.float32),
        jnp.zeros((row_count, head_count), jnp.float32),
        jnp.full((row_count, head_count), -1e30, jnp.float32),
    )

    def one_block(current, inputs):
        key_block, value_block, flag = inputs
        return (
            lax.cond(
                flag > 0,
                lambda state: absorb(state, query_heads, key_block, value_block, scale_factor),
                lambda state: state,
                current,
            ),
            None,
        )

    key_piece = lax.all_gather(key_tok, "tm", axis=0, tiled=False)
    value_piece = lax.all_gather(value_tok, "tm", axis=0, tiled=False)
    state, unused = lax.scan(one_block, start_state, (key_piece, value_piece, reach))
    cache_keys, cache_values = shifted((key_tok, value_tok), "tm", -1)
    accum, totals, highest = state
    attended_head = (accum / totals[..., None]).reshape(row_count, local_width).astype(jnp.bfloat16)
    attended = lax.all_to_all(attended_head, "seq", split_axis=0, concat_axis=1, tiled=True)
    gate_row = lax.dynamic_index_in_dim(gate_table, noise_step[0], 0, keepdims=False)
    updated = (
        hidden[0].astype(jnp.float32) + gate_row[None, :] * attended.astype(jnp.float32)
    ).astype(jnp.bfloat16)
    moved = shifted(updated, "tm", -1)
    advanced = jnp.where(group_index == final_index, fresh_latent, moved)[None]
    next_cache = jnp.stack([cache_keys, cache_values], axis=0)[None]
    return (advanced, next_cache)


def body(queries, *others):
    tm_count, seq_count = lax.axis_size("tm"), lax.axis_size("seq")
    _, tok, width = queries.shape
    count = tm_count * seq_count
    even = width % (count * HD) == 0 and tok % 8 == 0 and seq_count % 4 == 0 and tm_count > 2 and tm_count % 2 == 0
    return (spread_body if even else gather_body)(queries, *others)


def solution(mesh):
    placed = (
        P("tm", "seq", None),
        P("tm", "seq", None),
        P("tm", "seq", None),
        P("tm", "seq", None),
        P("seq", None),
        P(),
        P("tm"),
        P(),
    )
    return jax.shard_map(
        body,
        mesh=mesh,
        in_specs=placed,
        out_specs=(P("tm", "seq", None), P("tm", None, None, "seq")),
        check_vma=False,
    )
```

```python
import functools
import math

import jax
import jax.numpy as jnp
from jax import lax
from jax.experimental import pallas as pl
from jax.experimental.pallas import tpu as pltpu
from jax.sharding import PartitionSpec as P

HD = 128
BOTH = ("tm", "seq")
VMEM = pltpu.VMEM
SMEM = pltpu.SMEM
HBM = pltpu.HBM


def shifted(block, axis, distance):
    devices = range(lax.axis_size(axis))
    route = [(i - distance, i) for i in devices if i - distance in devices]
    return lax.ppermute(block, axis, route)


def pair_place(group, pair, pairs):
    place = (pair + pairs // 2) % pairs
    return place + group // 2 % 2 * (pairs - 1 - 2 * place)


def out_order(tm_count, seq_count):
    pairs = seq_count // 2
    return [
        (tm, 2 * pair_place(tm, pair, pairs) + member)
        for tm in range(tm_count)
        for pair in range(pairs)
        for member in range(2)
    ]


def pack_kernel(seq_count, parts, q_hbm, k_hbm, v_hbm, out_hbm, held, block, in_sems, out_sems):
    tok, width = held.shape[1:]
    wide = out_hbm.shape[1] // 3
    count = out_hbm.shape[0] // tok
    tm_count = count // seq_count
    span, members = width // parts, seq_count // parts
    order = out_order(tm_count, seq_count)
    copies = []
    for part in range(parts):
        columns = slice(part * span, (part + 1) * span)
        for place, ref in enumerate((q_hbm, k_hbm, v_hbm)):
            copies.append(
                pltpu.make_async_copy(
                    ref.at[0, :, columns], held.at[place, :, columns], in_sems.at[part, place]
                )
            )
            copies[-1].start()
    outs = []
    for part in range(parts):
        for place in range(3):
            copies[3 * part + place].wait()
        for tm in range(tm_count):
            for seq in range(part * members, (part + 1) * members, 2):
                first = order.index((tm, seq)) * tok
                for place in range(3):
                    rows = []
                    for member in (seq, seq + 1):
                        start = (member * tm_count + tm) * wide
                        rows.append(held[place, :, start : start + wide].astype(jnp.float32))
                    block[first : first + 2 * tok, place * wide : (place + 1) * wide] = jnp.concatenate(
                        rows, axis=0
                    ).astype(jnp.bfloat16)
            first = order.index((tm, part * members)) * tok
            rows = slice(first, first + members * tok)
            outs.append(
                pltpu.make_async_copy(block.at[rows], out_hbm.at[rows], out_sems.at[part, tm])
            )
            outs[-1].start()
    for out in outs:
        out.wait()


def residual_kernel(noise_ref, h_ref, gate_hbm, after_ref, out_ref, held, sem):
    step = noise_ref[0]
    steps = gate_hbm.shape[0]
    whole_tiles = steps // 8 * 8
    first = step // 8 * 8

    @pl.when(step < whole_tiles)
    def take_tile():
        rows = pl.ds(pl.multiple_of(first, 8), 8)
        copy = pltpu.make_async_copy(gate_hbm.at[rows], held, sem)
        copy.start()
        copy.wait()

    if steps > whole_tiles:

        @pl.when(step >= whole_tiles)
        def take_rest():
            copy = pltpu.make_async_copy(
                gate_hbm.at[whole_tiles:steps], held.at[0 : steps - whole_tiles], sem
            )
            copy.start()
            copy.wait()

    gate = held[pl.ds(step - first, 1), :]
    high = gate.astype(jnp.bfloat16).astype(jnp.float32)
    middle = (gate - high).astype(jnp.bfloat16).astype(jnp.float32)
    low = gate - high - middle
    parts = jnp.concatenate([high, middle, low, jnp.zeros((5, gate.shape[1]), jnp.float32)], axis=0)
    out_ref[...] = jnp.concatenate([h_ref[0].astype(jnp.float32), parts], axis=0).astype(jnp.bfloat16)


def partner(here, distance, groups):
    return here ^ distance if groups & (groups - 1) == 0 else (here + groups - distance) % groups


def distances(groups):
    return sorted(range(1, groups), key=lambda distance: (distance < groups // 2, distance))


def hand_over(group, seq_count, x_ref, out_ref, lanes=slice(None)):
    wide = x_ref.shape[1] // 3
    pairs = seq_count // 2
    step = out_ref.shape[1] // pairs
    for pair in range(pairs):
        first = pl.multiple_of((group * pairs + pair_place(group, pair, pairs)) * step, step)
        for kind in range(2):
            out_ref[kind, pair * step : (pair + 1) * step, lanes] = x_ref[
                pl.ds(first, step), (kind + 1) * wide : (kind + 2) * wide
            ]


def attend_kernel(groups, seq_count, pattern_ref, x_ref, after_ref, out_hbm, *refs):
    *hand_refs, held, sems = refs
    wide = held.shape[2]
    rows = held.shape[1]
    pairs = seq_count // 2
    step = rows // pairs
    across = (groups - 1) * rows
    factor = math.log2(math.e) / math.sqrt(HD)
    here = lax.axis_index("tm")
    lane = lax.broadcasted_iota(jnp.int32, (1, across), 1)
    ends, kept = [], []
    for source in range(groups):
        first = max(source, 1)
        ends.append(min(across, -(-(groups - first) * rows // 128) * 128))
        chosen = jnp.zeros((1, across), jnp.int32)
        for group in range(first, groups):
            start = (groups - 1 - group) * rows
            flag = pattern_ref[group : group + 1, source : source + 1]
            chosen = jnp.where((lane >= start) & (lane < start + rows), flag, chosen)
        kept.append(chosen[:, : ends[-1]] > 0)

    def take(group, first):
        return x_ref[group * rows : (group + 1) * rows, first : first + HD]

    copies = []

    def send(group):
        for place in (group - 1, groups - 1) if group == groups - 1 else (group - 1,):
            copies.append(
                pltpu.make_async_copy(
                    held.at[group - 1], out_hbm.at[place * rows : (place + 1) * rows], sems.at[place]
                )
            )
            copies[-1].start()

    def spread(row, fill):
        rest = across - row.shape[1]
        return jnp.concatenate([row, jnp.full((1, rest), fill, row.dtype)], axis=1) if rest else row

    for head in range(0, wide, HD):
        query = jnp.concatenate(
            [take(group, head) for group in range(groups - 1, 0, -1)], axis=0
        )
        query = jnp.transpose(query)
        value = jnp.transpose(
            jnp.concatenate([take(group, 2 * wide + head) for group in range(groups)], axis=0)
        )
        scores, highest = [], None
        for source in range(groups):
            key = take(source, wide + head)
            scores.append(
                jnp.dot(key, query[:, : ends[source]], preferred_element_type=jnp.float32)
            )
            peak = jnp.where(kept[source], jnp.max(scores[-1], axis=0, keepdims=True), -1e30)
            peak = spread(peak, -1e30)
            highest = peak if highest is None else jnp.maximum(highest, peak)
        highest = highest * factor
        total, probs = 0.0, []
        for source in range(groups):
            offset = jnp.where(kept[source], -highest[:, : ends[source]], -1e30)
            raised = jnp.exp2(scores[source] * factor + offset)
            total += spread(jnp.sum(raised, axis=0, keepdims=True), 0.0)
            probs.append(raised.astype(jnp.bfloat16))
        inverse = 1.0 / total
        last = head + HD == wide
        start, left, waiting = 0, None, groups - 1
        for source in range(groups - 1, 0, -1):
            stop = ends[source]
            if stop > start:
                numer = jnp.dot(
                    value[:, : (source + 1) * rows],
                    jnp.concatenate([p[:, start:stop] for p in probs[: source + 1]], axis=0),
                    preferred_element_type=jnp.float32,
                )
                result = jnp.transpose(numer * inverse[:, start:stop])
                left = result if left is None else jnp.concatenate([left, result], axis=0)
                start = stop
            while left is not None and left.shape[0] >= rows:
                ready = left[:rows].astype(jnp.bfloat16)
                for pair in range(pairs):
                    at = pair_place(waiting, pair, pairs) * step
                    to = pair_place(waiting - 1, pair, pairs) * step
                    held[waiting - 1, to : to + step, head : head + HD] = ready[at : at + step]
                left = left[rows:] if left.shape[0] > rows else None
                if last:
                    send(waiting)
                waiting -= 1
    for distance, hand_ref in zip(distances(groups), hand_refs):
        hand_over(lax.rem(partner(here, distance, groups) + 1, groups), seq_count, x_ref, hand_ref)
    for copy in copies:
        copy.wait()


def lanes_of(distance, groups, here, wide):
    source = partner(here, groups - distance if groups & (groups - 1) else distance, groups)
    return pl.ds(pl.multiple_of(source * wide, wide), wide)


def cache_kernel(groups, seq_count, x_ref, hand_ref, out_ref):
    wide = x_ref.shape[1] // 3
    here = lax.axis_index("tm")
    out_ref[...] = jnp.zeros_like(out_ref)

    @pl.when(here < groups - 1)
    def place():
        hand_over(here + 1, seq_count, x_ref, out_ref.at[0], lanes_of(0, groups, here, wide))
        out_ref[0, :, :, lanes_of(distances(groups)[0], groups, here, wide)] = hand_ref[...]


def finish_kernel(seq_count, tm_count, att_ref, moved_ref, fresh_ref, begun_hbm, *refs):
    *hand_refs, out_hbm, cache_hbm, held, sem, sems = refs
    tok = held.shape[1]
    wide = att_ref.shape[1]
    count = att_ref.shape[0] // tok
    order = out_order(tm_count, seq_count)
    here = lax.axis_index("tm")
    last = here == tm_count - 1
    copies = [
        pltpu.make_async_copy(
            block, cache_hbm.at[0, :, :, lanes_of(distance, tm_count, here, block.shape[2])], sems.at[index]
        )
        for index, (distance, block) in enumerate(zip(distances(tm_count)[1:], hand_refs))
    ]

    @pl.when(last)
    def take_fresh():
        copy = pltpu.make_async_copy(fresh_ref, out_hbm.at[0], sem)
        copy.start()
        copy.wait()

    @pl.when(jnp.logical_not(last))
    def take_update():
        for copy in copies:
            copy.start()
        for pair in range(count // 2):
            rows = att_ref[2 * pair * tok : 2 * (pair + 1) * tok, :].astype(jnp.float32)
            for half in range(2):
                tm, seq = order[2 * pair + half]
                start = (seq * tm_count + tm) * wide
                moved = moved_ref[:, start : start + wide].astype(jnp.float32)
                gate = (moved[tok : tok + 1] + moved[tok + 1 : tok + 2]) + moved[tok + 2 : tok + 3]
                result = moved[:tok] + gate * rows[half * tok : (half + 1) * tok]
                held[0, :, start : start + wide] = result.astype(jnp.bfloat16)
        copy = pltpu.make_async_copy(held, out_hbm, sem)
        copy.start()
        copy.wait()
        for copy in copies:
            copy.wait()


def whole(space=VMEM):
    return pl.BlockSpec(memory_space=space)


def run(kernel, name, outs, specs, operands, flops=0, scratch=(), aliases={}):
    def size(a):
        return math.prod(a.shape) * jnp.dtype(a.dtype).itemsize

    moved = sum(map(size, operands)) + sum(map(size, outs))
    results = pl.pallas_call(
        kernel,
        out_shape=outs,
        in_specs=specs,
        out_specs=[whole(getattr(a, "memory_space", VMEM)) for a in outs],
        scratch_shapes=scratch,
        input_output_aliases=aliases,
        compiler_params=pltpu.CompilerParams(vmem_limit_bytes=4 * moved + (4 << 20)),
        cost_estimate=pl.CostEstimate(flops=flops, bytes_accessed=moved, transcendentals=0),
        name=name,
    )(*operands)
    return results if len(outs) > 1 else results[0]


def spread_body(queries, keys_proj, values, hidden, fresh_latent, gate_table, noise_step, pattern):
    tm_count, seq_count = lax.axis_size("tm"), lax.axis_size("seq")
    count = tm_count * seq_count
    _, tok, width = queries.shape
    wide = width // count
    group_tok = tok * seq_count
    kind = queries.dtype
    DMA = pltpu.SemaphoreType.DMA
    parts = seq_count // 2

    packed = run(
        functools.partial(pack_kernel, seq_count, parts),
        "pack",
        [HBM((count * tok, 3 * wide), kind)],
        [whole(HBM)] * 3,
        [pltpu.with_memory_space_constraint(a, HBM) for a in (queries, keys_proj, values)],
        scratch=[
            VMEM((3, tok, width), kind),
            VMEM((count * tok, 3 * wide), kind),
            DMA((parts, 3)),
            DMA((parts, tm_count)),
        ],
    )
    out = [tm * seq_count + index for tm, index in out_order(tm_count, seq_count)]
    exchange = functools.partial(
        lax.all_to_all, axis_name=BOTH, split_axis=0, concat_axis=0, tiled=True
    )
    exchanged = exchange(packed, axis_index_groups=[out])

    residual = run(
        residual_kernel,
        "residual",
        [VMEM((tok + 8, width), kind)],
        [whole(SMEM), whole(), whole(HBM), whole(HBM)],
        (
            noise_step,
            hidden,
            pltpu.with_memory_space_constraint(gate_table, HBM),
            pltpu.with_memory_space_constraint(packed, HBM),
        ),
        scratch=[VMEM((8, width), jnp.float32), DMA],
    )
    moved = shifted(residual, "tm", -1)

    attended, *hands = run(
        functools.partial(attend_kernel, tm_count, seq_count),
        "attend",
        [HBM((count * tok, wide), kind)] + [VMEM((2, group_tok, wide), kind)] * (tm_count - 1),
        [whole(), whole(), whole(pl.ANY)],
        (pattern, exchanged, moved),
        flops=2 * count * tok * count * tok * wide,
        scratch=[VMEM((tm_count - 1, group_tok, wide), kind), DMA((tm_count,))],
    )
    returned = exchange(attended, axis_index_groups=[out])
    handed = []
    for distance, hand in zip(distances(tm_count), hands):
        route = [(i, partner(i, distance, tm_count)) for i in range(tm_count)]
        handed.append(lax.ppermute(hand, "tm", [(i, j) for i, j in route if j < tm_count - 1]))

    first, *rest = handed
    begun = run(
        functools.partial(cache_kernel, tm_count, seq_count),
        "cache",
        [jax.ShapeDtypeStruct((1, 2, group_tok, tm_count * wide), kind)],
        [whole()] * 2,
        (exchanged, first),
    )
    begun = pltpu.with_memory_space_constraint(begun, HBM)
    advanced, next_cache = run(
        functools.partial(finish_kernel, seq_count, tm_count),
        "finish",
        [HBM((1, tok, width), kind), HBM(begun.shape, kind)],
        [whole()] * 3 + [whole(HBM)] + [whole()] * len(rest),
        (returned, moved, fresh_latent, begun, *rest),
        scratch=[VMEM((1, tok, width), kind), DMA, DMA((len(rest),))],
        aliases={3: 1},
    )
    return (advanced, next_cache)


def absorb(state, query_heads, key_piece, value_piece, scale_factor):
    accum, totals, highest = state
    row_count, head_count, head_dim = query_heads.shape
    key_heads = key_piece.reshape(key_piece.shape[0], head_count, head_dim)
    value_heads = value_piece.reshape(value_piece.shape[0], head_count, head_dim)
    scores = (
        jnp.einsum("qhd,khd->qhk", query_heads, key_heads, preferred_element_type=jnp.float32)
        * scale_factor
    )
    raised = jnp.maximum(highest, jnp.max(scores, axis=-1))
    fade = jnp.exp(highest - raised)
    weights = jnp.exp(scores - raised[..., None])
    totals = totals * fade + jnp.sum(weights, axis=-1)
    accum = accum * fade[..., None] + jnp.einsum(
        "qhk,khd->qhd",
        weights.astype(jnp.bfloat16),
        value_heads,
        preferred_element_type=jnp.float32,
    )
    return (accum, totals, raised)


def gather_body(queries, keys_proj, values, hidden, fresh_latent, gate_table, noise_step, pattern):
    group_index = lax.axis_index("tm")
    final_index = lax.axis_size("tm") - 1
    query_tok, key_tok, value_tok = (
        lax.all_to_all(queries[0], "seq", split_axis=1, concat_axis=0, tiled=True),
        lax.all_to_all(keys_proj[0], "seq", split_axis=1, concat_axis=0, tiled=True),
        lax.all_to_all(values[0], "seq", split_axis=1, concat_axis=0, tiled=True),
    )
    row_count, local_width = query_tok.shape
    head_count = local_width // HD
    query_heads = query_tok.reshape(row_count, head_count, HD)
    scale_factor = 1.0 / math.sqrt(HD)
    reach = lax.dynamic_index_in_dim(pattern, group_index, 0, keepdims=False)
    start_state = (
        jnp.zeros((row_count, head_count, HD), jnp.float32),
        jnp.zeros((row_count, head_count), jnp.float32),
        jnp.full((row_count, head_count), -1e30, jnp.float32),
    )

    def one_block(current, inputs):
        key_block, value_block, flag = inputs
        return (
            lax.cond(
                flag > 0,
                lambda state: absorb(state, query_heads, key_block, value_block, scale_factor),
                lambda state: state,
                current,
            ),
            None,
        )

    key_piece = lax.all_gather(key_tok, "tm", axis=0, tiled=False)
    value_piece = lax.all_gather(value_tok, "tm", axis=0, tiled=False)
    state, unused = lax.scan(one_block, start_state, (key_piece, value_piece, reach))
    cache_keys, cache_values = shifted((key_tok, value_tok), "tm", -1)
    accum, totals, highest = state
    attended_head = (accum / totals[..., None]).reshape(row_count, local_width).astype(jnp.bfloat16)
    attended = lax.all_to_all(attended_head, "seq", split_axis=0, concat_axis=1, tiled=True)
    gate_row = lax.dynamic_index_in_dim(gate_table, noise_step[0], 0, keepdims=False)
    updated = (
        hidden[0].astype(jnp.float32) + gate_row[None, :] * attended.astype(jnp.float32)
    ).astype(jnp.bfloat16)
    moved = shifted(updated, "tm", -1)
    advanced = jnp.where(group_index == final_index, fresh_latent, moved)[None]
    next_cache = jnp.stack([cache_keys, cache_values], axis=0)[None]
    return (advanced, next_cache)


def body(queries, *others):
    tm_count, seq_count = lax.axis_size("tm"), lax.axis_size("seq")
    _, tok, width = queries.shape
    count = tm_count * seq_count
    even = width % (count * HD) == 0 and tok % 8 == 0 and seq_count % 4 == 0 and tm_count > 2 and tm_count % 2 == 0
    return (spread_body if even else gather_body)(queries, *others)


def solution(mesh):
    placed = (
        P("tm", "seq", None),
        P("tm", "seq", None),
        P("tm", "seq", None),
        P("tm", "seq", None),
        P("seq", None),
        P(),
        P("tm"),
        P(),
    )
    return jax.shard_map(
        body,
        mesh=mesh,
        in_specs=placed,
        out_specs=(P("tm", "seq", None), P("tm", None, None, "seq")),
        check_vma=False,
    )
```

```python
import functools
import math

import jax
import jax.numpy as jnp
from jax import lax
from jax.experimental import pallas as pl
from jax.experimental.pallas import tpu as pltpu
from jax.sharding import PartitionSpec as P

HD = 128
BOTH = ("tm", "seq")
VMEM = pltpu.VMEM
SMEM = pltpu.SMEM
HBM = pltpu.HBM


def shifted(block, axis, distance):
    devices = range(lax.axis_size(axis))
    route = [(i - distance, i) for i in devices if i - distance in devices]
    return lax.ppermute(block, axis, route)


def pair_place(group, pair, pairs):
    return pair + group // 2 % 2 * (pairs - 1 - 2 * pair)


def out_order(tm_count, seq_count):
    pairs = seq_count // 2
    return [
        (tm, 2 * pair_place(tm, pair, pairs) + member)
        for tm in range(tm_count)
        for pair in range(pairs)
        for member in range(2)
    ]


def pack_kernel(seq_count, parts, q_hbm, k_hbm, v_hbm, out_hbm, held, block, in_sems, out_sems):
    tok, width = held.shape[1:]
    wide = out_hbm.shape[1] // 3
    count = out_hbm.shape[0] // tok
    tm_count = count // seq_count
    span, members = width // parts, seq_count // parts
    order = out_order(tm_count, seq_count)
    copies = []
    for part in range(parts):
        columns = slice(part * span, (part + 1) * span)
        for place, ref in enumerate((q_hbm, k_hbm, v_hbm)):
            copies.append(
                pltpu.make_async_copy(
                    ref.at[0, :, columns], held.at[place, :, columns], in_sems.at[part, place]
                )
            )
            copies[-1].start()
    outs = []
    for part in range(parts):
        for place in range(3):
            copies[3 * part + place].wait()
        for tm in range(tm_count):
            for seq in range(part * members, (part + 1) * members, 2):
                first = order.index((tm, seq)) * tok
                for place in range(3):
                    rows = []
                    for member in (seq, seq + 1):
                        start = (member * tm_count + tm) * wide
                        rows.append(held[place, :, start : start + wide].astype(jnp.float32))
                    block[first : first + 2 * tok, place * wide : (place + 1) * wide] = jnp.concatenate(
                        rows, axis=0
                    ).astype(jnp.bfloat16)
            first = order.index((tm, part * members)) * tok
            rows = slice(first, first + members * tok)
            outs.append(
                pltpu.make_async_copy(block.at[rows], out_hbm.at[rows], out_sems.at[part, tm])
            )
            outs[-1].start()
    for out in outs:
        out.wait()


def residual_kernel(noise_ref, h_ref, gate_hbm, after_ref, out_ref, held, sem):
    step = noise_ref[0]
    steps = gate_hbm.shape[0]
    whole_tiles = steps // 8 * 8
    first = step // 8 * 8

    @pl.when(step < whole_tiles)
    def take_tile():
        rows = pl.ds(pl.multiple_of(first, 8), 8)
        copy = pltpu.make_async_copy(gate_hbm.at[rows], held, sem)
        copy.start()
        copy.wait()

    if steps > whole_tiles:

        @pl.when(step >= whole_tiles)
        def take_rest():
            copy = pltpu.make_async_copy(
                gate_hbm.at[whole_tiles:steps], held.at[0 : steps - whole_tiles], sem
            )
            copy.start()
            copy.wait()

    gate = held[pl.ds(step - first, 1), :]
    high = gate.astype(jnp.bfloat16).astype(jnp.float32)
    middle = (gate - high).astype(jnp.bfloat16).astype(jnp.float32)
    low = gate - high - middle
    parts = jnp.concatenate([high, middle, low, jnp.zeros((5, gate.shape[1]), jnp.float32)], axis=0)
    out_ref[...] = jnp.concatenate([h_ref[0].astype(jnp.float32), parts], axis=0).astype(jnp.bfloat16)


def partner(here, distance, groups):
    return here ^ distance if groups & (groups - 1) == 0 else (here + groups - distance) % groups


def distances(groups):
    return range(groups - 1, 0, -1)


def hand_over(group, seq_count, x_ref, out_ref, lanes=slice(None)):
    wide = x_ref.shape[1] // 3
    pairs = seq_count // 2
    step = out_ref.shape[1] // pairs
    for pair in range(pairs):
        first = pl.multiple_of((group * pairs + pair_place(group, pair, pairs)) * step, step)
        for kind in range(2):
            out_ref[kind, pair * step : (pair + 1) * step, lanes] = x_ref[
                pl.ds(first, step), (kind + 1) * wide : (kind + 2) * wide
            ]


def attend_kernel(groups, seq_count, pattern_ref, x_ref, after_ref, out_hbm, *refs):
    *hand_refs, held, sems = refs
    wide = held.shape[2]
    rows = held.shape[1]
    pairs = seq_count // 2
    step = rows // pairs
    across = (groups - 1) * rows
    factor = math.log2(math.e) / math.sqrt(HD)
    here = lax.axis_index("tm")
    lane = lax.broadcasted_iota(jnp.int32, (1, across), 1)
    ends, kept = [], []
    for source in range(groups):
        first = max(source, 1)
        ends.append(min(across, -(-(groups - first) * rows // 128) * 128))
        chosen = jnp.zeros((1, across), jnp.int32)
        for group in range(first, groups):
            start = (groups - 1 - group) * rows
            flag = pattern_ref[group : group + 1, source : source + 1]
            chosen = jnp.where((lane >= start) & (lane < start + rows), flag, chosen)
        kept.append(chosen[:, : ends[-1]] > 0)

    def take(group, first):
        return x_ref[group * rows : (group + 1) * rows, first : first + HD]

    copies = []

    def send(group):
        for place in (group - 1, groups - 1) if group == groups - 1 else (group - 1,):
            copies.append(
                pltpu.make_async_copy(
                    held.at[group - 1], out_hbm.at[place * rows : (place + 1) * rows], sems.at[place]
                )
            )
            copies[-1].start()

    def spread(row, fill):
        rest = across - row.shape[1]
        return jnp.concatenate([row, jnp.full((1, rest), fill, row.dtype)], axis=1) if rest else row

    for head in range(0, wide, HD):
        query = jnp.concatenate(
            [take(group, head) for group in range(groups - 1, 0, -1)], axis=0
        )
        query = jnp.transpose(query)
        value = jnp.transpose(
            jnp.concatenate([take(group, 2 * wide + head) for group in range(groups)], axis=0)
        )
        scores, highest = [], None
        for source in range(groups):
            key = take(source, wide + head)
            scores.append(
                jnp.dot(key, query[:, : ends[source]], preferred_element_type=jnp.float32)
            )
            peak = jnp.where(kept[source], jnp.max(scores[-1], axis=0, keepdims=True), -1e30)
            peak = spread(peak, -1e30)
            highest = peak if highest is None else jnp.maximum(highest, peak)
        highest = highest * factor
        total, probs = 0.0, []
        for source in range(groups):
            offset = jnp.where(kept[source], -highest[:, : ends[source]], -1e30)
            raised = jnp.exp2(scores[source] * factor + offset)
            total += spread(jnp.sum(raised, axis=0, keepdims=True), 0.0)
            probs.append(raised.astype(jnp.bfloat16))
        inverse = 1.0 / total
        last = head + HD == wide
        start, left, waiting = 0, None, groups - 1
        for source in range(groups - 1, 0, -1):
            stop = ends[source]
            if stop > start:
                numer = jnp.dot(
                    value[:, : (source + 1) * rows],
                    jnp.concatenate([p[:, start:stop] for p in probs[: source + 1]], axis=0),
                    preferred_element_type=jnp.float32,
                )
                result = jnp.transpose(numer * inverse[:, start:stop])
                left = result if left is None else jnp.concatenate([left, result], axis=0)
                start = stop
            while left is not None and left.shape[0] >= rows:
                ready = left[:rows].astype(jnp.bfloat16)
                for pair in range(pairs):
                    at = pair_place(waiting, pair, pairs) * step
                    to = pair_place(waiting - 1, pair, pairs) * step
                    held[waiting - 1, to : to + step, head : head + HD] = ready[at : at + step]
                left = left[rows:] if left.shape[0] > rows else None
                if last:
                    send(waiting)
                waiting -= 1
    for distance, hand_ref in zip(distances(groups), hand_refs):
        hand_over(lax.rem(partner(here, distance, groups) + 1, groups), seq_count, x_ref, hand_ref)
    for copy in copies:
        copy.wait()


def lanes_of(distance, groups, here, wide):
    source = partner(here, groups - distance if groups & (groups - 1) else distance, groups)
    return pl.ds(pl.multiple_of(source * wide, wide), wide)


def cache_kernel(groups, seq_count, x_ref, hand_ref, out_ref):
    wide = x_ref.shape[1] // 3
    here = lax.axis_index("tm")
    out_ref[...] = jnp.zeros_like(out_ref)

    @pl.when(here < groups - 1)
    def place():
        hand_over(here + 1, seq_count, x_ref, out_ref.at[0], lanes_of(0, groups, here, wide))
        out_ref[0, :, :, lanes_of(distances(groups)[0], groups, here, wide)] = hand_ref[...]


def cache_rest_kernel(groups, begun_hbm, after_ref, *refs):
    *hand_refs, out_hbm, sems = refs
    here = lax.axis_index("tm")

    @pl.when(here < groups - 1)
    def place():
        copies = [
            pltpu.make_async_copy(
                block, out_hbm.at[0, :, :, lanes_of(distance, groups, here, block.shape[2])], sems.at[index]
            )
            for index, (distance, block) in enumerate(zip(distances(groups)[1:], hand_refs))
        ]
        for copy in copies:
            copy.start()
        for copy in copies:
            copy.wait()


def update_kernel(seq_count, tm_count, att_ref, moved_ref, fresh_ref, after_ref, out_ref):
    tok = out_ref.shape[1]
    wide = att_ref.shape[1]
    count = att_ref.shape[0] // tok
    order = out_order(tm_count, seq_count)
    last = lax.axis_index("tm") == tm_count - 1

    @pl.when(last)
    def take_fresh():
        out_ref[0] = fresh_ref[...]

    @pl.when(jnp.logical_not(last))
    def take_update():
        for pair in range(count // 2):
            rows = att_ref[2 * pair * tok : 2 * (pair + 1) * tok, :].astype(jnp.float32)
            for half in range(2):
                source = 2 * pair + half
                tm, seq = order[source]
                start = (seq * tm_count + tm) * wide
                moved = moved_ref[:, start : start + wide].astype(jnp.float32)
                gate = (moved[tok : tok + 1] + moved[tok + 1 : tok + 2]) + moved[tok + 2 : tok + 3]
                result = moved[:tok] + gate * rows[half * tok : (half + 1) * tok]
                out_ref[0, :, start : start + wide] = result.astype(jnp.bfloat16)


def whole(space=VMEM):
    return pl.BlockSpec(memory_space=space)


def run(kernel, name, outs, specs, operands, flops=0, scratch=(), aliases={}):
    def size(a):
        return math.prod(a.shape) * jnp.dtype(a.dtype).itemsize

    moved = sum(map(size, operands)) + sum(map(size, outs))
    results = pl.pallas_call(
        kernel,
        out_shape=outs,
        in_specs=specs,
        out_specs=[whole(getattr(a, "memory_space", VMEM)) for a in outs],
        scratch_shapes=scratch,
        input_output_aliases=aliases,
        compiler_params=pltpu.CompilerParams(vmem_limit_bytes=4 * moved + (4 << 20)),
        cost_estimate=pl.CostEstimate(flops=flops, bytes_accessed=moved, transcendentals=0),
        name=name,
    )(*operands)
    return results if len(outs) > 1 else results[0]


def spread_body(queries, keys_proj, values, hidden, fresh_latent, gate_table, noise_step, pattern):
    tm_count, seq_count = lax.axis_size("tm"), lax.axis_size("seq")
    count = tm_count * seq_count
    _, tok, width = queries.shape
    wide = width // count
    group_tok = tok * seq_count
    kind = queries.dtype
    DMA = pltpu.SemaphoreType.DMA
    parts = seq_count // 2

    packed = run(
        functools.partial(pack_kernel, seq_count, parts),
        "pack",
        [HBM((count * tok, 3 * wide), kind)],
        [whole(HBM)] * 3,
        [pltpu.with_memory_space_constraint(a, HBM) for a in (queries, keys_proj, values)],
        scratch=[
            VMEM((3, tok, width), kind),
            VMEM((count * tok, 3 * wide), kind),
            DMA((parts, 3)),
            DMA((parts, tm_count)),
        ],
    )
    out = [tm * seq_count + index for tm, index in out_order(tm_count, seq_count)]
    exchange = functools.partial(
        lax.all_to_all, axis_name=BOTH, split_axis=0, concat_axis=0, tiled=True
    )
    exchanged = exchange(packed, axis_index_groups=[out])

    residual = run(
        residual_kernel,
        "residual",
        [VMEM((tok + 8, width), kind)],
        [whole(SMEM), whole(), whole(HBM), whole(HBM)],
        (
            noise_step,
            hidden,
            pltpu.with_memory_space_constraint(gate_table, HBM),
            pltpu.with_memory_space_constraint(packed, HBM),
        ),
        scratch=[VMEM((8, width), jnp.float32), DMA],
    )
    moved = shifted(residual, "tm", -1)

    attended, *hands = run(
        functools.partial(attend_kernel, tm_count, seq_count),
        "attend",
        [HBM((count * tok, wide), kind)] + [VMEM((2, group_tok, wide), kind)] * (tm_count - 1),
        [whole(), whole(), whole(pl.ANY)],
        (pattern, exchanged, moved),
        flops=2 * count * tok * count * tok * wide,
        scratch=[VMEM((tm_count - 1, group_tok, wide), kind), DMA((tm_count,))],
    )
    returned = exchange(attended, axis_index_groups=[out])
    handed = []
    for distance, hand in zip(distances(tm_count), hands):
        route = [(i, partner(i, distance, tm_count)) for i in range(tm_count)]
        handed.append(lax.ppermute(hand, "tm", [(i, j) for i, j in route if j < tm_count - 1]))

    first, *rest = handed
    begun = run(
        functools.partial(cache_kernel, tm_count, seq_count),
        "cache",
        [jax.ShapeDtypeStruct((1, 2, group_tok, tm_count * wide), kind)],
        [whole()] * 2,
        (exchanged, first),
    )
    begun = pltpu.with_memory_space_constraint(begun, HBM)
    advanced = run(
        functools.partial(update_kernel, seq_count, tm_count),
        "update",
        [jax.ShapeDtypeStruct((1, tok, width), kind)],
        [whole()] * 3 + [whole(HBM)],
        (returned, moved, fresh_latent, begun),
    )
    next_cache = run(
        functools.partial(cache_rest_kernel, tm_count),
        "cache_rest",
        [HBM(begun.shape, kind)],
        [whole(HBM)] * 2 + [whole()] * len(rest),
        (begun, pltpu.with_memory_space_constraint(advanced, HBM), *rest),
        scratch=[DMA((len(rest),))],
        aliases={0: 0},
    )
    return (advanced, next_cache)


def absorb(state, query_heads, key_piece, value_piece, scale_factor):
    accum, totals, highest = state
    row_count, head_count, head_dim = query_heads.shape
    key_heads = key_piece.reshape(key_piece.shape[0], head_count, head_dim)
    value_heads = value_piece.reshape(value_piece.shape[0], head_count, head_dim)
    scores = (
        jnp.einsum("qhd,khd->qhk", query_heads, key_heads, preferred_element_type=jnp.float32)
        * scale_factor
    )
    raised = jnp.maximum(highest, jnp.max(scores, axis=-1))
    fade = jnp.exp(highest - raised)
    weights = jnp.exp(scores - raised[..., None])
    totals = totals * fade + jnp.sum(weights, axis=-1)
    accum = accum * fade[..., None] + jnp.einsum(
        "qhk,khd->qhd",
        weights.astype(jnp.bfloat16),
        value_heads,
        preferred_element_type=jnp.float32,
    )
    return (accum, totals, raised)


def gather_body(queries, keys_proj, values, hidden, fresh_latent, gate_table, noise_step, pattern):
    group_index = lax.axis_index("tm")
    final_index = lax.axis_size("tm") - 1
    query_tok, key_tok, value_tok = (
        lax.all_to_all(queries[0], "seq", split_axis=1, concat_axis=0, tiled=True),
        lax.all_to_all(keys_proj[0], "seq", split_axis=1, concat_axis=0, tiled=True),
        lax.all_to_all(values[0], "seq", split_axis=1, concat_axis=0, tiled=True),
    )
    row_count, local_width = query_tok.shape
    head_count = local_width // HD
    query_heads = query_tok.reshape(row_count, head_count, HD)
    scale_factor = 1.0 / math.sqrt(HD)
    reach = lax.dynamic_index_in_dim(pattern, group_index, 0, keepdims=False)
    start_state = (
        jnp.zeros((row_count, head_count, HD), jnp.float32),
        jnp.zeros((row_count, head_count), jnp.float32),
        jnp.full((row_count, head_count), -1e30, jnp.float32),
    )

    def one_block(current, inputs):
        key_block, value_block, flag = inputs
        return (
            lax.cond(
                flag > 0,
                lambda state: absorb(state, query_heads, key_block, value_block, scale_factor),
                lambda state: state,
                current,
            ),
            None,
        )

    key_piece = lax.all_gather(key_tok, "tm", axis=0, tiled=False)
    value_piece = lax.all_gather(value_tok, "tm", axis=0, tiled=False)
    state, unused = lax.scan(one_block, start_state, (key_piece, value_piece, reach))
    cache_keys, cache_values = shifted((key_tok, value_tok), "tm", -1)
    accum, totals, highest = state
    attended_head = (accum / totals[..., None]).reshape(row_count, local_width).astype(jnp.bfloat16)
    attended = lax.all_to_all(attended_head, "seq", split_axis=0, concat_axis=1, tiled=True)
    gate_row = lax.dynamic_index_in_dim(gate_table, noise_step[0], 0, keepdims=False)
    updated = (
        hidden[0].astype(jnp.float32) + gate_row[None, :] * attended.astype(jnp.float32)
    ).astype(jnp.bfloat16)
    moved = shifted(updated, "tm", -1)
    advanced = jnp.where(group_index == final_index, fresh_latent, moved)[None]
    next_cache = jnp.stack([cache_keys, cache_values], axis=0)[None]
    return (advanced, next_cache)


def body(queries, *others):
    tm_count, seq_count = lax.axis_size("tm"), lax.axis_size("seq")
    _, tok, width = queries.shape
    count = tm_count * seq_count
    even = width % (count * HD) == 0 and tok % 8 == 0 and seq_count % 4 == 0 and tm_count > 2 and tm_count % 2 == 0
    return (spread_body if even else gather_body)(queries, *others)


def solution(mesh):
    placed = (
        P("tm", "seq", None),
        P("tm", "seq", None),
        P("tm", "seq", None),
        P("tm", "seq", None),
        P("seq", None),
        P(),
        P("tm"),
        P(),
    )
    return jax.shard_map(
        body,
        mesh=mesh,
        in_specs=placed,
        out_specs=(P("tm", "seq", None), P("tm", None, None, "seq")),
        check_vma=False,
    )
```
